256 devices in a mesh: dp: 16 (over z, y_lo), seq: 16 (over x, y_hi, core).
Axes of the slice: x: 4, y: 4 (y_hi: 2, y_lo: 2; y = y_hi * 2 + y_lo), z: 8, core: 2. Of those that a mesh axis runs over, the one named last changes fastest.
Arguments:
- question_embedding_matrix: bfloat16 [512, 4096], P(('dp', 'seq'))
- passage_embedding_matrix: bfloat16 [512, 4096], P(('dp', 'seq'))
- positive: int32 [512], P(('dp', 'seq')), may hold values from 0 to 511
- queries: bfloat16 [16, 2048, 2048], P('dp', 'seq')
- keys: bfloat16 [16, 2048, 512], P('dp', 'seq')
- values: bfloat16 [16, 2048, 512], P('dp', 'seq'), may hold values from -6 to 6
- later_grad: bfloat16 [16, 2048, 2048], P('dp', 'seq'), may hold values from -6 to 6
- lengths: int32 [16], P('dp'), may hold values from 1 to 2048, 24576 in all
- q_gain: float32 [128], replicated, may hold values from 0.5 to 5
- k_gain: float32 [128], replicated, may hold values from 0.5 to 5
- out_weight: bfloat16 [2048, 4096], P('seq', 'dp'), may hold values from -0.09375 to 0.09375
Outputs:
- mean_loss: float32 [], replicated
- query_grad: bfloat16 [512, 4096], P(('dp', 'seq'))
- doc_grad: bfloat16 [512, 4096], P(('dp', 'seq'))
- query_cot: bfloat16 [16, 2048, 2048], P('dp', 'seq')
- key_cot: bfloat16 [16, 2048, 512], P('dp', 'seq')
- value_cot: bfloat16 [16, 2048, 512], P('dp', 'seq')
- q_gain_grad: float32 [128], replicated
- k_gain_grad: float32 [128], replicated
The draws below stay inside these ranges and needn't reach their ends.
Inputs may be any that keep to these rules, and one draw needn't show every extreme that they name: `lengths`: every document has at least one valid token; the longest has exactly 2048.
All inputs are finite; a program needn't handle non-finite values. No bound on the sum of `lengths` on one device may be relied on, other than what follows from the above.
Results may differ from the reference program's by a relative error of at most 0.014.
The reference program's roundings to bfloat16 on the way count: a program that leaves them out, or rounds other values in their place, can miss the bound.
Values may be sent and summed in bfloat16 or wider, within the bound.
A program may use at most 128 MiB of HBM per device.

```python
import math
import jax
import jax.numpy as jnp
import numpy as np
from jax import lax

D = 4096
H = 16
KV = 4
HD = 128
S = 2048
DOCS = 16
PAIRS = 512


def embed_pair(key):
    query_part = 0.048 * jax.random.normal(jax.random.fold_in(key, 101), (PAIRS, D), jnp.float32)
    doc_part = 0.048 * jax.random.normal(jax.random.fold_in(key, 102), (PAIRS, D), jnp.float32)
    return (query_part, doc_part)


def attention_pair(key):
    query_part = jax.random.normal(jax.random.fold_in(key, 201), (DOCS, S, H * HD), jnp.float32)
    key_part = jax.random.normal(jax.random.fold_in(key, 202), (DOCS, S, KV * HD), jnp.float32)
    return (query_part, key_part)


def draw_question_embedding_matrix(key, part):
    query_part, doc_part = embed_pair(key)
    return query_part.astype(jnp.bfloat16)


def draw_passage_embedding_matrix(key, part):
    query_part, doc_part = embed_pair(key)
    return doc_part.astype(jnp.bfloat16)


def draw_queries(key, part):
    query_part, key_part = attention_pair(key)
    return query_part.astype(jnp.bfloat16)


def draw_keys(key, part):
    query_part, key_part = attention_pair(key)
    return key_part.astype(jnp.bfloat16)


def draw_q_gain(key, part):
    key = jax.random.fold_in(key, 5)
    return jnp.exp(jax.random.uniform(key, (HD,), jnp.float32, jnp.log(0.5), jnp.log(3.0)))


def draw_k_gain(key, part):
    key = jax.random.fold_in(key, 6)
    return jnp.exp(jax.random.uniform(key, (HD,), jnp.float32, jnp.log(0.5), jnp.log(3.0)))


def touch_ends(values, key, least, high):
    longest = values.shape.index(max(values.shape))
    spots = []
    for shift in (0, 1):
        where = [jax.random.randint(jax.random.fold_in(key, axis), (), 0, length) for axis, length in enumerate(values.shape)]
        where[longest] = (where[longest] + shift) % values.shape[longest]
        spots.append(tuple(where))
    return values.at[spots[0]].set(least).at[spots[1]].set(high)


def block_scale(rng, extent, pieces, low, largest):
    loudness = 1.0
    for dim, parts in pieces:
        draws = jax.random.uniform(jax.random.fold_in(jax.random.fold_in(rng, 6), dim), (parts,), jnp.float32, low / len(pieces), largest / len(pieces))
        loudness = loudness * jnp.repeat(jnp.exp(draws), extent[dim] // parts).reshape((-1,) + (1,) * (len(extent) - 1 - dim))
    return loudness


def profile(number_of, total, limit, slope):
    weights = [(1 << 20) // math.isqrt(standing ** slope) + 1 for standing in range(2, number_of + 1)]
    spare, counts = total - limit - (number_of - 1), [1] * (number_of - 1)
    while spare > 0:
        candidates = [i for i in range(number_of - 1) if counts[i] < limit]
        mass, left = sum([weights[i] for i in candidates]), spare
        for i in candidates:
            more = min(limit - counts[i], max(1, left * weights[i] // mass), spare)
            counts[i] = counts[i] + more
            spare = spare - more
    return np.array([limit] + counts)


def uneven_parts(own_key, count, total, bound, lean):
    if count == 2:
        one = jax.random.randint(own_key, (), max(1, total - bound), min(bound, total - 1) + 1)
        return jnp.stack([one, total - one])
    sizes = jnp.asarray(profile(count, total, bound, lean), jnp.int32)
    pairs = (count - 1) // 2
    donor, taker = sizes[1:1 + 2 * pairs:2], sizes[2:2 + 2 * pairs:2]
    room = jnp.minimum(donor - 1, bound - taker)
    passed = jax.random.randint(jax.random.fold_in(own_key, 1), (pairs,), 0, 1 << 20) % (room + 1)
    sizes = sizes.at[1:1 + 2 * pairs:2].set(donor - passed).at[2:2 + 2 * pairs:2].set(taker + passed)
    return sizes[jax.random.permutation(jax.random.fold_in(own_key, 2), count)]


def gaussian(stream_key, shape, width, limit, split=(), kind=jnp.bfloat16):
    values = jax.random.normal(stream_key, shape, jnp.float32) * width
    if len(split) > 0:
        values = block_scale(stream_key, shape, split, -0.22, 0.18) * values
    return jnp.clip(values, min=-limit, max=limit).astype(kind)


def setup_inputs(seed: int = 0) -> dict:
    streams_of = jax.random.split(jax.random.key(seed), 12)
    return {
        "question_embedding_matrix": draw_question_embedding_matrix(jax.random.fold_in(streams_of[11], 71), 0),
        "passage_embedding_matrix": draw_passage_embedding_matrix(jax.random.fold_in(streams_of[11], 71), 0),
        "positive": touch_ends(jax.random.randint(streams_of[2], (PAIRS,), 0, PAIRS), jax.random.fold_in(streams_of[2], 1), 0, PAIRS - 1).astype(jnp.int32),
        "queries": draw_queries(jax.random.fold_in(streams_of[11], 71), 0),
        "keys": draw_keys(jax.random.fold_in(streams_of[11], 71), 0),
        "values": gaussian(streams_of[5], (DOCS, S, KV * HD), 1.0, 6.0, ((0, 16), (1, 16))),
        "later_grad": gaussian(streams_of[6], (DOCS, S, H * HD), 1.0, 6.0, ((0, 16), (1, 16))),
        "lengths": uneven_parts(streams_of[7], DOCS, 3 * DOCS * S // 4, S, 1).astype(jnp.int32),
        "q_gain": draw_q_gain(jax.random.fold_in(streams_of[11], 71), 0),
        "k_gain": draw_k_gain(jax.random.fold_in(streams_of[11], 71), 0),
        "out_weight": gaussian(streams_of[10], (H * HD, D), D ** -0.5, 0.09375, ((0, 16), (1, 16))),
    }


sharpness_divisor = 0.05
epsilon = 1e-06
rope_base = 1000000.0

def quantized_affinity_matrix(values_in):
    return lax.optimization_barrier(values_in.astype(jnp.bfloat16))

def rms_rope(inputs, gain, positions):
    head_dim = inputs.shape[-1]
    half_dim = head_dim // 2
    normed = inputs * lax.rsqrt(lax.optimization_barrier(jnp.mean(inputs * inputs, axis=-1, keepdims=True)) + epsilon) * gain
    frequency = rope_base ** (-2.0 * jnp.arange(half_dim, dtype=jnp.float32) / head_dim)
    angles = positions.astype(jnp.float32)[:, None] * frequency[None, :]
    cosine = jnp.cos(angles)[:, None, :]
    sine = jnp.sin(angles)[:, None, :]
    first_half = normed[..., :half_dim]
    second_half = normed[..., half_dim:]
    return jnp.concatenate([first_half * cosine - second_half * sine, second_half * cosine + first_half * sine], axis=-1)

def attend(query_rot, key_rot, value_head, grad_head, valid_len):
    length = key_rot.shape[0]
    scaling = key_rot.shape[1] ** (-0.5)
    row_index = jnp.arange(length)[:, None]
    col_index = jnp.arange(length)[None, :]
    allowed = (col_index <= row_index) & (col_index < valid_len)
    query_wide = query_rot.astype(jnp.float32)
    key_wide = key_rot.astype(jnp.float32)
    value_wide = value_head.astype(jnp.float32)
    grad_wide = grad_head.astype(jnp.float32)
    scores = jnp.einsum('gtd,ud->gtu', query_wide, key_wide) * scaling
    scores = jnp.where(allowed[None], scores, -1e+30)
    highest = lax.optimization_barrier(jnp.max(scores, axis=-1, keepdims=True))
    expon = jnp.exp(scores - highest)
    probs = expon / lax.optimization_barrier(jnp.sum(expon, axis=-1, keepdims=True))
    probs_low = quantized_affinity_matrix(probs).astype(jnp.float32)
    attn_out = jnp.einsum('gtu,ud->gtd', probs_low, value_wide)
    row_dot = lax.optimization_barrier(jnp.sum(grad_wide * attn_out, axis=-1, keepdims=True))
    value_grad = jnp.einsum('gtu,gtd->ud', probs_low, grad_wide)
    prob_grad = jnp.einsum('gtd,ud->gtu', grad_wide, value_wide)
    score_grad = quantized_affinity_matrix(probs * (prob_grad - row_dot) * scaling).astype(jnp.float32)
    query_grad = jnp.einsum('gtu,ud->gtd', score_grad, key_wide)
    key_grad = jnp.einsum('gtu,gtd->ud', score_grad, query_wide)
    return (query_grad, key_grad, value_grad)

def reference(question_embedding_matrix, passage_embedding_matrix, positive, queries, keys, values, later_grad, lengths, q_gain, k_gain, out_weight):
    affinity_matrix = jnp.dot(question_embedding_matrix, passage_embedding_matrix.T, preferred_element_type=jnp.float32) / sharpness_divisor
    highest = lax.optimization_barrier(jnp.max(affinity_matrix, axis=1, keepdims=True))
    normalizer_logsum = highest[:, 0] + jnp.log(lax.optimization_barrier(jnp.sum(jnp.exp(affinity_matrix - highest), axis=1)))
    positive_match_mask = (jnp.arange(PAIRS)[None, :] == positive[:, None]).astype(jnp.float32)
    picked = lax.optimization_barrier(jnp.sum(affinity_matrix * positive_match_mask, axis=1))
    loss_sum = jnp.sum(normalizer_logsum - picked)
    normalized_affinity_shares = quantized_affinity_matrix((jnp.exp(affinity_matrix - normalizer_logsum[:, None]) - positive_match_mask) / sharpness_divisor)
    query_grad = jnp.dot(normalized_affinity_shares, passage_embedding_matrix, preferred_element_type=jnp.float32).astype(jnp.bfloat16)
    doc_grad = jnp.dot(normalized_affinity_shares.T, question_embedding_matrix, preferred_element_type=jnp.float32).astype(jnp.bfloat16)
    span_rows = doc_grad[::PAIRS // DOCS]
    tail = jnp.dot(span_rows, out_weight.T, preferred_element_type=jnp.float32)

    def one_document(inputs):
        query_doc, key_doc, value_doc, later_doc, valid_len, tail_doc = inputs
        length = query_doc.shape[0]
        head_dim = q_gain.shape[0]
        heads = query_doc.shape[1] // head_dim
        groups = key_doc.shape[1] // head_dim
        ratio = heads // groups
        positions = jnp.arange(length)

        def rope_at(inputs_in, gain):
            return rms_rope(inputs_in, gain, positions)
        q_rot, q_back = jax.vjp(rope_at, query_doc.reshape(length, heads, head_dim).astype(jnp.float32), q_gain)
        k_rot, k_back = jax.vjp(rope_at, key_doc.reshape(length, groups, head_dim).astype(jnp.float32), k_gain)
        q_low = quantized_affinity_matrix(q_rot)
        k_low = quantized_affinity_matrix(k_rot)
        row_index = jnp.arange(length)[:, None]
        last_row = jnp.where(row_index == valid_len - 1, 1.0, 0.0)
        grad_rows = jnp.where(row_index < valid_len, later_doc.astype(jnp.float32) + last_row * tail_doc[None, :], 0.0)
        grad_rows = quantized_affinity_matrix(grad_rows).reshape(length, heads, head_dim)
        value_heads = value_doc.reshape(length, groups, head_dim)
        query_list, key_list, value_list = ([], [], [])
        for group in range(groups):
            lower = group * ratio
            upper = lower + ratio
            query_part, key_part, value_part = attend(q_low[:, lower:upper].transpose(1, 0, 2), k_low[:, group], value_heads[:, group], grad_rows[:, lower:upper].transpose(1, 0, 2), valid_len)
            query_list.append(query_part.transpose(1, 0, 2))
            key_list.append(key_part)
            value_list.append(value_part)
        query_rgrad = quantized_affinity_matrix(jnp.concatenate(query_list, axis=1)).astype(jnp.float32)
        key_rgrad = quantized_affinity_matrix(jnp.stack(key_list, axis=1)).astype(jnp.float32)
        value_cot = jnp.stack(value_list, axis=1).reshape(length, groups * head_dim).astype(jnp.bfloat16)
        query_in, q_gain_part = q_back(query_rgrad)
        key_in, k_gain_part = k_back(key_rgrad)
        return (query_in.reshape(length, heads * head_dim).astype(jnp.bfloat16), key_in.reshape(length, groups * head_dim).astype(jnp.bfloat16), value_cot, q_gain_part, k_gain_part)
    query_cot, key_cot, value_cot, q_gain_parts, k_gain_parts = lax.map(one_document, (queries, keys, values, later_grad, lengths, tail))
    return (loss_sum / PAIRS, query_grad, doc_grad, query_cot, key_cot, value_cot, lax.optimization_barrier(jnp.sum(q_gain_parts, axis=0)), lax.optimization_barrier(jnp.sum(k_gain_parts, axis=0)))
```

```python
import functools
import math

import jax
import jax.numpy as jnp
from jax import lax
from jax.experimental import pallas as pl
from jax.experimental.pallas import tpu as pltpu
from jax.sharding import PartitionSpec as P

sharpness = 0.05
epsilon = 1e-06
rope_base = 1000000.0
lowest = -1e30
MESH = pl.DeviceIdType.MESH
f32 = jnp.float32
bf16 = jnp.bfloat16
VMEM = pl.BlockSpec(memory_space=pltpu.VMEM)
limit = 58 * 1024 * 1024
count = 16
pairs = 32
chunks = 32
q_stride = 40
scaling = 128 ** (-0.5)
phases = (
    "q_msg", "p_msg", "tile", "part", "span", "tail_part", "q_term", "d_term", "gain_seq",
    "gain_dp", "kv_x", "kv_y", "kv_core", "kv_both", "q", "grad", "dq", "core_sum", "y_sum",
    "x_out", "tail",
)
phase_of = {name: i for i, name in enumerate(phases)}


def mm(a, b):
    return lax.dot_general(a, b, (((1,), (0,)), ((), ())), preferred_element_type=f32)


def mm_nt(a, b):
    return lax.dot_general(a, b, (((1,), (1,)), ((), ())), preferred_element_type=f32)


def mm_tn(a, b):
    return lax.dot_general(a, b, (((0,), (0,)), ((), ())), preferred_element_type=f32)


def loop(first, last, step):
    def body(i, carry):
        step(i)
        return carry

    lax.fori_loop(first, last, body, 0)


def swap_halves(x):
    return pltpu.roll(x, 64, 1)


def normed_rope(x, gain, cosine, sine):
    scale = lax.rsqrt(jnp.mean(x * x, axis=-1, keepdims=True) + epsilon)
    y = x * scale * gain
    return y * cosine + swap_halves(y) * sine


def normed_rope_back(x, gain, cosine, sine, grad):
    scale = lax.rsqrt(jnp.mean(x * x, axis=-1, keepdims=True) + epsilon)
    n = x * scale
    dy = grad * cosine - swap_halves(grad) * sine
    gain_part = dy * n
    dn = dy * gain
    dx = scale * (dn - n * jnp.mean(dn * n, axis=-1, keepdims=True))
    return dx, gain_part


def slot_sum(ref):
    total = ref[0]
    for i in range(1, count):
        total = total + ref[i]
    return total


def whole(
    lengths, queries, keys, values, later, q_emb, p_emb, pos_hi, pos_lo, out_w, q_gain, k_gain,
    cosine, sine,
    loss_out, q_grad_out, d_grad_out, q_cot, k_cot, v_cot, gains_out,
    q_f32, q_msg, p_f32, p_msg, q_all, p_all, q_wide, p_wide, q_cols, p_cols, q_part, tiles,
    w_span, q_terms, d_terms, q_slots, d_slots, tail_slots, tail_send, tail_in,
    kv_stage, q_stage, grad_stage, kv_h, q_h, grad_h,
    scores, prob_grads, shares, dq_acc, dkv, dq_stage, dq_slots,
    core_slots, y_stage, y_slots, x_stage, x_slots, seq_slots, dp_slots,
    send_sem, recv_sem,
):
    d, j = lax.axis_index("dp"), lax.axis_index("seq")
    x, y, c = j // 4, (j // 2) % 2, j % 2
    rank = 2 * x + c
    barrier = pltpu.get_barrier_semaphore()

    def remote(name, src, dst, to_slot, from_slot, dp, seq):
        phase = phase_of[name]
        return pltpu.make_async_remote_copy(
            src_ref=src,
            dst_ref=dst,
            send_sem=send_sem.at[phase, to_slot],
            recv_sem=recv_sem.at[phase, from_slot],
            device_id=(dp, seq),
            device_id_type=MESH,
        )

    def others(step, me, size=count):
        loop(1, size, lambda o: step(lax.rem(me + o, size)))

    class Axis:
        def __init__(self, name, axis, src, dst):
            self.name, self.src, self.dst = name, src, dst
            self.me = d if axis == "dp" else j
            self.place = (lambda p: (p, j)) if axis == "dp" else (lambda p: (d, p))

        def send(self):
            others(
                lambda p: remote(
                    self.name, self.src(p), self.dst(self.me), p, self.me, *self.place(p)
                ).start(),
                self.me,
            )

        def arrive(self):
            others(
                lambda p: remote(
                    self.name, self.src(p), self.dst(p), p, p, *self.place(p)
                ).wait_recv(),
                self.me,
            )

        def sent(self):
            others(
                lambda p: remote(
                    self.name, self.src(p), self.dst(self.me), p, self.me, *self.place(p)
                ).wait_send(),
                self.me,
            )

    others(
        lambda p: pl.semaphore_signal(barrier, inc=1, device_id=(d, p), device_id_type=MESH), j
    )
    others(
        lambda p: pl.semaphore_signal(barrier, inc=1, device_id=(p, j), device_id_type=MESH), d
    )

    def lanes(h):
        return pl.ds(pl.multiple_of(h * 128, 128), 128)

    def q_rows(s):
        return pl.ds(pl.multiple_of(s * 2 * q_stride, 16), 2 * q_stride)

    def p_rows(s):
        return pl.ds(pl.multiple_of(s * 2 * chunks, 16), 2 * chunks)

    q_f32[...] = jnp.zeros_like(q_f32)
    q_own, p_own = q_emb[...].astype(f32), p_emb[...].astype(f32)
    for i in range(chunks):
        q_f32[pl.ds(i, 2, stride=q_stride), :] = q_own[:, i * 128 : i * 128 + 128]
        p_f32[pl.ds(i, 2, stride=chunks), :] = p_own[:, i * 128 : i * 128 + 128]
    q_f32[pl.ds(chunks, 2, stride=q_stride), :] = pos_hi[...]
    q_f32[pl.ds(chunks + 1, 2, stride=q_stride), :] = pos_lo[...]
    q_msg[...] = q_f32[...].astype(bf16)
    p_msg[...] = p_f32[...].astype(bf16)
    q_all[q_rows(j), :] = q_msg[...]
    p_all[p_rows(d), :] = p_msg[...]

    def stage_kv(g):
        rot = normed_rope(keys[:, lanes(g)].astype(f32), k_gain[...], cosine[...], sine[...])
        kv_stage[g, 0] = rot.astype(bf16)
        kv_stage[g, 1] = values[:, lanes(g)]

    loop(0, 4, stage_kv)
    pl.semaphore_wait(barrier, 2 * (count - 1))

    q_x = Axis("q_msg", "seq", lambda p: q_msg, lambda s: q_all.at[q_rows(s)])
    p_x = Axis("p_msg", "dp", lambda p: p_msg, lambda s: p_all.at[p_rows(s)])
    q_x.send()
    p_x.send()

    def kv_spot(a, b, e):
        return kv_h.at[:, a, b, e]

    def kv_x(to, source):
        return remote("kv_x", kv_stage.at[to], kv_spot(source, y, c), to, source, d, 4 * to + 2 * y + c)

    others(lambda p: kv_x(p, x).start(), x, 4)
    kv_h[:, x, y, c] = kv_stage[x]

    def kv_pass(name, a, b, e, seq):
        return remote(name, kv_spot(a, b, e), kv_spot(a, b, e), a, a, d, seq)

    over_y = 4 * x + 2 * (1 - y) + c
    over_core = 4 * x + 2 * y + (1 - c)

    def pass_on(a):
        kv_pass("kv_y", a, y, c, over_y).start()
        kv_pass("kv_core", a, y, c, over_core).start()

    pass_on(x)

    def stage_q(h):
        rot = normed_rope(queries[:, lanes(h)].astype(f32), q_gain[...], cosine[...], sine[...])
        q_stage[h // 2, h % 2] = rot.astype(bf16)

    def seat(r):
        return 4 * (r // 2) + 2 * y + r % 2

    def head_copy(name, stage, held, to, source):
        return remote(
            name, stage.at[to], held.at[source // 2, :, source % 2], to, source, d, seat(to)
        )

    loop(0, 16, stage_q)
    others(lambda p: head_copy("q", q_stage, q_h, p, rank).start(), rank, 8)
    q_h[x, :, c] = q_stage[rank]

    def stage_grad(h):
        grad_stage[h // 2, h % 2] = later[:, lanes(h)]

    loop(0, 16, stage_grad)
    others(lambda p: head_copy("grad", grad_stage, grad_h, p, rank).start(), rank, 8)
    grad_h[x, :, c] = grad_stage[rank]
    dkv[...] = jnp.zeros_like(dkv)

    q_x.arrive()
    p_x.arrive()
    q_wide[...] = q_all[...].astype(f32)
    p_wide[...] = p_all[...].astype(f32)
    for i in range(chunks):
        half = pl.ds((i % 2) * 128, 128)
        q_cols[i // 2, :, half] = q_wide[pl.ds(i, pairs, stride=q_stride), :].astype(bf16)
        p_cols[i // 2, :, half] = p_wide[pl.ds(i, pairs, stride=chunks), :].astype(bf16)
    positive = (
        2.0 * q_wide[pl.ds(chunks, pairs, stride=q_stride), :]
        + q_wide[pl.ds(chunks + 1, pairs, stride=q_stride), :]
    )
    q_part[d] = q_cols[d]
    part_x = Axis("part", "dp", lambda p: q_cols.at[p], lambda s: q_part.at[s])
    part_x.send()

    def four(block):
        return jnp.concatenate([block] * (128 // pairs), axis=0)

    logits = mm_nt(q_cols[0], four(p_cols[0]))
    for b in range(1, count):
        logits = logits + mm_nt(q_cols[b], four(p_cols[b]))
    logits = logits / sharpness
    lane = lax.broadcasted_iota(jnp.int32, (pairs, 128), 1)
    real = lane < pairs
    base = jnp.where(real, (lane >> 1) * pairs + (lane & 1), -(1 << 20)).astype(f32)
    tiles[j] = jnp.where(real, logits, lowest)
    tile_x = Axis("tile", "seq", lambda p: tiles.at[j], lambda s: tiles.at[s])
    tile_x.send()

    def pass_arrived(a):
        kv_x(a, a).wait_recv()
        pass_on(a)

    others(pass_arrived, x, 4)

    tile_x.arrive()
    high = tiles[0]
    for i in range(1, count):
        high = jnp.maximum(high, tiles[i])
    high = jnp.max(high, axis=1, keepdims=True)
    mass = jnp.zeros((pairs, 128), f32)
    hit = jnp.zeros((pairs, 128), f32)
    for i in range(count):
        mass = mass + jnp.exp(tiles[i] - high)
        hit = hit + jnp.where(base + 2.0 * i == positive, tiles[i], 0.0)
    log_total = high + jnp.log(jnp.sum(mass, axis=1, keepdims=True))
    picked = jnp.sum(hit, axis=1, keepdims=True)
    loss_part = jnp.sum(log_total - picked, axis=0, keepdims=True)

    def weights_of(tile, index):
        onehot = jnp.where(base + 2.0 * index == positive, 1.0, 0.0)
        return (jnp.exp(tile - log_total) - onehot) / sharpness

    w_span[d] = weights_of(tiles[0], 0.0).astype(bf16)
    span_x = Axis("span", "dp", lambda p: w_span.at[d], lambda s: w_span.at[s])
    span_x.send()
    mine = weights_of(tiles[j], j.astype(f32))
    w = mine.astype(bf16)
    w_t = jnp.transpose(mine)[:pairs].astype(bf16)

    def pass_from_y(o):
        a = lax.rem(x + o, 4)
        kv_pass("kv_y", a, 1 - y, c, over_y).wait_recv()
        kv_pass("kv_both", a, 1 - y, c, over_core).start()

    loop(0, 4, pass_from_y)

    part_x.arrive()
    span_x.arrive()
    span = mm_tn(w_span[...].reshape(pairs * count, 128), q_part[...].reshape(pairs * count, 256))
    span = span[:pairs].astype(bf16)
    tail_slots[d, pl.ds(0, pairs)] = mm_nt(span, out_w[...])
    tail_slots[d, pl.ds(pairs, 8)] = jnp.broadcast_to(loss_part, (8, 128))
    tail_x = Axis("tail_part", "dp", lambda p: tail_slots.at[d], lambda s: tail_slots.at[s])
    tail_x.send()

    def kv_core_arrive(a):
        kv_pass("kv_core", a, y, 1 - c, over_core).wait_recv()
        kv_pass("kv_both", a, 1 - y, 1 - c, over_core).wait_recv()

    loop(0, 4, kv_core_arrive)
    others(lambda p: head_copy("q", q_stage, q_h, p, p).wait_recv(), rank, 8)
    length = lengths[0]
    key_spot = lax.broadcasted_iota(jnp.int32, (512, 512), 0)
    query_spot = lax.broadcasted_iota(jnp.int32, (512, 512), 1) & 255

    def fold(block, op):
        return op(block.reshape(64, 8, 512), axis=0)

    def spot_of(a, b):
        return (a * (a + 1)) // 2 + b

    def softmax_rows(o):
        a = 3 - o
        q = q_h[a].reshape(512, 128)

        def first(b, top, diagonal):
            s = mm_nt(kv_h[0, b].reshape(512, 128), q) * (scaling * math.log2(math.e))
            allowed = key_spot < length - b * 512
            if diagonal:
                allowed = allowed & (key_spot - query_spot <= 256 * y)
            s = jnp.where(allowed, s, lowest)
            scores[spot_of(a, b)] = s
            return jnp.maximum(top, fold(s, jnp.max))

        top = jnp.full((8, 512), lowest, f32)
        top = lax.fori_loop(0, a, lambda b, t: first(b, t, False), top)
        top = jnp.max(first(a, top, True), axis=0, keepdims=True)

        def second(b, total):
            e = jnp.exp2(scores[spot_of(a, b)] - top)
            scores[spot_of(a, b)] = e
            return total + fold(e, jnp.sum)

        total = lax.fori_loop(0, a + 1, second, jnp.zeros((8, 512), f32))
        shares[a] = jnp.broadcast_to(1.0 / jnp.sum(total, axis=0, keepdims=True), (8, 512))

    loop(0, 4, softmax_rows)

    tail_x.arrive()
    tails = slot_sum(tail_slots)
    line = lax.broadcasted_iota(jnp.int32, (pairs, 128), 0)
    tail = jnp.sum(jnp.where(line == 2 * d, tails[:pairs], 0.0), axis=0, keepdims=True)
    loss_out[...] = tails[pairs:] / (pairs * count)
    tail_send[...] = jnp.broadcast_to(tail, (8, 128))
    tail_core = (j // 2) % 2

    def tail_copy(b, slot, seq):
        return remote("tail", tail_send, tail_in.at[slot], b, slot, d, seq)

    for b in range(2):
        to = 4 * x + 2 * b + tail_core
        pl.when(to != j)(lambda b=b, to=to: tail_copy(b, j % 2, to).start())

        @pl.when(to == j)
        def _():
            tail_in[j % 2] = tail_send[...]

    for b in range(count):
        q_term = mm(w, four(p_cols[b]))
        d_term = mm(w_t, q_cols[b])
        for half in range(2):
            rows = pl.ds(2 * b + half, pairs, stride=chunks)
            q_terms[rows, :] = q_term[:, half * 128 : half * 128 + 128]
            d_terms[rows, :] = d_term[:, half * 128 : half * 128 + 128]
    q_slots[j] = q_terms[p_rows(j), :]
    d_slots[d] = d_terms[p_rows(d), :]
    d_term_x = Axis("d_term", "dp", lambda p: d_terms.at[p_rows(p)], lambda s: d_slots.at[s])
    q_term_x = Axis("q_term", "seq", lambda p: q_terms.at[p_rows(p)], lambda s: q_slots.at[s])
    d_term_x.send()
    q_term_x.send()

    others(lambda p: head_copy("grad", grad_stage, grad_h, p, p).wait_recv(), rank, 8)
    for b in range(2):
        source = 4 * x + 2 * c + b
        pl.when(source != j)(lambda b=b, source=source: tail_copy(0, b, source).wait_recv())
    row = lax.broadcasted_iota(jnp.int32, (512, 1), 0)
    row_token = (row & 255) + 256 * y

    def core_copy(a):
        return remote("core_sum", dkv.at[:, a, :, 1 - c], core_slots.at[a], a, a, d, over_core)

    def y_copy(a):
        return remote("y_sum", y_stage.at[a], y_slots.at[a], a, a, d, over_y)

    def x_copy(to, source):
        return remote("x_out", x_stage.at[to], x_slots.at[source], to, source, d, 4 * to + 2 * y + c)

    def dq_copy(a, e, source):
        return remote(
            "dq", dq_stage.at[a, :, e], dq_slots.at[source], 2 * a + e, source, d, 4 * a + 2 * y + e
        )

    def grad_rows(a):
        q = q_h[a].reshape(512, 128)
        spot = row_token + 512 * a
        extra = jnp.where(row < 256, tail_in[0, 0:1], tail_in[1, 0:1])
        grad = grad_h[a].reshape(512, 128).astype(f32) + jnp.where(spot == length - 1, 1.0, 0.0) * extra
        grad = jnp.where(spot < length, grad, 0.0).astype(bf16)
        share = shares[a, 0:1]

        def third(b, dots):
            low = (scores[spot_of(a, b)] * share).astype(bf16)
            prob_grad = mm_nt(kv_h[1, b].reshape(512, 128), grad)
            prob_grads[b] = prob_grad
            dkv[1, b] += mm(low, grad).reshape(2, 2, 128, 128)
            return dots + fold(low.astype(f32) * prob_grad, jnp.sum)

        dots = lax.fori_loop(0, a + 1, third, jnp.zeros((8, 512), f32))
        row_dot = jnp.sum(dots, axis=0, keepdims=True)
        factor = share * scaling
        dq_acc[...] = jnp.zeros_like(dq_acc)

        def fourth(b):
            sg = (scores[spot_of(a, b)] * factor * (prob_grads[b] - row_dot)).astype(bf16)
            dkv[0, b] += mm(sg, q).reshape(2, 2, 128, 128)
            dq_acc[...] += mm_tn(kv_h[0, b].reshape(512, 128), sg)

        loop(0, a + 1, fourth)
        dq_stage[a] = jnp.transpose(dq_acc[...]).astype(bf16).reshape(2, 2, 128, 128)

    def send_y(a):
        core_copy(a).wait_recv()
        y_stage[a] = dkv[:, a, 1 - y, c] + core_slots[a, :, 1 - y]
        y_copy(a).start()

    def send_x(a):
        y_copy(a).wait_recv()
        total = dkv[:, a, y, c] + core_slots[a, :, y] + y_slots[a]
        x_stage[a] = total.astype(bf16)

        @pl.when(a != x)
        def _():
            x_copy(a, x).start()

        @pl.when(a == x)
        def _():
            x_slots[x] = x_stage[a]

    def quarter(o):
        a = 3 - o
        grad_rows(a)
        core_copy(a).start()
        for e in range(2):

            @pl.when(2 * a + e != rank)
            def _():
                dq_copy(a, e, rank).start()

            @pl.when(2 * a + e == rank)
            def _():
                dq_slots[rank] = dq_stage[a, :, e]

        pl.when(o >= 1)(lambda: send_y(a + 1))
        pl.when(o >= 2)(lambda: send_x(a + 2))

    loop(0, 4, quarter)
    send_y(0)
    send_x(1)

    d_term_x.arrive()
    d_sum = slot_sum(d_slots)
    q_term_x.arrive()
    q_sum = slot_sum(q_slots)
    q_f32[pl.ds(0, 2 * chunks), :] = q_sum
    p_f32[...] = d_sum
    for i in range(chunks):
        part = pl.ds(i * 128, 128)
        q_grad_out[:, part] = q_f32[pl.ds(i, 2, stride=chunks), :].astype(bf16)
        d_grad_out[:, part] = p_f32[pl.ds(i, 2, stride=chunks), :].astype(bf16)
    send_x(0)

    others(lambda p: dq_copy(x, c, p).wait_recv(), rank, 8)

    def gain_fold(block):
        return jnp.sum(block.reshape(16, 8, 128), axis=0)

    def query_head(h, total):
        grad = dq_slots[h // 2, h % 2].astype(f32)
        dx, part = normed_rope_back(
            queries[:, lanes(h)].astype(f32), q_gain[...], cosine[...], sine[...], grad
        )
        q_cot[:, lanes(h)] = dx.astype(bf16)
        return total + gain_fold(part)

    q_total = lax.fori_loop(0, 16, query_head, jnp.zeros((8, 128), f32))
    others(lambda p: x_copy(p, p).wait_recv(), x, 4)

    def key_head(g, total):
        v_cot[:, lanes(g)] = x_slots[g, 1]
        dx, part = normed_rope_back(
            keys[:, lanes(g)].astype(f32), k_gain[...], cosine[...], sine[...],
            x_slots[g, 0].astype(f32),
        )
        k_cot[:, lanes(g)] = dx.astype(bf16)
        return total + gain_fold(part)

    k_total = lax.fori_loop(0, 4, key_head, jnp.zeros((8, 128), f32))
    seq_slots[j, pl.ds(0, 8)] = q_total
    seq_slots[j, pl.ds(8, 8)] = k_total
    gain_seq = Axis("gain_seq", "seq", lambda p: seq_slots.at[j], lambda s: seq_slots.at[s])
    gain_seq.send()
    gain_seq.arrive()
    dp_slots[d] = slot_sum(seq_slots)
    gain_dp = Axis("gain_dp", "dp", lambda p: dp_slots.at[d], lambda s: dp_slots.at[s])
    gain_dp.send()
    gain_dp.arrive()
    gains = slot_sum(dp_slots)
    gains_out[0:1, :] = jnp.sum(gains[:8], axis=0, keepdims=True)
    gains_out[1:2, :] = jnp.sum(gains[8:], axis=0, keepdims=True)

    for sends in (q_x, p_x, part_x, tile_x, span_x, tail_x, d_term_x, q_term_x, gain_seq, gain_dp):
        sends.sent()
    others(lambda p: kv_x(p, x).wait_send(), x, 4)
    others(lambda p: head_copy("q", q_stage, q_h, p, rank).wait_send(), rank, 8)
    others(lambda p: head_copy("grad", grad_stage, grad_h, p, rank).wait_send(), rank, 8)
    for b in range(2):
        to = 4 * x + 2 * b + tail_core
        pl.when(to != j)(lambda b=b, to=to: tail_copy(b, j % 2, to).wait_send())

    def left(a):
        kv_pass("kv_y", a, y, c, over_y).wait_send()
        kv_pass("kv_core", a, y, c, over_core).wait_send()
        kv_pass("kv_both", a, 1 - y, c, over_core).wait_send()
        core_copy(a).wait_send()
        y_copy(a).wait_send()
        pl.when(a != x)(lambda: x_copy(a, x).wait_send())
        for e in range(2):
            pl.when(2 * a + e != rank)(lambda e=e: dq_copy(a, e, rank).wait_send())

    loop(0, 4, left)


def shards(
    question_embedding_matrix,
    passage_embedding_matrix,
    positive,
    queries,
    keys,
    values,
    later_grad,
    lengths,
    q_gain,
    k_gain,
    out_weight,
):
    tokens = queries.shape[1]
    positions = lax.axis_index("seq") * tokens + jnp.arange(tokens)
    frequency = rope_base ** (-2.0 * jnp.arange(64, dtype=f32) / 128)
    angles = positions.astype(f32)[:, None] * frequency[None, :]
    cosine, sine = jnp.cos(angles), jnp.sin(angles)
    cosine = jnp.concatenate([cosine, cosine], axis=1)
    sine = jnp.concatenate([-sine, sine], axis=1)
    pos_hi = jnp.broadcast_to((positive >> 1).astype(f32)[:, None], (2, 128))
    pos_lo = jnp.broadcast_to((positive & 1).astype(f32)[:, None], (2, 128))
    out = jax.ShapeDtypeStruct
    vm = pltpu.VMEM
    sems = pltpu.SemaphoreType.DMA((len(phases), count))
    loss, query_grad, doc_grad, query_cot, key_cot, value_cot, gains = pl.pallas_call(
        whole,
        out_shape=[
            out((8, 128), f32),
            out(question_embedding_matrix.shape, bf16),
            out(passage_embedding_matrix.shape, bf16),
            out(queries.shape[1:], bf16),
            out(keys.shape[1:], bf16),
            out(values.shape[1:], bf16),
            out((2, 128), f32),
        ],
        in_specs=[pl.BlockSpec(memory_space=pltpu.SMEM)] + [VMEM] * 13,
        out_specs=[VMEM] * 7,
        scratch_shapes=[
            vm((2 * q_stride, 128), f32),
            vm((2 * q_stride, 128), bf16),
            vm((2 * chunks, 128), f32),
            vm((2 * chunks, 128), bf16),
            vm((2 * q_stride * count, 128), bf16),
            vm((2 * chunks * count, 128), bf16),
            vm((2 * q_stride * count, 128), f32),
            vm((2 * chunks * count, 128), f32),
            vm((count, pairs, 256), bf16),
            vm((count, pairs, 256), bf16),
            vm((count, pairs, 256), bf16),
            vm((count, pairs, 128), f32),
            vm((count, pairs, 128), bf16),
            vm((pairs * chunks, 128), f32),
            vm((pairs * chunks, 128), f32),
            vm((count, 2 * chunks, 128), f32),
            vm((count, 2 * chunks, 128), f32),
            vm((count, pairs + 8, 128), f32),
            vm((8, 128), f32),
            vm((2, 8, 128), f32),
            vm((4, 2, 128, 128), bf16),
            vm((8, 2, 128, 128), bf16),
            vm((8, 2, 128, 128), bf16),
            vm((2, 4, 2, 2, 128, 128), bf16),
            vm((4, 2, 2, 128, 128), bf16),
            vm((4, 2, 2, 128, 128), bf16),
            vm((10, 512, 512), f32),
            vm((4, 512, 512), f32),
            vm((4, 8, 512), f32),
            vm((128, 512), f32),
            vm((2, 4, 2, 2, 128, 128), f32),
            vm((4, 2, 2, 128, 128), bf16),
            vm((8, 2, 128, 128), bf16),
            vm((4, 2, 2, 128, 128), f32),
            vm((4, 2, 128, 128), f32),
            vm((4, 2, 128, 128), f32),
            vm((4, 2, 128, 128), bf16),
            vm((4, 2, 128, 128), bf16),
            vm((count, 16, 128), f32),
            vm((count, 16, 128), f32),
            sems,
            sems,
        ],
        compiler_params=pltpu.CompilerParams(
            collective_id=0, has_side_effects=True, vmem_limit_bytes=limit
        ),
    )(
        lengths, queries[0], keys[0], values[0], later_grad[0],
        question_embedding_matrix, passage_embedding_matrix, pos_hi, pos_lo, out_weight,
        q_gain[None, :], k_gain[None, :], cosine, sine,
    )
    return (
        loss[0, 0],
        query_grad,
        doc_grad,
        query_cot[None],
        key_cot[None],
        value_cot[None],
        gains[0],
        gains[1],
    )


def solution(mesh):
    in_specs = (
        P(("dp", "seq"), None),
        P(("dp", "seq"), None),
        P(("dp", "seq")),
        P("dp", "seq", None),
        P("dp", "seq", None),
        P("dp", "seq", None),
        P("dp", "seq", None),
        P("dp"),
        P(),
        P(),
        P("seq", "dp"),
    )
    out_specs = (
        P(),
        P(("dp", "seq"), None),
        P(("dp", "seq"), None),
        P("dp", "seq", None),
        P("dp", "seq", None),
        P("dp", "seq", None),
        P(),
        P(),
    )
    return jax.shard_map(
        shards, mesh=mesh, in_specs=in_specs, out_specs=out_specs, check_vma=False
    )
```

```python
import functools
import math

import jax
import jax.numpy as jnp
import numpy as np
from jax import lax
from jax.experimental import pallas as pl
from jax.experimental.pallas import tpu as pltpu
from jax.sharding import PartitionSpec as P

sharpness = 0.05
epsilon = 1e-06
rope_base = 1000000.0
lowest = -1e30
MESH = pl.DeviceIdType.MESH
f32 = jnp.float32
bf16 = jnp.bfloat16
VMEM = pl.BlockSpec(memory_space=pltpu.VMEM)
limit = 58 * 1024 * 1024
count = 16
pairs = 32
chunks = 32
q_stride = 40
scaling = 128 ** (-0.5)
phases = (
    "q_y", "q_x", "q_core", "p_y", "p_z", "tile", "part", "span", "tail_part", "tail",
    "d_z", "d_y", "term_core", "term_x", "term_y", "gain_seq", "gain_dp",
    "kv_x", "kv_y", "kv_core", "kv_both", "q", "grad", "dq", "core_k", "core_v", "y_k", "y_v", "x_k", "x_v",
)
phase_of = {name: i for i, name in enumerate(phases)}


def mm(a, b):
    return lax.dot_general(a, b, (((1,), (0,)), ((), ())), preferred_element_type=f32)


def mm_nt(a, b):
    return lax.dot_general(a, b, (((1,), (1,)), ((), ())), preferred_element_type=f32)


def mm_tn(a, b):
    return lax.dot_general(a, b, (((0,), (0,)), ((), ())), preferred_element_type=f32)


def loop(first, last, step):
    def body(i, carry):
        step(i)
        return carry

    lax.fori_loop(first, last, body, 0)


def swap_halves(x):
    return pltpu.roll(x, 64, 1)


def normed_rope(x, gain, cosine, sine):
    scale = lax.rsqrt(jnp.mean(x * x, axis=-1, keepdims=True) + epsilon)
    y = x * scale * gain
    return y * cosine + swap_halves(y) * sine


def normed_rope_back(x, gain, cosine, sine, grad):
    scale = lax.rsqrt(jnp.mean(x * x, axis=-1, keepdims=True) + epsilon)
    n = x * scale
    dy = grad * cosine - swap_halves(grad) * sine
    gain_part = dy * n
    dn = dy * gain
    dx = scale * (dn - n * jnp.mean(dn * n, axis=-1, keepdims=True))
    return dx, gain_part


def slot_sum(ref):
    total = ref[0]
    for i in range(1, count):
        total = total + ref[i]
    return total


def whole(
    lengths, positive_in, table, queries, keys, values, later, q_emb, p_emb, out_w, q_gain, k_gain,
    loss_out, gains_out, q_grad_out, d_grad_out, q_cot, k_cot, v_cot,
    turn, cosine, sine,
    q_f32, p_f32, q_all, p_all, q_wide, p_wide, q_cols, p_cols, tiles,
    q_part, spans, q_terms, d_terms, core_in, q_mid, q_in, q_last, q_end,
    d_in, d_last, d_end, tail_stage, tail_slots, tail_send, tail_in,
    kv_stage, q_stage, grad_stage, kv_h, q_h, grad_h,
    grad_low, scores, prob_grads, shares, dots, dq_acc, dkv, dq_stage, dq_slots,
    core_slots, y_stage, y_slots, x_stage, x_slots, seq_slots, dp_slots,
    send_sem, recv_sem, own_sem,
):
    d, j = lax.axis_index("dp"), lax.axis_index("seq")
    x, y, c = j // 4, (j // 2) % 2, j % 2
    z, low = d // 2, d % 2
    rank = 2 * x + c
    barrier = pltpu.get_barrier_semaphore()

    def remote(name, src, dst, slot, dp, seq):
        phase = phase_of[name]
        return pltpu.make_async_remote_copy(
            src_ref=src,
            dst_ref=dst,
            send_sem=send_sem.at[phase],
            recv_sem=recv_sem.at[phase, slot],
            device_id=(dp, seq),
            device_id_type=MESH,
        )

    def bulk(name, ref):
        return remote(name, ref, ref, 0, d, j)

    def others(step, me, size=count):
        for o in range(1, size):
            step(lax.rem(me + o, size))

    others(
        lambda p: pl.semaphore_signal(barrier, inc=1, device_id=(d, p), device_id_type=MESH), j
    )
    others(
        lambda p: pl.semaphore_signal(barrier, inc=1, device_id=(p, j), device_id_type=MESH), d
    )
    turn_copy = pltpu.make_async_copy(
        table.at[pl.ds(pl.multiple_of(j * 128, 128), 128)], turn, own_sem.at[0]
    )
    turn_copy.start()

    def lanes(h):
        return pl.ds(pl.multiple_of(h * 128, 128), 128)

    def q_rows(s, size=1):
        return pl.ds(pl.multiple_of(s * 2 * q_stride, 16), size * 2 * q_stride)

    def p_rows(s, size=1):
        return pl.ds(pl.multiple_of(s * 2 * chunks, 16), size * 2 * chunks)

    place = 8 * c + 2 * x + y
    q_f32[...] = jnp.zeros_like(q_f32)
    q_own, p_own = q_emb[...].astype(f32), p_emb[...].astype(f32)
    for i in range(chunks):
        q_f32[pl.ds(i, 2, stride=q_stride), :] = q_own[:, i * 128 : i * 128 + 128]
        p_f32[pl.ds(i, 2, stride=chunks), :] = p_own[:, i * 128 : i * 128 + 128]
    for i in range(2):
        index = positive_in[i]
        spot = i * q_stride + chunks
        q_f32[spot : spot + 1, :] = jnp.full((1, 128), index >> 1, jnp.int32).astype(f32)
        q_f32[spot + 1 : spot + 2, :] = jnp.full((1, 128), index & 1, jnp.int32).astype(f32)
    q_all[q_rows(place), :] = q_f32[...].astype(bf16)
    p_all[p_rows(d), :] = p_f32[...].astype(bf16)
    turn_copy.wait()
    first_half = lax.broadcasted_iota(jnp.int32, (128, 128), 1) < 64
    turned = swap_halves(turn[...])
    cosine[...] = jnp.where(first_half, turn[...], turned)
    sine[...] = jnp.where(first_half, -turned, turn[...])

    def stage_kv(g):
        rot = normed_rope(keys[:, lanes(g)].astype(f32), k_gain[...], cosine[...], sine[...])
        kv_stage[g, 0] = rot.astype(bf16)
        kv_stage[g, 1] = values[:, lanes(g)]

    loop(0, 4, stage_kv)
    pl.semaphore_wait(barrier, 2 * (count - 1))

    over_y = 4 * x + 2 * (1 - y) + c
    over_core = 4 * x + 2 * y + (1 - c)
    over_low = d + 1 - 2 * low

    def beside(p):
        return 4 * p + 2 * y + c

    def gather(name, ref, rows, dp, seq):
        return remote(name, ref.at[rows, :], ref.at[rows, :], 0, dp, seq)

    gather("q_y", q_all, q_rows(place), d, over_y).start()
    gather("p_y", p_all, p_rows(d), over_low, j).start()

    def kv_spot(a, b, e):
        return kv_h.at[:, a, b, e]

    def kv_x(to, source):
        return remote("kv_x", kv_stage.at[to], kv_spot(source, y, c), source, d, beside(to))

    others(lambda p: kv_x(p, x).start(), x, 4)
    kv_h[:, x, y, c] = kv_stage[x]

    def kv_pass(name, a, b, e, seq):
        return remote(name, kv_spot(a, b, e), kv_spot(a, b, e), a, d, seq)

    def pass_on(a):
        kv_pass("kv_y", a, y, c, over_y).start()
        kv_pass("kv_core", a, y, c, over_core).start()

    pass_on(x)

    def stage_q(h):
        rot = normed_rope(queries[:, lanes(h)].astype(f32), q_gain[...], cosine[...], sine[...])
        q_stage[h // 2, h % 2] = rot.astype(bf16)

    def seat(r):
        return 4 * (r // 2) + 2 * y + r % 2

    def head_send(name, stage, held):
        others(
            lambda p: remote(
                name, stage.at[p], held.at[x, :, c], 0, d, seat(p)
            ).start(),
            rank,
            8,
        )
        held[x, :, c] = stage[rank]

    loop(0, 16, stage_q)
    gather("q_y", q_all, q_rows(place), d, over_y).wait_recv()
    own_pair = q_rows(8 * c + 2 * x, 2)
    others(lambda p: gather("q_x", q_all, own_pair, d, beside(p)).start(), x, 4)
    gather("p_y", p_all, p_rows(d), over_low, j).wait_recv()
    own_low = p_rows(2 * z, 2)
    others(lambda p: gather("p_z", p_all, own_low, 2 * p + low, j).start(), z, 8)
    head_send("q", q_stage, q_h)

    bulk("q_x", q_all.at[q_rows(0, 6), :]).wait_recv()
    gather("q_core", q_all, q_rows(8 * c, 8), d, over_core).start()

    def stage_grad(h):
        grad_stage[h // 2, h % 2] = later[:, lanes(h)]

    loop(0, 16, stage_grad)
    dkv[...] = jnp.zeros_like(dkv)

    bulk("p_z", p_all.at[p_rows(0, 14), :]).wait_recv()
    gather("q_core", q_all, q_rows(8 * c, 8), d, over_core).wait_recv()
    q_wide[...] = q_all[...].astype(f32)
    p_wide[...] = p_all[...].astype(f32)
    for i in range(chunks):
        half = pl.ds((i % 2) * 128, 128)
        q_cols[i // 2, :, half] = q_wide[pl.ds(i, pairs, stride=q_stride), :].astype(bf16)
        p_cols[i // 2, :, half] = p_wide[pl.ds(i, pairs, stride=chunks), :].astype(bf16)
    positive = (
        2.0 * q_wide[pl.ds(chunks, pairs, stride=q_stride), :]
        + q_wide[pl.ds(chunks + 1, pairs, stride=q_stride), :]
    )

    def four(block):
        return jnp.concatenate([block] * (128 // pairs), axis=0)

    def one(block):
        return block[:32] + block[32:64] + block[64:96] + block[96:]

    logits = mm_nt(q_cols[0], four(p_cols[0]))
    for b in range(1, count):
        logits = logits + mm_nt(q_cols[b], four(p_cols[b]))
    logits = logits / sharpness
    quarter_of = lax.broadcasted_iota(jnp.int32, (8, 128), 1) >> 5

    def pack(block):
        packed = block[:8]
        for i in range(1, 4):
            packed = jnp.where(quarter_of == i, block[8 * i : 8 * i + 8], packed)
        return packed

    tiles[j] = pack(logits)

    def tile_copy(p):
        return remote("tile", tiles.at[j], tiles.at[j], 0, d, p)

    others(lambda p: tile_copy(p).start(), j)

    def part_copy(p):
        return remote("part", q_cols.at[p], q_part.at[d], 0, p, j)

    others(lambda p: part_copy(p).start(), d)
    q_part[d] = q_cols[d]
    head_send("grad", grad_stage, grad_h)
    lane = lax.broadcasted_iota(jnp.int32, (pairs, 128), 1)
    line = lax.broadcasted_iota(jnp.int32, (pairs, 128), 0)
    real = (lane >> 5) == (line >> 3)
    base = jnp.where(real, ((lane & 31) >> 1) * pairs + (lane & 1), -(1 << 20)).astype(f32)

    def pass_arrived(a):
        kv_x(a, a).wait_recv()
        pass_on(a)

    others(pass_arrived, x, 4)

    bulk("tile", tiles.at[pl.ds(0, count - 1)]).wait_recv()
    high = tiles[0]
    for i in range(1, count):
        high = jnp.maximum(high, tiles[i])
    high = jnp.max(jnp.where(real, four(high), lowest), axis=1, keepdims=True)
    mass = jnp.zeros((pairs, 128), f32)
    hit = jnp.zeros((pairs, 128), f32)
    for i in range(count):
        tile = four(tiles[i])
        mass = mass + jnp.where(real, jnp.exp(tile - high), 0.0)
        hit = hit + jnp.where(base + 2.0 * i == positive, tile, 0.0)
    log_total = high + jnp.log(jnp.sum(mass, axis=1, keepdims=True))
    picked = jnp.sum(hit, axis=1, keepdims=True)
    loss_part = jnp.sum(log_total - picked, axis=0, keepdims=True)

    def weights_of(tile, index):
        onehot = jnp.where(base + 2.0 * index == positive, 1.0, 0.0)
        return jnp.where(real, (jnp.exp(four(tile) - log_total) - onehot) / sharpness, 0.0)

    spans[d] = pack(weights_of(tiles[0], 0.0).astype(bf16).astype(f32))

    def span_copy(p):
        return remote("span", spans.at[d], spans.at[d], 0, p, j)

    others(lambda p: span_copy(p).start(), d)
    mine = weights_of(tiles[j], j.astype(f32))
    w = mine.astype(bf16)
    w_t = one(jnp.transpose(mine)).astype(bf16)

    def pass_from_y(o):
        a = lax.rem(x + o, 4)
        kv_pass("kv_y", a, 1 - y, c, over_y).wait_recv()
        kv_pass("kv_both", a, 1 - y, c, over_core).start()

    pass_from_y(0)

    for b in range(count):
        q_term = mm(w, four(p_cols[b]))
        d_term = mm(w_t, q_cols[b])
        for half in range(2):
            rows = pl.ds(2 * b + half, pairs, stride=chunks)
            q_terms[rows, :] = q_term[:, half * 128 : half * 128 + 128]
            d_terms[rows, :] = d_term[:, half * 128 : half * 128 + 128]
    pass_from_y(1)

    bulk("part", q_part.at[pl.ds(0, count - 1)]).wait_recv()
    bulk("span", spans.at[pl.ds(0, count - 1)]).wait_recv()
    span = jnp.zeros((128, 256), f32)
    for i in range(count):
        weights = jnp.where(real, four(spans[i]), 0.0).astype(bf16)
        span = span + mm_tn(weights, q_part[i])
    span = one(span).astype(bf16)
    tail_rows = mm_nt(span, out_w[...])
    for i in range(count):
        tail_stage[i, pl.ds(0, 4)] = jnp.broadcast_to(tail_rows[2 * i : 2 * i + 1], (4, 128))
        tail_stage[i, pl.ds(4, 4)] = jnp.broadcast_to(loss_part, (4, 128))

    def tail_part(p):
        return remote("tail_part", tail_stage.at[p], tail_slots.at[d], 0, p, j)

    others(lambda p: tail_part(p).start(), d)
    tail_slots[d] = tail_stage[d]

    def d_copy(p):
        return remote("d_z", d_terms.at[p_rows(2 * p, 2), :], d_in.at[z], 0, 2 * p + low, j)

    others(lambda p: d_copy(p).start(), z, 8)
    d_in[z] = d_terms[p_rows(2 * z, 2), :]
    core_send = remote("term_core", q_terms.at[p_rows(8 * (1 - c), 8), :], core_in, 0, d, over_core)
    core_send.start()
    pass_from_y(2)
    pass_from_y(3)

    def kv_core_arrive(a):
        kv_pass("kv_core", a, y, 1 - c, over_core).wait_recv()
        kv_pass("kv_both", a, 1 - y, 1 - c, over_core).wait_recv()

    loop(0, 4, kv_core_arrive)
    bulk("q", q_stage.at[pl.ds(0, 7)]).wait_recv()
    length = lengths[0]
    key_spot = lax.broadcasted_iota(jnp.int32, (512, 512), 0)
    query_spot = lax.broadcasted_iota(jnp.int32, (512, 512), 1) & 255

    def fold(block, op):
        return op(block.reshape(64, 8, 512), axis=0)

    def spot_of(a, b):
        return (a * (a + 1)) // 2 + b

    def softmax_rows(o):
        a = 3 - o
        q = q_h[a].reshape(512, 128)

        def first(b, top, diagonal):
            s = mm_nt(kv_h[0, b].reshape(512, 128), q) * (scaling * math.log2(math.e))
            allowed = key_spot < length - b * 512
            if diagonal:
                allowed = allowed & (key_spot - query_spot <= 256 * y)
            s = jnp.where(allowed, s, lowest)
            scores[spot_of(a, b)] = s
            return jnp.maximum(top, fold(s, jnp.max))

        top = jnp.full((8, 512), lowest, f32)
        top = lax.fori_loop(0, a, lambda b, t: first(b, t, False), top)
        top = jnp.max(first(a, top, True), axis=0, keepdims=True)

        def second(b, total):
            e = jnp.exp2(scores[spot_of(a, b)] - top)
            scores[spot_of(a, b)] = e
            return total + fold(e, jnp.sum)

        total = lax.fori_loop(0, a + 1, second, jnp.zeros((8, 512), f32))
        shares[a] = jnp.broadcast_to(1.0 / jnp.sum(total, axis=0, keepdims=True), (8, 512))

    loop(0, 4, softmax_rows)

    bulk("tail_part", tail_slots.at[pl.ds(0, count - 1)]).wait_recv()
    tails = slot_sum(tail_slots)
    loss_out[...] = tails[4:5] / (pairs * count)
    tail_send[...] = jnp.broadcast_to(tails[0:1], (8, 128))

    def tail_copy(slot, seq):
        return remote("tail", tail_send, tail_in.at[slot], slot, d, seq)

    for b in range(2):
        to = 4 * x + 2 * b + y
        pl.when(to != j)(lambda to=to: tail_copy(j % 2, to).start())

        @pl.when(to == j)
        def _():
            tail_in[j % 2] = tail_send[...]

    core_send.wait_recv()
    sums = q_terms[p_rows(8 * c, 8), :] + core_in[...]
    q_mid[...] = sums.reshape(4, 128, 128)

    def term_x(p):
        return remote("term_x", q_mid.at[p], q_in.at[x], 0, d, beside(p))

    others(lambda p: term_x(p).start(), x, 4)
    q_in[x] = q_mid[x]

    bulk("grad", grad_stage.at[pl.ds(0, 7)]).wait_recv()
    for b in range(2):
        source = 4 * x + 2 * c + b
        pl.when(source != j)(lambda b=b, source=source: tail_copy(b, source).wait_recv())
    row = lax.broadcasted_iota(jnp.int32, (512, 1), 0)
    row_token = (row & 255) + 256 * y

    def core_copy(t, a):
        name = ("core_k", "core_v")[t]
        return remote(name, dkv.at[t, a, :, 1 - c], core_slots.at[t, a], a, d, over_core)

    def y_copy(t, a):
        return remote(("y_k", "y_v")[t], y_stage.at[t, a], y_slots.at[t, a], a, d, over_y)

    def x_copy(t, to):
        name = ("x_k", "x_v")[t]
        return remote(name, x_stage.at[t, to], x_slots.at[t, x], 0, d, beside(to))

    def dq_copy(a, e):
        return remote("dq", dq_stage.at[a, :, e], dq_slots.at[rank], 0, d, 4 * a + 2 * y + e)

    def send_y(t, a):
        core_copy(t, a).wait_recv()
        y_stage[t, a] = dkv[t, a, 1 - y, c] + core_slots[t, a, 1 - y]
        y_copy(t, a).start()

    def send_x(t, a):
        y_copy(t, a).wait_recv()
        total = dkv[t, a, y, c] + core_slots[t, a, y] + y_slots[t, a]
        x_stage[t, a] = total.astype(bf16)

        @pl.when(a != x)
        def _():
            x_copy(t, a).start()

        @pl.when(a == x)
        def _():
            x_slots[t, x] = x_stage[t, a]

    def make_grad(a):
        spot = row_token + 512 * a
        extra = jnp.where(row < 256, tail_in[0, 0:1], tail_in[1, 0:1])
        last = jnp.where(spot == length - 1, 1.0, 0.0)
        grad = grad_h[a].reshape(512, 128).astype(f32) + last * extra
        grad_low[a] = jnp.where(spot < length, grad, 0.0).astype(bf16)

    loop(0, 4, make_grad)
    dots[...] = jnp.zeros_like(dots)

    def value_block(o):
        b = 3 - o

        def rows(a):
            low = (scores[spot_of(a, b)] * shares[a, 0:1]).astype(bf16)
            prob_grad = mm_nt(kv_h[1, b].reshape(512, 128), grad_low[a])
            prob_grads[spot_of(a, b)] = prob_grad
            dkv[1, b] += mm(low, grad_low[a]).reshape(2, 2, 128, 128)
            dots[a] += fold(low.astype(f32) * prob_grad, jnp.sum)

        loop(b, 4, rows)
        core_copy(1, b).start()
        pl.when(o >= 1)(lambda: send_y(1, b + 1))

    loop(0, 4, value_block)

    def quarter(o):
        a = 3 - o
        q = q_h[a].reshape(512, 128)
        row_dot = jnp.sum(dots[a], axis=0, keepdims=True)
        factor = shares[a, 0:1] * scaling
        dq_acc[...] = jnp.zeros_like(dq_acc)

        def keys_of(b):
            spot = spot_of(a, b)
            sg = (scores[spot] * factor * (prob_grads[spot] - row_dot)).astype(bf16)
            dkv[0, b] += mm(sg, q).reshape(2, 2, 128, 128)
            dq_acc[...] += mm_tn(kv_h[0, b].reshape(512, 128), sg)

        loop(0, a + 1, keys_of)
        core_copy(0, a).start()
        dq_stage[a] = jnp.transpose(dq_acc[...]).astype(bf16).reshape(2, 2, 128, 128)
        for e in range(2):

            @pl.when(2 * a + e != rank)
            def _():
                dq_copy(a, e).start()

            @pl.when(2 * a + e == rank)
            def _():
                dq_slots[rank] = dq_stage[a, :, e]

        pl.when(o == 0)(lambda: send_y(1, 0))
        pl.when(o >= 1)(lambda: send_y(0, a + 1))
        send_x(1, a)
        pl.when(o >= 2)(lambda: send_x(0, a + 2))

    loop(0, 4, quarter)
    send_y(0, 0)
    bulk("term_x", q_in.at[pl.ds(0, 3)]).wait_recv()
    q_last[...] = (q_in[0] + q_in[1] + q_in[2] + q_in[3]).reshape(2, 64, 128)
    term_y = remote("term_y", q_last.at[1 - y], q_end, 0, d, over_y)
    term_y.start()
    bulk("d_z", d_in.at[pl.ds(0, 7)]).wait_recv()
    d_sum = d_in[0]
    for i in range(1, 8):
        d_sum = d_sum + d_in[i]
    d_last[...] = d_sum.reshape(2, 64, 128)
    d_y = remote("d_y", d_last.at[1 - low], d_end, 0, over_low, j)
    d_y.start()
    send_x(0, 1)

    bulk("dq", dq_slots.at[pl.ds(0, 7)]).wait_recv()

    def gain_fold(block):
        return jnp.sum(block.reshape(16, 8, 128), axis=0)

    def query_head(h, total):
        grad = dq_slots[h // 2, h % 2].astype(f32)
        dx, part = normed_rope_back(
            queries[:, lanes(h)].astype(f32), q_gain[...], cosine[...], sine[...], grad
        )
        q_cot[:, lanes(h)] = dx.astype(bf16)
        return total + gain_fold(part)

    q_total = lax.fori_loop(0, 16, query_head, jnp.zeros((8, 128), f32))
    send_x(0, 0)
    term_y.wait_recv()
    d_y.wait_recv()
    q_f32[pl.ds(0, 2 * chunks), :] = q_last[y] + q_end[...]
    p_f32[...] = d_last[low] + d_end[...]
    for i in range(chunks):
        part = pl.ds(i * 128, 128)
        q_grad_out[:, part] = q_f32[pl.ds(i, 2, stride=chunks), :].astype(bf16)
        d_grad_out[:, part] = p_f32[pl.ds(i, 2, stride=chunks), :].astype(bf16)
    bulk("x_v", x_slots.at[1, pl.ds(0, 3)]).wait_recv()
    bulk("x_k", x_slots.at[0, pl.ds(0, 3)]).wait_recv()

    def key_head(g, total):
        v_cot[:, lanes(g)] = x_slots[1, g]
        dx, part = normed_rope_back(
            keys[:, lanes(g)].astype(f32), k_gain[...], cosine[...], sine[...],
            x_slots[0, g].astype(f32),
        )
        k_cot[:, lanes(g)] = dx.astype(bf16)
        return total + gain_fold(part)

    k_total = lax.fori_loop(0, 4, key_head, jnp.zeros((8, 128), f32))
    seq_slots[j, pl.ds(0, 4)] = q_total[:4] + q_total[4:]
    seq_slots[j, pl.ds(4, 4)] = k_total[:4] + k_total[4:]

    def gain_seq(p):
        return remote("gain_seq", seq_slots.at[j], seq_slots.at[j], 0, d, p)

    others(lambda p: gain_seq(p).start(), j)
    bulk("gain_seq", seq_slots.at[pl.ds(0, count - 1)]).wait_recv()
    dp_slots[d] = slot_sum(seq_slots)

    def gain_dp(p):
        return remote("gain_dp", dp_slots.at[d], dp_slots.at[d], 0, p, j)

    others(lambda p: gain_dp(p).start(), d)
    bulk("gain_dp", dp_slots.at[pl.ds(0, count - 1)]).wait_recv()
    gains = slot_sum(dp_slots)
    gains_out[0:1, :] = jnp.sum(gains[:4], axis=0, keepdims=True)
    gains_out[1:2, :] = jnp.sum(gains[4:], axis=0, keepdims=True)

    gather("q_y", q_all, q_rows(place), d, over_y).wait_send()
    gather("p_y", p_all, p_rows(d), over_low, j).wait_send()
    gather("q_core", q_all, q_rows(8 * c, 8), d, over_core).wait_send()
    for name, ref in (
        ("q_x", q_all.at[q_rows(0, 6), :]),
        ("p_z", p_all.at[p_rows(0, 14), :]),
        ("tile", tiles.at[pl.ds(0, count - 1)]),
        ("part", q_part.at[pl.ds(0, count - 1)]),
        ("span", spans.at[pl.ds(0, count - 1)]),
        ("tail_part", tail_slots.at[pl.ds(0, count - 1)]),
        ("d_z", d_in.at[pl.ds(0, 7)]),
        ("term_x", q_in.at[pl.ds(0, 3)]),
        ("gain_seq", seq_slots.at[pl.ds(0, count - 1)]),
        ("gain_dp", dp_slots.at[pl.ds(0, count - 1)]),
        ("kv_x", kv_stage.at[pl.ds(0, 3)]),
        ("kv_y", kv_h.at[:, :, 0, 0]),
        ("kv_core", kv_h.at[:, :, 0, 0]),
        ("kv_both", kv_h.at[:, :, 0, 0]),
        ("q", q_stage.at[pl.ds(0, 7)]),
        ("grad", grad_stage.at[pl.ds(0, 7)]),
        ("dq", dq_slots.at[pl.ds(0, 7)]),
        ("core_k", core_slots.at[0]),
        ("core_v", core_slots.at[1]),
        ("y_k", y_stage.at[0]),
        ("y_v", y_stage.at[1]),
        ("x_k", x_slots.at[0, pl.ds(0, 3)]),
        ("x_v", x_slots.at[1, pl.ds(0, 3)]),
    ):
        bulk(name, ref).wait_send()
    core_send.wait_send()
    term_y.wait_send()
    d_y.wait_send()
    for b in range(2):
        to = 4 * x + 2 * b + y
        pl.when(to != j)(lambda to=to: tail_copy(j % 2, to).wait_send())


def finish(loss, gains, *refs):
    size = (len(refs) - 3) // 2
    loss_out, q_out, k_out = refs[size : size + 3]
    loss_out[...] = loss[0:1, 0:1]
    q_out[...] = gains[0:1, :]
    k_out[...] = gains[1:2, :]
    for made, out in zip(refs[:size], refs[size + 3 :]):
        out[...] = made[...]


def shards(
    question_embedding_matrix,
    passage_embedding_matrix,
    positive,
    queries,
    keys,
    values,
    later_grad,
    lengths,
    q_gain,
    k_gain,
    out_weight,
):
    angles = np.arange(2048)[:, None] * rope_base ** (-2.0 * np.arange(64) / 128)[None, :]
    table = jnp.asarray(np.concatenate([np.cos(angles), np.sin(angles)], axis=1).astype(np.float32))
    out = jax.ShapeDtypeStruct
    vm = pltpu.VMEM
    smem = pl.BlockSpec(memory_space=pltpu.SMEM)
    anywhere = pl.BlockSpec(memory_space=pl.ANY)
    results = [
        out(question_embedding_matrix.shape, bf16),
        out(passage_embedding_matrix.shape, bf16),
        out(queries.shape[1:], bf16),
        out(keys.shape[1:], bf16),
        out(values.shape[1:], bf16),
    ]
    loss, gains, *made = pl.pallas_call(
        whole,
        out_shape=[out((1, 128), f32), out((2, 128), f32)] + results,
        in_specs=[smem, smem, anywhere] + [VMEM] * 9,
        out_specs=[VMEM] * 7,
        scratch_shapes=[
            vm((128, 128), f32),
            vm((128, 128), f32),
            vm((128, 128), f32),
            vm((2 * q_stride, 128), f32),
            vm((2 * chunks, 128), f32),
            vm((2 * q_stride * count, 128), bf16),
            vm((2 * chunks * count, 128), bf16),
            vm((2 * q_stride * count, 128), f32),
            vm((2 * chunks * count, 128), f32),
            vm((count, pairs, 256), bf16),
            vm((count, pairs, 256), bf16),
            vm((count, 8, 128), f32),
            vm((count, pairs, 256), bf16),
            vm((count, 8, 128), f32),
            vm((pairs * chunks, 128), f32),
            vm((pairs * chunks, 128), f32),
            vm((pairs * chunks // 2, 128), f32),
            vm((4, 128, 128), f32),
            vm((4, 128, 128), f32),
            vm((2, 64, 128), f32),
            vm((64, 128), f32),
            vm((8, 128, 128), f32),
            vm((2, 64, 128), f32),
            vm((64, 128), f32),
            vm((count, 8, 128), f32),
            vm((count, 8, 128), f32),
            vm((8, 128), f32),
            vm((2, 8, 128), f32),
            vm((4, 2, 128, 128), bf16),
            vm((8, 2, 128, 128), bf16),
            vm((8, 2, 128, 128), bf16),
            vm((2, 4, 2, 2, 128, 128), bf16),
            vm((4, 2, 2, 128, 128), bf16),
            vm((4, 2, 2, 128, 128), bf16),
            vm((4, 512, 128), bf16),
            vm((10, 512, 512), f32),
            vm((10, 512, 512), f32),
            vm((4, 8, 512), f32),
            vm((4, 8, 512), f32),
            vm((128, 512), f32),
            vm((2, 4, 2, 2, 128, 128), f32),
            vm((4, 2, 2, 128, 128), bf16),
            vm((8, 2, 128, 128), bf16),
            vm((2, 4, 2, 128, 128), f32),
            vm((2, 4, 128, 128), f32),
            vm((2, 4, 128, 128), f32),
            vm((2, 4, 128, 128), bf16),
            vm((2, 4, 128, 128), bf16),
            vm((count, 8, 128), f32),
            vm((count, 8, 128), f32),
            pltpu.SemaphoreType.DMA((len(phases),)),
            pltpu.SemaphoreType.DMA((len(phases), 4)),
            pltpu.SemaphoreType.DMA((1,)),
        ],
        compiler_params=pltpu.CompilerParams(
            collective_id=0, has_side_effects=True, vmem_limit_bytes=limit
        ),
    )(
        lengths, positive, table, queries[0], keys[0], values[0], later_grad[0],
        question_embedding_matrix, passage_embedding_matrix, out_weight,
        q_gain[None, :], k_gain[None, :],
    )
    loss, q_gain_grad, k_gain_grad, query_grad, doc_grad, query_cot, key_cot, value_cot = (
        pl.pallas_call(
            finish,
            out_shape=[out((1, 1), f32), out((1, 128), f32), out((1, 128), f32)] + results,
            in_specs=[VMEM] * 7,
            out_specs=[VMEM] * 8,
        )(loss, gains, *made)
    )
    return (
        loss.reshape(()),
        query_grad,
        doc_grad,
        query_cot[None],
        key_cot[None],
        value_cot[None],
        q_gain_grad[0],
        k_gain_grad[0],
    )


def solution(mesh):
    in_specs = (
        P(("dp", "seq"), None),
        P(("dp", "seq"), None),
        P(("dp", "seq")),
        P("dp", "seq", None),
        P("dp", "seq", None),
        P("dp", "seq", None),
        P("dp", "seq", None),
        P("dp"),
        P(),
        P(),
        P("seq", "dp"),
    )
    out_specs = (
        P(),
        P(("dp", "seq"), None),
        P(("dp", "seq"), None),
        P("dp", "seq", None),
        P("dp", "seq", None),
        P("dp", "seq", None),
        P(),
        P(),
    )
    return jax.shard_map(
        shards, mesh=mesh, in_specs=in_specs, out_specs=out_specs, check_vma=False
    )
```

```python
import functools
import math

import jax
import jax.numpy as jnp
import numpy as np
from jax import lax
from jax.experimental import pallas as pl
from jax.experimental.pallas import tpu as pltpu
from jax.sharding import PartitionSpec as P

sharpness = 0.05
epsilon = 1e-06
rope_base = 1000000.0
lowest = -1e30
MESH = pl.DeviceIdType.MESH
f32 = jnp.float32
bf16 = jnp.bfloat16
VMEM = pl.BlockSpec(memory_space=pltpu.VMEM)
limit = 58 * 1024 * 1024
count = 16
pairs = 32
chunks = 32
q_stride = 40
scaling = 128 ** (-0.5)
phases = (
    "q_y", "q_x", "q_core", "p_y", "p_z", "tile", "part", "span", "tail_part", "tail",
    "d_z", "d_y", "term_core", "term_x", "term_y", "gain_seq", "gain_dp",
    "kv_x", "kv_y", "kv_core", "kv_both", "q", "grad", "dq", "core_k", "core_v", "y_k", "y_v", "x_k", "x_v",
)
phase_of = {name: i for i, name in enumerate(phases)}


def mm(a, b):
    return lax.dot_general(a, b, (((1,), (0,)), ((), ())), preferred_element_type=f32)


def mm_nt(a, b):
    return lax.dot_general(a, b, (((1,), (1,)), ((), ())), preferred_element_type=f32)


def mm_tn(a, b):
    return lax.dot_general(a, b, (((0,), (0,)), ((), ())), preferred_element_type=f32)


def loop(first, last, step):
    def body(i, carry):
        step(i)
        return carry

    lax.fori_loop(first, last, body, 0)


def swap_halves(x):
    return pltpu.roll(x, 64, 1)


def normed_rope(x, gain, cosine, sine):
    scale = lax.rsqrt(jnp.mean(x * x, axis=-1, keepdims=True) + epsilon)
    y = x * scale * gain
    return y * cosine + swap_halves(y) * sine


def normed_rope_back(x, gain, cosine, sine, grad):
    scale = lax.rsqrt(jnp.mean(x * x, axis=-1, keepdims=True) + epsilon)
    n = x * scale
    dy = grad * cosine - swap_halves(grad) * sine
    gain_part = dy * n
    dn = dy * gain
    dx = scale * (dn - n * jnp.mean(dn * n, axis=-1, keepdims=True))
    return dx, gain_part


def slot_sum(ref):
    total = ref[0]
    for i in range(1, count):
        total = total + ref[i]
    return total


def whole(
    lengths, positive_in, table, queries, keys, values, later, q_emb, p_emb, out_w, q_gain, k_gain,
    loss_out, gains_out, q_grad_out, d_grad_out, q_cot, k_cot, v_cot,
    turn, cosine, sine,
    q_f32, p_f32, q_all, p_all, q_wide, p_wide, q_cols, p_cols, tiles,
    q_part, spans, q_terms, d_terms, core_in, q_mid, q_in, q_last, q_end,
    d_in, d_last, d_end, tail_stage, tail_slots, tail_send, tail_in,
    kv_stage, q_stage, grad_stage, kv_h, q_h, grad_h,
    grad_low, scores, prob_grads, shares, dots, k_turn, dq_acc, dkv, dq_stage, dq_slots,
    core_slots, y_stage, y_slots, x_stage, x_slots, seq_slots, dp_slots,
    send_sem, recv_sem, own_sem,
):
    d, j = lax.axis_index("dp"), lax.axis_index("seq")
    x, y, c = j // 4, (j // 2) % 2, j % 2
    z, low = d // 2, d % 2
    rank = 2 * x + c
    barrier = pltpu.get_barrier_semaphore()

    def remote(name, src, dst, slot, dp, seq):
        phase = phase_of[name]
        return pltpu.make_async_remote_copy(
            src_ref=src,
            dst_ref=dst,
            send_sem=send_sem.at[phase],
            recv_sem=recv_sem.at[phase, slot],
            device_id=(dp, seq),
            device_id_type=MESH,
        )

    def bulk(name, ref):
        return remote(name, ref, ref, 0, d, j)

    def others(step, me, size=count):
        for o in range(1, size):
            step(lax.rem(me + o, size))

    others(
        lambda p: pl.semaphore_signal(barrier, inc=1, device_id=(d, p), device_id_type=MESH), j
    )
    others(
        lambda p: pl.semaphore_signal(barrier, inc=1, device_id=(p, j), device_id_type=MESH), d
    )
    turn_copy = pltpu.make_async_copy(
        table.at[pl.ds(pl.multiple_of(j * 128, 128), 128)], turn, own_sem.at[0]
    )
    turn_copy.start()

    def lanes(h):
        return pl.ds(pl.multiple_of(h * 128, 128), 128)

    def q_rows(s, size=1):
        return pl.ds(pl.multiple_of(s * 2 * q_stride, 16), size * 2 * q_stride)

    def p_rows(s, size=1):
        return pl.ds(pl.multiple_of(s * 2 * chunks, 16), size * 2 * chunks)

    place = 8 * c + 2 * x + y
    q_f32[...] = jnp.zeros_like(q_f32)
    q_own, p_own = q_emb[...].astype(f32), p_emb[...].astype(f32)
    for i in range(chunks):
        q_f32[pl.ds(i, 2, stride=q_stride), :] = q_own[:, i * 128 : i * 128 + 128]
        p_f32[pl.ds(i, 2, stride=chunks), :] = p_own[:, i * 128 : i * 128 + 128]
    for i in range(2):
        index = positive_in[i]
        spot = i * q_stride + chunks
        q_f32[spot : spot + 1, :] = jnp.full((1, 128), index >> 1, jnp.int32).astype(f32)
        q_f32[spot + 1 : spot + 2, :] = jnp.full((1, 128), index & 1, jnp.int32).astype(f32)
    q_all[q_rows(place), :] = q_f32[...].astype(bf16)
    p_all[p_rows(d), :] = p_f32[...].astype(bf16)
    turn_copy.wait()
    first_half = lax.broadcasted_iota(jnp.int32, (128, 128), 1) < 64
    turned = swap_halves(turn[...])
    cosine[...] = jnp.where(first_half, turn[...], turned)
    sine[...] = jnp.where(first_half, -turned, turn[...])

    def stage_kv(g):
        rot = normed_rope(keys[:, lanes(g)].astype(f32), k_gain[...], cosine[...], sine[...])
        kv_stage[g, 0] = rot.astype(bf16)
        kv_stage[g, 1] = values[:, lanes(g)]

    loop(0, 4, stage_kv)
    pl.semaphore_wait(barrier, 2 * (count - 1))

    over_y = 4 * x + 2 * (1 - y) + c
    over_core = 4 * x + 2 * y + (1 - c)
    over_low = d + 1 - 2 * low

    def beside(p):
        return 4 * p + 2 * y + c

    def gather(name, ref, rows, dp, seq):
        return remote(name, ref.at[rows, :], ref.at[rows, :], 0, dp, seq)

    gather("q_y", q_all, q_rows(place), d, over_y).start()
    gather("p_y", p_all, p_rows(d), over_low, j).start()

    def kv_spot(a, b, e):
        return kv_h.at[:, a, b, e]

    def kv_x(to, source):
        return remote("kv_x", kv_stage.at[to], kv_spot(source, y, c), source, d, beside(to))

    others(lambda p: kv_x(p, x).start(), x, 4)
    kv_h[:, x, y, c] = kv_stage[x]

    def kv_pass(name, a, b, e, seq):
        return remote(name, kv_spot(a, b, e), kv_spot(a, b, e), a, d, seq)

    def pass_on(a):
        kv_pass("kv_y", a, y, c, over_y).start()
        kv_pass("kv_core", a, y, c, over_core).start()

    pass_on(x)

    def stage_q(h):
        rot = normed_rope(queries[:, lanes(h)].astype(f32), q_gain[...], cosine[...], sine[...])
        q_stage[h // 2, h % 2] = rot.astype(bf16)

    def seat(r):
        return 4 * (r // 2) + 2 * y + r % 2

    def head_send(name, stage, held):
        others(
            lambda p: remote(
                name, stage.at[p], held.at[x, :, c], 0, d, seat(p)
            ).start(),
            rank,
            8,
        )
        held[x, :, c] = stage[rank]

    loop(0, 16, stage_q)
    gather("q_y", q_all, q_rows(place), d, over_y).wait_recv()
    own_pair = q_rows(8 * c + 2 * x, 2)
    others(lambda p: gather("q_x", q_all, own_pair, d, beside(p)).start(), x, 4)
    gather("p_y", p_all, p_rows(d), over_low, j).wait_recv()
    own_low = p_rows(2 * z, 2)
    others(lambda p: gather("p_z", p_all, own_low, 2 * p + low, j).start(), z, 8)
    head_send("q", q_stage, q_h)

    bulk("q_x", q_all.at[q_rows(0, 6), :]).wait_recv()
    gather("q_core", q_all, q_rows(8 * c, 8), d, over_core).start()

    def stage_grad(h):
        grad_stage[h // 2, h % 2] = later[:, lanes(h)]

    loop(0, 16, stage_grad)
    dkv[...] = jnp.zeros_like(dkv)

    bulk("p_z", p_all.at[p_rows(0, 14), :]).wait_recv()
    gather("q_core", q_all, q_rows(8 * c, 8), d, over_core).wait_recv()
    q_wide[...] = q_all[...].astype(f32)
    p_wide[...] = p_all[...].astype(f32)
    for i in range(chunks):
        half = pl.ds((i % 2) * 128, 128)
        q_cols[i // 2, :, half] = q_wide[pl.ds(i, pairs, stride=q_stride), :].astype(bf16)
        p_cols[i // 2, :, half] = p_wide[pl.ds(i, pairs, stride=chunks), :].astype(bf16)
    positive = (
        2.0 * q_wide[pl.ds(chunks, pairs, stride=q_stride), :]
        + q_wide[pl.ds(chunks + 1, pairs, stride=q_stride), :]
    )

    def four(block):
        return jnp.concatenate([block] * (128 // pairs), axis=0)

    def one(block):
        return block[:32] + block[32:64] + block[64:96] + block[96:]

    logits = mm_nt(q_cols[0], four(p_cols[0]))
    for b in range(1, count):
        logits = logits + mm_nt(q_cols[b], four(p_cols[b]))
    logits = logits / sharpness
    quarter_of = lax.broadcasted_iota(jnp.int32, (8, 128), 1) >> 5

    def pack(block):
        packed = block[:8]
        for i in range(1, 4):
            packed = jnp.where(quarter_of == i, block[8 * i : 8 * i + 8], packed)
        return packed

    tiles[j] = pack(logits)

    def tile_copy(p):
        return remote("tile", tiles.at[j], tiles.at[j], 0, d, p)

    others(lambda p: tile_copy(p).start(), j)

    def part_copy(p):
        return remote("part", q_cols.at[p], q_part.at[d], 0, p, j)

    others(lambda p: part_copy(p).start(), d)
    q_part[d] = q_cols[d]
    head_send("grad", grad_stage, grad_h)
    lane = lax.broadcasted_iota(jnp.int32, (pairs, 128), 1)
    line = lax.broadcasted_iota(jnp.int32, (pairs, 128), 0)
    real = (lane >> 5) == (line >> 3)
    base = jnp.where(real, ((lane & 31) >> 1) * pairs + (lane & 1), -(1 << 20)).astype(f32)

    def pass_arrived(a):
        kv_x(a, a).wait_recv()
        pass_on(a)

    others(pass_arrived, x, 4)

    bulk("tile", tiles.at[pl.ds(0, count - 1)]).wait_recv()
    high = tiles[0]
    for i in range(1, count):
        high = jnp.maximum(high, tiles[i])
    high = jnp.max(jnp.where(real, four(high), lowest), axis=1, keepdims=True)
    mass = jnp.zeros((pairs, 128), f32)
    hit = jnp.zeros((pairs, 128), f32)
    for i in range(count):
        tile = four(tiles[i])
        mass = mass + jnp.where(real, jnp.exp(tile - high), 0.0)
        hit = hit + jnp.where(base + 2.0 * i == positive, tile, 0.0)
    log_total = high + jnp.log(jnp.sum(mass, axis=1, keepdims=True))
    picked = jnp.sum(hit, axis=1, keepdims=True)
    loss_part = jnp.sum(log_total - picked, axis=0, keepdims=True)

    def weights_of(tile, index):
        onehot = jnp.where(base + 2.0 * index == positive, 1.0, 0.0)
        return jnp.where(real, (jnp.exp(four(tile) - log_total) - onehot) / sharpness, 0.0)

    spans[d] = pack(weights_of(tiles[0], 0.0).astype(bf16).astype(f32))

    def span_copy(p):
        return remote("span", spans.at[d], spans.at[d], 0, p, j)

    others(lambda p: span_copy(p).start(), d)
    mine = weights_of(tiles[j], j.astype(f32))
    w = mine.astype(bf16)
    w_t = one(jnp.transpose(mine)).astype(bf16)

    def pass_from_y(o):
        a = lax.rem(x + o, 4)
        kv_pass("kv_y", a, 1 - y, c, over_y).wait_recv()
        kv_pass("kv_both", a, 1 - y, c, over_core).start()

    loop(0, 4, pass_from_y)


    def kv_core_arrive(a):
        kv_pass("kv_core", a, y, 1 - c, over_core).wait_recv()
        kv_pass("kv_both", a, 1 - y, 1 - c, over_core).wait_recv()

    loop(0, 4, kv_core_arrive)
    bulk("q", q_stage.at[pl.ds(0, 7)]).wait_recv()
    length = lengths[0]
    key_spot = lax.broadcasted_iota(jnp.int32, (512, 512), 0)
    query_spot = lax.broadcasted_iota(jnp.int32, (512, 512), 1) & 255

    def fold(block, op):
        return op(block.reshape(64, 8, 512), axis=0)

    def spot_of(a, b):
        return (a * (a + 1)) // 2 + b

    def softmax_rows(o):
        a = 3 - o
        q = q_h[a].reshape(512, 128)

        def first(b, top, diagonal):
            s = mm_nt(kv_h[0, b].reshape(512, 128), q) * (scaling * math.log2(math.e))
            allowed = key_spot < length - b * 512
            if diagonal:
                allowed = allowed & (key_spot - query_spot <= 256 * y)
            s = jnp.where(allowed, s, lowest)
            scores[spot_of(a, b)] = s
            return jnp.maximum(top, fold(s, jnp.max))

        top = jnp.full((8, 512), lowest, f32)
        top = lax.fori_loop(0, a, lambda b, t: first(b, t, False), top)
        top = jnp.max(first(a, top, True), axis=0, keepdims=True)

        def second(b, total):
            e = jnp.exp2(scores[spot_of(a, b)] - top)
            scores[spot_of(a, b)] = e
            return total + fold(e, jnp.sum)

        total = lax.fori_loop(0, a + 1, second, jnp.zeros((8, 512), f32))
        shares[a] = jnp.broadcast_to(1.0 / jnp.sum(total, axis=0, keepdims=True), (8, 512))

    softmax_rows(0)

    bulk("part", q_part.at[pl.ds(0, count - 1)]).wait_recv()
    bulk("span", spans.at[pl.ds(0, count - 1)]).wait_recv()
    span = jnp.zeros((128, 256), f32)
    for i in range(count):
        weights = jnp.where(real, four(spans[i]), 0.0).astype(bf16)
        span = span + mm_tn(weights, q_part[i])
    span = one(span).astype(bf16)
    tail_rows = mm_nt(span, out_w[...])
    for i in range(count):
        tail_stage[i, pl.ds(0, 4)] = jnp.broadcast_to(tail_rows[2 * i : 2 * i + 1], (4, 128))
        tail_stage[i, pl.ds(4, 4)] = jnp.broadcast_to(loss_part, (4, 128))

    def tail_part(p):
        return remote("tail_part", tail_stage.at[p], tail_slots.at[d], 0, p, j)

    others(lambda p: tail_part(p).start(), d)
    tail_slots[d] = tail_stage[d]

    loop(1, 4, softmax_rows)

    bulk("tail_part", tail_slots.at[pl.ds(0, count - 1)]).wait_recv()
    tails = slot_sum(tail_slots)
    loss_out[...] = tails[4:5] / (pairs * count)
    tail_send[...] = jnp.broadcast_to(tails[0:1], (8, 128))

    def tail_copy(slot, seq):
        return remote("tail", tail_send, tail_in.at[slot], slot, d, seq)

    for b in range(2):
        to = 4 * x + 2 * b + y
        pl.when(to != j)(lambda to=to: tail_copy(j % 2, to).start())

        @pl.when(to == j)
        def _():
            tail_in[j % 2] = tail_send[...]

    for b in range(count):
        q_term = mm(w, four(p_cols[b]))
        d_term = mm(w_t, q_cols[b])
        for half in range(2):
            rows = pl.ds(2 * b + half, pairs, stride=chunks)
            q_terms[rows, :] = q_term[:, half * 128 : half * 128 + 128]
            d_terms[rows, :] = d_term[:, half * 128 : half * 128 + 128]

    def d_copy(p):
        return remote("d_z", d_terms.at[p_rows(2 * p, 2), :], d_in.at[z], 0, 2 * p + low, j)

    others(lambda p: d_copy(p).start(), z, 8)
    d_in[z] = d_terms[p_rows(2 * z, 2), :]
    core_send = remote("term_core", q_terms.at[p_rows(8 * (1 - c), 8), :], core_in, 0, d, over_core)
    core_send.start()
    bulk("grad", grad_stage.at[pl.ds(0, 7)]).wait_recv()
    for b in range(2):
        source = 4 * x + 2 * c + b
        pl.when(source != j)(lambda b=b, source=source: tail_copy(b, source).wait_recv())
    row = lax.broadcasted_iota(jnp.int32, (512, 1), 0)
    row_token = (row & 255) + 256 * y

    def core_copy(t, a):
        name = ("core_k", "core_v")[t]
        return remote(name, dkv.at[t, a, :, 1 - c], core_slots.at[t, a], a, d, over_core)

    def y_copy(t, a):
        return remote(("y_k", "y_v")[t], y_stage.at[t, a], y_slots.at[t, a], a, d, over_y)

    def x_copy(t, to):
        name = ("x_k", "x_v")[t]
        return remote(name, x_stage.at[t, to], x_slots.at[t, x], 0, d, beside(to))

    def dq_copy(a, e):
        return remote("dq", dq_stage.at[a, :, e], dq_slots.at[rank], 0, d, 4 * a + 2 * y + e)

    def send_y(t, a):
        core_copy(t, a).wait_recv()
        y_stage[t, a] = dkv[t, a, 1 - y, c] + core_slots[t, a, 1 - y]
        y_copy(t, a).start()

    def send_x(t, a):
        y_copy(t, a).wait_recv()
        total = dkv[t, a, y, c] + core_slots[t, a, y] + y_slots[t, a]
        x_stage[t, a] = total.astype(bf16)

        @pl.when(a != x)
        def _():
            x_copy(t, a).start()

        @pl.when(a == x)
        def _():
            x_slots[t, x] = x_stage[t, a]

    def make_grad(a):
        spot = row_token + 512 * a
        extra = jnp.where(row < 256, tail_in[0, 0:1], tail_in[1, 0:1])
        last = jnp.where(spot == length - 1, 1.0, 0.0)
        grad = grad_h[a].reshape(512, 128).astype(f32) + last * extra
        grad_low[a] = jnp.where(spot < length, grad, 0.0).astype(bf16)

    def turn_keys(b):
        k_turn[b] = jnp.transpose(kv_h[0, b].reshape(512, 128).astype(f32)).astype(bf16)

    loop(0, 4, turn_keys)
    loop(0, 4, make_grad)
    dots[...] = jnp.zeros_like(dots)

    def value_block(o):
        b = 3 - o

        def rows(a):
            low = (scores[spot_of(a, b)] * shares[a, 0:1]).astype(bf16)
            prob_grad = mm_nt(kv_h[1, b].reshape(512, 128), grad_low[a])
            prob_grads[spot_of(a, b)] = prob_grad
            dkv[1, b] += mm(low, grad_low[a]).reshape(2, 2, 128, 128)
            dots[a] += fold(low.astype(f32) * prob_grad, jnp.sum)

        loop(b, 4, rows)
        core_copy(1, b).start()
        pl.when(o >= 1)(lambda: send_y(1, b + 1))

    loop(0, 4, value_block)
    core_send.wait_recv()
    sums = q_terms[p_rows(8 * c, 8), :] + core_in[...]
    q_mid[...] = sums.reshape(4, 128, 128)

    def term_x(p):
        return remote("term_x", q_mid.at[p], q_in.at[x], 0, d, beside(p))

    others(lambda p: term_x(p).start(), x, 4)
    q_in[x] = q_mid[x]

    def quarter(o):
        a = 3 - o
        q = q_h[a].reshape(512, 128)
        row_dot = jnp.sum(dots[a], axis=0, keepdims=True)
        factor = shares[a, 0:1] * scaling
        dq_acc[...] = jnp.zeros_like(dq_acc)

        def keys_of(b):
            spot = spot_of(a, b)
            sg = (scores[spot] * factor * (prob_grads[spot] - row_dot)).astype(bf16)
            dkv[0, b] += mm(sg, q).reshape(2, 2, 128, 128)
            dq_acc[...] += mm(k_turn[b], sg)

        loop(0, a + 1, keys_of)
        core_copy(0, a).start()
        dq_stage[a] = jnp.transpose(dq_acc[...]).astype(bf16).reshape(2, 2, 128, 128)
        for e in range(2):

            @pl.when(2 * a + e != rank)
            def _():
                dq_copy(a, e).start()

            @pl.when(2 * a + e == rank)
            def _():
                dq_slots[rank] = dq_stage[a, :, e]

        pl.when(o == 0)(lambda: send_y(1, 0))
        pl.when(o >= 1)(lambda: send_y(0, a + 1))
        send_x(1, a)
        pl.when(o >= 2)(lambda: send_x(0, a + 2))

    loop(0, 4, quarter)
    send_y(0, 0)
    bulk("term_x", q_in.at[pl.ds(0, 3)]).wait_recv()
    q_last[...] = (q_in[0] + q_in[1] + q_in[2] + q_in[3]).reshape(2, 64, 128)
    term_y = remote("term_y", q_last.at[1 - y], q_end, 0, d, over_y)
    term_y.start()
    bulk("d_z", d_in.at[pl.ds(0, 7)]).wait_recv()
    d_sum = d_in[0]
    for i in range(1, 8):
        d_sum = d_sum + d_in[i]
    d_last[...] = d_sum.reshape(2, 64, 128)
    d_y = remote("d_y", d_last.at[1 - low], d_end, 0, over_low, j)
    d_y.start()
    send_x(0, 1)

    bulk("dq", dq_slots.at[pl.ds(0, 7)]).wait_recv()

    def gain_fold(block):
        return jnp.sum(block.reshape(16, 8, 128), axis=0)

    def query_head(h, total):
        grad = dq_slots[h // 2, h % 2].astype(f32)
        dx, part = normed_rope_back(
            queries[:, lanes(h)].astype(f32), q_gain[...], cosine[...], sine[...], grad
        )
        q_cot[:, lanes(h)] = dx.astype(bf16)
        return total + gain_fold(part)

    q_total = lax.fori_loop(0, 16, query_head, jnp.zeros((8, 128), f32))
    send_x(0, 0)
    term_y.wait_recv()
    d_y.wait_recv()
    q_f32[pl.ds(0, 2 * chunks), :] = q_last[y] + q_end[...]
    p_f32[...] = d_last[low] + d_end[...]
    for i in range(chunks):
        part = pl.ds(i * 128, 128)
        q_grad_out[:, part] = q_f32[pl.ds(i, 2, stride=chunks), :].astype(bf16)
        d_grad_out[:, part] = p_f32[pl.ds(i, 2, stride=chunks), :].astype(bf16)
    bulk("x_v", x_slots.at[1, pl.ds(0, 3)]).wait_recv()
    bulk("x_k", x_slots.at[0, pl.ds(0, 3)]).wait_recv()

    def key_head(g, total):
        v_cot[:, lanes(g)] = x_slots[1, g]
        dx, part = normed_rope_back(
            keys[:, lanes(g)].astype(f32), k_gain[...], cosine[...], sine[...],
            x_slots[0, g].astype(f32),
        )
        k_cot[:, lanes(g)] = dx.astype(bf16)
        return total + gain_fold(part)

    k_total = lax.fori_loop(0, 4, key_head, jnp.zeros((8, 128), f32))
    seq_slots[j, pl.ds(0, 4)] = q_total[:4] + q_total[4:]
    seq_slots[j, pl.ds(4, 4)] = k_total[:4] + k_total[4:]

    def gain_seq(p):
        return remote("gain_seq", seq_slots.at[j], seq_slots.at[j], 0, d, p)

    others(lambda p: gain_seq(p).start(), j)
    bulk("gain_seq", seq_slots.at[pl.ds(0, count - 1)]).wait_recv()
    dp_slots[d] = slot_sum(seq_slots)

    def gain_dp(p):
        return remote("gain_dp", dp_slots.at[d], dp_slots.at[d], 0, p, j)

    others(lambda p: gain_dp(p).start(), d)
    bulk("gain_dp", dp_slots.at[pl.ds(0, count - 1)]).wait_recv()
    gains = slot_sum(dp_slots)
    gains_out[0:1, :] = jnp.sum(gains[:4], axis=0, keepdims=True)
    gains_out[1:2, :] = jnp.sum(gains[4:], axis=0, keepdims=True)

    gather("q_y", q_all, q_rows(place), d, over_y).wait_send()
    gather("p_y", p_all, p_rows(d), over_low, j).wait_send()
    gather("q_core", q_all, q_rows(8 * c, 8), d, over_core).wait_send()
    for name, ref in (
        ("q_x", q_all.at[q_rows(0, 6), :]),
        ("p_z", p_all.at[p_rows(0, 14), :]),
        ("tile", tiles.at[pl.ds(0, count - 1)]),
        ("part", q_part.at[pl.ds(0, count - 1)]),
        ("span", spans.at[pl.ds(0, count - 1)]),
        ("tail_part", tail_slots.at[pl.ds(0, count - 1)]),
        ("d_z", d_in.at[pl.ds(0, 7)]),
        ("term_x", q_in.at[pl.ds(0, 3)]),
        ("gain_seq", seq_slots.at[pl.ds(0, count - 1)]),
        ("gain_dp", dp_slots.at[pl.ds(0, count - 1)]),
        ("kv_x", kv_stage.at[pl.ds(0, 3)]),
        ("kv_y", kv_h.at[:, :, 0, 0]),
        ("kv_core", kv_h.at[:, :, 0, 0]),
        ("kv_both", kv_h.at[:, :, 0, 0]),
        ("q", q_stage.at[pl.ds(0, 7)]),
        ("grad", grad_stage.at[pl.ds(0, 7)]),
        ("dq", dq_slots.at[pl.ds(0, 7)]),
        ("core_k", core_slots.at[0]),
        ("core_v", core_slots.at[1]),
        ("y_k", y_stage.at[0]),
        ("y_v", y_stage.at[1]),
        ("x_k", x_slots.at[0, pl.ds(0, 3)]),
        ("x_v", x_slots.at[1, pl.ds(0, 3)]),
    ):
        bulk(name, ref).wait_send()
    core_send.wait_send()
    term_y.wait_send()
    d_y.wait_send()
    for b in range(2):
        to = 4 * x + 2 * b + y
        pl.when(to != j)(lambda to=to: tail_copy(j % 2, to).wait_send())


def finish(loss, gains, *refs):
    size = (len(refs) - 3) // 2
    loss_out, q_out, k_out = refs[size : size + 3]
    loss_out[...] = loss[0:1, 0:1]
    q_out[...] = gains[0:1, :]
    k_out[...] = gains[1:2, :]
    for made, out in zip(refs[:size], refs[size + 3 :]):
        out[...] = made[...]


def shards(
    question_embedding_matrix,
    passage_embedding_matrix,
    positive,
    queries,
    keys,
    values,
    later_grad,
    lengths,
    q_gain,
    k_gain,
    out_weight,
):
    angles = np.arange(2048)[:, None] * rope_base ** (-2.0 * np.arange(64) / 128)[None, :]
    table = jnp.asarray(np.concatenate([np.cos(angles), np.sin(angles)], axis=1).astype(np.float32))
    out = jax.ShapeDtypeStruct
    vm = pltpu.VMEM
    smem = pl.BlockSpec(memory_space=pltpu.SMEM)
    anywhere = pl.BlockSpec(memory_space=pl.ANY)
    results = [
        out(question_embedding_matrix.shape, bf16),
        out(passage_embedding_matrix.shape, bf16),
        out(queries.shape[1:], bf16),
        out(keys.shape[1:], bf16),
        out(values.shape[1:], bf16),
    ]
    loss, gains, *made = pl.pallas_call(
        whole,
        out_shape=[out((1, 128), f32), out((2, 128), f32)] + results,
        in_specs=[smem, smem, anywhere] + [VMEM] * 9,
        out_specs=[VMEM] * 7,
        scratch_shapes=[
            vm((128, 128), f32),
            vm((128, 128), f32),
            vm((128, 128), f32),
            vm((2 * q_stride, 128), f32),
            vm((2 * chunks, 128), f32),
            vm((2 * q_stride * count, 128), bf16),
            vm((2 * chunks * count, 128), bf16),
            vm((2 * q_stride * count, 128), f32),
            vm((2 * chunks * count, 128), f32),
            vm((count, pairs, 256), bf16),
            vm((count, pairs, 256), bf16),
            vm((count, 8, 128), f32),
            vm((count, pairs, 256), bf16),
            vm((count, 8, 128), f32),
            vm((pairs * chunks, 128), f32),
            vm((pairs * chunks, 128), f32),
            vm((pairs * chunks // 2, 128), f32),
            vm((4, 128, 128), f32),
            vm((4, 128, 128), f32),
            vm((2, 64, 128), f32),
            vm((64, 128), f32),
            vm((8, 128, 128), f32),
            vm((2, 64, 128), f32),
            vm((64, 128), f32),
            vm((count, 8, 128), f32),
            vm((count, 8, 128), f32),
            vm((8, 128), f32),
            vm((2, 8, 128), f32),
            vm((4, 2, 128, 128), bf16),
            vm((8, 2, 128, 128), bf16),
            vm((8, 2, 128, 128), bf16),
            vm((2, 4, 2, 2, 128, 128), bf16),
            vm((4, 2, 2, 128, 128), bf16),
            vm((4, 2, 2, 128, 128), bf16),
            vm((4, 512, 128), bf16),
            vm((10, 512, 512), f32),
            vm((10, 512, 512), f32),
            vm((4, 8, 512), f32),
            vm((4, 8, 512), f32),
            vm((4, 128, 512), bf16),
            vm((128, 512), f32),
            vm((2, 4, 2, 2, 128, 128), f32),
            vm((4, 2, 2, 128, 128), bf16),
            vm((8, 2, 128, 128), bf16),
            vm((2, 4, 2, 128, 128), f32),
            vm((2, 4, 128, 128), f32),
            vm((2, 4, 128, 128), f32),
            vm((2, 4, 128, 128), bf16),
            vm((2, 4, 128, 128), bf16),
            vm((count, 8, 128), f32),
            vm((count, 8, 128), f32),
            pltpu.SemaphoreType.DMA((len(phases),)),
            pltpu.SemaphoreType.DMA((len(phases), 4)),
            pltpu.SemaphoreType.DMA((1,)),
        ],
        compiler_params=pltpu.CompilerParams(
            collective_id=0, has_side_effects=True, vmem_limit_bytes=limit
        ),
    )(
        lengths, positive, table, queries[0], keys[0], values[0], later_grad[0],
        question_embedding_matrix, passage_embedding_matrix, out_weight,
        q_gain[None, :], k_gain[None, :],
    )
    loss, q_gain_grad, k_gain_grad, query_grad, doc_grad, query_cot, key_cot, value_cot = (
        pl.pallas_call(
            finish,
            out_shape=[out((1, 1), f32), out((1, 128), f32), out((1, 128), f32)] + results,
            in_specs=[VMEM] * 7,
            out_specs=[VMEM] * 8,
        )(loss, gains, *made)
    )
    return (
        loss.reshape(()),
        query_grad,
        doc_grad,
        query_cot[None],
        key_cot[None],
        value_cot[None],
        q_gain_grad[0],
        k_gain_grad[0],
    )


def solution(mesh):
    in_specs = (
        P(("dp", "seq"), None),
        P(("dp", "seq"), None),
        P(("dp", "seq")),
        P("dp", "seq", None),
        P("dp", "seq", None),
        P("dp", "seq", None),
        P("dp", "seq", None),
        P("dp"),
        P(),
        P(),
        P("seq", "dp"),
    )
    out_specs = (
        P(),
        P(("dp", "seq"), None),
        P(("dp", "seq"), None),
        P("dp", "seq", None),
        P("dp", "seq", None),
        P("dp", "seq", None),
        P(),
        P(),
    )
    return jax.shard_map(
        shards, mesh=mesh, in_specs=in_specs, out_specs=out_specs, check_vma=False
    )
```

```python
import functools
import math

import jax
import jax.numpy as jnp
import numpy as np
from jax import lax
from jax.experimental import pallas as pl
from jax.experimental.pallas import tpu as pltpu
from jax.sharding import PartitionSpec as P

sharpness = 0.05
epsilon = 1e-06
rope_base = 1000000.0
lowest = -1e30
MESH = pl.DeviceIdType.MESH
f32 = jnp.float32
bf16 = jnp.bfloat16
VMEM = pl.BlockSpec(memory_space=pltpu.VMEM)
limit = 58 * 1024 * 1024
count = 16
pairs = 32
chunks = 32
q_stride = 40
scaling = 128 ** (-0.5)
phases = (
    "q_y", "q_x", "q_core", "p_y", "p_z", "tile", "part", "span", "tail_part", "tail",
    "d_z", "d_y", "term_core", "term_x", "term_y", "gain_seq", "gain_dp",
    "k_x", "k_y", "k_core", "k_both", "v_x", "v_y", "v_core", "v_both", "q", "grad", "dq", "core_sum_k", "core_sum_v", "y_sum_k", "y_sum_v",
    "x_out_k", "x_out_v",
)
phase_of = {name: i for i, name in enumerate(phases)}


def mm(a, b):
    return lax.dot_general(a, b, (((1,), (0,)), ((), ())), preferred_element_type=f32)


def mm_nt(a, b):
    return lax.dot_general(a, b, (((1,), (1,)), ((), ())), preferred_element_type=f32)


def mm_tn(a, b):
    return lax.dot_general(a, b, (((0,), (0,)), ((), ())), preferred_element_type=f32)


def loop(first, last, step, unroll=None):
    def body(i, carry):
        step(i)
        return carry

    lax.fori_loop(first, last, body, 0, unroll=unroll)


def swap_halves(x):
    return pltpu.roll(x, 64, 1)


def normed_rope(x, gain, cosine, sine):
    scale = lax.rsqrt(jnp.mean(x * x, axis=-1, keepdims=True) + epsilon)
    y = x * scale * gain
    return y * cosine + swap_halves(y) * sine


def normed_rope_back(x, gain, cosine, sine, grad):
    scale = lax.rsqrt(jnp.mean(x * x, axis=-1, keepdims=True) + epsilon)
    n = x * scale
    dy = grad * cosine - swap_halves(grad) * sine
    gain_part = dy * n
    dn = dy * gain
    dx = scale * (dn - n * jnp.mean(dn * n, axis=-1, keepdims=True))
    return dx, gain_part


def slot_sum(ref):
    total = ref[0]
    for i in range(1, count):
        total = total + ref[i]
    return total


def whole(
    lengths, positive_in, table, queries, keys, values, later, q_emb, p_emb, out_w, q_gain, k_gain,
    loss_out, gains_out, q_grad_out, d_grad_out, q_cot, k_cot, v_cot,
    turn, cosine, sine,
    q_f32, p_f32, q_all, p_all, q_wide, p_wide, q_cols, p_cols, tiles,
    q_part, spans, q_terms, d_terms, core_in, q_mid, q_in, q_last, q_end,
    d_in, d_last, d_end, tail_stage, tail_slots, tail_send, tail_in,
    kv_stage, q_stage, grad_stage, kv_h, q_h, grad_h,
    grad_low, scores, prob_grads, shares, dots, k_turn, dq_acc, dkv, dq_stage, dq_slots,
    core_slots, y_stage, y_slots, x_stage, x_slots, seq_slots, dp_slots,
    send_sem, recv_sem, own_sem,
):
    d, j = lax.axis_index("dp"), lax.axis_index("seq")
    x, y, c = j // 4, (j // 2) % 2, j % 2
    z, low = d // 2, d % 2
    rank = 2 * x + c
    barrier = pltpu.get_barrier_semaphore()

    def remote(name, src, dst, slot, dp, seq):
        phase = phase_of[name]
        return pltpu.make_async_remote_copy(
            src_ref=src,
            dst_ref=dst,
            send_sem=send_sem.at[phase],
            recv_sem=recv_sem.at[phase, slot],
            device_id=(dp, seq),
            device_id_type=MESH,
        )

    def bulk(name, ref):
        return remote(name, ref, ref, 0, d, j)

    def others(step, me, size=count):
        for o in range(1, size):
            step(lax.rem(me + o, size))

    others(
        lambda p: pl.semaphore_signal(barrier, inc=1, device_id=(d, p), device_id_type=MESH), j
    )
    others(
        lambda p: pl.semaphore_signal(barrier, inc=1, device_id=(p, j), device_id_type=MESH), d
    )
    turn_copy = pltpu.make_async_copy(
        table.at[pl.ds(pl.multiple_of(j * 128, 128), 128)], turn, own_sem.at[0]
    )
    turn_copy.start()

    def lanes(h):
        return pl.ds(pl.multiple_of(h * 128, 128), 128)

    def q_rows(s, size=1):
        return pl.ds(pl.multiple_of(s * 2 * q_stride, 16), size * 2 * q_stride)

    def p_rows(s, size=1):
        return pl.ds(pl.multiple_of(s * 2 * chunks, 16), size * 2 * chunks)

    place = 8 * c + 2 * x + y
    q_f32[...] = jnp.zeros_like(q_f32)
    q_own, p_own = q_emb[...].astype(f32), p_emb[...].astype(f32)
    for i in range(chunks):
        q_f32[pl.ds(i, 2, stride=q_stride), :] = q_own[:, i * 128 : i * 128 + 128]
        p_f32[pl.ds(i, 2, stride=chunks), :] = p_own[:, i * 128 : i * 128 + 128]
    for i in range(2):
        index = positive_in[i]
        spot = i * q_stride + chunks
        q_f32[spot : spot + 1, :] = jnp.full((1, 128), index >> 1, jnp.int32).astype(f32)
        q_f32[spot + 1 : spot + 2, :] = jnp.full((1, 128), index & 1, jnp.int32).astype(f32)
    q_all[q_rows(place), :] = q_f32[...].astype(bf16)
    p_all[p_rows(d), :] = p_f32[...].astype(bf16)
    turn_copy.wait()
    first_half = lax.broadcasted_iota(jnp.int32, (128, 128), 1) < 64
    turned = swap_halves(turn[...])
    cosine[...] = jnp.where(first_half, turn[...], turned)
    sine[...] = jnp.where(first_half, -turned, turn[...])

    def stage_kv(g):
        rot = normed_rope(keys[:, lanes(g)].astype(f32), k_gain[...], cosine[...], sine[...])
        kv_stage[g, 0] = rot.astype(bf16)
        kv_stage[g, 1] = values[:, lanes(g)]

    loop(0, 4, stage_kv, unroll=True)
    pl.semaphore_wait(barrier, 2 * (count - 1))

    over_y = 4 * x + 2 * (1 - y) + c
    over_core = 4 * x + 2 * y + (1 - c)
    over_low = d + 1 - 2 * low

    def beside(p):
        return 4 * p + 2 * y + c

    def gather(name, ref, rows, dp, seq):
        return remote(name, ref.at[rows, :], ref.at[rows, :], 0, dp, seq)

    gather("q_y", q_all, q_rows(place), d, over_y).start()
    gather("p_y", p_all, p_rows(d), over_low, j).start()

    def x_copies(t, step):
        def copy(to):
            name, src = ("k_x", "v_x")[t], kv_stage.at[to, t]
            step(remote(name, src, kv_h.at[t, x, y, c], 0, d, beside(to)))

        others(copy, x, 4)

    def kv_pass(t, way, of_y, of_core, seq):
        block = kv_h.at[t, :, of_y, of_core]
        return remote("kv"[t] + way, block, block, 0, d, seq)

    def pass_on(t):
        bulk(("k_x", "v_x")[t], kv_h.at[t, pl.ds(0, 3), y, c]).wait_recv()
        kv_pass(t, "_y", y, c, over_y).start()
        kv_pass(t, "_core", y, c, over_core).start()

    def pass_from_y(t):
        kv_pass(t, "_y", 1 - y, c, over_y).wait_recv()
        kv_pass(t, "_both", 1 - y, c, over_core).start()

    def kv_arrive(t):
        kv_pass(t, "_core", y, 1 - c, over_core).wait_recv()
        kv_pass(t, "_both", 1 - y, 1 - c, over_core).wait_recv()

    x_copies(0, lambda copy: copy.start())
    kv_h[:, x, y, c] = kv_stage[x]

    def stage_q(h):
        rot = normed_rope(queries[:, lanes(h)].astype(f32), q_gain[...], cosine[...], sine[...])
        q_stage[h // 2, h % 2] = rot.astype(bf16)

    def seat(r):
        return 4 * (r // 2) + 2 * y + r % 2

    def head_send(name, stage, held):
        others(
            lambda p: remote(
                name, stage.at[p], held.at[x, :, c], 0, d, seat(p)
            ).start(),
            rank,
            8,
        )
        held[x, :, c] = stage[rank]

    loop(0, 16, stage_q, unroll=4)
    gather("q_y", q_all, q_rows(place), d, over_y).wait_recv()
    own_pair = q_rows(8 * c + 2 * x, 2)
    others(lambda p: gather("q_x", q_all, own_pair, d, beside(p)).start(), x, 4)
    gather("p_y", p_all, p_rows(d), over_low, j).wait_recv()
    own_low = p_rows(2 * z, 2)
    others(lambda p: gather("p_z", p_all, own_low, 2 * p + low, j).start(), z, 8)
    pass_on(0)
    head_send("q", q_stage, q_h)

    bulk("q_x", q_all.at[q_rows(0, 6), :]).wait_recv()
    gather("q_core", q_all, q_rows(8 * c, 8), d, over_core).start()

    def stage_grad(h):
        grad_stage[h // 2, h % 2] = later[:, lanes(h)]

    loop(0, 16, stage_grad)
    dkv[...] = jnp.zeros_like(dkv)

    bulk("p_z", p_all.at[p_rows(0, 14), :]).wait_recv()
    gather("q_core", q_all, q_rows(8 * c, 8), d, over_core).wait_recv()
    q_wide[...] = q_all[...].astype(f32)
    p_wide[...] = p_all[...].astype(f32)
    for i in range(chunks):
        half = pl.ds((i % 2) * 128, 128)
        q_cols[i // 2, :, half] = q_wide[pl.ds(i, pairs, stride=q_stride), :].astype(bf16)
        p_cols[i // 2, :, half] = p_wide[pl.ds(i, pairs, stride=chunks), :].astype(bf16)
    positive = (
        2.0 * q_wide[pl.ds(chunks, pairs, stride=q_stride), :]
        + q_wide[pl.ds(chunks + 1, pairs, stride=q_stride), :]
    )

    def four(block):
        return jnp.concatenate([block] * (128 // pairs), axis=0)

    def one(block):
        return block[:32] + block[32:64] + block[64:96] + block[96:]

    logits = mm_nt(q_cols[0], four(p_cols[0]))
    for b in range(1, count):
        logits = logits + mm_nt(q_cols[b], four(p_cols[b]))
    logits = logits / sharpness
    quarter_of = lax.broadcasted_iota(jnp.int32, (8, 128), 1) >> 5

    def pack(block):
        packed = block[:8]
        for i in range(1, 4):
            packed = jnp.where(quarter_of == i, block[8 * i : 8 * i + 8], packed)
        return packed

    tiles[j] = pack(logits)

    def tile_copy(p):
        return remote("tile", tiles.at[j], tiles.at[j], 0, d, p)

    others(lambda p: tile_copy(p).start(), j)
    x_copies(1, lambda copy: copy.start())

    def part_copy(p):
        return remote("part", q_cols.at[p], q_part.at[d], 0, p, j)

    others(lambda p: part_copy(p).start(), d)
    q_part[d] = q_cols[d]
    head_send("grad", grad_stage, grad_h)
    lane = lax.broadcasted_iota(jnp.int32, (pairs, 128), 1)
    line = lax.broadcasted_iota(jnp.int32, (pairs, 128), 0)
    real = (lane >> 5) == (line >> 3)
    base = jnp.where(real, ((lane & 31) >> 1) * pairs + (lane & 1), -(1 << 20)).astype(f32)

    pass_from_y(0)

    bulk("tile", tiles.at[pl.ds(0, count - 1)]).wait_recv()
    high = tiles[0]
    for i in range(1, count):
        high = jnp.maximum(high, tiles[i])
    high = jnp.max(jnp.where(real, four(high), lowest), axis=1, keepdims=True)
    mass = jnp.zeros((pairs, 128), f32)
    hit = jnp.zeros((pairs, 128), f32)
    for i in range(count):
        tile = four(tiles[i])
        mass = mass + jnp.where(real, jnp.exp(tile - high), 0.0)
        hit = hit + jnp.where(base + 2.0 * i == positive, tile, 0.0)
    log_total = high + jnp.log(jnp.sum(mass, axis=1, keepdims=True))
    picked = jnp.sum(hit, axis=1, keepdims=True)
    loss_part = jnp.sum(log_total - picked, axis=0, keepdims=True)

    def weights_of(tile, index):
        onehot = jnp.where(base + 2.0 * index == positive, 1.0, 0.0)
        return jnp.where(real, (jnp.exp(four(tile) - log_total) - onehot) / sharpness, 0.0)

    spans[d] = pack(weights_of(tiles[0], 0.0).astype(bf16).astype(f32))

    def span_copy(p):
        return remote("span", spans.at[d], spans.at[d], 0, p, j)

    others(lambda p: span_copy(p).start(), d)
    mine = weights_of(tiles[j], j.astype(f32))
    w = mine.astype(bf16)
    w_t = one(jnp.transpose(mine)).astype(bf16)

    pass_on(1)

    kv_arrive(0)
    bulk("q", q_stage.at[pl.ds(0, 7)]).wait_recv()
    length = lengths[0]
    key_spot = lax.broadcasted_iota(jnp.int32, (512, 512), 0)
    query_spot = lax.broadcasted_iota(jnp.int32, (512, 512), 1) & 255

    def fold(block, op):
        return op(block.reshape(64, 8, 512), axis=0)

    def spot_of(a, b):
        return (a * (a + 1)) // 2 + b

    def softmax_rows(o):
        a = 3 - o
        q = q_h[a].reshape(512, 128)

        def first(b, top, diagonal):
            s = mm_nt(kv_h[0, b].reshape(512, 128), q) * (scaling * math.log2(math.e))
            allowed = key_spot < length - b * 512
            if diagonal:
                allowed = allowed & (key_spot - query_spot <= 256 * y)
            s = jnp.where(allowed, s, lowest)
            scores[spot_of(a, b)] = s
            return jnp.maximum(top, fold(s, jnp.max))

        top = jnp.full((8, 512), lowest, f32)
        top = lax.fori_loop(0, a, lambda b, t: first(b, t, False), top)
        top = jnp.max(first(a, top, True), axis=0, keepdims=True)

        def second(b, total):
            e = jnp.exp2(scores[spot_of(a, b)] - top)
            scores[spot_of(a, b)] = e
            return total + fold(e, jnp.sum)

        total = lax.fori_loop(0, a + 1, second, jnp.zeros((8, 512), f32))
        shares[a] = jnp.broadcast_to(1.0 / jnp.sum(total, axis=0, keepdims=True), (8, 512))

    softmax_rows(0)

    bulk("part", q_part.at[pl.ds(0, count - 1)]).wait_recv()
    bulk("span", spans.at[pl.ds(0, count - 1)]).wait_recv()
    span = jnp.zeros((128, 256), f32)
    for i in range(count):
        weights = jnp.where(real, four(spans[i]), 0.0).astype(bf16)
        span = span + mm_tn(weights, q_part[i])
    span = one(span).astype(bf16)
    tail_rows = mm_nt(span, out_w[...])
    for i in range(count):
        tail_stage[i, pl.ds(0, 4)] = jnp.broadcast_to(tail_rows[2 * i : 2 * i + 1], (4, 128))
        tail_stage[i, pl.ds(4, 4)] = jnp.broadcast_to(loss_part, (4, 128))

    def tail_part(p):
        return remote("tail_part", tail_stage.at[p], tail_slots.at[d], 0, p, j)

    others(lambda p: tail_part(p).start(), d)
    tail_slots[d] = tail_stage[d]

    pass_from_y(1)
    loop(1, 4, softmax_rows)

    bulk("tail_part", tail_slots.at[pl.ds(0, count - 1)]).wait_recv()
    tails = slot_sum(tail_slots)
    loss_out[...] = tails[4:5] / (pairs * count)
    tail_send[...] = jnp.broadcast_to(tails[0:1], (8, 128))

    def tail_copy(slot, seq):
        return remote("tail", tail_send, tail_in.at[slot], slot, d, seq)

    for b in range(2):
        to = 4 * x + 2 * b + y
        pl.when(to != j)(lambda to=to: tail_copy(j % 2, to).start())

        @pl.when(to == j)
        def _():
            tail_in[j % 2] = tail_send[...]

    for b in range(count):
        q_term = mm(w, four(p_cols[b]))
        d_term = mm(w_t, q_cols[b])
        for half in range(2):
            rows = pl.ds(2 * b + half, pairs, stride=chunks)
            q_terms[rows, :] = q_term[:, half * 128 : half * 128 + 128]
            d_terms[rows, :] = d_term[:, half * 128 : half * 128 + 128]

    def d_copy(p):
        return remote("d_z", d_terms.at[p_rows(2 * p, 2), :], d_in.at[z], 0, 2 * p + low, j)

    others(lambda p: d_copy(p).start(), z, 8)
    d_in[z] = d_terms[p_rows(2 * z, 2), :]
    core_send = remote("term_core", q_terms.at[p_rows(8 * (1 - c), 8), :], core_in, 0, d, over_core)
    core_send.start()
    kv_arrive(1)
    bulk("grad", grad_stage.at[pl.ds(0, 7)]).wait_recv()
    for b in range(2):
        source = 4 * x + 2 * c + b
        pl.when(source != j)(lambda b=b, source=source: tail_copy(b, source).wait_recv())
    row = lax.broadcasted_iota(jnp.int32, (512, 1), 0)
    row_token = (row & 255) + 256 * y

    def core_copy(t, a):
        name = ("core_sum_k", "core_sum_v")[t]
        return remote(name, dkv.at[t, a, :, 1 - c], core_slots.at[t, a], a, d, over_core)

    def y_copy(t, a):
        return remote(("y_sum_k", "y_sum_v")[t], y_stage.at[t, a], y_slots.at[t, a], a, d, over_y)

    def x_copy(t, to):
        name = ("x_out_k", "x_out_v")[t]
        return remote(name, x_stage.at[t, to], x_slots.at[t, x], 0, d, beside(to))

    def dq_copy(a, e):
        return remote("dq", dq_stage.at[a, :, e], dq_slots.at[rank], 0, d, 4 * a + 2 * y + e)

    def send_y(t, a):
        core_copy(t, a).wait_recv()
        y_stage[t, a] = dkv[t, a, 1 - y, c] + core_slots[t, a, 1 - y]
        y_copy(t, a).start()

    def send_x(t, a):
        y_copy(t, a).wait_recv()
        total = dkv[t, a, y, c] + core_slots[t, a, y] + y_slots[t, a]
        x_stage[t, a] = total.astype(bf16)

        @pl.when(a != x)
        def _():
            x_copy(t, a).start()

        @pl.when(a == x)
        def _():
            x_slots[t, x] = x_stage[t, a]

    def make_grad(a):
        spot = row_token + 512 * a
        extra = jnp.where(row < 256, tail_in[0, 0:1], tail_in[1, 0:1])
        last = jnp.where(spot == length - 1, 1.0, 0.0)
        grad = grad_h[a].reshape(512, 128).astype(f32) + last * extra
        grad_low[a] = jnp.where(spot < length, grad, 0.0).astype(bf16)

    def turn_keys(b):
        k_turn[b] = jnp.transpose(kv_h[0, b].reshape(512, 128).astype(f32)).astype(bf16)

    loop(0, 4, turn_keys)
    loop(0, 4, make_grad)
    dots[...] = jnp.zeros_like(dots)

    def value_block(o):
        b = 3 - o

        def rows(a):
            low = (scores[spot_of(a, b)] * shares[a, 0:1]).astype(bf16)
            prob_grad = mm_nt(kv_h[1, b].reshape(512, 128), grad_low[a])
            prob_grads[spot_of(a, b)] = prob_grad
            dkv[1, b] += mm(low, grad_low[a]).reshape(2, 2, 128, 128)
            dots[a] += fold(low.astype(f32) * prob_grad, jnp.sum)

        loop(b, 4, rows)
        core_copy(1, b).start()
        pl.when(o >= 1)(lambda: send_y(1, b + 1))

    loop(0, 4, value_block)
    core_send.wait_recv()
    sums = q_terms[p_rows(8 * c, 8), :] + core_in[...]
    q_mid[...] = sums.reshape(4, 128, 128)

    def term_x(p):
        return remote("term_x", q_mid.at[p], q_in.at[x], 0, d, beside(p))

    others(lambda p: term_x(p).start(), x, 4)
    q_in[x] = q_mid[x]

    def quarter(o):
        a = 3 - o
        q = q_h[a].reshape(512, 128)
        row_dot = jnp.sum(dots[a], axis=0, keepdims=True)
        factor = shares[a, 0:1] * scaling
        dq_acc[...] = jnp.zeros_like(dq_acc)

        def keys_of(b):
            spot = spot_of(a, b)
            sg = (scores[spot] * factor * (prob_grads[spot] - row_dot)).astype(bf16)
            dkv[0, b] += mm(sg, q).reshape(2, 2, 128, 128)
            dq_acc[...] += mm(k_turn[b], sg)

        loop(0, a + 1, keys_of)
        core_copy(0, a).start()
        dq_stage[a] = jnp.transpose(dq_acc[...]).astype(bf16).reshape(2, 2, 128, 128)
        for e in range(2):

            @pl.when(2 * a + e != rank)
            def _():
                dq_copy(a, e).start()

            @pl.when(2 * a + e == rank)
            def _():
                dq_slots[rank] = dq_stage[a, :, e]

        pl.when(o == 0)(lambda: send_y(1, 0))
        pl.when(o >= 1)(lambda: send_y(0, a + 1))
        send_x(1, a)
        pl.when(o >= 2)(lambda: send_x(0, a + 2))

    loop(0, 4, quarter)
    send_y(0, 0)
    bulk("term_x", q_in.at[pl.ds(0, 3)]).wait_recv()
    q_last[...] = (q_in[0] + q_in[1] + q_in[2] + q_in[3]).reshape(2, 64, 128)
    term_y = remote("term_y", q_last.at[1 - y], q_end, 0, d, over_y)
    term_y.start()
    bulk("d_z", d_in.at[pl.ds(0, 7)]).wait_recv()
    d_sum = d_in[0]
    for i in range(1, 8):
        d_sum = d_sum + d_in[i]
    d_last[...] = d_sum.reshape(2, 64, 128)
    d_y = remote("d_y", d_last.at[1 - low], d_end, 0, over_low, j)
    d_y.start()
    send_x(0, 1)

    bulk("dq", dq_slots.at[pl.ds(0, 7)]).wait_recv()

    def gain_fold(block):
        return jnp.sum(block.reshape(16, 8, 128), axis=0)

    def query_head(h, total):
        grad = dq_slots[h // 2, h % 2].astype(f32)
        dx, part = normed_rope_back(
            queries[:, lanes(h)].astype(f32), q_gain[...], cosine[...], sine[...], grad
        )
        q_cot[:, lanes(h)] = dx.astype(bf16)
        return total + gain_fold(part)

    q_total = lax.fori_loop(0, 16, query_head, jnp.zeros((8, 128), f32), unroll=4)
    send_x(0, 0)
    term_y.wait_recv()
    d_y.wait_recv()
    q_f32[pl.ds(0, 2 * chunks), :] = q_last[y] + q_end[...]
    p_f32[...] = d_last[low] + d_end[...]
    for i in range(chunks):
        part = pl.ds(i * 128, 128)
        q_grad_out[:, part] = q_f32[pl.ds(i, 2, stride=chunks), :].astype(bf16)
        d_grad_out[:, part] = p_f32[pl.ds(i, 2, stride=chunks), :].astype(bf16)
    bulk("x_out_v", x_slots.at[1, pl.ds(0, 3)]).wait_recv()
    bulk("x_out_k", x_slots.at[0, pl.ds(0, 3)]).wait_recv()

    def key_head(g, total):
        v_cot[:, lanes(g)] = x_slots[1, g]
        dx, part = normed_rope_back(
            keys[:, lanes(g)].astype(f32), k_gain[...], cosine[...], sine[...],
            x_slots[0, g].astype(f32),
        )
        k_cot[:, lanes(g)] = dx.astype(bf16)
        return total + gain_fold(part)

    k_total = lax.fori_loop(0, 4, key_head, jnp.zeros((8, 128), f32), unroll=True)
    seq_slots[j, pl.ds(0, 4)] = q_total[:4] + q_total[4:]
    seq_slots[j, pl.ds(4, 4)] = k_total[:4] + k_total[4:]

    def gain_seq(p):
        return remote("gain_seq", seq_slots.at[j], seq_slots.at[j], 0, d, p)

    others(lambda p: gain_seq(p).start(), j)
    bulk("gain_seq", seq_slots.at[pl.ds(0, count - 1)]).wait_recv()
    dp_slots[d] = slot_sum(seq_slots)

    def gain_dp(p):
        return remote("gain_dp", dp_slots.at[d], dp_slots.at[d], 0, p, j)

    others(lambda p: gain_dp(p).start(), d)
    bulk("gain_dp", dp_slots.at[pl.ds(0, count - 1)]).wait_recv()
    gains = slot_sum(dp_slots)
    gains_out[0:1, :] = jnp.sum(gains[:4], axis=0, keepdims=True)
    gains_out[1:2, :] = jnp.sum(gains[4:], axis=0, keepdims=True)

    gather("q_y", q_all, q_rows(place), d, over_y).wait_send()
    gather("p_y", p_all, p_rows(d), over_low, j).wait_send()
    gather("q_core", q_all, q_rows(8 * c, 8), d, over_core).wait_send()
    for name, ref in (
        ("q_x", q_all.at[q_rows(0, 6), :]),
        ("p_z", p_all.at[p_rows(0, 14), :]),
        ("tile", tiles.at[pl.ds(0, count - 1)]),
        ("part", q_part.at[pl.ds(0, count - 1)]),
        ("span", spans.at[pl.ds(0, count - 1)]),
        ("tail_part", tail_slots.at[pl.ds(0, count - 1)]),
        ("d_z", d_in.at[pl.ds(0, 7)]),
        ("term_x", q_in.at[pl.ds(0, 3)]),
        ("gain_seq", seq_slots.at[pl.ds(0, count - 1)]),
        ("gain_dp", dp_slots.at[pl.ds(0, count - 1)]),
        ("k_x", kv_stage.at[pl.ds(0, 3), 0]),
        ("v_x", kv_stage.at[pl.ds(0, 3), 1]),
        ("k_y", kv_h.at[0, :, 0, 0]),
        ("v_y", kv_h.at[1, :, 0, 0]),
        ("k_core", kv_h.at[0, :, 0, 0]),
        ("v_core", kv_h.at[1, :, 0, 0]),
        ("k_both", kv_h.at[0, :, 0, 0]),
        ("v_both", kv_h.at[1, :, 0, 0]),
        ("q", q_stage.at[pl.ds(0, 7)]),
        ("grad", grad_stage.at[pl.ds(0, 7)]),
        ("dq", dq_slots.at[pl.ds(0, 7)]),
        ("core_sum_k", core_slots.at[0]),
        ("core_sum_v", core_slots.at[1]),
        ("y_sum_k", y_stage.at[0]),
        ("y_sum_v", y_stage.at[1]),
        ("x_out_k", x_slots.at[0, pl.ds(0, 3)]),
        ("x_out_v", x_slots.at[1, pl.ds(0, 3)]),
    ):
        bulk(name, ref).wait_send()
    core_send.wait_send()
    term_y.wait_send()
    d_y.wait_send()
    for b in range(2):
        to = 4 * x + 2 * b + y
        pl.when(to != j)(lambda to=to: tail_copy(j % 2, to).wait_send())


def finish(loss, gains, *refs):
    size = (len(refs) - 3) // 2
    loss_out, q_out, k_out = refs[size : size + 3]
    loss_out[...] = loss[0:1, 0:1]
    q_out[...] = gains[0:1, :]
    k_out[...] = gains[1:2, :]
    for made, out in zip(refs[:size], refs[size + 3 :]):
        out[...] = made[...]


def shards(
    question_embedding_matrix,
    passage_embedding_matrix,
    positive,
    queries,
    keys,
    values,
    later_grad,
    lengths,
    q_gain,
    k_gain,
    out_weight,
):
    angles = np.arange(2048)[:, None] * rope_base ** (-2.0 * np.arange(64) / 128)[None, :]
    table = jnp.asarray(np.concatenate([np.cos(angles), np.sin(angles)], axis=1).astype(np.float32))
    out = jax.ShapeDtypeStruct
    vm = pltpu.VMEM
    smem = pl.BlockSpec(memory_space=pltpu.SMEM)
    anywhere = pl.BlockSpec(memory_space=pl.ANY)
    results = [
        out(question_embedding_matrix.shape, bf16),
        out(passage_embedding_matrix.shape, bf16),
        out(queries.shape[1:], bf16),
        out(keys.shape[1:], bf16),
        out(values.shape[1:], bf16),
    ]
    loss, gains, *made = pl.pallas_call(
        whole,
        out_shape=[out((1, 128), f32), out((2, 128), f32)] + results,
        in_specs=[smem, smem, anywhere] + [VMEM] * 9,
        out_specs=[VMEM] * 7,
        scratch_shapes=[
            vm((128, 128), f32),
            vm((128, 128), f32),
            vm((128, 128), f32),
            vm((2 * q_stride, 128), f32),
            vm((2 * chunks, 128), f32),
            vm((2 * q_stride * count, 128), bf16),
            vm((2 * chunks * count, 128), bf16),
            vm((2 * q_stride * count, 128), f32),
            vm((2 * chunks * count, 128), f32),
            vm((count, pairs, 256), bf16),
            vm((count, pairs, 256), bf16),
            vm((count, 8, 128), f32),
            vm((count, pairs, 256), bf16),
            vm((count, 8, 128), f32),
            vm((pairs * chunks, 128), f32),
            vm((pairs * chunks, 128), f32),
            vm((pairs * chunks // 2, 128), f32),
            vm((4, 128, 128), f32),
            vm((4, 128, 128), f32),
            vm((2, 64, 128), f32),
            vm((64, 128), f32),
            vm((8, 128, 128), f32),
            vm((2, 64, 128), f32),
            vm((64, 128), f32),
            vm((count, 8, 128), f32),
            vm((count, 8, 128), f32),
            vm((8, 128), f32),
            vm((2, 8, 128), f32),
            vm((4, 2, 128, 128), bf16),
            vm((8, 2, 128, 128), bf16),
            vm((8, 2, 128, 128), bf16),
            vm((2, 4, 2, 2, 128, 128), bf16),
            vm((4, 2, 2, 128, 128), bf16),
            vm((4, 2, 2, 128, 128), bf16),
            vm((4, 512, 128), bf16),
            vm((10, 512, 512), f32),
            vm((10, 512, 512), f32),
            vm((4, 8, 512), f32),
            vm((4, 8, 512), f32),
            vm((4, 128, 512), bf16),
            vm((128, 512), f32),
            vm((2, 4, 2, 2, 128, 128), f32),
            vm((4, 2, 2, 128, 128), bf16),
            vm((8, 2, 128, 128), bf16),
            vm((2, 4, 2, 128, 128), f32),
            vm((2, 4, 128, 128), f32),
            vm((2, 4, 128, 128), f32),
            vm((2, 4, 128, 128), bf16),
            vm((2, 4, 128, 128), bf16),
            vm((count, 8, 128), f32),
            vm((count, 8, 128), f32),
            pltpu.SemaphoreType.DMA((len(phases),)),
            pltpu.SemaphoreType.DMA((len(phases), 4)),
            pltpu.SemaphoreType.DMA((1,)),
        ],
        compiler_params=pltpu.CompilerParams(
            collective_id=0, has_side_effects=True, vmem_limit_bytes=limit
        ),
    )(
        lengths, positive, table, queries[0], keys[0], values[0], later_grad[0],
        question_embedding_matrix, passage_embedding_matrix, out_weight,
        q_gain[None, :], k_gain[None, :],
    )
    loss, q_gain_grad, k_gain_grad, query_grad, doc_grad, query_cot, key_cot, value_cot = (
        pl.pallas_call(
            finish,
            out_shape=[out((1, 1), f32), out((1, 128), f32), out((1, 128), f32)] + results,
            in_specs=[VMEM] * 7,
            out_specs=[VMEM] * 8,
        )(loss, gains, *made)
    )
    return (
        loss.reshape(()),
        query_grad,
        doc_grad,
        query_cot[None],
        key_cot[None],
        value_cot[None],
        q_gain_grad[0],
        k_gain_grad[0],
    )


def solution(mesh):
    in_specs = (
        P(("dp", "seq"), None),
        P(("dp", "seq"), None),
        P(("dp", "seq")),
        P("dp", "seq", None),
        P("dp", "seq", None),
        P("dp", "seq", None),
        P("dp", "seq", None),
        P("dp"),
        P(),
        P(),
        P("seq", "dp"),
    )
    out_specs = (
        P(),
        P(("dp", "seq"), None),
        P(("dp", "seq"), None),
        P("dp", "seq", None),
        P("dp", "seq", None),
        P("dp", "seq", None),
        P(),
        P(),
    )
    return jax.shard_map(
        shards, mesh=mesh, in_specs=in_specs, out_specs=out_specs, check_vma=False
    )
```

```python
import functools
import math

import jax
import jax.numpy as jnp
import numpy as np
from jax import lax
from jax.experimental import pallas as pl
from jax.experimental.pallas import tpu as pltpu
from jax.sharding import PartitionSpec as P

sharpness = 0.05
epsilon = 1e-06
rope_base = 1000000.0
lowest = -1e30
MESH = pl.DeviceIdType.MESH
f32 = jnp.float32
bf16 = jnp.bfloat16
VMEM = pl.BlockSpec(memory_space=pltpu.VMEM)
limit = 58 * 1024 * 1024
count = 16
pairs = 32
chunks = 32
q_stride = 40
scaling = 128 ** (-0.5)
phases = (
    "q_y", "q_x", "q_core", "p_y", "p_z", "tile", "part", "span", "tail_part", "tail",
    "d_z", "d_y", "term_core", "term_x", "term_y", "gain_seq", "gain_dp",
    "k_x", "k_y", "k_core", "k_both", "v_x", "v_y", "v_core", "v_both", "q", "grad", "dq", "core_sum_k", "core_sum_v", "y_sum_k", "y_sum_v",
    "x_out_k", "x_out_v",
)
phase_of = {name: i for i, name in enumerate(phases)}


def mm(a, b):
    return lax.dot_general(a, b, (((1,), (0,)), ((), ())), preferred_element_type=f32)


def mm_nt(a, b):
    return lax.dot_general(a, b, (((1,), (1,)), ((), ())), preferred_element_type=f32)


def mm_tn(a, b):
    return lax.dot_general(a, b, (((0,), (0,)), ((), ())), preferred_element_type=f32)


def loop(first, last, step, unroll=None):
    def body(i, carry):
        step(i)
        return carry

    lax.fori_loop(first, last, body, 0, unroll=unroll)


def swap_halves(x):
    return pltpu.roll(x, 64, 1)


def normed_rope(x, gain, cosine, sine):
    scale = lax.rsqrt(jnp.mean(x * x, axis=-1, keepdims=True) + epsilon)
    y = x * scale * gain
    return y * cosine + swap_halves(y) * sine


def normed_rope_back(x, gain, cosine, sine, grad):
    scale = lax.rsqrt(jnp.mean(x * x, axis=-1, keepdims=True) + epsilon)
    n = x * scale
    dy = grad * cosine - swap_halves(grad) * sine
    gain_part = dy * n
    dn = dy * gain
    dx = scale * (dn - n * jnp.mean(dn * n, axis=-1, keepdims=True))
    return dx, gain_part


def slot_sum(ref):
    total = ref[0]
    for i in range(1, count):
        total = total + ref[i]
    return total


def whole(
    lengths, positive_in, table, queries, keys, values, later, q_emb, p_emb, out_w, q_gain, k_gain,
    loss_out, gains_out, q_grad_out, d_grad_out, q_cot, k_cot, v_cot,
    turn, cosine, sine,
    q_f32, p_f32, q_all, p_all, q_wide, p_wide, q_cols, p_cols, tiles,
    q_part, spans, q_terms, d_terms, core_in, q_mid, q_in, q_last, q_end,
    d_in, d_last, d_end, tail_stage, tail_slots, tail_send, tail_in,
    kv_stage, q_stage, grad_stage, kv_h, q_h, grad_h,
    grad_low, grad_turn, scores, tops, sums, factors, attn, k_turn, v_turn, dq_acc, dkv, dq_stage, dq_slots,
    core_slots, y_stage, y_slots, x_stage, x_slots, seq_slots, dp_slots,
    send_sem, recv_sem, own_sem,
):
    d, j = lax.axis_index("dp"), lax.axis_index("seq")
    x, y, c = j // 4, (j // 2) % 2, j % 2
    z, low = d // 2, d % 2
    rank = 2 * x + c
    barrier = pltpu.get_barrier_semaphore()

    def remote(name, src, dst, slot, dp, seq):
        phase = phase_of[name]
        return pltpu.make_async_remote_copy(
            src_ref=src,
            dst_ref=dst,
            send_sem=send_sem.at[phase],
            recv_sem=recv_sem.at[phase, slot],
            device_id=(dp, seq),
            device_id_type=MESH,
        )

    def bulk(name, ref):
        return remote(name, ref, ref, 0, d, j)

    def others(step, me, size=count):
        for o in range(1, size):
            step(lax.rem(me + o, size))

    others(
        lambda p: pl.semaphore_signal(barrier, inc=1, device_id=(d, p), device_id_type=MESH), j
    )
    others(
        lambda p: pl.semaphore_signal(barrier, inc=1, device_id=(p, j), device_id_type=MESH), d
    )
    turn_copy = pltpu.make_async_copy(
        table.at[pl.ds(pl.multiple_of(j * 128, 128), 128)], turn, own_sem.at[0]
    )
    turn_copy.start()

    def lanes(h):
        return pl.ds(pl.multiple_of(h * 128, 128), 128)

    def q_rows(s, size=1):
        return pl.ds(pl.multiple_of(s * 2 * q_stride, 16), size * 2 * q_stride)

    def p_rows(s, size=1):
        return pl.ds(pl.multiple_of(s * 2 * chunks, 16), size * 2 * chunks)

    place = 8 * c + 2 * x + y
    q_f32[...] = jnp.zeros_like(q_f32)
    q_own, p_own = q_emb[...].astype(f32), p_emb[...].astype(f32)
    for i in range(chunks):
        q_f32[pl.ds(i, 2, stride=q_stride), :] = q_own[:, i * 128 : i * 128 + 128]
        p_f32[pl.ds(i, 2, stride=chunks), :] = p_own[:, i * 128 : i * 128 + 128]
    for i in range(2):
        index = positive_in[i]
        spot = i * q_stride + chunks
        q_f32[spot : spot + 1, :] = jnp.full((1, 128), index >> 1, jnp.int32).astype(f32)
        q_f32[spot + 1 : spot + 2, :] = jnp.full((1, 128), index & 1, jnp.int32).astype(f32)
    q_all[q_rows(place), :] = q_f32[...].astype(bf16)
    p_all[p_rows(d), :] = p_f32[...].astype(bf16)
    turn_copy.wait()
    first_half = lax.broadcasted_iota(jnp.int32, (128, 128), 1) < 64
    turned = swap_halves(turn[...])
    cosine[...] = jnp.where(first_half, turn[...], turned)
    sine[...] = jnp.where(first_half, -turned, turn[...])

    def stage_kv(g):
        rot = normed_rope(keys[:, lanes(g)].astype(f32), k_gain[...], cosine[...], sine[...])
        kv_stage[g, 0] = rot.astype(bf16)
        kv_stage[g, 1] = values[:, lanes(g)]

    loop(0, 4, stage_kv, unroll=True)
    pl.semaphore_wait(barrier, 2 * (count - 1))

    over_y = 4 * x + 2 * (1 - y) + c
    over_core = 4 * x + 2 * y + (1 - c)
    over_low = d + 1 - 2 * low

    def beside(p):
        return 4 * p + 2 * y + c

    def gather(name, ref, rows, dp, seq):
        return remote(name, ref.at[rows, :], ref.at[rows, :], 0, dp, seq)

    gather("q_y", q_all, q_rows(place), d, over_y).start()
    gather("p_y", p_all, p_rows(d), over_low, j).start()

    def x_copies(t, step):
        def copy(to):
            name, src = ("k_x", "v_x")[t], kv_stage.at[to, t]
            step(remote(name, src, kv_h.at[t, x, y, c], 0, d, beside(to)))

        others(copy, x, 4)

    def kv_pass(t, way, of_y, of_core, seq):
        block = kv_h.at[t, :, of_y, of_core]
        return remote("kv"[t] + way, block, block, 0, d, seq)

    def pass_on(t):
        bulk(("k_x", "v_x")[t], kv_h.at[t, pl.ds(0, 3), y, c]).wait_recv()
        kv_pass(t, "_y", y, c, over_y).start()
        kv_pass(t, "_core", y, c, over_core).start()

    def pass_from_y(t):
        kv_pass(t, "_y", 1 - y, c, over_y).wait_recv()
        kv_pass(t, "_both", 1 - y, c, over_core).start()

    def kv_arrive(t):
        kv_pass(t, "_core", y, 1 - c, over_core).wait_recv()
        kv_pass(t, "_both", 1 - y, 1 - c, over_core).wait_recv()

    x_copies(0, lambda copy: copy.start())
    kv_h[:, x, y, c] = kv_stage[x]

    def stage_q(h):
        rot = normed_rope(queries[:, lanes(h)].astype(f32), q_gain[...], cosine[...], sine[...])
        q_stage[h // 2, h % 2] = rot.astype(bf16)

    def seat(r):
        return 4 * (r // 2) + 2 * y + r % 2

    def head_send(name, stage, held):
        others(
            lambda p: remote(
                name, stage.at[p], held.at[x, :, c], 0, d, seat(p)
            ).start(),
            rank,
            8,
        )
        held[x, :, c] = stage[rank]

    loop(0, 16, stage_q, unroll=4)
    gather("q_y", q_all, q_rows(place), d, over_y).wait_recv()
    own_pair = q_rows(8 * c + 2 * x, 2)
    others(lambda p: gather("q_x", q_all, own_pair, d, beside(p)).start(), x, 4)
    gather("p_y", p_all, p_rows(d), over_low, j).wait_recv()
    own_low = p_rows(2 * z, 2)
    others(lambda p: gather("p_z", p_all, own_low, 2 * p + low, j).start(), z, 8)
    pass_on(0)
    head_send("q", q_stage, q_h)

    bulk("q_x", q_all.at[q_rows(0, 6), :]).wait_recv()
    gather("q_core", q_all, q_rows(8 * c, 8), d, over_core).start()

    def stage_grad(h):
        grad_stage[h // 2, h % 2] = later[:, lanes(h)]

    loop(0, 16, stage_grad)
    dkv[...] = jnp.zeros_like(dkv)

    bulk("p_z", p_all.at[p_rows(0, 14), :]).wait_recv()
    gather("q_core", q_all, q_rows(8 * c, 8), d, over_core).wait_recv()
    q_wide[...] = q_all[...].astype(f32)
    p_wide[...] = p_all[...].astype(f32)
    for i in range(chunks):
        half = pl.ds((i % 2) * 128, 128)
        q_cols[i // 2, :, half] = q_wide[pl.ds(i, pairs, stride=q_stride), :].astype(bf16)
        p_cols[i // 2, :, half] = p_wide[pl.ds(i, pairs, stride=chunks), :].astype(bf16)
    positive = (
        2.0 * q_wide[pl.ds(chunks, pairs, stride=q_stride), :]
        + q_wide[pl.ds(chunks + 1, pairs, stride=q_stride), :]
    )

    def four(block):
        return jnp.concatenate([block] * (128 // pairs), axis=0)

    def one(block):
        return block[:32] + block[32:64] + block[64:96] + block[96:]

    logits = mm_nt(q_cols[0], four(p_cols[0]))
    for b in range(1, count):
        logits = logits + mm_nt(q_cols[b], four(p_cols[b]))
    logits = logits / sharpness
    quarter_of = lax.broadcasted_iota(jnp.int32, (8, 128), 1) >> 5

    def pack(block):
        packed = block[:8]
        for i in range(1, 4):
            packed = jnp.where(quarter_of == i, block[8 * i : 8 * i + 8], packed)
        return packed

    tiles[j] = pack(logits)

    def tile_copy(p):
        return remote("tile", tiles.at[j], tiles.at[j], 0, d, p)

    others(lambda p: tile_copy(p).start(), j)
    x_copies(1, lambda copy: copy.start())

    def part_copy(p):
        return remote("part", q_cols.at[p], q_part.at[d], 0, p, j)

    others(lambda p: part_copy(p).start(), d)
    q_part[d] = q_cols[d]
    head_send("grad", grad_stage, grad_h)
    lane = lax.broadcasted_iota(jnp.int32, (pairs, 128), 1)
    line = lax.broadcasted_iota(jnp.int32, (pairs, 128), 0)
    real = (lane >> 5) == (line >> 3)
    base = jnp.where(real, ((lane & 31) >> 1) * pairs + (lane & 1), -(1 << 20)).astype(f32)

    pass_from_y(0)

    bulk("tile", tiles.at[pl.ds(0, count - 1)]).wait_recv()
    high = tiles[0]
    for i in range(1, count):
        high = jnp.maximum(high, tiles[i])
    high = jnp.max(jnp.where(real, four(high), lowest), axis=1, keepdims=True)
    mass = jnp.zeros((pairs, 128), f32)
    hit = jnp.zeros((pairs, 128), f32)
    for i in range(count):
        tile = four(tiles[i])
        mass = mass + jnp.where(real, jnp.exp(tile - high), 0.0)
        hit = hit + jnp.where(base + 2.0 * i == positive, tile, 0.0)
    log_total = high + jnp.log(jnp.sum(mass, axis=1, keepdims=True))
    picked = jnp.sum(hit, axis=1, keepdims=True)
    loss_part = jnp.sum(log_total - picked, axis=0, keepdims=True)

    def weights_of(tile, index):
        onehot = jnp.where(base + 2.0 * index == positive, 1.0, 0.0)
        return jnp.where(real, (jnp.exp(four(tile) - log_total) - onehot) / sharpness, 0.0)

    spans[d] = pack(weights_of(tiles[0], 0.0).astype(bf16).astype(f32))

    def span_copy(p):
        return remote("span", spans.at[d], spans.at[d], 0, p, j)

    others(lambda p: span_copy(p).start(), d)
    mine = weights_of(tiles[j], j.astype(f32))
    w = mine.astype(bf16)
    w_t = one(jnp.transpose(mine)).astype(bf16)

    pass_on(1)

    kv_arrive(0)
    bulk("q", q_stage.at[pl.ds(0, 7)]).wait_recv()
    length = lengths[0]
    key_line = lax.broadcasted_iota(jnp.int32, (128, 1), 0)
    ahead = lax.broadcasted_iota(jnp.int32, (128, 256), 0) - lax.broadcasted_iota(
        jnp.int32, (128, 256), 1
    )
    tops[...] = jnp.full_like(tops, lowest)
    sums[...] = jnp.zeros_like(sums)

    def spot_of(a, b):
        return (a * (a + 1)) // 2 + b

    def softmax_rows(o):
        a = 3 - o

        def strips(b, diagonal):
            keys_b = kv_h[0, b].reshape(4, 128, 128)
            for half in range(2):
                q = q_h[a, half].reshape(256, 128)
                across = slice(half * 256, half * 256 + 256)
                for i in range(4):
                    start = b * 512 + i * 128
                    bias = jnp.where(key_line < length - start, 0.0, lowest)
                    s = mm_nt(keys_b[i], q) * (scaling * math.log2(math.e)) + bias
                    if diagonal:
                        s = jnp.where(ahead <= 256 * y - i * 128, s, lowest)
                    top = jnp.max(s, axis=0, keepdims=True)
                    e = jnp.exp2(s - top)
                    scores[spot_of(a, b), i * 128 : i * 128 + 128, across] = e
                    tops[a, b, i : i + 1, across] = top
                    sums[a, b, i : i + 1, across] = jnp.sum(e, axis=0, keepdims=True)

        loop(0, a, lambda b: strips(b, False))
        strips(a, True)
        part_tops = tops[a].reshape(32, 512)
        part = jnp.exp2(part_tops - jnp.max(part_tops, axis=0, keepdims=True))
        total = jnp.sum(part * sums[a].reshape(32, 512), axis=0, keepdims=True)
        factors[a] = (part * (1.0 / total)).reshape(4, 8, 512)

    softmax_rows(0)

    bulk("part", q_part.at[pl.ds(0, count - 1)]).wait_recv()
    bulk("span", spans.at[pl.ds(0, count - 1)]).wait_recv()
    span = jnp.zeros((128, 256), f32)
    for i in range(count):
        weights = jnp.where(real, four(spans[i]), 0.0).astype(bf16)
        span = span + mm_tn(weights, q_part[i])
    span = one(span).astype(bf16)
    tail_rows = mm_nt(span, out_w[...])
    for i in range(count):
        tail_stage[i, pl.ds(0, 4)] = jnp.broadcast_to(tail_rows[2 * i : 2 * i + 1], (4, 128))
        tail_stage[i, pl.ds(4, 4)] = jnp.broadcast_to(loss_part, (4, 128))

    def tail_part(p):
        return remote("tail_part", tail_stage.at[p], tail_slots.at[d], 0, p, j)

    others(lambda p: tail_part(p).start(), d)
    tail_slots[d] = tail_stage[d]

    pass_from_y(1)
    loop(1, 4, softmax_rows)

    bulk("tail_part", tail_slots.at[pl.ds(0, count - 1)]).wait_recv()
    tails = slot_sum(tail_slots)
    loss_out[...] = tails[4:5] / (pairs * count)
    tail_send[...] = jnp.broadcast_to(tails[0:1], (8, 128))

    def tail_copy(slot, seq):
        return remote("tail", tail_send, tail_in.at[slot], slot, d, seq)

    for b in range(2):
        to = 4 * x + 2 * b + y
        pl.when(to != j)(lambda to=to: tail_copy(j % 2, to).start())

        @pl.when(to == j)
        def _():
            tail_in[j % 2] = tail_send[...]

    for b in range(count):
        q_term = mm(w, four(p_cols[b]))
        d_term = mm(w_t, q_cols[b])
        for half in range(2):
            rows = pl.ds(2 * b + half, pairs, stride=chunks)
            q_terms[rows, :] = q_term[:, half * 128 : half * 128 + 128]
            d_terms[rows, :] = d_term[:, half * 128 : half * 128 + 128]

    def d_copy(p):
        return remote("d_z", d_terms.at[p_rows(2 * p, 2), :], d_in.at[z], 0, 2 * p + low, j)

    others(lambda p: d_copy(p).start(), z, 8)
    d_in[z] = d_terms[p_rows(2 * z, 2), :]
    core_send = remote("term_core", q_terms.at[p_rows(8 * (1 - c), 8), :], core_in, 0, d, over_core)
    core_send.start()
    kv_arrive(1)
    bulk("grad", grad_stage.at[pl.ds(0, 7)]).wait_recv()
    for b in range(2):
        source = 4 * x + 2 * c + b
        pl.when(source != j)(lambda b=b, source=source: tail_copy(b, source).wait_recv())
    row = lax.broadcasted_iota(jnp.int32, (512, 1), 0)
    row_token = (row & 255) + 256 * y

    def core_copy(t, a):
        name = ("core_sum_k", "core_sum_v")[t]
        return remote(name, dkv.at[t, a, :, 1 - c], core_slots.at[t, a], a, d, over_core)

    def y_copy(t, a):
        return remote(("y_sum_k", "y_sum_v")[t], y_stage.at[t, a], y_slots.at[t, a], a, d, over_y)

    def x_copy(t, to):
        name = ("x_out_k", "x_out_v")[t]
        return remote(name, x_stage.at[t, to], x_slots.at[t, x], 0, d, beside(to))

    def dq_copy(a, e):
        return remote("dq", dq_stage.at[a, :, e], dq_slots.at[rank], 0, d, 4 * a + 2 * y + e)

    def send_y(t, a):
        core_copy(t, a).wait_recv()
        y_stage[t, a] = dkv[t, a, 1 - y, c] + core_slots[t, a, 1 - y]
        y_copy(t, a).start()

    def send_x(t, a):
        y_copy(t, a).wait_recv()
        total = dkv[t, a, y, c] + core_slots[t, a, y] + y_slots[t, a]
        x_stage[t, a] = total.astype(bf16)

        @pl.when(a != x)
        def _():
            x_copy(t, a).start()

        @pl.when(a == x)
        def _():
            x_slots[t, x] = x_stage[t, a]

    def make_grad(a):
        spot = row_token + 512 * a
        extra = jnp.where(row < 256, tail_in[0, 0:1], tail_in[1, 0:1])
        last = jnp.where(spot == length - 1, 1.0, 0.0)
        grad = grad_h[a].reshape(512, 128).astype(f32) + last * extra
        grad_low[a] = jnp.where(spot < length, grad, 0.0).astype(bf16)

    def turned_block(block):
        return jnp.transpose(block.reshape(512, 128).astype(f32))

    def turn_block(b):
        k_turn[b] = turned_block(kv_h[0, b]).astype(bf16)
        v_turn[b] = turned_block(kv_h[1, b]).astype(bf16)
        grad_turn[b] = turned_block(grad_low[b])

    loop(0, 4, make_grad)
    loop(0, 4, turn_block)
    attn[...] = jnp.zeros_like(attn)

    def value_block(o):
        b = 3 - o

        def rows(a):
            spot = spot_of(a, b)
            low_b = jnp.concatenate(
                [
                    (scores[spot, i * 128 : i * 128 + 128] * factors[a, b, i : i + 1]).astype(bf16)
                    for i in range(4)
                ],
                axis=0,
            )
            dkv[1, b] += mm(low_b, grad_low[a]).reshape(2, 2, 128, 128)
            attn[a] += mm(v_turn[b], low_b)

        loop(b, 4, rows)
        core_copy(1, b).start()
        pl.when(o >= 1)(lambda: send_y(1, b + 1))

    loop(0, 4, value_block)
    core_send.wait_recv()
    both = q_terms[p_rows(8 * c, 8), :] + core_in[...]
    q_mid[...] = both.reshape(4, 128, 128)

    def term_x(p):
        return remote("term_x", q_mid.at[p], q_in.at[x], 0, d, beside(p))

    others(lambda p: term_x(p).start(), x, 4)
    q_in[x] = q_mid[x]

    def quarter(o):
        a = 3 - o
        q = q_h[a].reshape(512, 128)
        row_dot = jnp.sum(grad_turn[a] * attn[a], axis=0, keepdims=True)
        dq_acc[...] = jnp.zeros_like(dq_acc)

        def keys_of(b):
            spot = spot_of(a, b)
            values_b = kv_h[1, b].reshape(4, 128, 128)
            parts = []
            for i in range(4):
                prob_grad = mm_nt(values_b[i], grad_low[a])
                probs = scores[spot, i * 128 : i * 128 + 128] * (factors[a, b, i : i + 1] * scaling)
                parts.append((probs * (prob_grad - row_dot)).astype(bf16))
            sg = jnp.concatenate(parts, axis=0)
            dkv[0, b] += mm(sg, q).reshape(2, 2, 128, 128)
            dq_acc[...] += mm(k_turn[b], sg)

        loop(0, a + 1, keys_of)
        core_copy(0, a).start()
        dq_stage[a] = jnp.transpose(dq_acc[...]).astype(bf16).reshape(2, 2, 128, 128)
        for e in range(2):

            @pl.when(2 * a + e != rank)
            def _():
                dq_copy(a, e).start()

            @pl.when(2 * a + e == rank)
            def _():
                dq_slots[rank] = dq_stage[a, :, e]

        pl.when(o == 0)(lambda: send_y(1, 0))
        pl.when(o >= 1)(lambda: send_y(0, a + 1))
        send_x(1, a)
        pl.when(o >= 2)(lambda: send_x(0, a + 2))

    loop(0, 4, quarter)
    send_y(0, 0)
    bulk("term_x", q_in.at[pl.ds(0, 3)]).wait_recv()
    q_last[...] = (q_in[0] + q_in[1] + q_in[2] + q_in[3]).reshape(2, 64, 128)
    term_y = remote("term_y", q_last.at[1 - y], q_end, 0, d, over_y)
    term_y.start()
    bulk("d_z", d_in.at[pl.ds(0, 7)]).wait_recv()
    d_sum = d_in[0]
    for i in range(1, 8):
        d_sum = d_sum + d_in[i]
    d_last[...] = d_sum.reshape(2, 64, 128)
    d_y = remote("d_y", d_last.at[1 - low], d_end, 0, over_low, j)
    d_y.start()
    send_x(0, 1)

    bulk("dq", dq_slots.at[pl.ds(0, 7)]).wait_recv()

    def gain_fold(block):
        return jnp.sum(block.reshape(16, 8, 128), axis=0)

    def query_head(h, total):
        grad = dq_slots[h // 2, h % 2].astype(f32)
        dx, part = normed_rope_back(
            queries[:, lanes(h)].astype(f32), q_gain[...], cosine[...], sine[...], grad
        )
        q_cot[:, lanes(h)] = dx.astype(bf16)
        return total + gain_fold(part)

    q_total = lax.fori_loop(0, 16, query_head, jnp.zeros((8, 128), f32), unroll=4)
    send_x(0, 0)
    term_y.wait_recv()
    d_y.wait_recv()
    q_f32[pl.ds(0, 2 * chunks), :] = q_last[y] + q_end[...]
    p_f32[...] = d_last[low] + d_end[...]
    for i in range(chunks):
        part = pl.ds(i * 128, 128)
        q_grad_out[:, part] = q_f32[pl.ds(i, 2, stride=chunks), :].astype(bf16)
        d_grad_out[:, part] = p_f32[pl.ds(i, 2, stride=chunks), :].astype(bf16)
    bulk("x_out_v", x_slots.at[1, pl.ds(0, 3)]).wait_recv()
    bulk("x_out_k", x_slots.at[0, pl.ds(0, 3)]).wait_recv()

    def key_head(g, total):
        v_cot[:, lanes(g)] = x_slots[1, g]
        dx, part = normed_rope_back(
            keys[:, lanes(g)].astype(f32), k_gain[...], cosine[...], sine[...],
            x_slots[0, g].astype(f32),
        )
        k_cot[:, lanes(g)] = dx.astype(bf16)
        return total + gain_fold(part)

    k_total = lax.fori_loop(0, 4, key_head, jnp.zeros((8, 128), f32), unroll=True)
    seq_slots[j, pl.ds(0, 4)] = q_total[:4] + q_total[4:]
    seq_slots[j, pl.ds(4, 4)] = k_total[:4] + k_total[4:]

    def gain_seq(p):
        return remote("gain_seq", seq_slots.at[j], seq_slots.at[j], 0, d, p)

    others(lambda p: gain_seq(p).start(), j)
    bulk("gain_seq", seq_slots.at[pl.ds(0, count - 1)]).wait_recv()
    dp_slots[d] = slot_sum(seq_slots)

    def gain_dp(p):
        return remote("gain_dp", dp_slots.at[d], dp_slots.at[d], 0, p, j)

    others(lambda p: gain_dp(p).start(), d)
    bulk("gain_dp", dp_slots.at[pl.ds(0, count - 1)]).wait_recv()
    gains = slot_sum(dp_slots)
    gains_out[0:1, :] = jnp.sum(gains[:4], axis=0, keepdims=True)
    gains_out[1:2, :] = jnp.sum(gains[4:], axis=0, keepdims=True)

    gather("q_y", q_all, q_rows(place), d, over_y).wait_send()
    gather("p_y", p_all, p_rows(d), over_low, j).wait_send()
    gather("q_core", q_all, q_rows(8 * c, 8), d, over_core).wait_send()
    for name, ref in (
        ("q_x", q_all.at[q_rows(0, 6), :]),
        ("p_z", p_all.at[p_rows(0, 14), :]),
        ("tile", tiles.at[pl.ds(0, count - 1)]),
        ("part", q_part.at[pl.ds(0, count - 1)]),
        ("span", spans.at[pl.ds(0, count - 1)]),
        ("tail_part", tail_slots.at[pl.ds(0, count - 1)]),
        ("d_z", d_in.at[pl.ds(0, 7)]),
        ("term_x", q_in.at[pl.ds(0, 3)]),
        ("gain_seq", seq_slots.at[pl.ds(0, count - 1)]),
        ("gain_dp", dp_slots.at[pl.ds(0, count - 1)]),
        ("k_x", kv_stage.at[pl.ds(0, 3), 0]),
        ("v_x", kv_stage.at[pl.ds(0, 3), 1]),
        ("k_y", kv_h.at[0, :, 0, 0]),
        ("v_y", kv_h.at[1, :, 0, 0]),
        ("k_core", kv_h.at[0, :, 0, 0]),
        ("v_core", kv_h.at[1, :, 0, 0]),
        ("k_both", kv_h.at[0, :, 0, 0]),
        ("v_both", kv_h.at[1, :, 0, 0]),
        ("q", q_stage.at[pl.ds(0, 7)]),
        ("grad", grad_stage.at[pl.ds(0, 7)]),
        ("dq", dq_slots.at[pl.ds(0, 7)]),
        ("core_sum_k", core_slots.at[0]),
        ("core_sum_v", core_slots.at[1]),
        ("y_sum_k", y_stage.at[0]),
        ("y_sum_v", y_stage.at[1]),
        ("x_out_k", x_slots.at[0, pl.ds(0, 3)]),
        ("x_out_v", x_slots.at[1, pl.ds(0, 3)]),
    ):
        bulk(name, ref).wait_send()
    core_send.wait_send()
    term_y.wait_send()
    d_y.wait_send()
    for b in range(2):
        to = 4 * x + 2 * b + y
        pl.when(to != j)(lambda to=to: tail_copy(j % 2, to).wait_send())


def finish(loss, gains, *refs):
    size = (len(refs) - 3) // 2
    loss_out, q_out, k_out = refs[size : size + 3]
    loss_out[...] = loss[0:1, 0:1]
    q_out[...] = gains[0:1, :]
    k_out[...] = gains[1:2, :]
    for made, out in zip(refs[:size], refs[size + 3 :]):
        out[...] = made[...]


def shards(
    question_embedding_matrix,
    passage_embedding_matrix,
    positive,
    queries,
    keys,
    values,
    later_grad,
    lengths,
    q_gain,
    k_gain,
    out_weight,
):
    angles = np.arange(2048)[:, None] * rope_base ** (-2.0 * np.arange(64) / 128)[None, :]
    table = jnp.asarray(np.concatenate([np.cos(angles), np.sin(angles)], axis=1).astype(np.float32))
    out = jax.ShapeDtypeStruct
    vm = pltpu.VMEM
    smem = pl.BlockSpec(memory_space=pltpu.SMEM)
    anywhere = pl.BlockSpec(memory_space=pl.ANY)
    results = [
        out(question_embedding_matrix.shape, bf16),
        out(passage_embedding_matrix.shape, bf16),
        out(queries.shape[1:], bf16),
        out(keys.shape[1:], bf16),
        out(values.shape[1:], bf16),
    ]
    loss, gains, *made = pl.pallas_call(
        whole,
        out_shape=[out((1, 128), f32), out((2, 128), f32)] + results,
        in_specs=[smem, smem, anywhere] + [VMEM] * 9,
        out_specs=[VMEM] * 7,
        scratch_shapes=[
            vm((128, 128), f32),
            vm((128, 128), f32),
            vm((128, 128), f32),
            vm((2 * q_stride, 128), f32),
            vm((2 * chunks, 128), f32),
            vm((2 * q_stride * count, 128), bf16),
            vm((2 * chunks * count, 128), bf16),
            vm((2 * q_stride * count, 128), f32),
            vm((2 * chunks * count, 128), f32),
            vm((count, pairs, 256), bf16),
            vm((count, pairs, 256), bf16),
            vm((count, 8, 128), f32),
            vm((count, pairs, 256), bf16),
            vm((count, 8, 128), f32),
            vm((pairs * chunks, 128), f32),
            vm((pairs * chunks, 128), f32),
            vm((pairs * chunks // 2, 128), f32),
            vm((4, 128, 128), f32),
            vm((4, 128, 128), f32),
            vm((2, 64, 128), f32),
            vm((64, 128), f32),
            vm((8, 128, 128), f32),
            vm((2, 64, 128), f32),
            vm((64, 128), f32),
            vm((count, 8, 128), f32),
            vm((count, 8, 128), f32),
            vm((8, 128), f32),
            vm((2, 8, 128), f32),
            vm((4, 2, 128, 128), bf16),
            vm((8, 2, 128, 128), bf16),
            vm((8, 2, 128, 128), bf16),
            vm((2, 4, 2, 2, 128, 128), bf16),
            vm((4, 2, 2, 128, 128), bf16),
            vm((4, 2, 2, 128, 128), bf16),
            vm((4, 512, 128), bf16),
            vm((4, 128, 512), f32),
            vm((10, 512, 512), f32),
            vm((4, 4, 8, 512), f32),
            vm((4, 4, 8, 512), f32),
            vm((4, 4, 8, 512), f32),
            vm((4, 128, 512), f32),
            vm((4, 128, 512), bf16),
            vm((4, 128, 512), bf16),
            vm((128, 512), f32),
            vm((2, 4, 2, 2, 128, 128), f32),
            vm((4, 2, 2, 128, 128), bf16),
            vm((8, 2, 128, 128), bf16),
            vm((2, 4, 2, 128, 128), f32),
            vm((2, 4, 128, 128), f32),
            vm((2, 4, 128, 128), f32),
            vm((2, 4, 128, 128), bf16),
            vm((2, 4, 128, 128), bf16),
            vm((count, 8, 128), f32),
            vm((count, 8, 128), f32),
            pltpu.SemaphoreType.DMA((len(phases),)),
            pltpu.SemaphoreType.DMA((len(phases), 4)),
            pltpu.SemaphoreType.DMA((1,)),
        ],
        compiler_params=pltpu.CompilerParams(
            collective_id=0, has_side_effects=True, vmem_limit_bytes=limit
        ),
    )(
        lengths, positive, table, queries[0], keys[0], values[0], later_grad[0],
        question_embedding_matrix, passage_embedding_matrix, out_weight,
        q_gain[None, :], k_gain[None, :],
    )
    loss, q_gain_grad, k_gain_grad, query_grad, doc_grad, query_cot, key_cot, value_cot = (
        pl.pallas_call(
            finish,
            out_shape=[out((1, 1), f32), out((1, 128), f32), out((1, 128), f32)] + results,
            in_specs=[VMEM] * 7,
            out_specs=[VMEM] * 8,
        )(loss, gains, *made)
    )
    return (
        loss.reshape(()),
        query_grad,
        doc_grad,
        query_cot[None],
        key_cot[None],
        value_cot[None],
        q_gain_grad[0],
        k_gain_grad[0],
    )


def solution(mesh):
    in_specs = (
        P(("dp", "seq"), None),
        P(("dp", "seq"), None),
        P(("dp", "seq")),
        P("dp", "seq", None),
        P("dp", "seq", None),
        P("dp", "seq", None),
        P("dp", "seq", None),
        P("dp"),
        P(),
        P(),
        P("seq", "dp"),
    )
    out_specs = (
        P(),
        P(("dp", "seq"), None),
        P(("dp", "seq"), None),
        P("dp", "seq", None),
        P("dp", "seq", None),
        P("dp", "seq", None),
        P(),
        P(),
    )
    return jax.shard_map(
        shards, mesh=mesh, in_specs=in_specs, out_specs=out_specs, check_vma=False
    )
```

```python
import functools
import math

import jax
import jax.numpy as jnp
import numpy as np
from jax import lax
from jax.experimental import pallas as pl
from jax.experimental.pallas import tpu as pltpu
from jax.sharding import PartitionSpec as P

sharpness = 0.05
epsilon = 1e-06
rope_base = 1000000.0
lowest = -1e30
MESH = pl.DeviceIdType.MESH
f32 = jnp.float32
bf16 = jnp.bfloat16
VMEM = pl.BlockSpec(memory_space=pltpu.VMEM)
limit = 58 * 1024 * 1024
count = 16
pairs = 32
chunks = 32
q_stride = 40
scaling = 128 ** (-0.5)
phases = (
    "q_y", "q_x", "q_core", "p_y", "p_z", "tile", "part", "part_core", "span", "tail_part", "tail",
    "d_out", "term_core", "term_x", "term_y", "gain_seq", "gain_dp",
    "k_x", "k_y", "k_core", "k_both", "v_x", "v_y", "v_core", "v_both", "q", "grad", "dq", "core_sum_k", "core_sum_v", "y_sum_k", "y_sum_v",
    "x_out_k", "x_out_v",
)
phase_of = {name: i for i, name in enumerate(phases)}


def mm(a, b):
    return lax.dot_general(a, b, (((1,), (0,)), ((), ())), preferred_element_type=f32)


def mm_nt(a, b):
    return lax.dot_general(a, b, (((1,), (1,)), ((), ())), preferred_element_type=f32)


def mm_tn(a, b):
    return lax.dot_general(a, b, (((0,), (0,)), ((), ())), preferred_element_type=f32)


def loop(first, last, step, unroll=None):
    def body(i, carry):
        step(i)
        return carry

    lax.fori_loop(first, last, body, 0, unroll=unroll)


def swap_halves(x):
    return pltpu.roll(x, 64, 1)


def normed_rope(x, gain, cosine, sine):
    scale = lax.rsqrt(jnp.mean(x * x, axis=-1, keepdims=True) + epsilon)
    y = x * scale * gain
    return y * cosine + swap_halves(y) * sine


def normed_rope_back(x, gain, cosine, sine, grad):
    scale = lax.rsqrt(jnp.mean(x * x, axis=-1, keepdims=True) + epsilon)
    n = x * scale
    dy = grad * cosine - swap_halves(grad) * sine
    gain_part = dy * n
    dn = dy * gain
    dx = scale * (dn - n * jnp.mean(dn * n, axis=-1, keepdims=True))
    return dx, gain_part


def slot_sum(ref):
    total = ref[0]
    for i in range(1, count):
        total = total + ref[i]
    return total


def whole(
    lengths, positive_in, table, queries, keys, values, later, q_emb, p_emb, out_w, q_gain, k_gain,
    loss_out, gains_out, q_grad_out, d_grad_out, q_cot, k_cot, v_cot,
    turn, cosine, sine,
    q_f32, p_f32, q_all, p_all, q_wide, p_wide, q_cols, p_cols, tiles,
    q_part, spans, span_cat, q_terms, core_in, q_mid, q_in, q_last, q_end,
    d_sum, d_stage, d_in, tail_stage, tail_slots, tail_send, tail_in,
    kv_stage, q_stage, grad_stage, kv_h, q_h, grad_h,
    grad_low, grad_turn, scores, tops, sums, factors, attn, k_turn, v_turn, dq_acc, dkv, dq_stage, dq_slots,
    core_slots, y_stage, y_slots, x_stage, x_slots, seq_slots, dp_slots,
    send_sem, recv_sem, own_sem,
):
    d, j = lax.axis_index("dp"), lax.axis_index("seq")
    x, y, c = j // 4, (j // 2) % 2, j % 2
    z, low = d // 2, d % 2
    rank = 2 * x + c
    barrier = pltpu.get_barrier_semaphore()

    def remote(name, src, dst, slot, dp, seq):
        phase = phase_of[name]
        return pltpu.make_async_remote_copy(
            src_ref=src,
            dst_ref=dst,
            send_sem=send_sem.at[phase],
            recv_sem=recv_sem.at[phase, slot],
            device_id=(dp, seq),
            device_id_type=MESH,
        )

    def bulk(name, ref):
        return remote(name, ref, ref, 0, d, j)

    def others(step, me, size=count):
        for o in range(1, size):
            step(lax.rem(me + o, size))

    others(
        lambda p: pl.semaphore_signal(barrier, inc=1, device_id=(d, p), device_id_type=MESH), j
    )
    others(
        lambda p: pl.semaphore_signal(barrier, inc=1, device_id=(p, j), device_id_type=MESH), d
    )
    turn_copy = pltpu.make_async_copy(
        table.at[pl.ds(pl.multiple_of(j * 128, 128), 128)], turn, own_sem.at[0]
    )
    turn_copy.start()

    def lanes(h):
        return pl.ds(pl.multiple_of(h * 128, 128), 128)

    def q_rows(s, size=1):
        return pl.ds(pl.multiple_of(s * 2 * q_stride, 16), size * 2 * q_stride)

    def p_rows(s, size=1):
        return pl.ds(pl.multiple_of(s * 2 * chunks, 16), size * 2 * chunks)

    place = 8 * c + 2 * x + y
    q_f32[...] = jnp.zeros_like(q_f32)
    q_own, p_own = q_emb[...].astype(f32), p_emb[...].astype(f32)
    for i in range(chunks):
        q_f32[pl.ds(i, 2, stride=q_stride), :] = q_own[:, i * 128 : i * 128 + 128]
        p_f32[pl.ds(i, 2, stride=chunks), :] = p_own[:, i * 128 : i * 128 + 128]
    for i in range(2):
        index = positive_in[i]
        spot = i * q_stride + chunks
        q_f32[spot : spot + 1, :] = jnp.full((1, 128), index >> 1, jnp.int32).astype(f32)
        q_f32[spot + 1 : spot + 2, :] = jnp.full((1, 128), index & 1, jnp.int32).astype(f32)
    q_all[q_rows(place), :] = q_f32[...].astype(bf16)
    p_all[p_rows(d), :] = p_f32[...].astype(bf16)
    turn_copy.wait()
    first_half = lax.broadcasted_iota(jnp.int32, (128, 128), 1) < 64
    turned = swap_halves(turn[...])
    cosine[...] = jnp.where(first_half, turn[...], turned)
    sine[...] = jnp.where(first_half, -turned, turn[...])

    def stage_kv(g):
        rot = normed_rope(keys[:, lanes(g)].astype(f32), k_gain[...], cosine[...], sine[...])
        kv_stage[g, 0] = rot.astype(bf16)
        kv_stage[g, 1] = values[:, lanes(g)]

    loop(0, 4, stage_kv, unroll=True)
    pl.semaphore_wait(barrier, 2 * (count - 1))

    over_y = 4 * x + 2 * (1 - y) + c
    over_core = 4 * x + 2 * y + (1 - c)
    over_low = d + 1 - 2 * low

    def beside(p):
        return 4 * p + 2 * y + c

    def gather(name, ref, rows, dp, seq):
        return remote(name, ref.at[rows, :], ref.at[rows, :], 0, dp, seq)

    gather("q_y", q_all, q_rows(place), d, over_y).start()
    gather("p_y", p_all, p_rows(d), over_low, j).start()

    def x_copies(t, step):
        def copy(to):
            name, src = ("k_x", "v_x")[t], kv_stage.at[to, t]
            step(remote(name, src, kv_h.at[t, x, y, c], 0, d, beside(to)))

        others(copy, x, 4)

    def kv_pass(t, way, of_y, of_core, seq):
        block = kv_h.at[t, :, of_y, of_core]
        return remote("kv"[t] + way, block, block, 0, d, seq)

    def pass_on(t):
        bulk(("k_x", "v_x")[t], kv_h.at[t, pl.ds(0, 3), y, c]).wait_recv()
        kv_pass(t, "_y", y, c, over_y).start()
        kv_pass(t, "_core", y, c, over_core).start()

    def pass_from_y(t):
        kv_pass(t, "_y", 1 - y, c, over_y).wait_recv()
        kv_pass(t, "_both", 1 - y, c, over_core).start()

    def kv_arrive(t):
        kv_pass(t, "_core", y, 1 - c, over_core).wait_recv()
        kv_pass(t, "_both", 1 - y, 1 - c, over_core).wait_recv()

    x_copies(0, lambda copy: copy.start())
    kv_h[:, x, y, c] = kv_stage[x]

    def stage_q(h):
        rot = normed_rope(queries[:, lanes(h)].astype(f32), q_gain[...], cosine[...], sine[...])
        q_stage[h // 2, h % 2] = rot.astype(bf16)

    def seat(r):
        return 4 * (r // 2) + 2 * y + r % 2

    def head_send(name, stage, held):
        others(
            lambda p: remote(
                name, stage.at[p], held.at[x, :, c], 0, d, seat(p)
            ).start(),
            rank,
            8,
        )
        held[x, :, c] = stage[rank]

    loop(0, 16, stage_q, unroll=4)
    gather("q_y", q_all, q_rows(place), d, over_y).wait_recv()
    own_pair = q_rows(8 * c + 2 * x, 2)
    others(lambda p: gather("q_x", q_all, own_pair, d, beside(p)).start(), x, 4)
    gather("p_y", p_all, p_rows(d), over_low, j).wait_recv()
    own_low = p_rows(2 * z, 2)
    others(lambda p: gather("p_z", p_all, own_low, 2 * p + low, j).start(), z, 8)
    pass_on(0)
    head_send("q", q_stage, q_h)

    bulk("q_x", q_all.at[q_rows(0, 6), :]).wait_recv()
    gather("q_core", q_all, q_rows(8 * c, 8), d, over_core).start()

    def stage_grad(h):
        grad_stage[h // 2, h % 2] = later[:, lanes(h)]

    loop(0, 16, stage_grad)
    dkv[...] = jnp.zeros_like(dkv)

    bulk("p_z", p_all.at[p_rows(0, 14), :]).wait_recv()
    gather("q_core", q_all, q_rows(8 * c, 8), d, over_core).wait_recv()
    q_wide[...] = q_all[...].astype(f32)
    p_wide[...] = p_all[...].astype(f32)
    for i in range(chunks):
        half = pl.ds((i % 2) * 128, 128)
        q_cols[i // 2, :, half] = q_wide[pl.ds(i, pairs, stride=q_stride), :].astype(bf16)
        p_cols[i // 2, :, half] = p_wide[pl.ds(i, pairs, stride=chunks), :].astype(bf16)
    positive = (
        2.0 * q_wide[pl.ds(chunks, pairs, stride=q_stride), :]
        + q_wide[pl.ds(chunks + 1, pairs, stride=q_stride), :]
    )

    def four(block):
        return jnp.concatenate([block] * (128 // pairs), axis=0)

    def one(block):
        return block[:32] + block[32:64] + block[64:96] + block[96:]

    logits = mm_nt(q_cols[0], four(p_cols[0]))
    for b in range(1, count):
        logits = logits + mm_nt(q_cols[b], four(p_cols[b]))
    logits = logits / sharpness
    quarter_of = lax.broadcasted_iota(jnp.int32, (8, 128), 1) >> 5

    def pack(block):
        packed = block[:8]
        for i in range(1, 4):
            packed = jnp.where(quarter_of == i, block[8 * i : 8 * i + 8], packed)
        return packed

    tiles[j] = pack(logits)

    def tile_copy(p):
        return remote("tile", tiles.at[j], tiles.at[j], 0, d, p)

    others(lambda p: tile_copy(p).start(), j)
    x_copies(1, lambda copy: copy.start())

    def half_of(core):
        return pl.ds(pl.multiple_of(16 * core, 16), 16)

    def part_copy(p):
        return remote(
            "part", q_cols.at[p, half_of(c)], q_part.at[d, half_of(c)], 0, p, j
        )

    others(lambda p: part_copy(p).start(), d)
    q_part[d, half_of(c)] = q_cols[d, half_of(c)]
    head_send("grad", grad_stage, grad_h)
    lane = lax.broadcasted_iota(jnp.int32, (pairs, 128), 1)
    line = lax.broadcasted_iota(jnp.int32, (pairs, 128), 0)
    real = (lane >> 5) == (line >> 3)
    base = jnp.where(real, ((lane & 31) >> 1) * pairs + (lane & 1), -(1 << 20)).astype(f32)

    pass_from_y(0)

    bulk("tile", tiles.at[pl.ds(0, count - 1)]).wait_recv()
    high = tiles[0]
    for i in range(1, count):
        high = jnp.maximum(high, tiles[i])
    high = jnp.max(jnp.where(real, four(high), lowest), axis=1, keepdims=True)
    mass = jnp.zeros((pairs, 128), f32)
    hit = jnp.zeros((pairs, 128), f32)
    for i in range(count):
        tile = four(tiles[i])
        mass = mass + jnp.where(real, jnp.exp(tile - high), 0.0)
        hit = hit + jnp.where(base + 2.0 * i == positive, tile, 0.0)
    log_total = high + jnp.log(jnp.sum(mass, axis=1, keepdims=True))
    picked = jnp.sum(hit, axis=1, keepdims=True)
    loss_part = jnp.sum(log_total - picked, axis=0, keepdims=True)

    def weights_of(tile, index):
        onehot = jnp.where(base + 2.0 * index == positive, 1.0, 0.0)
        return jnp.where(real, (jnp.exp(four(tile) - log_total) - onehot) / sharpness, 0.0)

    mine = weights_of(tiles[j], j.astype(f32)).astype(bf16)
    spans[d, pl.ds(0, 8)] = pack(weights_of(tiles[0], 0.0).astype(bf16).astype(f32))
    spans[d, pl.ds(8, 8)] = pack(mine.astype(f32))

    def span_copy(p):
        return remote("span", spans.at[d], spans.at[d], 0, p, j)

    others(lambda p: span_copy(p).start(), d)
    pass_on(1)

    kv_arrive(0)
    bulk("q", q_stage.at[pl.ds(0, 7)]).wait_recv()
    length = lengths[0]
    key_line = lax.broadcasted_iota(jnp.int32, (128, 1), 0)
    ahead = lax.broadcasted_iota(jnp.int32, (128, 256), 0) - lax.broadcasted_iota(
        jnp.int32, (128, 256), 1
    )
    tops[...] = jnp.full_like(tops, lowest)
    sums[...] = jnp.zeros_like(sums)

    def spot_of(a, b):
        return (a * (a + 1)) // 2 + b

    def softmax_rows(o):
        a = 3 - o

        def strips(b, diagonal):
            keys_b = kv_h[0, b].reshape(4, 128, 128)
            for half in range(2):
                q = q_h[a, half].reshape(256, 128)
                across = slice(half * 256, half * 256 + 256)
                for i in range(4):
                    start = b * 512 + i * 128
                    bias = jnp.where(key_line < length - start, 0.0, lowest)
                    s = mm_nt(keys_b[i], q) * (scaling * math.log2(math.e)) + bias
                    if diagonal:
                        s = jnp.where(ahead <= 256 * y - i * 128, s, lowest)
                    top = jnp.max(s, axis=0, keepdims=True)
                    e = jnp.exp2(s - top)
                    scores[spot_of(a, b), i * 128 : i * 128 + 128, across] = e
                    tops[a, b, i : i + 1, across] = top
                    sums[a, b, i : i + 1, across] = jnp.sum(e, axis=0, keepdims=True)

        loop(0, a, lambda b: strips(b, False))
        strips(a, True)
        part_tops = tops[a].reshape(32, 512)
        part = jnp.exp2(part_tops - jnp.max(part_tops, axis=0, keepdims=True))
        total = jnp.sum(part * sums[a].reshape(32, 512), axis=0, keepdims=True)
        factors[a] = (part * (1.0 / total)).reshape(4, 8, 512)

    softmax_rows(0)
    bulk("part", q_part.at[pl.ds(0, count - 1), pl.ds(0, 16)]).wait_recv()
    part_core = remote(
        "part_core", q_part.at[:, half_of(c)], q_part.at[:, half_of(c)], 0, d, over_core
    )
    part_core.start()
    softmax_rows(1)

    bulk("span", spans.at[pl.ds(0, count - 1)]).wait_recv()
    for i in range(count):
        for t in range(2):
            weights = jnp.where(real, four(spans[i, t * 8 : t * 8 + 8]), 0.0)
            span_cat[i, :, t * 128 : t * 128 + 128] = weights.astype(bf16)
    remote(
        "part_core", q_part.at[:, half_of(1 - c)], q_part.at[:, half_of(1 - c)], 0, d, over_core
    ).wait_recv()
    span_sums = mm_tn(
        span_cat[...].reshape(pairs * count, 256), q_part[...].reshape(pairs * count, 256)
    )
    span = one(span_sums[:128]).astype(bf16)
    d_sums = one(span_sums[128:])
    d_sum[pl.ds(0, pairs), :] = d_sums[:, :128]
    d_sum[pl.ds(pairs, pairs), :] = d_sums[:, 128:]
    tail_rows = mm_nt(span, out_w[...])
    for i in range(count):
        tail_stage[i, pl.ds(0, 4)] = jnp.broadcast_to(tail_rows[2 * i : 2 * i + 1], (4, 128))
        tail_stage[i, pl.ds(4, 4)] = jnp.broadcast_to(loss_part, (4, 128))

    def tail_part(p):
        return remote("tail_part", tail_stage.at[p], tail_slots.at[d], 0, p, j)

    others(lambda p: tail_part(p).start(), d)
    tail_slots[d] = tail_stage[d]

    pass_from_y(1)
    loop(2, 4, softmax_rows)

    bulk("tail_part", tail_slots.at[pl.ds(0, count - 1)]).wait_recv()
    tails = slot_sum(tail_slots)
    loss_out[...] = tails[4:5] / (pairs * count)
    tail_send[...] = jnp.broadcast_to(tails[0:1], (8, 128))

    def tail_copy(slot, seq):
        return remote("tail", tail_send, tail_in.at[slot], slot, d, seq)

    for b in range(2):
        to = 4 * x + 2 * b + y
        pl.when(to != j)(lambda to=to: tail_copy(j % 2, to).start())

        @pl.when(to == j)
        def _():
            tail_in[j % 2] = tail_send[...]

    d_stage[...] = jnp.zeros_like(d_stage)
    for r in range(2):
        for half in range(2):
            d_stage[pl.ds(2 * r + half, count, stride=8), :] = d_sum[
                pl.ds(half * pairs + r, count, stride=2), :
            ]

    def d_rows(s):
        return pl.ds(pl.multiple_of(s * 8, 8), 8)

    def d_copy(p):
        return remote("d_out", d_stage.at[d_rows(p), :], d_in.at[d_rows(d), :], 0, p, j)

    others(lambda p: d_copy(p).start(), d)
    d_in[d_rows(d), :] = d_stage[d_rows(d), :]

    for b in range(count):
        q_term = mm(mine, four(p_cols[b]))
        for half in range(2):
            rows = pl.ds(2 * b + half, pairs, stride=chunks)
            q_terms[rows, :] = q_term[:, half * 128 : half * 128 + 128]
    core_send = remote("term_core", q_terms.at[p_rows(8 * (1 - c), 8), :], core_in, 0, d, over_core)
    core_send.start()
    kv_arrive(1)
    bulk("grad", grad_stage.at[pl.ds(0, 7)]).wait_recv()
    for b in range(2):
        source = 4 * x + 2 * c + b
        pl.when(source != j)(lambda b=b, source=source: tail_copy(b, source).wait_recv())
    row = lax.broadcasted_iota(jnp.int32, (512, 1), 0)
    row_token = (row & 255) + 256 * y

    def core_copy(t, a):
        name = ("core_sum_k", "core_sum_v")[t]
        return remote(name, dkv.at[t, a, :, 1 - c], core_slots.at[t, a], a, d, over_core)

    def y_copy(t, a):
        return remote(("y_sum_k", "y_sum_v")[t], y_stage.at[t, a], y_slots.at[t, a], a, d, over_y)

    def x_copy(t, to):
        name = ("x_out_k", "x_out_v")[t]
        return remote(name, x_stage.at[t, to], x_slots.at[t, x], 0, d, beside(to))

    def dq_copy(a, e):
        return remote("dq", dq_stage.at[a, :, e], dq_slots.at[rank], 0, d, 4 * a + 2 * y + e)

    def send_y(t, a):
        core_copy(t, a).wait_recv()
        y_stage[t, a] = dkv[t, a, 1 - y, c] + core_slots[t, a, 1 - y]
        y_copy(t, a).start()

    def send_x(t, a):
        y_copy(t, a).wait_recv()
        total = dkv[t, a, y, c] + core_slots[t, a, y] + y_slots[t, a]
        x_stage[t, a] = total.astype(bf16)

        @pl.when(a != x)
        def _():
            x_copy(t, a).start()

        @pl.when(a == x)
        def _():
            x_slots[t, x] = x_stage[t, a]

    def make_grad(a):
        spot = row_token + 512 * a
        extra = jnp.where(row < 256, tail_in[0, 0:1], tail_in[1, 0:1])
        last = jnp.where(spot == length - 1, 1.0, 0.0)
        grad = grad_h[a].reshape(512, 128).astype(f32) + last * extra
        grad_low[a] = jnp.where(spot < length, grad, 0.0).astype(bf16)

    def turned_block(block):
        return jnp.transpose(block.reshape(512, 128).astype(f32))

    def turn_block(b):
        k_turn[b] = turned_block(kv_h[0, b]).astype(bf16)
        v_turn[b] = turned_block(kv_h[1, b]).astype(bf16)
        grad_turn[b] = turned_block(grad_low[b])

    loop(0, 4, make_grad)
    loop(0, 4, turn_block)
    attn[...] = jnp.zeros_like(attn)

    def value_block(o):
        b = 3 - o

        def rows(a):
            spot = spot_of(a, b)
            low_b = jnp.concatenate(
                [
                    (scores[spot, i * 128 : i * 128 + 128] * factors[a, b, i : i + 1]).astype(bf16)
                    for i in range(4)
                ],
                axis=0,
            )
            dkv[1, b] += mm(low_b, grad_low[a]).reshape(2, 2, 128, 128)
            attn[a] += mm(v_turn[b], low_b)

        loop(b, 4, rows)
        core_copy(1, b).start()
        pl.when(o >= 1)(lambda: send_y(1, b + 1))

    loop(0, 4, value_block)
    core_send.wait_recv()
    both = q_terms[p_rows(8 * c, 8), :] + core_in[...]
    q_mid[...] = both.reshape(4, 128, 128)

    def term_x(p):
        return remote("term_x", q_mid.at[p], q_in.at[x], 0, d, beside(p))

    others(lambda p: term_x(p).start(), x, 4)
    q_in[x] = q_mid[x]

    def quarter(o):
        a = 3 - o
        q = q_h[a].reshape(512, 128)
        row_dot = jnp.sum(grad_turn[a] * attn[a], axis=0, keepdims=True)
        dq_acc[...] = jnp.zeros_like(dq_acc)

        def keys_of(b):
            spot = spot_of(a, b)
            values_b = kv_h[1, b].reshape(4, 128, 128)
            parts = []
            for i in range(4):
                prob_grad = mm_nt(values_b[i], grad_low[a])
                probs = scores[spot, i * 128 : i * 128 + 128] * (factors[a, b, i : i + 1] * scaling)
                parts.append((probs * (prob_grad - row_dot)).astype(bf16))
            sg = jnp.concatenate(parts, axis=0)
            dkv[0, b] += mm(sg, q).reshape(2, 2, 128, 128)
            dq_acc[...] += mm(k_turn[b], sg)

        loop(0, a + 1, keys_of)
        core_copy(0, a).start()
        dq_stage[a] = jnp.transpose(dq_acc[...]).astype(bf16).reshape(2, 2, 128, 128)
        for e in range(2):

            @pl.when(2 * a + e != rank)
            def _():
                dq_copy(a, e).start()

            @pl.when(2 * a + e == rank)
            def _():
                dq_slots[rank] = dq_stage[a, :, e]

        pl.when(o == 0)(lambda: send_y(1, 0))
        pl.when(o >= 1)(lambda: send_y(0, a + 1))
        send_x(1, a)
        pl.when(o >= 2)(lambda: send_x(0, a + 2))

    loop(0, 4, quarter)
    send_y(0, 0)
    bulk("term_x", q_in.at[pl.ds(0, 3)]).wait_recv()
    q_last[...] = (q_in[0] + q_in[1] + q_in[2] + q_in[3]).reshape(2, 64, 128)
    term_y = remote("term_y", q_last.at[1 - y], q_end, 0, d, over_y)
    term_y.start()
    send_x(0, 1)

    bulk("dq", dq_slots.at[pl.ds(0, 7)]).wait_recv()

    def gain_fold(block):
        return jnp.sum(block.reshape(16, 8, 128), axis=0)

    def query_head(h, total):
        grad = dq_slots[h // 2, h % 2].astype(f32)
        dx, part = normed_rope_back(
            queries[:, lanes(h)].astype(f32), q_gain[...], cosine[...], sine[...], grad
        )
        q_cot[:, lanes(h)] = dx.astype(bf16)
        return total + gain_fold(part)

    q_total = lax.fori_loop(0, 16, query_head, jnp.zeros((8, 128), f32), unroll=4)
    send_x(0, 0)
    term_y.wait_recv()
    bulk("d_out", d_in.at[pl.ds(0, 8 * (count - 1)), :]).wait_recv()
    q_f32[pl.ds(0, 2 * chunks), :] = q_last[y] + q_end[...]
    for i in range(chunks):
        part = pl.ds(i * 128, 128)
        q_grad_out[:, part] = q_f32[pl.ds(i, 2, stride=chunks), :].astype(bf16)
        d_row = 8 * (i // 2) + i % 2
        d_grad_out[:, part] = d_in[pl.ds(d_row, 2, stride=2), :].astype(bf16)
    bulk("x_out_v", x_slots.at[1, pl.ds(0, 3)]).wait_recv()
    bulk("x_out_k", x_slots.at[0, pl.ds(0, 3)]).wait_recv()

    def key_head(g, total):
        v_cot[:, lanes(g)] = x_slots[1, g]
        dx, part = normed_rope_back(
            keys[:, lanes(g)].astype(f32), k_gain[...], cosine[...], sine[...],
            x_slots[0, g].astype(f32),
        )
        k_cot[:, lanes(g)] = dx.astype(bf16)
        return total + gain_fold(part)

    k_total = lax.fori_loop(0, 4, key_head, jnp.zeros((8, 128), f32), unroll=True)
    seq_slots[j, pl.ds(0, 4)] = q_total[:4] + q_total[4:]
    seq_slots[j, pl.ds(4, 4)] = k_total[:4] + k_total[4:]

    def gain_seq(p):
        return remote("gain_seq", seq_slots.at[j], seq_slots.at[j], 0, d, p)

    others(lambda p: gain_seq(p).start(), j)
    bulk("gain_seq", seq_slots.at[pl.ds(0, count - 1)]).wait_recv()
    dp_slots[d] = slot_sum(seq_slots)

    def gain_dp(p):
        return remote("gain_dp", dp_slots.at[d], dp_slots.at[d], 0, p, j)

    others(lambda p: gain_dp(p).start(), d)
    bulk("gain_dp", dp_slots.at[pl.ds(0, count - 1)]).wait_recv()
    gains = slot_sum(dp_slots)
    gains_out[0:1, :] = jnp.sum(gains[:4], axis=0, keepdims=True)
    gains_out[1:2, :] = jnp.sum(gains[4:], axis=0, keepdims=True)

    gather("q_y", q_all, q_rows(place), d, over_y).wait_send()
    gather("p_y", p_all, p_rows(d), over_low, j).wait_send()
    gather("q_core", q_all, q_rows(8 * c, 8), d, over_core).wait_send()
    for name, ref in (
        ("q_x", q_all.at[q_rows(0, 6), :]),
        ("p_z", p_all.at[p_rows(0, 14), :]),
        ("tile", tiles.at[pl.ds(0, count - 1)]),
        ("part", q_part.at[pl.ds(0, count - 1), pl.ds(0, 16)]),
        ("span", spans.at[pl.ds(0, count - 1)]),
        ("tail_part", tail_slots.at[pl.ds(0, count - 1)]),
        ("d_out", d_in.at[pl.ds(0, 8 * (count - 1)), :]),
        ("term_x", q_in.at[pl.ds(0, 3)]),
        ("gain_seq", seq_slots.at[pl.ds(0, count - 1)]),
        ("gain_dp", dp_slots.at[pl.ds(0, count - 1)]),
        ("k_x", kv_stage.at[pl.ds(0, 3), 0]),
        ("v_x", kv_stage.at[pl.ds(0, 3), 1]),
        ("k_y", kv_h.at[0, :, 0, 0]),
        ("v_y", kv_h.at[1, :, 0, 0]),
        ("k_core", kv_h.at[0, :, 0, 0]),
        ("v_core", kv_h.at[1, :, 0, 0]),
        ("k_both", kv_h.at[0, :, 0, 0]),
        ("v_both", kv_h.at[1, :, 0, 0]),
        ("q", q_stage.at[pl.ds(0, 7)]),
        ("grad", grad_stage.at[pl.ds(0, 7)]),
        ("dq", dq_slots.at[pl.ds(0, 7)]),
        ("core_sum_k", core_slots.at[0]),
        ("core_sum_v", core_slots.at[1]),
        ("y_sum_k", y_stage.at[0]),
        ("y_sum_v", y_stage.at[1]),
        ("x_out_k", x_slots.at[0, pl.ds(0, 3)]),
        ("x_out_v", x_slots.at[1, pl.ds(0, 3)]),
    ):
        bulk(name, ref).wait_send()
    core_send.wait_send()
    term_y.wait_send()
    part_core.wait_send()
    for b in range(2):
        to = 4 * x + 2 * b + y
        pl.when(to != j)(lambda to=to: tail_copy(j % 2, to).wait_send())


def finish(loss, gains, *refs):
    size = (len(refs) - 3) // 2
    loss_out, q_out, k_out = refs[size : size + 3]
    loss_out[...] = loss[0:1, 0:1]
    q_out[...] = gains[0:1, :]
    k_out[...] = gains[1:2, :]
    for made, out in zip(refs[:size], refs[size + 3 :]):
        out[...] = made[...]


def shards(
    question_embedding_matrix,
    passage_embedding_matrix,
    positive,
    queries,
    keys,
    values,
    later_grad,
    lengths,
    q_gain,
    k_gain,
    out_weight,
):
    angles = np.arange(2048)[:, None] * rope_base ** (-2.0 * np.arange(64) / 128)[None, :]
    table = jnp.asarray(np.concatenate([np.cos(angles), np.sin(angles)], axis=1).astype(np.float32))
    out = jax.ShapeDtypeStruct
    vm = pltpu.VMEM
    smem = pl.BlockSpec(memory_space=pltpu.SMEM)
    anywhere = pl.BlockSpec(memory_space=pl.ANY)
    results = [
        out(question_embedding_matrix.shape, bf16),
        out(passage_embedding_matrix.shape, bf16),
        out(queries.shape[1:], bf16),
        out(keys.shape[1:], bf16),
        out(values.shape[1:], bf16),
    ]
    loss, gains, *made = pl.pallas_call(
        whole,
        out_shape=[out((1, 128), f32), out((2, 128), f32)] + results,
        in_specs=[smem, smem, anywhere] + [VMEM] * 9,
        out_specs=[VMEM] * 7,
        scratch_shapes=[
            vm((128, 128), f32),
            vm((128, 128), f32),
            vm((128, 128), f32),
            vm((2 * q_stride, 128), f32),
            vm((2 * chunks, 128), f32),
            vm((2 * q_stride * count, 128), bf16),
            vm((2 * chunks * count, 128), bf16),
            vm((2 * q_stride * count, 128), f32),
            vm((2 * chunks * count, 128), f32),
            vm((count, pairs, 256), bf16),
            vm((count, pairs, 256), bf16),
            vm((count, 8, 128), f32),
            vm((count, pairs, 256), bf16),
            vm((count, 16, 128), f32),
            vm((count, pairs, 256), bf16),
            vm((pairs * chunks, 128), f32),
            vm((pairs * chunks // 2, 128), f32),
            vm((4, 128, 128), f32),
            vm((4, 128, 128), f32),
            vm((2, 64, 128), f32),
            vm((64, 128), f32),
            vm((2 * pairs, 128), f32),
            vm((8 * count, 128), f32),
            vm((8 * count, 128), f32),
            vm((count, 8, 128), f32),
            vm((count, 8, 128), f32),
            vm((8, 128), f32),
            vm((2, 8, 128), f32),
            vm((4, 2, 128, 128), bf16),
            vm((8, 2, 128, 128), bf16),
            vm((8, 2, 128, 128), bf16),
            vm((2, 4, 2, 2, 128, 128), bf16),
            vm((4, 2, 2, 128, 128), bf16),
            vm((4, 2, 2, 128, 128), bf16),
            vm((4, 512, 128), bf16),
            vm((4, 128, 512), f32),
            vm((10, 512, 512), f32),
            vm((4, 4, 8, 512), f32),
            vm((4, 4, 8, 512), f32),
            vm((4, 4, 8, 512), f32),
            vm((4, 128, 512), f32),
            vm((4, 128, 512), bf16),
            vm((4, 128, 512), bf16),
            vm((128, 512), f32),
            vm((2, 4, 2, 2, 128, 128), f32),
            vm((4, 2, 2, 128, 128), bf16),
            vm((8, 2, 128, 128), bf16),
            vm((2, 4, 2, 128, 128), f32),
            vm((2, 4, 128, 128), f32),
            vm((2, 4, 128, 128), f32),
            vm((2, 4, 128, 128), bf16),
            vm((2, 4, 128, 128), bf16),
            vm((count, 8, 128), f32),
            vm((count, 8, 128), f32),
            pltpu.SemaphoreType.DMA((len(phases),)),
            pltpu.SemaphoreType.DMA((len(phases), 4)),
            pltpu.SemaphoreType.DMA((1,)),
        ],
        compiler_params=pltpu.CompilerParams(
            collective_id=0, has_side_effects=True, vmem_limit_bytes=limit
        ),
    )(
        lengths, positive, table, queries[0], keys[0], values[0], later_grad[0],
        question_embedding_matrix, passage_embedding_matrix, out_weight,
        q_gain[None, :], k_gain[None, :],
    )
    loss, q_gain_grad, k_gain_grad, query_grad, doc_grad, query_cot, key_cot, value_cot = (
        pl.pallas_call(
            finish,
            out_shape=[out((1, 1), f32), out((1, 128), f32), out((1, 128), f32)] + results,
            in_specs=[VMEM] * 7,
            out_specs=[VMEM] * 8,
        )(loss, gains, *made)
    )
    return (
        loss.reshape(()),
        query_grad,
        doc_grad,
        query_cot[None],
        key_cot[None],
        value_cot[None],
        q_gain_grad[0],
        k_gain_grad[0],
    )


def solution(mesh):
    in_specs = (
        P(("dp", "seq"), None),
        P(("dp", "seq"), None),
        P(("dp", "seq")),
        P("dp", "seq", None),
        P("dp", "seq", None),
        P("dp", "seq", None),
        P("dp", "seq", None),
        P("dp"),
        P(),
        P(),
        P("seq", "dp"),
    )
    out_specs = (
        P(),
        P(("dp", "seq"), None),
        P(("dp", "seq"), None),
        P("dp", "seq", None),
        P("dp", "seq", None),
        P("dp", "seq", None),
        P(),
        P(),
    )
    return jax.shard_map(
        shards, mesh=mesh, in_specs=in_specs, out_specs=out_specs, check_vma=False
    )
```

```python
import functools
import math

import jax
import jax.numpy as jnp
import numpy as np
from jax import lax
from jax.experimental import pallas as pl
from jax.experimental.pallas import tpu as pltpu
from jax.sharding import PartitionSpec as P

sharpness = 0.05
epsilon = 1e-06
rope_base = 1000000.0
lowest = -1e30
MESH = pl.DeviceIdType.MESH
f32 = jnp.float32
bf16 = jnp.bfloat16
VMEM = pl.BlockSpec(memory_space=pltpu.VMEM)
limit = 58 * 1024 * 1024
count = 16
pairs = 32
chunks = 32
q_stride = 40
scaling = 128 ** (-0.5)
phases = (
    "q_msg", "p_msg", "tile", "part", "part_core", "span", "tail_part", "w_out",
    "d_out", "term_core", "term_x", "term_y", "gain_seq", "gain_dp",
    "k_x", "k_y", "k_core", "k_both", "v_x", "v_y", "v_core", "v_both", "q", "grad", "dq", "core_sum_k", "core_sum_v", "y_sum_k", "y_sum_v",
    "x_out_k", "x_out_v",
)
phase_of = {name: i for i, name in enumerate(phases)}


def mm(a, b):
    return lax.dot_general(a, b, (((1,), (0,)), ((), ())), preferred_element_type=f32)


def mm_nt(a, b):
    return lax.dot_general(a, b, (((1,), (1,)), ((), ())), preferred_element_type=f32)


def mm_tn(a, b):
    return lax.dot_general(a, b, (((0,), (0,)), ((), ())), preferred_element_type=f32)


def loop(first, last, step, unroll=None):
    def body(i, carry):
        step(i)
        return carry

    lax.fori_loop(first, last, body, 0, unroll=unroll)


def swap_halves(x):
    return pltpu.roll(x, 64, 1)


def normed_rope(x, gain, cosine, sine):
    scale = lax.rsqrt(jnp.mean(x * x, axis=-1, keepdims=True) + epsilon)
    y = x * scale * gain
    return y * cosine + swap_halves(y) * sine


def normed_rope_back(x, gain, cosine, sine, grad):
    scale = lax.rsqrt(jnp.mean(x * x, axis=-1, keepdims=True) + epsilon)
    n = x * scale
    dy = grad * cosine - swap_halves(grad) * sine
    gain_part = dy * n
    dn = dy * gain
    dx = scale * (dn - n * jnp.mean(dn * n, axis=-1, keepdims=True))
    return dx, gain_part


def slot_sum(ref):
    total = ref[0]
    for i in range(1, count):
        total = total + ref[i]
    return total


def whole(
    lengths, positive_in, table, queries, keys, values, later, q_emb, p_emb, out_w, q_gain, k_gain,
    loss_out, gains_out, q_grad_out, d_grad_out, q_cot, k_cot, v_cot,
    turn, cosine, sine,
    q_f32, p_f32, q_all, p_all, q_wide, p_wide, q_cols, p_cols, tiles,
    q_part, spans, span_cat, q_terms, core_in, q_mid, q_in, q_last, q_end,
    d_sum, d_stage, d_in, tail_stage, tail_slots, tail_in, w_in,
    kv_stage, q_stage, grad_stage, kv_h, q_h, grad_h,
    grad_low, grad_turn, scores, tops, sums, factors, attn, k_turn, v_turn, dq_acc, dkv, dq_stage, dq_slots,
    core_slots, y_stage, y_slots, x_stage, x_slots, seq_slots, dp_slots,
    send_sem, recv_sem, own_sem,
):
    d, j = lax.axis_index("dp"), lax.axis_index("seq")
    x, y, c = j // 4, (j // 2) % 2, j % 2
    z, low = d // 2, d % 2
    rank = 2 * x + c
    barrier = pltpu.get_barrier_semaphore()

    def remote(name, src, dst, slot, dp, seq):
        phase = phase_of[name]
        return pltpu.make_async_remote_copy(
            src_ref=src,
            dst_ref=dst,
            send_sem=send_sem.at[phase],
            recv_sem=recv_sem.at[phase, slot],
            device_id=(dp, seq),
            device_id_type=MESH,
        )

    def bulk(name, ref):
        return remote(name, ref, ref, 0, d, j)

    def others(step, me, size=count):
        for o in range(1, size):
            step(lax.rem(me + o, size))

    others(
        lambda p: pl.semaphore_signal(barrier, inc=1, device_id=(d, p), device_id_type=MESH), j
    )
    others(
        lambda p: pl.semaphore_signal(barrier, inc=1, device_id=(p, j), device_id_type=MESH), d
    )
    turn_copy = pltpu.make_async_copy(
        table.at[pl.ds(pl.multiple_of(j * 128, 128), 128)], turn, own_sem.at[0]
    )
    turn_copy.start()

    def lanes(h):
        return pl.ds(pl.multiple_of(h * 128, 128), 128)

    def q_rows(s, size=1):
        return pl.ds(pl.multiple_of(s * 2 * q_stride, 16), size * 2 * q_stride)

    def p_rows(s, size=1):
        return pl.ds(pl.multiple_of(s * 2 * chunks, 16), size * 2 * chunks)

    place = 8 * c + 2 * x + y
    q_f32[...] = jnp.zeros_like(q_f32)
    q_own, p_own = q_emb[...].astype(f32), p_emb[...].astype(f32)
    for i in range(chunks):
        q_f32[pl.ds(i, 2, stride=q_stride), :] = q_own[:, i * 128 : i * 128 + 128]
        p_f32[pl.ds(i, 2, stride=chunks), :] = p_own[:, i * 128 : i * 128 + 128]
    for i in range(2):
        index = positive_in[i]
        spot = i * q_stride + chunks
        q_f32[spot : spot + 1, :] = jnp.full((1, 128), index >> 1, jnp.int32).astype(f32)
        q_f32[spot + 1 : spot + 2, :] = jnp.full((1, 128), index & 1, jnp.int32).astype(f32)
    q_all[q_rows(place), :] = q_f32[...].astype(bf16)
    p_all[p_rows(d), :] = p_f32[...].astype(bf16)
    turn_copy.wait()
    first_half = lax.broadcasted_iota(jnp.int32, (128, 128), 1) < 64
    turned = swap_halves(turn[...])
    cosine[...] = jnp.where(first_half, turn[...], turned)
    sine[...] = jnp.where(first_half, -turned, turn[...])

    def stage_kv(g):
        rot = normed_rope(keys[:, lanes(g)].astype(f32), k_gain[...], cosine[...], sine[...])
        kv_stage[g, 0] = rot.astype(bf16)
        kv_stage[g, 1] = values[:, lanes(g)]

    loop(0, 4, stage_kv, unroll=True)
    pl.semaphore_wait(barrier, 2 * (count - 1))

    over_y = 4 * x + 2 * (1 - y) + c
    over_core = 4 * x + 2 * y + (1 - c)
    over_low = d + 1 - 2 * low

    def beside(p):
        return 4 * p + 2 * y + c

    def q_copy(p):
        rows = q_all.at[q_rows(place), :]
        return remote("q_msg", rows, rows, 0, d, p)

    def p_copy(p):
        rows = p_all.at[p_rows(d), :]
        return remote("p_msg", rows, rows, 0, p, j)

    others(lambda p: q_copy(p).start(), j)
    others(lambda p: p_copy(p).start(), d)

    def x_copies(t, step):
        def copy(to):
            name, src = ("k_x", "v_x")[t], kv_stage.at[to, t]
            step(remote(name, src, kv_h.at[t, x, y, c], 0, d, beside(to)))

        others(copy, x, 4)

    def kv_pass(t, way, of_y, of_core, seq):
        block = kv_h.at[t, :, of_y, of_core]
        return remote("kv"[t] + way, block, block, 0, d, seq)

    def pass_on(t):
        bulk(("k_x", "v_x")[t], kv_h.at[t, pl.ds(0, 3), y, c]).wait_recv()
        kv_pass(t, "_y", y, c, over_y).start()
        kv_pass(t, "_core", y, c, over_core).start()

    def pass_from_y(t):
        kv_pass(t, "_y", 1 - y, c, over_y).wait_recv()
        kv_pass(t, "_both", 1 - y, c, over_core).start()

    def kv_arrive(t):
        kv_pass(t, "_core", y, 1 - c, over_core).wait_recv()
        kv_pass(t, "_both", 1 - y, 1 - c, over_core).wait_recv()

    x_copies(0, lambda copy: copy.start())
    kv_h[:, x, y, c] = kv_stage[x]

    def stage_q(h):
        rot = normed_rope(queries[:, lanes(h)].astype(f32), q_gain[...], cosine[...], sine[...])
        q_stage[h // 2, h % 2] = rot.astype(bf16)

    def seat(r):
        return 4 * (r // 2) + 2 * y + r % 2

    def head_send(name, stage, held):
        others(
            lambda p: remote(
                name, stage.at[p], held.at[x, :, c], 0, d, seat(p)
            ).start(),
            rank,
            8,
        )
        held[x, :, c] = stage[rank]

    loop(0, 16, stage_q, unroll=4)

    def w_copy(slot, seq):
        return remote("w_out", out_w, w_in.at[slot], slot, d, seq)

    def w_targets(step):
        for b in range(2):
            to = 4 * x + 2 * b + y
            pl.when(to != j)(lambda to=to: step(w_copy(j % 2, to)))

    w_targets(lambda copy: copy.start())

    @pl.when(c == y)
    def _():
        w_in[j % 2] = out_w[...]

    pass_on(0)
    head_send("q", q_stage, q_h)

    def stage_grad(h):
        grad_stage[h // 2, h % 2] = later[:, lanes(h)]

    loop(0, 16, stage_grad)
    dkv[...] = jnp.zeros_like(dkv)

    bulk("q_msg", q_all.at[q_rows(0, count - 1), :]).wait_recv()
    bulk("p_msg", p_all.at[p_rows(0, count - 1), :]).wait_recv()
    q_wide[...] = q_all[...].astype(f32)
    p_wide[...] = p_all[...].astype(f32)
    for i in range(chunks):
        half = pl.ds((i % 2) * 128, 128)
        q_cols[i // 2, :, half] = q_wide[pl.ds(i, pairs, stride=q_stride), :].astype(bf16)
        p_cols[i // 2, :, half] = p_wide[pl.ds(i, pairs, stride=chunks), :].astype(bf16)
    positive = (
        2.0 * q_wide[pl.ds(chunks, pairs, stride=q_stride), :]
        + q_wide[pl.ds(chunks + 1, pairs, stride=q_stride), :]
    )

    def four(block):
        return jnp.concatenate([block] * (128 // pairs), axis=0)

    def one(block):
        return block[:32] + block[32:64] + block[64:96] + block[96:]

    logits = mm_nt(q_cols[0], four(p_cols[0]))
    for b in range(1, count):
        logits = logits + mm_nt(q_cols[b], four(p_cols[b]))
    logits = logits / sharpness
    quarter_of = lax.broadcasted_iota(jnp.int32, (8, 128), 1) >> 5

    def pack(block):
        packed = block[:8]
        for i in range(1, 4):
            packed = jnp.where(quarter_of == i, block[8 * i : 8 * i + 8], packed)
        return packed

    tiles[j] = pack(logits)

    def tile_copy(p):
        return remote("tile", tiles.at[j], tiles.at[j], 0, d, p)

    others(lambda p: tile_copy(p).start(), j)
    x_copies(1, lambda copy: copy.start())

    def half_of(core):
        return pl.ds(pl.multiple_of(16 * core, 16), 16)

    def part_copy(p):
        return remote(
            "part", q_cols.at[p, half_of(c)], q_part.at[d, half_of(c)], 0, p, j
        )

    others(lambda p: part_copy(p).start(), d)
    q_part[d, half_of(c)] = q_cols[d, half_of(c)]
    head_send("grad", grad_stage, grad_h)
    lane = lax.broadcasted_iota(jnp.int32, (pairs, 128), 1)
    line = lax.broadcasted_iota(jnp.int32, (pairs, 128), 0)
    real = (lane >> 5) == (line >> 3)
    base = jnp.where(real, ((lane & 31) >> 1) * pairs + (lane & 1), -(1 << 20)).astype(f32)

    pass_from_y(0)

    bulk("tile", tiles.at[pl.ds(0, count - 1)]).wait_recv()
    high = tiles[0]
    for i in range(1, count):
        high = jnp.maximum(high, tiles[i])
    high = jnp.max(jnp.where(real, four(high), lowest), axis=1, keepdims=True)
    mass = jnp.zeros((pairs, 128), f32)
    hit = jnp.zeros((pairs, 128), f32)
    for i in range(count):
        tile = four(tiles[i])
        mass = mass + jnp.where(real, jnp.exp(tile - high), 0.0)
        hit = hit + jnp.where(base + 2.0 * i == positive, tile, 0.0)
    log_total = high + jnp.log(jnp.sum(mass, axis=1, keepdims=True))
    picked = jnp.sum(hit, axis=1, keepdims=True)
    loss_part = jnp.sum(log_total - picked, axis=0, keepdims=True)

    def weights_of(tile, index):
        onehot = jnp.where(base + 2.0 * index == positive, 1.0, 0.0)
        return jnp.where(real, (jnp.exp(four(tile) - log_total) - onehot) / sharpness, 0.0)

    mine = weights_of(tiles[j], j.astype(f32)).astype(bf16)
    spans[d, pl.ds(0, 8)] = pack(weights_of(tiles[0], 0.0).astype(bf16).astype(f32))
    spans[d, pl.ds(8, 8)] = pack(mine.astype(f32))

    def span_copy(p):
        return remote("span", spans.at[d], spans.at[d], 0, p, j)

    others(lambda p: span_copy(p).start(), d)
    pass_on(1)

    kv_arrive(0)
    bulk("q", q_stage.at[pl.ds(0, 7)]).wait_recv()
    length = lengths[0]
    key_line = lax.broadcasted_iota(jnp.int32, (128, 1), 0)
    ahead = lax.broadcasted_iota(jnp.int32, (128, 256), 0) - lax.broadcasted_iota(
        jnp.int32, (128, 256), 1
    )
    tops[...] = jnp.full_like(tops, lowest)
    sums[...] = jnp.zeros_like(sums)

    def spot_of(a, b):
        return (a * (a + 1)) // 2 + b

    def softmax_rows(o):
        a = 3 - o

        def strips(b, diagonal):
            keys_b = kv_h[0, b].reshape(4, 128, 128)
            for half in range(2):
                q = q_h[a, half].reshape(256, 128)
                across = slice(half * 256, half * 256 + 256)
                for i in range(4):
                    start = b * 512 + i * 128
                    bias = jnp.where(key_line < length - start, 0.0, lowest)
                    s = mm_nt(keys_b[i], q) * (scaling * math.log2(math.e)) + bias
                    if diagonal:
                        s = jnp.where(ahead <= 256 * y - i * 128, s, lowest)
                    top = jnp.max(s, axis=0, keepdims=True)
                    e = jnp.exp2(s - top)
                    scores[spot_of(a, b), i * 128 : i * 128 + 128, across] = e
                    tops[a, b, i : i + 1, across] = top
                    sums[a, b, i : i + 1, across] = jnp.sum(e, axis=0, keepdims=True)

        loop(0, a, lambda b: strips(b, False))
        strips(a, True)
        part_tops = tops[a].reshape(32, 512)
        part = jnp.exp2(part_tops - jnp.max(part_tops, axis=0, keepdims=True))
        total = jnp.sum(part * sums[a].reshape(32, 512), axis=0, keepdims=True)
        factors[a] = (part * (1.0 / total)).reshape(4, 8, 512)

    softmax_rows(0)
    bulk("part", q_part.at[pl.ds(0, count - 1), pl.ds(0, 16)]).wait_recv()
    part_core = remote(
        "part_core", q_part.at[:, half_of(c)], q_part.at[:, half_of(c)], 0, d, over_core
    )
    part_core.start()
    softmax_rows(1)

    bulk("span", spans.at[pl.ds(0, count - 1)]).wait_recv()
    for i in range(count):
        for t in range(2):
            weights = jnp.where(real, four(spans[i, t * 8 : t * 8 + 8]), 0.0)
            span_cat[i, :, t * 128 : t * 128 + 128] = weights.astype(bf16)
    remote(
        "part_core", q_part.at[:, half_of(1 - c)], q_part.at[:, half_of(1 - c)], 0, d, over_core
    ).wait_recv()
    span_sums = mm_tn(
        span_cat[...].reshape(pairs * count, 256), q_part[...].reshape(pairs * count, 256)
    )
    span = one(span_sums[:128]).astype(bf16)
    d_sums = one(span_sums[128:])
    d_sum[pl.ds(0, pairs), :] = d_sums[:, :128]
    d_sum[pl.ds(pairs, pairs), :] = d_sums[:, 128:]
    for b in range(2):
        source = 4 * x + 2 * c + b
        pl.when(source != j)(lambda b=b, source=source: w_copy(b, source).wait_recv())
    rows_a, rows_b = mm_nt(span, w_in[0]), mm_nt(span, w_in[1])
    for i in range(count):
        tail_stage[i, pl.ds(0, 2)] = jnp.broadcast_to(rows_a[2 * i : 2 * i + 1], (2, 128))
        tail_stage[i, pl.ds(2, 2)] = jnp.broadcast_to(rows_b[2 * i : 2 * i + 1], (2, 128))
        tail_stage[i, pl.ds(4, 4)] = jnp.broadcast_to(loss_part, (4, 128))

    def tail_part(p):
        return remote("tail_part", tail_stage.at[p], tail_slots.at[d], 0, p, j)

    others(lambda p: tail_part(p).start(), d)
    tail_slots[d] = tail_stage[d]

    pass_from_y(1)
    loop(2, 4, softmax_rows)

    bulk("tail_part", tail_slots.at[pl.ds(0, count - 1)]).wait_recv()
    tails = slot_sum(tail_slots)
    loss_out[...] = tails[4:5] / (pairs * count)
    tail_in[...] = tails

    d_stage[...] = jnp.zeros_like(d_stage)
    for r in range(2):
        for half in range(2):
            d_stage[pl.ds(2 * r + half, count, stride=8), :] = d_sum[
                pl.ds(half * pairs + r, count, stride=2), :
            ]

    def d_rows(s):
        return pl.ds(pl.multiple_of(s * 8, 8), 8)

    def d_copy(p):
        return remote("d_out", d_stage.at[d_rows(p), :], d_in.at[d_rows(d), :], 0, p, j)

    others(lambda p: d_copy(p).start(), d)
    d_in[d_rows(d), :] = d_stage[d_rows(d), :]

    for b in range(count):
        q_term = mm(mine, four(p_cols[b]))
        for half in range(2):
            rows = pl.ds(2 * b + half, pairs, stride=chunks)
            q_terms[rows, :] = q_term[:, half * 128 : half * 128 + 128]
    core_send = remote("term_core", q_terms.at[p_rows(8 * (1 - c), 8), :], core_in, 0, d, over_core)
    core_send.start()
    kv_arrive(1)
    bulk("grad", grad_stage.at[pl.ds(0, 7)]).wait_recv()
    row = lax.broadcasted_iota(jnp.int32, (512, 1), 0)
    row_token = (row & 255) + 256 * y

    def core_copy(t, a):
        name = ("core_sum_k", "core_sum_v")[t]
        return remote(name, dkv.at[t, a, :, 1 - c], core_slots.at[t, a], a, d, over_core)

    def y_copy(t, a):
        return remote(("y_sum_k", "y_sum_v")[t], y_stage.at[t, a], y_slots.at[t, a], a, d, over_y)

    def x_copy(t, to):
        name = ("x_out_k", "x_out_v")[t]
        return remote(name, x_stage.at[t, to], x_slots.at[t, x], 0, d, beside(to))

    def dq_copy(a, e):
        return remote("dq", dq_stage.at[a, :, e], dq_slots.at[rank], 0, d, 4 * a + 2 * y + e)

    def send_y(t, a):
        core_copy(t, a).wait_recv()
        y_stage[t, a] = dkv[t, a, 1 - y, c] + core_slots[t, a, 1 - y]
        y_copy(t, a).start()

    def send_x(t, a):
        y_copy(t, a).wait_recv()
        total = dkv[t, a, y, c] + core_slots[t, a, y] + y_slots[t, a]
        x_stage[t, a] = total.astype(bf16)

        @pl.when(a != x)
        def _():
            x_copy(t, a).start()

        @pl.when(a == x)
        def _():
            x_slots[t, x] = x_stage[t, a]

    def make_grad(a):
        spot = row_token + 512 * a
        extra = jnp.where(row < 256, tail_in[0:1], tail_in[2:3])
        last = jnp.where(spot == length - 1, 1.0, 0.0)
        grad = grad_h[a].reshape(512, 128).astype(f32) + last * extra
        grad_low[a] = jnp.where(spot < length, grad, 0.0).astype(bf16)

    def turned_block(block):
        return jnp.transpose(block.reshape(512, 128).astype(f32))

    def turn_block(b):
        k_turn[b] = turned_block(kv_h[0, b]).astype(bf16)
        v_turn[b] = turned_block(kv_h[1, b]).astype(bf16)
        grad_turn[b] = turned_block(grad_low[b])

    loop(0, 4, make_grad)
    loop(0, 4, turn_block)
    attn[...] = jnp.zeros_like(attn)

    def value_block(o):
        b = 3 - o

        def rows(a):
            spot = spot_of(a, b)
            low_b = jnp.concatenate(
                [
                    (scores[spot, i * 128 : i * 128 + 128] * factors[a, b, i : i + 1]).astype(bf16)
                    for i in range(4)
                ],
                axis=0,
            )
            dkv[1, b] += mm(low_b, grad_low[a]).reshape(2, 2, 128, 128)
            attn[a] += mm(v_turn[b], low_b)

        loop(b, 4, rows)
        core_copy(1, b).start()
        pl.when(o >= 1)(lambda: send_y(1, b + 1))

    loop(0, 4, value_block)
    core_send.wait_recv()
    both = q_terms[p_rows(8 * c, 8), :] + core_in[...]
    q_mid[...] = both.reshape(4, 128, 128)

    def term_x(p):
        return remote("term_x", q_mid.at[p], q_in.at[x], 0, d, beside(p))

    others(lambda p: term_x(p).start(), x, 4)
    q_in[x] = q_mid[x]

    def quarter(o):
        a = 3 - o
        q = q_h[a].reshape(512, 128)
        row_dot = jnp.sum(grad_turn[a] * attn[a], axis=0, keepdims=True)
        dq_acc[...] = jnp.zeros_like(dq_acc)

        def keys_of(b):
            spot = spot_of(a, b)
            values_b = kv_h[1, b].reshape(4, 128, 128)
            parts = []
            for i in range(4):
                prob_grad = mm_nt(values_b[i], grad_low[a])
                probs = scores[spot, i * 128 : i * 128 + 128] * (factors[a, b, i : i + 1] * scaling)
                parts.append((probs * (prob_grad - row_dot)).astype(bf16))
            sg = jnp.concatenate(parts, axis=0)
            dkv[0, b] += mm(sg, q).reshape(2, 2, 128, 128)
            dq_acc[...] += mm(k_turn[b], sg)

        loop(0, a + 1, keys_of)
        core_copy(0, a).start()
        dq_stage[a] = jnp.transpose(dq_acc[...]).astype(bf16).reshape(2, 2, 128, 128)
        for e in range(2):

            @pl.when(2 * a + e != rank)
            def _():
                dq_copy(a, e).start()

            @pl.when(2 * a + e == rank)
            def _():
                dq_slots[rank] = dq_stage[a, :, e]

        pl.when(o == 0)(lambda: send_y(1, 0))
        pl.when(o >= 1)(lambda: send_y(0, a + 1))
        send_x(1, a)
        pl.when(o >= 2)(lambda: send_x(0, a + 2))

    loop(0, 4, quarter)
    send_y(0, 0)
    bulk("term_x", q_in.at[pl.ds(0, 3)]).wait_recv()
    q_last[...] = (q_in[0] + q_in[1] + q_in[2] + q_in[3]).reshape(2, 64, 128)
    term_y = remote("term_y", q_last.at[1 - y], q_end, 0, d, over_y)
    term_y.start()
    send_x(0, 1)

    bulk("dq", dq_slots.at[pl.ds(0, 7)]).wait_recv()

    def gain_fold(block):
        return jnp.sum(block.reshape(16, 8, 128), axis=0)

    def query_head(h, total):
        grad = dq_slots[h // 2, h % 2].astype(f32)
        dx, part = normed_rope_back(
            queries[:, lanes(h)].astype(f32), q_gain[...], cosine[...], sine[...], grad
        )
        q_cot[:, lanes(h)] = dx.astype(bf16)
        return total + gain_fold(part)

    q_total = lax.fori_loop(0, 16, query_head, jnp.zeros((8, 128), f32), unroll=4)
    send_x(0, 0)
    term_y.wait_recv()
    bulk("d_out", d_in.at[pl.ds(0, 8 * (count - 1)), :]).wait_recv()
    q_f32[pl.ds(0, 2 * chunks), :] = q_last[y] + q_end[...]
    for i in range(chunks):
        part = pl.ds(i * 128, 128)
        q_grad_out[:, part] = q_f32[pl.ds(i, 2, stride=chunks), :].astype(bf16)
        d_row = 8 * (i // 2) + i % 2
        d_grad_out[:, part] = d_in[pl.ds(d_row, 2, stride=2), :].astype(bf16)
    bulk("x_out_v", x_slots.at[1, pl.ds(0, 3)]).wait_recv()
    bulk("x_out_k", x_slots.at[0, pl.ds(0, 3)]).wait_recv()

    def key_head(g, total):
        v_cot[:, lanes(g)] = x_slots[1, g]
        dx, part = normed_rope_back(
            keys[:, lanes(g)].astype(f32), k_gain[...], cosine[...], sine[...],
            x_slots[0, g].astype(f32),
        )
        k_cot[:, lanes(g)] = dx.astype(bf16)
        return total + gain_fold(part)

    k_total = lax.fori_loop(0, 4, key_head, jnp.zeros((8, 128), f32), unroll=True)
    seq_slots[j, pl.ds(0, 4)] = q_total[:4] + q_total[4:]
    seq_slots[j, pl.ds(4, 4)] = k_total[:4] + k_total[4:]

    def gain_seq(p):
        return remote("gain_seq", seq_slots.at[j], seq_slots.at[j], 0, d, p)

    others(lambda p: gain_seq(p).start(), j)
    bulk("gain_seq", seq_slots.at[pl.ds(0, count - 1)]).wait_recv()
    dp_slots[d] = slot_sum(seq_slots)

    def gain_dp(p):
        return remote("gain_dp", dp_slots.at[d], dp_slots.at[d], 0, p, j)

    others(lambda p: gain_dp(p).start(), d)
    bulk("gain_dp", dp_slots.at[pl.ds(0, count - 1)]).wait_recv()
    gains = slot_sum(dp_slots)
    gains_out[0:1, :] = jnp.sum(gains[:4], axis=0, keepdims=True)
    gains_out[1:2, :] = jnp.sum(gains[4:], axis=0, keepdims=True)

    for name, ref in (
        ("q_msg", q_all.at[q_rows(0, count - 1), :]),
        ("p_msg", p_all.at[p_rows(0, count - 1), :]),
        ("tile", tiles.at[pl.ds(0, count - 1)]),
        ("part", q_part.at[pl.ds(0, count - 1), pl.ds(0, 16)]),
        ("span", spans.at[pl.ds(0, count - 1)]),
        ("tail_part", tail_slots.at[pl.ds(0, count - 1)]),
        ("d_out", d_in.at[pl.ds(0, 8 * (count - 1)), :]),
        ("term_x", q_in.at[pl.ds(0, 3)]),
        ("gain_seq", seq_slots.at[pl.ds(0, count - 1)]),
        ("gain_dp", dp_slots.at[pl.ds(0, count - 1)]),
        ("k_x", kv_stage.at[pl.ds(0, 3), 0]),
        ("v_x", kv_stage.at[pl.ds(0, 3), 1]),
        ("k_y", kv_h.at[0, :, 0, 0]),
        ("v_y", kv_h.at[1, :, 0, 0]),
        ("k_core", kv_h.at[0, :, 0, 0]),
        ("v_core", kv_h.at[1, :, 0, 0]),
        ("k_both", kv_h.at[0, :, 0, 0]),
        ("v_both", kv_h.at[1, :, 0, 0]),
        ("q", q_stage.at[pl.ds(0, 7)]),
        ("grad", grad_stage.at[pl.ds(0, 7)]),
        ("dq", dq_slots.at[pl.ds(0, 7)]),
        ("core_sum_k", core_slots.at[0]),
        ("core_sum_v", core_slots.at[1]),
        ("y_sum_k", y_stage.at[0]),
        ("y_sum_v", y_stage.at[1]),
        ("x_out_k", x_slots.at[0, pl.ds(0, 3)]),
        ("x_out_v", x_slots.at[1, pl.ds(0, 3)]),
    ):
        bulk(name, ref).wait_send()
    core_send.wait_send()
    term_y.wait_send()
    part_core.wait_send()
    w_targets(lambda copy: copy.wait_send())


def finish(loss, gains, *refs):
    size = (len(refs) - 3) // 2
    loss_out, q_out, k_out = refs[size : size + 3]
    loss_out[...] = loss[0:1, 0:1]
    q_out[...] = gains[0:1, :]
    k_out[...] = gains[1:2, :]
    for made, out in zip(refs[:size], refs[size + 3 :]):
        out[...] = made[...]


def shards(
    question_embedding_matrix,
    passage_embedding_matrix,
    positive,
    queries,
    keys,
    values,
    later_grad,
    lengths,
    q_gain,
    k_gain,
    out_weight,
):
    angles = np.arange(2048)[:, None] * rope_base ** (-2.0 * np.arange(64) / 128)[None, :]
    table = jnp.asarray(np.concatenate([np.cos(angles), np.sin(angles)], axis=1).astype(np.float32))
    out = jax.ShapeDtypeStruct
    vm = pltpu.VMEM
    smem = pl.BlockSpec(memory_space=pltpu.SMEM)
    anywhere = pl.BlockSpec(memory_space=pl.ANY)
    results = [
        out(question_embedding_matrix.shape, bf16),
        out(passage_embedding_matrix.shape, bf16),
        out(queries.shape[1:], bf16),
        out(keys.shape[1:], bf16),
        out(values.shape[1:], bf16),
    ]
    loss, gains, *made = pl.pallas_call(
        whole,
        out_shape=[out((1, 128), f32), out((2, 128), f32)] + results,
        in_specs=[smem, smem, anywhere] + [VMEM] * 9,
        out_specs=[VMEM] * 7,
        scratch_shapes=[
            vm((128, 128), f32),
            vm((128, 128), f32),
            vm((128, 128), f32),
            vm((2 * q_stride, 128), f32),
            vm((2 * chunks, 128), f32),
            vm((2 * q_stride * count, 128), bf16),
            vm((2 * chunks * count, 128), bf16),
            vm((2 * q_stride * count, 128), f32),
            vm((2 * chunks * count, 128), f32),
            vm((count, pairs, 256), bf16),
            vm((count, pairs, 256), bf16),
            vm((count, 8, 128), f32),
            vm((count, pairs, 256), bf16),
            vm((count, 16, 128), f32),
            vm((count, pairs, 256), bf16),
            vm((pairs * chunks, 128), f32),
            vm((pairs * chunks // 2, 128), f32),
            vm((4, 128, 128), f32),
            vm((4, 128, 128), f32),
            vm((2, 64, 128), f32),
            vm((64, 128), f32),
            vm((2 * pairs, 128), f32),
            vm((8 * count, 128), f32),
            vm((8 * count, 128), f32),
            vm((count, 8, 128), f32),
            vm((count, 8, 128), f32),
            vm((8, 128), f32),
            vm((2, 128, 256), bf16),
            vm((4, 2, 128, 128), bf16),
            vm((8, 2, 128, 128), bf16),
            vm((8, 2, 128, 128), bf16),
            vm((2, 4, 2, 2, 128, 128), bf16),
            vm((4, 2, 2, 128, 128), bf16),
            vm((4, 2, 2, 128, 128), bf16),
            vm((4, 512, 128), bf16),
            vm((4, 128, 512), f32),
            vm((10, 512, 512), f32),
            vm((4, 4, 8, 512), f32),
            vm((4, 4, 8, 512), f32),
            vm((4, 4, 8, 512), f32),
            vm((4, 128, 512), f32),
            vm((4, 128, 512), bf16),
            vm((4, 128, 512), bf16),
            vm((128, 512), f32),
            vm((2, 4, 2, 2, 128, 128), f32),
            vm((4, 2, 2, 128, 128), bf16),
            vm((8, 2, 128, 128), bf16),
            vm((2, 4, 2, 128, 128), f32),
            vm((2, 4, 128, 128), f32),
            vm((2, 4, 128, 128), f32),
            vm((2, 4, 128, 128), bf16),
            vm((2, 4, 128, 128), bf16),
            vm((count, 8, 128), f32),
            vm((count, 8, 128), f32),
            pltpu.SemaphoreType.DMA((len(phases),)),
            pltpu.SemaphoreType.DMA((len(phases), 4)),
            pltpu.SemaphoreType.DMA((1,)),
        ],
        compiler_params=pltpu.CompilerParams(
            collective_id=0, has_side_effects=True, vmem_limit_bytes=limit
        ),
    )(
        lengths, positive, table, queries[0], keys[0], values[0], later_grad[0],
        question_embedding_matrix, passage_embedding_matrix, out_weight,
        q_gain[None, :], k_gain[None, :],
    )
    loss, q_gain_grad, k_gain_grad, query_grad, doc_grad, query_cot, key_cot, value_cot = (
        pl.pallas_call(
            finish,
            out_shape=[out((1, 1), f32), out((1, 128), f32), out((1, 128), f32)] + results,
            in_specs=[VMEM] * 7,
            out_specs=[VMEM] * 8,
        )(loss, gains, *made)
    )
    return (
        loss.reshape(()),
        query_grad,
        doc_grad,
        query_cot[None],
        key_cot[None],
        value_cot[None],
        q_gain_grad[0],
        k_gain_grad[0],
    )


def solution(mesh):
    in_specs = (
        P(("dp", "seq"), None),
        P(("dp", "seq"), None),
        P(("dp", "seq")),
        P("dp", "seq", None),
        P("dp", "seq", None),
        P("dp", "seq", None),
        P("dp", "seq", None),
        P("dp"),
        P(),
        P(),
        P("seq", "dp"),
    )
    out_specs = (
        P(),
        P(("dp", "seq"), None),
        P(("dp", "seq"), None),
        P("dp", "seq", None),
        P("dp", "seq", None),
        P("dp", "seq", None),
        P(),
        P(),
    )
    return jax.shard_map(
        shards, mesh=mesh, in_specs=in_specs, out_specs=out_specs, check_vma=False
    )
```

```python
import functools
import math

import jax
import jax.numpy as jnp
import numpy as np
from jax import lax
from jax.experimental import pallas as pl
from jax.experimental.pallas import tpu as pltpu
from jax.sharding import PartitionSpec as P

sharpness = 0.05
epsilon = 1e-06
rope_base = 1000000.0
lowest = -1e30
MESH = pl.DeviceIdType.MESH
f32 = jnp.float32
bf16 = jnp.bfloat16
VMEM = pl.BlockSpec(memory_space=pltpu.VMEM)
limit = 58 * 1024 * 1024
count = 16
pairs = 32
chunks = 32
q_stride = 40
scaling = 128 ** (-0.5)
phases = (
    "q_msg", "p_msg", "tile", "part", "part_core", "span", "tail_part", "w_out",
    "d_out", "term_core", "term_x", "term_y", "gain_seq", "gain_dp",
    "k_x", "k_y", "k_core", "k_both", "v_x", "v_y", "v_core", "v_both", "q", "grad", "dq", "core_sum_k", "core_sum_v", "y_sum_k", "y_sum_v",
    "x_out_k", "x_out_v",
)
phase_of = {name: i for i, name in enumerate(phases)}


def mm(a, b):
    return lax.dot_general(a, b, (((1,), (0,)), ((), ())), preferred_element_type=f32)


def mm_nt(a, b):
    return lax.dot_general(a, b, (((1,), (1,)), ((), ())), preferred_element_type=f32)


def mm_tn(a, b):
    return lax.dot_general(a, b, (((0,), (0,)), ((), ())), preferred_element_type=f32)


def loop(first, last, step, unroll=None):
    def body(i, carry):
        step(i)
        return carry

    lax.fori_loop(first, last, body, 0, unroll=unroll)


def swap_halves(x):
    return pltpu.roll(x, 64, 1)


def normed_rope(x, gain, cosine, sine):
    scale = lax.rsqrt(jnp.mean(x * x, axis=-1, keepdims=True) + epsilon)
    y = x * scale * gain
    return y * cosine + swap_halves(y) * sine


def normed_rope_back(x, gain, cosine, sine, grad):
    scale = lax.rsqrt(jnp.mean(x * x, axis=-1, keepdims=True) + epsilon)
    n = x * scale
    dy = grad * cosine - swap_halves(grad) * sine
    gain_part = dy * n
    dn = dy * gain
    dx = scale * (dn - n * jnp.mean(dn * n, axis=-1, keepdims=True))
    return dx, gain_part


def slot_sum(ref):
    total = ref[0]
    for i in range(1, count):
        total = total + ref[i]
    return total


def whole(
    lengths, positive_in, table, queries, keys, values, later, q_emb, p_emb, out_w, q_gain, k_gain,
    loss_out, gains_out, q_grad_out, d_grad_out, q_cot, k_cot, v_cot,
    turn, cosine, sine,
    q_f32, p_f32, q_all, p_all, q_wide, p_wide, q_cols, p_cols, tiles,
    q_part, spans, span_cat, q_terms, core_in, q_mid, q_in, q_last, q_end,
    d_sum, d_stage, d_in, tail_stage, tail_slots, tail_in, w_in,
    kv_stage, q_stage, grad_stage, kv_h, q_h, grad_h,
    grad_low, grad_turn, grad_cat, last_probs, scores, tops, sums, factors, attn, k_turn, v_turn, dq_acc, dkv, dq_stage, dq_slots,
    core_slots, y_stage, y_slots, x_stage, x_slots, seq_slots, dp_slots,
    send_sem, recv_sem, own_sem,
):
    d, j = lax.axis_index("dp"), lax.axis_index("seq")
    x, y, c = j // 4, (j // 2) % 2, j % 2
    z, low = d // 2, d % 2
    rank = 2 * x + c
    barrier = pltpu.get_barrier_semaphore()

    def remote(name, src, dst, slot, dp, seq):
        phase = phase_of[name]
        return pltpu.make_async_remote_copy(
            src_ref=src,
            dst_ref=dst,
            send_sem=send_sem.at[phase],
            recv_sem=recv_sem.at[phase, slot],
            device_id=(dp, seq),
            device_id_type=MESH,
        )

    def bulk(name, ref):
        return remote(name, ref, ref, 0, d, j)

    def others(step, me, size=count):
        for o in sorted(range(1, size), key=lambda o: abs(o - size // 2)):
            step(lax.rem(me + o, size))

    others(
        lambda p: pl.semaphore_signal(barrier, inc=1, device_id=(d, p), device_id_type=MESH), j
    )
    others(
        lambda p: pl.semaphore_signal(barrier, inc=1, device_id=(p, j), device_id_type=MESH), d
    )
    turn_copy = pltpu.make_async_copy(
        table.at[pl.ds(pl.multiple_of(j * 128, 128), 128)], turn, own_sem.at[0]
    )
    turn_copy.start()

    def lanes(h):
        return pl.ds(pl.multiple_of(h * 128, 128), 128)

    def q_rows(s, size=1):
        return pl.ds(pl.multiple_of(s * 2 * q_stride, 16), size * 2 * q_stride)

    def p_rows(s, size=1):
        return pl.ds(pl.multiple_of(s * 2 * chunks, 16), size * 2 * chunks)

    place = 8 * c + 2 * x + y
    q_f32[...] = jnp.zeros_like(q_f32)
    q_own, p_own = q_emb[...].astype(f32), p_emb[...].astype(f32)
    for i in range(chunks):
        q_f32[pl.ds(i, 2, stride=q_stride), :] = q_own[:, i * 128 : i * 128 + 128]
        p_f32[pl.ds(i, 2, stride=chunks), :] = p_own[:, i * 128 : i * 128 + 128]
    for i in range(2):
        index = positive_in[i]
        spot = i * q_stride + chunks
        q_f32[spot : spot + 1, :] = jnp.full((1, 128), index >> 1, jnp.int32).astype(f32)
        q_f32[spot + 1 : spot + 2, :] = jnp.full((1, 128), index & 1, jnp.int32).astype(f32)
    q_all[q_rows(place), :] = q_f32[...].astype(bf16)
    p_all[p_rows(d), :] = p_f32[...].astype(bf16)
    turn_copy.wait()
    first_half = lax.broadcasted_iota(jnp.int32, (128, 128), 1) < 64
    turned = swap_halves(turn[...])
    cosine[...] = jnp.where(first_half, turn[...], turned)
    sine[...] = jnp.where(first_half, -turned, turn[...])

    def stage_kv(g):
        rot = normed_rope(keys[:, lanes(g)].astype(f32), k_gain[...], cosine[...], sine[...])
        kv_stage[g, 0] = rot.astype(bf16)
        kv_stage[g, 1] = values[:, lanes(g)]

    loop(0, 4, stage_kv, unroll=True)
    pl.semaphore_wait(barrier, 2 * (count - 1))

    over_y = 4 * x + 2 * (1 - y) + c
    over_core = 4 * x + 2 * y + (1 - c)
    over_low = d + 1 - 2 * low

    def beside(p):
        return 4 * p + 2 * y + c

    def q_copy(p):
        rows = q_all.at[q_rows(place), :]
        return remote("q_msg", rows, rows, 0, d, p)

    def p_copy(p):
        rows = p_all.at[p_rows(d), :]
        return remote("p_msg", rows, rows, 0, p, j)

    others(lambda p: q_copy(p).start(), j)
    others(lambda p: p_copy(p).start(), d)

    def x_copies(t, step):
        def copy(to):
            name, src = ("k_x", "v_x")[t], kv_stage.at[to, t]
            step(remote(name, src, kv_h.at[t, x, y, c], 0, d, beside(to)))

        others(copy, x, 4)

    def kv_pass(t, way, of_y, of_core, seq):
        block = kv_h.at[t, :, of_y, of_core]
        return remote("kv"[t] + way, block, block, 0, d, seq)

    def pass_on(t):
        bulk(("k_x", "v_x")[t], kv_h.at[t, pl.ds(0, 3), y, c]).wait_recv()
        kv_pass(t, "_y", y, c, over_y).start()
        kv_pass(t, "_core", y, c, over_core).start()

    def pass_from_y(t):
        kv_pass(t, "_y", 1 - y, c, over_y).wait_recv()
        kv_pass(t, "_both", 1 - y, c, over_core).start()

    def kv_arrive(t):
        kv_pass(t, "_core", y, 1 - c, over_core).wait_recv()
        kv_pass(t, "_both", 1 - y, 1 - c, over_core).wait_recv()

    x_copies(0, lambda copy: copy.start())
    kv_h[:, x, y, c] = kv_stage[x]

    def stage_q(h):
        rot = normed_rope(queries[:, lanes(h)].astype(f32), q_gain[...], cosine[...], sine[...])
        q_stage[h // 2, h % 2] = rot.astype(bf16)

    def seat(r):
        return 4 * (r // 2) + 2 * y + r % 2

    def head_send(name, stage, held):
        others(
            lambda p: remote(
                name, stage.at[p], held.at[x, :, c], 0, d, seat(p)
            ).start(),
            rank,
            8,
        )
        held[x, :, c] = stage[rank]

    loop(0, 16, stage_q, unroll=4)

    def w_copy(slot, seq):
        return remote("w_out", out_w, w_in.at[slot], slot, d, seq)

    def w_targets(step):
        for b in range(2):
            to = 4 * x + 2 * b + y
            pl.when(to != j)(lambda to=to: step(w_copy(j % 2, to)))

    w_targets(lambda copy: copy.start())

    @pl.when(c == y)
    def _():
        w_in[j % 2] = out_w[...]

    pass_on(0)
    head_send("q", q_stage, q_h)

    def stage_grad(h):
        grad_stage[h // 2, h % 2] = later[:, lanes(h)]

    loop(0, 16, stage_grad)
    dkv[...] = jnp.zeros_like(dkv)

    bulk("q_msg", q_all.at[q_rows(0, count - 1), :]).wait_recv()
    bulk("p_msg", p_all.at[p_rows(0, count - 1), :]).wait_recv()
    q_wide[...] = q_all[...].astype(f32)
    p_wide[...] = p_all[...].astype(f32)
    for i in range(chunks):
        half = pl.ds((i % 2) * 128, 128)
        q_cols[i // 2, :, half] = q_wide[pl.ds(i, pairs, stride=q_stride), :].astype(bf16)
        p_cols[i // 2, :, half] = p_wide[pl.ds(i, pairs, stride=chunks), :].astype(bf16)
    positive = (
        2.0 * q_wide[pl.ds(chunks, pairs, stride=q_stride), :]
        + q_wide[pl.ds(chunks + 1, pairs, stride=q_stride), :]
    )

    def four(block):
        return jnp.concatenate([block] * (128 // pairs), axis=0)

    def one(block):
        return block[:32] + block[32:64] + block[64:96] + block[96:]

    logits = mm_nt(q_cols[0], four(p_cols[0]))
    for b in range(1, count):
        logits = logits + mm_nt(q_cols[b], four(p_cols[b]))
    logits = logits / sharpness
    quarter_of = lax.broadcasted_iota(jnp.int32, (8, 128), 1) >> 5

    def pack(block):
        packed = block[:8]
        for i in range(1, 4):
            packed = jnp.where(quarter_of == i, block[8 * i : 8 * i + 8], packed)
        return packed

    tiles[j] = pack(logits)

    def tile_copy(p):
        return remote("tile", tiles.at[j], tiles.at[j], 0, d, p)

    others(lambda p: tile_copy(p).start(), j)
    x_copies(1, lambda copy: copy.start())

    def half_of(core):
        return pl.ds(pl.multiple_of(16 * core, 16), 16)

    def part_copy(p):
        return remote(
            "part", q_cols.at[p, half_of(c)], q_part.at[d, half_of(c)], 0, p, j
        )

    others(lambda p: part_copy(p).start(), d)
    q_part[d, half_of(c)] = q_cols[d, half_of(c)]
    head_send("grad", grad_stage, grad_h)
    lane = lax.broadcasted_iota(jnp.int32, (pairs, 128), 1)
    line = lax.broadcasted_iota(jnp.int32, (pairs, 128), 0)
    real = (lane >> 5) == (line >> 3)
    base = jnp.where(real, ((lane & 31) >> 1) * pairs + (lane & 1), -(1 << 20)).astype(f32)

    pass_from_y(0)

    bulk("tile", tiles.at[pl.ds(0, count - 1)]).wait_recv()
    high = tiles[0]
    for i in range(1, count):
        high = jnp.maximum(high, tiles[i])
    high = jnp.max(jnp.where(real, four(high), lowest), axis=1, keepdims=True)
    mass = jnp.zeros((pairs, 128), f32)
    hit = jnp.zeros((pairs, 128), f32)
    for i in range(count):
        tile = four(tiles[i])
        mass = mass + jnp.where(real, jnp.exp(tile - high), 0.0)
        hit = hit + jnp.where(base + 2.0 * i == positive, tile, 0.0)
    log_total = high + jnp.log(jnp.sum(mass, axis=1, keepdims=True))
    picked = jnp.sum(hit, axis=1, keepdims=True)
    loss_part = jnp.sum(log_total - picked, axis=0, keepdims=True)

    def weights_of(tile, index):
        onehot = jnp.where(base + 2.0 * index == positive, 1.0, 0.0)
        return jnp.where(real, (jnp.exp(four(tile) - log_total) - onehot) / sharpness, 0.0)

    mine = weights_of(tiles[j], j.astype(f32)).astype(bf16)
    spans[d, pl.ds(0, 8)] = pack(weights_of(tiles[0], 0.0).astype(bf16).astype(f32))
    spans[d, pl.ds(8, 8)] = pack(mine.astype(f32))

    def span_copy(p):
        return remote("span", spans.at[d], spans.at[d], 0, p, j)

    others(lambda p: span_copy(p).start(), d)
    pass_on(1)

    kv_arrive(0)
    bulk("q", q_stage.at[pl.ds(0, 7)]).wait_recv()
    length = lengths[0]
    key_line = lax.broadcasted_iota(jnp.int32, (128, 1), 0)
    ahead = lax.broadcasted_iota(jnp.int32, (128, 256), 0) - lax.broadcasted_iota(
        jnp.int32, (128, 256), 1
    )
    tops[...] = jnp.full_like(tops, lowest)
    sums[...] = jnp.zeros_like(sums)

    def spot_of(a, b):
        return (a * (a + 1)) // 2 + b

    def softmax_rows(o):
        a = 3 - o

        def strips(b, diagonal):
            keys_b = kv_h[0, b].reshape(4, 128, 128)
            for half in range(2):
                q = q_h[a, half].reshape(256, 128)
                across = slice(half * 256, half * 256 + 256)
                for i in range(4):
                    start = b * 512 + i * 128
                    bias = jnp.where(key_line < length - start, 0.0, lowest)
                    s = mm_nt(keys_b[i], q) * (scaling * math.log2(math.e)) + bias
                    if diagonal:
                        s = jnp.where(ahead <= 256 * y - i * 128, s, lowest)
                    top = jnp.max(s, axis=0, keepdims=True)
                    e = jnp.exp2(s - top)
                    scores[spot_of(a, b), i * 128 : i * 128 + 128, across] = e
                    tops[a, b, i : i + 1, across] = top
                    sums[a, b, i : i + 1, across] = jnp.sum(e, axis=0, keepdims=True)

        loop(0, a, lambda b: strips(b, False))
        strips(a, True)
        part_tops = tops[a].reshape(32, 512)
        part = jnp.exp2(part_tops - jnp.max(part_tops, axis=0, keepdims=True))
        total = jnp.sum(part * sums[a].reshape(32, 512), axis=0, keepdims=True)
        factors[a] = (part * (1.0 / total)).reshape(4, 8, 512)

    softmax_rows(0)
    bulk("part", q_part.at[pl.ds(0, count - 1), pl.ds(0, 16)]).wait_recv()
    part_core = remote(
        "part_core", q_part.at[:, half_of(c)], q_part.at[:, half_of(c)], 0, d, over_core
    )
    part_core.start()
    softmax_rows(1)

    bulk("span", spans.at[pl.ds(0, count - 1)]).wait_recv()
    for i in range(count):
        for t in range(2):
            weights = jnp.where(real, four(spans[i, t * 8 : t * 8 + 8]), 0.0)
            span_cat[i, :, t * 128 : t * 128 + 128] = weights.astype(bf16)
    remote(
        "part_core", q_part.at[:, half_of(1 - c)], q_part.at[:, half_of(1 - c)], 0, d, over_core
    ).wait_recv()
    span_sums = mm_tn(
        span_cat[...].reshape(pairs * count, 256), q_part[...].reshape(pairs * count, 256)
    )
    span = one(span_sums[:128]).astype(bf16)
    d_sums = one(span_sums[128:])
    d_sum[pl.ds(0, pairs), :] = d_sums[:, :128]
    d_sum[pl.ds(pairs, pairs), :] = d_sums[:, 128:]
    for b in range(2):
        source = 4 * x + 2 * c + b
        pl.when(source != j)(lambda b=b, source=source: w_copy(b, source).wait_recv())
    rows_a, rows_b = mm_nt(span, w_in[0]), mm_nt(span, w_in[1])
    for i in range(count):
        tail_stage[i, pl.ds(0, 2)] = jnp.broadcast_to(rows_a[2 * i : 2 * i + 1], (2, 128))
        tail_stage[i, pl.ds(2, 2)] = jnp.broadcast_to(rows_b[2 * i : 2 * i + 1], (2, 128))
        tail_stage[i, pl.ds(4, 4)] = jnp.broadcast_to(loss_part, (4, 128))

    def tail_part(p):
        return remote("tail_part", tail_stage.at[p], tail_slots.at[d], 0, p, j)

    others(lambda p: tail_part(p).start(), d)
    tail_slots[d] = tail_stage[d]

    pass_from_y(1)
    loop(2, 4, softmax_rows)

    d_stage[...] = jnp.zeros_like(d_stage)
    for r in range(2):
        for half in range(2):
            d_stage[pl.ds(2 * r + half, count, stride=8), :] = d_sum[
                pl.ds(half * pairs + r, count, stride=2), :
            ]

    def d_rows(s):
        return pl.ds(pl.multiple_of(s * 8, 8), 8)

    def d_copy(p):
        return remote("d_out", d_stage.at[d_rows(p), :], d_in.at[d_rows(d), :], 0, p, j)

    others(lambda p: d_copy(p).start(), d)
    d_in[d_rows(d), :] = d_stage[d_rows(d), :]

    for b in range(count):
        q_term = mm(mine, four(p_cols[b]))
        for half in range(2):
            rows = pl.ds(2 * b + half, pairs, stride=chunks)
            q_terms[rows, :] = q_term[:, half * 128 : half * 128 + 128]
    core_send = remote("term_core", q_terms.at[p_rows(8 * (1 - c), 8), :], core_in, 0, d, over_core)
    core_send.start()
    kv_arrive(1)
    bulk("grad", grad_stage.at[pl.ds(0, 7)]).wait_recv()
    row = lax.broadcasted_iota(jnp.int32, (512, 1), 0)
    row_token = (row & 255) + 256 * y

    def core_copy(t, a):
        name = ("core_sum_k", "core_sum_v")[t]
        return remote(name, dkv.at[t, a, :, 1 - c], core_slots.at[t, a], a, d, over_core)

    def y_copy(t, a):
        return remote(("y_sum_k", "y_sum_v")[t], y_stage.at[t, a], y_slots.at[t, a], a, d, over_y)

    def x_copy(t, to):
        name = ("x_out_k", "x_out_v")[t]
        return remote(name, x_stage.at[t, to], x_slots.at[t, x], 0, d, beside(to))

    def dq_copy(a, e):
        return remote("dq", dq_stage.at[a, :, e], dq_slots.at[rank], 0, d, 4 * a + 2 * y + e)

    def send_y(t, a):
        core_copy(t, a).wait_recv()
        y_stage[t, a] = dkv[t, a, 1 - y, c] + core_slots[t, a, 1 - y]
        y_copy(t, a).start()

    def send_x(t, a):
        y_copy(t, a).wait_recv()
        total = dkv[t, a, y, c] + core_slots[t, a, y] + y_slots[t, a]
        x_stage[t, a] = total.astype(bf16)

        @pl.when(a != x)
        def _():
            x_copy(t, a).start()

        @pl.when(a == x)
        def _():
            x_slots[t, x] = x_stage[t, a]

    def make_grad(a):
        spot = row_token + 512 * a
        extra = jnp.where(row < 256, tail_in[0:1], tail_in[2:3])
        last = jnp.where(spot == length - 1, 1.0, 0.0)
        grad = grad_h[a].reshape(512, 128).astype(f32) + last * extra
        grad_low[a] = jnp.where(spot < length, grad, 0.0).astype(bf16)

    def turned_block(block):
        return jnp.transpose(block.reshape(512, 128).astype(f32))

    def turn_block(b):
        k_turn[b] = turned_block(kv_h[0, b]).astype(bf16)
        v_turn[b] = turned_block(kv_h[1, b]).astype(bf16)

    loop(0, 4, turn_block)

    last_lane = lax.broadcasted_iota(jnp.int32, (512, 128), 1)

    def first_grad(a):
        spot = row_token + 512 * a
        early = jnp.where(spot < length - 1, grad_h[a].reshape(512, 128).astype(f32), 0.0)
        grad_cat[a, :, :128] = early.astype(bf16)
        last = jnp.where(spot == length - 1, 1.0, 0.0)
        grad_cat[a, :, 128:] = jnp.where(last_lane == row >> 8, last, 0.0).astype(bf16)

    loop(0, 4, first_grad)
    last_probs[...] = jnp.zeros_like(last_probs)
    attn[...] = jnp.zeros_like(attn)

    def value_block(o):
        b = 3 - o

        def rows(a):
            spot = spot_of(a, b)
            low_b = jnp.concatenate(
                [
                    (scores[spot, i * 128 : i * 128 + 128] * factors[a, b, i : i + 1]).astype(bf16)
                    for i in range(4)
                ],
                axis=0,
            )
            terms = mm(low_b, grad_cat[a])
            dkv[1, b] += terms[:, :128].reshape(2, 2, 128, 128)
            last_probs[b] += terms[:, 128:]
            attn[a] += mm(v_turn[b], low_b)

        loop(b, 4, rows)

    loop(0, 4, value_block)
    core_send.wait_recv()
    both = q_terms[p_rows(8 * c, 8), :] + core_in[...]
    q_mid[...] = both.reshape(4, 128, 128)

    def term_x(p):
        return remote("term_x", q_mid.at[p], q_in.at[x], 0, d, beside(p))

    others(lambda p: term_x(p).start(), x, 4)
    q_in[x] = q_mid[x]

    bulk("tail_part", tail_slots.at[pl.ds(0, count - 1)]).wait_recv()
    tails = slot_sum(tail_slots)
    loss_out[...] = tails[4:5] / (pairs * count)
    tail_in[...] = tails

    last_grad = jnp.zeros((128, 128), f32)
    for a in range(4):
        last_grad = last_grad + mm_tn(grad_cat[a, :, 128:], grad_h[a].reshape(512, 128))
    head_line = lax.broadcasted_iota(jnp.int32, (128, 128), 0)
    both_tails = jnp.where(head_line == 0, tails[0:1], jnp.where(head_line == 1, tails[2:3], 0.0))
    last_low = (last_grad + both_tails).astype(bf16)

    def last_row(o):
        b = 3 - o
        dkv[1, b] += mm(last_probs[b].astype(bf16), last_low).reshape(2, 2, 128, 128)
        core_copy(1, b).start()

    loop(0, 4, last_row)

    def all_grad(a):
        make_grad(a)
        grad_turn[a] = turned_block(grad_low[a])

    loop(0, 4, all_grad)
    loop(0, 4, lambda o: send_y(1, 3 - o))

    def quarter(o):
        a = 3 - o
        q = q_h[a].reshape(512, 128)
        row_dot = jnp.sum(grad_turn[a] * attn[a], axis=0, keepdims=True)
        dq_acc[...] = jnp.zeros_like(dq_acc)

        def keys_of(b):
            spot = spot_of(a, b)
            values_b = kv_h[1, b].reshape(4, 128, 128)
            parts = []
            for i in range(4):
                prob_grad = mm_nt(values_b[i], grad_low[a])
                probs = scores[spot, i * 128 : i * 128 + 128] * (factors[a, b, i : i + 1] * scaling)
                parts.append((probs * (prob_grad - row_dot)).astype(bf16))
            sg = jnp.concatenate(parts, axis=0)
            dkv[0, b] += mm(sg, q).reshape(2, 2, 128, 128)
            dq_acc[...] += mm(k_turn[b], sg)

        loop(0, a + 1, keys_of)
        core_copy(0, a).start()
        dq_stage[a] = jnp.transpose(dq_acc[...]).astype(bf16).reshape(2, 2, 128, 128)
        for e in range(2):

            @pl.when(2 * a + e != rank)
            def _():
                dq_copy(a, e).start()

            @pl.when(2 * a + e == rank)
            def _():
                dq_slots[rank] = dq_stage[a, :, e]

        pl.when(o >= 1)(lambda: send_y(0, a + 1))
        send_x(1, a)
        pl.when(o >= 2)(lambda: send_x(0, a + 2))

    loop(0, 4, quarter)
    send_y(0, 0)
    bulk("term_x", q_in.at[pl.ds(0, 3)]).wait_recv()
    q_last[...] = (q_in[0] + q_in[1] + q_in[2] + q_in[3]).reshape(2, 64, 128)
    term_y = remote("term_y", q_last.at[1 - y], q_end, 0, d, over_y)
    term_y.start()
    send_x(0, 1)

    bulk("dq", dq_slots.at[pl.ds(0, 7)]).wait_recv()

    def gain_fold(block):
        return jnp.sum(block.reshape(16, 8, 128), axis=0)

    def query_head(h, total):
        grad = dq_slots[h // 2, h % 2].astype(f32)
        dx, part = normed_rope_back(
            queries[:, lanes(h)].astype(f32), q_gain[...], cosine[...], sine[...], grad
        )
        q_cot[:, lanes(h)] = dx.astype(bf16)
        return total + gain_fold(part)

    q_total = lax.fori_loop(0, 16, query_head, jnp.zeros((8, 128), f32), unroll=4)
    send_x(0, 0)
    term_y.wait_recv()
    bulk("d_out", d_in.at[pl.ds(0, 8 * (count - 1)), :]).wait_recv()
    q_f32[pl.ds(0, 2 * chunks), :] = q_last[y] + q_end[...]
    for i in range(chunks):
        part = pl.ds(i * 128, 128)
        q_grad_out[:, part] = q_f32[pl.ds(i, 2, stride=chunks), :].astype(bf16)
        d_row = 8 * (i // 2) + i % 2
        d_grad_out[:, part] = d_in[pl.ds(d_row, 2, stride=2), :].astype(bf16)
    bulk("x_out_v", x_slots.at[1, pl.ds(0, 3)]).wait_recv()
    bulk("x_out_k", x_slots.at[0, pl.ds(0, 3)]).wait_recv()

    def key_head(g, total):
        v_cot[:, lanes(g)] = x_slots[1, g]
        dx, part = normed_rope_back(
            keys[:, lanes(g)].astype(f32), k_gain[...], cosine[...], sine[...],
            x_slots[0, g].astype(f32),
        )
        k_cot[:, lanes(g)] = dx.astype(bf16)
        return total + gain_fold(part)

    k_total = lax.fori_loop(0, 4, key_head, jnp.zeros((8, 128), f32), unroll=True)
    seq_slots[j, pl.ds(0, 4)] = q_total[:4] + q_total[4:]
    seq_slots[j, pl.ds(4, 4)] = k_total[:4] + k_total[4:]

    def gain_seq(p):
        return remote("gain_seq", seq_slots.at[j], seq_slots.at[j], 0, d, p)

    others(lambda p: gain_seq(p).start(), j)
    bulk("gain_seq", seq_slots.at[pl.ds(0, count - 1)]).wait_recv()
    dp_slots[d] = slot_sum(seq_slots)

    def gain_dp(p):
        return remote("gain_dp", dp_slots.at[d], dp_slots.at[d], 0, p, j)

    others(lambda p: gain_dp(p).start(), d)
    bulk("gain_dp", dp_slots.at[pl.ds(0, count - 1)]).wait_recv()
    gains = slot_sum(dp_slots)
    gains_out[0:1, :] = jnp.sum(gains[:4], axis=0, keepdims=True)
    gains_out[1:2, :] = jnp.sum(gains[4:], axis=0, keepdims=True)

    for name, ref in (
        ("q_msg", q_all.at[q_rows(0, count - 1), :]),
        ("p_msg", p_all.at[p_rows(0, count - 1), :]),
        ("tile", tiles.at[pl.ds(0, count - 1)]),
        ("part", q_part.at[pl.ds(0, count - 1), pl.ds(0, 16)]),
        ("span", spans.at[pl.ds(0, count - 1)]),
        ("tail_part", tail_slots.at[pl.ds(0, count - 1)]),
        ("d_out", d_in.at[pl.ds(0, 8 * (count - 1)), :]),
        ("term_x", q_in.at[pl.ds(0, 3)]),
        ("gain_seq", seq_slots.at[pl.ds(0, count - 1)]),
        ("gain_dp", dp_slots.at[pl.ds(0, count - 1)]),
        ("k_x", kv_stage.at[pl.ds(0, 3), 0]),
        ("v_x", kv_stage.at[pl.ds(0, 3), 1]),
        ("k_y", kv_h.at[0, :, 0, 0]),
        ("v_y", kv_h.at[1, :, 0, 0]),
        ("k_core", kv_h.at[0, :, 0, 0]),
        ("v_core", kv_h.at[1, :, 0, 0]),
        ("k_both", kv_h.at[0, :, 0, 0]),
        ("v_both", kv_h.at[1, :, 0, 0]),
        ("q", q_stage.at[pl.ds(0, 7)]),
        ("grad", grad_stage.at[pl.ds(0, 7)]),
        ("dq", dq_slots.at[pl.ds(0, 7)]),
        ("core_sum_k", core_slots.at[0]),
        ("core_sum_v", core_slots.at[1]),
        ("y_sum_k", y_stage.at[0]),
        ("y_sum_v", y_stage.at[1]),
        ("x_out_k", x_slots.at[0, pl.ds(0, 3)]),
        ("x_out_v", x_slots.at[1, pl.ds(0, 3)]),
    ):
        bulk(name, ref).wait_send()
    core_send.wait_send()
    term_y.wait_send()
    part_core.wait_send()
    w_targets(lambda copy: copy.wait_send())


def finish(loss, gains, *refs):
    size = (len(refs) - 3) // 2
    loss_out, q_out, k_out = refs[size : size + 3]
    loss_out[...] = loss[0:1, 0:1]
    q_out[...] = gains[0:1, :]
    k_out[...] = gains[1:2, :]
    for made, out in zip(refs[:size], refs[size + 3 :]):
        out[...] = made[...]


def shards(
    question_embedding_matrix,
    passage_embedding_matrix,
    positive,
    queries,
    keys,
    values,
    later_grad,
    lengths,
    q_gain,
    k_gain,
    out_weight,
):
    angles = np.arange(2048)[:, None] * rope_base ** (-2.0 * np.arange(64) / 128)[None, :]
    table = jnp.asarray(np.concatenate([np.cos(angles), np.sin(angles)], axis=1).astype(np.float32))
    out = jax.ShapeDtypeStruct
    vm = pltpu.VMEM
    smem = pl.BlockSpec(memory_space=pltpu.SMEM)
    anywhere = pl.BlockSpec(memory_space=pl.ANY)
    results = [
        out(question_embedding_matrix.shape, bf16),
        out(passage_embedding_matrix.shape, bf16),
        out(queries.shape[1:], bf16),
        out(keys.shape[1:], bf16),
        out(values.shape[1:], bf16),
    ]
    loss, gains, *made = pl.pallas_call(
        whole,
        out_shape=[out((1, 128), f32), out((2, 128), f32)] + results,
        in_specs=[smem, smem, anywhere] + [VMEM] * 9,
        out_specs=[VMEM] * 7,
        scratch_shapes=[
            vm((128, 128), f32),
            vm((128, 128), f32),
            vm((128, 128), f32),
            vm((2 * q_stride, 128), f32),
            vm((2 * chunks, 128), f32),
            vm((2 * q_stride * count, 128), bf16),
            vm((2 * chunks * count, 128), bf16),
            vm((2 * q_stride * count, 128), f32),
            vm((2 * chunks * count, 128), f32),
            vm((count, pairs, 256), bf16),
            vm((count, pairs, 256), bf16),
            vm((count, 8, 128), f32),
            vm((count, pairs, 256), bf16),
            vm((count, 16, 128), f32),
            vm((count, pairs, 256), bf16),
            vm((pairs * chunks, 128), f32),
            vm((pairs * chunks // 2, 128), f32),
            vm((4, 128, 128), f32),
            vm((4, 128, 128), f32),
            vm((2, 64, 128), f32),
            vm((64, 128), f32),
            vm((2 * pairs, 128), f32),
            vm((8 * count, 128), f32),
            vm((8 * count, 128), f32),
            vm((count, 8, 128), f32),
            vm((count, 8, 128), f32),
            vm((8, 128), f32),
            vm((2, 128, 256), bf16),
            vm((4, 2, 128, 128), bf16),
            vm((8, 2, 128, 128), bf16),
            vm((8, 2, 128, 128), bf16),
            vm((2, 4, 2, 2, 128, 128), bf16),
            vm((4, 2, 2, 128, 128), bf16),
            vm((4, 2, 2, 128, 128), bf16),
            vm((4, 512, 128), bf16),
            vm((4, 128, 512), f32),
            vm((4, 512, 256), bf16),
            vm((4, 512, 128), f32),
            vm((10, 512, 512), f32),
            vm((4, 4, 8, 512), f32),
            vm((4, 4, 8, 512), f32),
            vm((4, 4, 8, 512), f32),
            vm((4, 128, 512), f32),
            vm((4, 128, 512), bf16),
            vm((4, 128, 512), bf16),
            vm((128, 512), f32),
            vm((2, 4, 2, 2, 128, 128), f32),
            vm((4, 2, 2, 128, 128), bf16),
            vm((8, 2, 128, 128), bf16),
            vm((2, 4, 2, 128, 128), f32),
            vm((2, 4, 128, 128), f32),
            vm((2, 4, 128, 128), f32),
            vm((2, 4, 128, 128), bf16),
            vm((2, 4, 128, 128), bf16),
            vm((count, 8, 128), f32),
            vm((count, 8, 128), f32),
            pltpu.SemaphoreType.DMA((len(phases),)),
            pltpu.SemaphoreType.DMA((len(phases), 4)),
            pltpu.SemaphoreType.DMA((1,)),
        ],
        compiler_params=pltpu.CompilerParams(
            collective_id=0, has_side_effects=True, vmem_limit_bytes=limit
        ),
    )(
        lengths, positive, table, queries[0], keys[0], values[0], later_grad[0],
        question_embedding_matrix, passage_embedding_matrix, out_weight,
        q_gain[None, :], k_gain[None, :],
    )
    loss, q_gain_grad, k_gain_grad, query_grad, doc_grad, query_cot, key_cot, value_cot = (
        pl.pallas_call(
            finish,
            out_shape=[out((1, 1), f32), out((1, 128), f32), out((1, 128), f32)] + results,
            in_specs=[VMEM] * 7,
            out_specs=[VMEM] * 8,
        )(loss, gains, *made)
    )
    return (
        loss.reshape(()),
        query_grad,
        doc_grad,
        query_cot[None],
        key_cot[None],
        value_cot[None],
        q_gain_grad[0],
        k_gain_grad[0],
    )


def solution(mesh):
    in_specs = (
        P(("dp", "seq"), None),
        P(("dp", "seq"), None),
        P(("dp", "seq")),
        P("dp", "seq", None),
        P("dp", "seq", None),
        P("dp", "seq", None),
        P("dp", "seq", None),
        P("dp"),
        P(),
        P(),
        P("seq", "dp"),
    )
    out_specs = (
        P(),
        P(("dp", "seq"), None),
        P(("dp", "seq"), None),
        P("dp", "seq", None),
        P("dp", "seq", None),
        P("dp", "seq", None),
        P(),
        P(),
    )
    return jax.shard_map(
        shards, mesh=mesh, in_specs=in_specs, out_specs=out_specs, check_vma=False
    )
```

```python
import functools
import math

import jax
import jax.numpy as jnp
import numpy as np
from jax import lax
from jax.experimental import pallas as pl
from jax.experimental.pallas import tpu as pltpu
from jax.sharding import PartitionSpec as P

sharpness = 0.05
epsilon = 1e-06
rope_base = 1000000.0
lowest = -1e30
MESH = pl.DeviceIdType.MESH
f32 = jnp.float32
bf16 = jnp.bfloat16
VMEM = pl.BlockSpec(memory_space=pltpu.VMEM)
limit = 58 * 1024 * 1024
count = 16
pairs = 32
chunks = 32
q_stride = 40
scaling = 128 ** (-0.5)
phases = (
    "q_msg", "p_msg", "tile", "part", "part_core", "span", "tail_part", "w_out",
    "d_out", "term_core", "term_x", "term_y", "gain_seq", "gain_dp",
    "k_x", "k_y", "k_core", "k_both", "v_x", "v_y", "v_core", "v_both", "q", "grad", "dq", "core_sum_k", "core_sum_v", "y_sum_k", "y_sum_v",
    "x_out_k", "x_out_v", "last",
)
phase_of = {name: i for i, name in enumerate(phases)}


def mm(a, b):
    return lax.dot_general(a, b, (((1,), (0,)), ((), ())), preferred_element_type=f32)


def mm_nt(a, b):
    return lax.dot_general(a, b, (((1,), (1,)), ((), ())), preferred_element_type=f32)


def mm_tn(a, b):
    return lax.dot_general(a, b, (((0,), (0,)), ((), ())), preferred_element_type=f32)


def loop(first, last, step, unroll=None):
    def body(i, carry):
        step(i)
        return carry

    lax.fori_loop(first, last, body, 0, unroll=unroll)


def swap_halves(x):
    return pltpu.roll(x, 64, 1)


def normed_rope(x, gain, cosine, sine):
    scale = lax.rsqrt(jnp.mean(x * x, axis=-1, keepdims=True) + epsilon)
    y = x * scale * gain
    return y * cosine + swap_halves(y) * sine


def normed_rope_back(x, gain, cosine, sine, grad):
    scale = lax.rsqrt(jnp.mean(x * x, axis=-1, keepdims=True) + epsilon)
    n = x * scale
    dy = grad * cosine - swap_halves(grad) * sine
    gain_part = dy * n
    dn = dy * gain
    dx = scale * (dn - n * jnp.mean(dn * n, axis=-1, keepdims=True))
    return dx, gain_part


def slot_sum(ref):
    total = ref[0]
    for i in range(1, count):
        total = total + ref[i]
    return total


def whole(
    lengths, positive_in, table, queries, keys, values, later, q_emb, p_emb, out_w, q_gain, k_gain,
    loss_out, gains_out, q_grad_out, d_grad_out, q_cot, k_cot, v_cot,
    turn, cosine, sine,
    q_f32, p_f32, q_all, p_all, q_wide, p_wide, q_cols, p_cols, tiles,
    q_part, spans, span_cat, q_terms, core_in, q_mid, q_in, q_last, q_end,
    d_sum, d_stage, d_in, tail_stage, tail_slots, tail_in, w_in,
    kv_stage, q_stage, grad_stage, kv_h, q_h, grad_h,
    grad_low, grad_turn, grad_cat, stats, last_send, last_in, last_rows, scores, tops, sums, factors, attn, k_turn, v_turn, dq_acc, dkv, dq_stage, dq_slots,
    core_slots, y_stage, y_slots, x_stage, x_slots, seq_slots, dp_slots,
    send_sem, recv_sem, own_sem,
):
    d, j = lax.axis_index("dp"), lax.axis_index("seq")
    x, y, c = j // 4, (j // 2) % 2, j % 2
    z, low = d // 2, d % 2
    rank = 2 * x + c
    barrier = pltpu.get_barrier_semaphore()

    def remote(name, src, dst, slot, dp, seq):
        phase = phase_of[name]
        return pltpu.make_async_remote_copy(
            src_ref=src,
            dst_ref=dst,
            send_sem=send_sem.at[phase],
            recv_sem=recv_sem.at[phase, slot],
            device_id=(dp, seq),
            device_id_type=MESH,
        )

    def bulk(name, ref):
        return remote(name, ref, ref, 0, d, j)

    def others(step, me, size=count):
        for o in sorted(range(1, size), key=lambda o: abs(o - size // 2)):
            step(lax.rem(me + o, size))

    others(
        lambda p: pl.semaphore_signal(barrier, inc=1, device_id=(d, p), device_id_type=MESH), j
    )
    others(
        lambda p: pl.semaphore_signal(barrier, inc=1, device_id=(p, j), device_id_type=MESH), d
    )
    turn_copy = pltpu.make_async_copy(
        table.at[pl.ds(pl.multiple_of(j * 128, 128), 128)], turn, own_sem.at[0]
    )
    turn_copy.start()

    def lanes(h):
        return pl.ds(pl.multiple_of(h * 128, 128), 128)

    def q_rows(s, size=1):
        return pl.ds(pl.multiple_of(s * 2 * q_stride, 16), size * 2 * q_stride)

    def p_rows(s, size=1):
        return pl.ds(pl.multiple_of(s * 2 * chunks, 16), size * 2 * chunks)

    place = 8 * c + 2 * x + y
    q_f32[...] = jnp.zeros_like(q_f32)
    q_own, p_own = q_emb[...].astype(f32), p_emb[...].astype(f32)
    for i in range(chunks):
        q_f32[pl.ds(i, 2, stride=q_stride), :] = q_own[:, i * 128 : i * 128 + 128]
        p_f32[pl.ds(i, 2, stride=chunks), :] = p_own[:, i * 128 : i * 128 + 128]
    for i in range(2):
        index = positive_in[i]
        spot = i * q_stride + chunks
        q_f32[spot : spot + 1, :] = jnp.full((1, 128), index >> 1, jnp.int32).astype(f32)
        q_f32[spot + 1 : spot + 2, :] = jnp.full((1, 128), index & 1, jnp.int32).astype(f32)
    q_all[q_rows(place), :] = q_f32[...].astype(bf16)
    p_all[p_rows(d), :] = p_f32[...].astype(bf16)
    turn_copy.wait()
    first_half = lax.broadcasted_iota(jnp.int32, (128, 128), 1) < 64
    turned = swap_halves(turn[...])
    cosine[...] = jnp.where(first_half, turn[...], turned)
    sine[...] = jnp.where(first_half, -turned, turn[...])

    def stage_kv(g):
        rot = normed_rope(keys[:, lanes(g)].astype(f32), k_gain[...], cosine[...], sine[...])
        kv_stage[g, 0] = rot.astype(bf16)
        kv_stage[g, 1] = values[:, lanes(g)]

    loop(0, 4, stage_kv, unroll=True)
    pl.semaphore_wait(barrier, 2 * (count - 1))

    over_y = 4 * x + 2 * (1 - y) + c
    over_core = 4 * x + 2 * y + (1 - c)
    over_low = d + 1 - 2 * low

    def beside(p):
        return 4 * p + 2 * y + c

    def q_copy(p):
        rows = q_all.at[q_rows(place), :]
        return remote("q_msg", rows, rows, 0, d, p)

    def p_copy(p):
        rows = p_all.at[p_rows(d), :]
        return remote("p_msg", rows, rows, 0, p, j)

    others(lambda p: q_copy(p).start(), j)
    others(lambda p: p_copy(p).start(), d)

    def x_copies(t, step):
        def copy(to):
            name, src = ("k_x", "v_x")[t], kv_stage.at[to, t]
            step(remote(name, src, kv_h.at[t, x, y, c], 0, d, beside(to)))

        others(copy, x, 4)

    def kv_pass(t, way, of_y, of_core, seq):
        block = kv_h.at[t, :, of_y, of_core]
        return remote("kv"[t] + way, block, block, 0, d, seq)

    def pass_on(t):
        bulk(("k_x", "v_x")[t], kv_h.at[t, pl.ds(0, 3), y, c]).wait_recv()
        kv_pass(t, "_y", y, c, over_y).start()
        kv_pass(t, "_core", y, c, over_core).start()

    def pass_from_y(t):
        kv_pass(t, "_y", 1 - y, c, over_y).wait_recv()
        kv_pass(t, "_both", 1 - y, c, over_core).start()

    def kv_arrive(t):
        kv_pass(t, "_core", y, 1 - c, over_core).wait_recv()
        kv_pass(t, "_both", 1 - y, 1 - c, over_core).wait_recv()

    x_copies(0, lambda copy: copy.start())
    kv_h[:, x, y, c] = kv_stage[x]

    def stage_q(h):
        rot = normed_rope(queries[:, lanes(h)].astype(f32), q_gain[...], cosine[...], sine[...])
        q_stage[h // 2, h % 2] = rot.astype(bf16)

    def seat(r):
        return 4 * (r // 2) + 2 * y + r % 2

    def head_send(name, stage, held):
        others(
            lambda p: remote(
                name, stage.at[p], held.at[x, :, c], 0, d, seat(p)
            ).start(),
            rank,
            8,
        )
        held[x, :, c] = stage[rank]

    loop(0, 16, stage_q, unroll=4)

    def w_copy(slot, seq):
        return remote("w_out", out_w, w_in.at[slot], slot, d, seq)

    def w_targets(step):
        for b in range(2):
            to = 4 * x + 2 * b + y
            pl.when(to != j)(lambda to=to: step(w_copy(j % 2, to)))

    w_targets(lambda copy: copy.start())

    @pl.when(c == y)
    def _():
        w_in[j % 2] = out_w[...]

    pass_on(0)
    head_send("q", q_stage, q_h)

    def stage_grad(h):
        grad_stage[h // 2, h % 2] = later[:, lanes(h)]

    loop(0, 16, stage_grad)
    dkv[...] = jnp.zeros_like(dkv)

    bulk("q_msg", q_all.at[q_rows(0, count - 1), :]).wait_recv()
    bulk("p_msg", p_all.at[p_rows(0, count - 1), :]).wait_recv()
    q_wide[...] = q_all[...].astype(f32)
    p_wide[...] = p_all[...].astype(f32)
    for i in range(chunks):
        half = pl.ds((i % 2) * 128, 128)
        q_cols[i // 2, :, half] = q_wide[pl.ds(i, pairs, stride=q_stride), :].astype(bf16)
        p_cols[i // 2, :, half] = p_wide[pl.ds(i, pairs, stride=chunks), :].astype(bf16)
    positive = (
        2.0 * q_wide[pl.ds(chunks, pairs, stride=q_stride), :]
        + q_wide[pl.ds(chunks + 1, pairs, stride=q_stride), :]
    )

    def four(block):
        return jnp.concatenate([block] * (128 // pairs), axis=0)

    def one(block):
        return block[:32] + block[32:64] + block[64:96] + block[96:]

    logits = mm_nt(q_cols[0], four(p_cols[0]))
    for b in range(1, count):
        logits = logits + mm_nt(q_cols[b], four(p_cols[b]))
    logits = logits / sharpness
    quarter_of = lax.broadcasted_iota(jnp.int32, (8, 128), 1) >> 5

    def pack(block):
        packed = block[:8]
        for i in range(1, 4):
            packed = jnp.where(quarter_of == i, block[8 * i : 8 * i + 8], packed)
        return packed

    tiles[j] = pack(logits)

    def tile_copy(p):
        return remote("tile", tiles.at[j], tiles.at[j], 0, d, p)

    others(lambda p: tile_copy(p).start(), j)
    x_copies(1, lambda copy: copy.start())

    def half_of(core):
        return pl.ds(pl.multiple_of(16 * core, 16), 16)

    def part_copy(p):
        return remote(
            "part", q_cols.at[p, half_of(c)], q_part.at[d, half_of(c)], 0, p, j
        )

    others(lambda p: part_copy(p).start(), d)
    q_part[d, half_of(c)] = q_cols[d, half_of(c)]
    head_send("grad", grad_stage, grad_h)
    lane = lax.broadcasted_iota(jnp.int32, (pairs, 128), 1)
    line = lax.broadcasted_iota(jnp.int32, (pairs, 128), 0)
    real = (lane >> 5) == (line >> 3)
    base = jnp.where(real, ((lane & 31) >> 1) * pairs + (lane & 1), -(1 << 20)).astype(f32)

    pass_from_y(0)

    bulk("tile", tiles.at[pl.ds(0, count - 1)]).wait_recv()
    high = tiles[0]
    for i in range(1, count):
        high = jnp.maximum(high, tiles[i])
    high = jnp.max(jnp.where(real, four(high), lowest), axis=1, keepdims=True)
    mass = jnp.zeros((pairs, 128), f32)
    hit = jnp.zeros((pairs, 128), f32)
    for i in range(count):
        tile = four(tiles[i])
        mass = mass + jnp.where(real, jnp.exp(tile - high), 0.0)
        hit = hit + jnp.where(base + 2.0 * i == positive, tile, 0.0)
    log_total = high + jnp.log(jnp.sum(mass, axis=1, keepdims=True))
    picked = jnp.sum(hit, axis=1, keepdims=True)
    loss_part = jnp.sum(log_total - picked, axis=0, keepdims=True)

    def weights_of(tile, index):
        onehot = jnp.where(base + 2.0 * index == positive, 1.0, 0.0)
        return jnp.where(real, (jnp.exp(four(tile) - log_total) - onehot) / sharpness, 0.0)

    mine = weights_of(tiles[j], j.astype(f32)).astype(bf16)
    spans[d, pl.ds(0, 8)] = pack(weights_of(tiles[0], 0.0).astype(bf16).astype(f32))
    spans[d, pl.ds(8, 8)] = pack(mine.astype(f32))

    def span_copy(p):
        return remote("span", spans.at[d], spans.at[d], 0, p, j)

    others(lambda p: span_copy(p).start(), d)
    pass_on(1)

    kv_arrive(0)
    bulk("q", q_stage.at[pl.ds(0, 7)]).wait_recv()
    length = lengths[0]
    key_line = lax.broadcasted_iota(jnp.int32, (128, 1), 0)
    ahead = lax.broadcasted_iota(jnp.int32, (128, 256), 0) - lax.broadcasted_iota(
        jnp.int32, (128, 256), 1
    )
    tops[...] = jnp.full_like(tops, lowest)
    sums[...] = jnp.zeros_like(sums)

    def spot_of(a, b):
        return (a * (a + 1)) // 2 + b

    def softmax_rows(o):
        a = 3 - o

        def strips(b, diagonal):
            keys_b = kv_h[0, b].reshape(4, 128, 128)
            for half in range(2):
                q = q_h[a, half].reshape(256, 128)
                across = slice(half * 256, half * 256 + 256)
                for i in range(4):
                    start = b * 512 + i * 128
                    bias = jnp.where(key_line < length - start, 0.0, lowest)
                    s = mm_nt(keys_b[i], q) * (scaling * math.log2(math.e)) + bias
                    if diagonal:
                        s = jnp.where(ahead <= 256 * y - i * 128, s, lowest)
                    top = jnp.max(s, axis=0, keepdims=True)
                    e = jnp.exp2(s - top)
                    scores[spot_of(a, b), i * 128 : i * 128 + 128, across] = e
                    tops[a, b, i : i + 1, across] = top
                    sums[a, b, i : i + 1, across] = jnp.sum(e, axis=0, keepdims=True)

        loop(0, a, lambda b: strips(b, False))
        strips(a, True)
        part_tops = tops[a].reshape(32, 512)
        peak = jnp.max(part_tops, axis=0, keepdims=True)
        part = jnp.exp2(part_tops - peak)
        total = jnp.sum(part * sums[a].reshape(32, 512), axis=0, keepdims=True)
        factors[a] = (part * (1.0 / total)).reshape(4, 8, 512)
        stats[a, 0:1] = peak
        stats[a, 1:2] = 1.0 / total

    softmax_rows(0)
    bulk("part", q_part.at[pl.ds(0, count - 1), pl.ds(0, 16)]).wait_recv()
    part_core = remote(
        "part_core", q_part.at[:, half_of(c)], q_part.at[:, half_of(c)], 0, d, over_core
    )
    part_core.start()
    softmax_rows(1)

    bulk("span", spans.at[pl.ds(0, count - 1)]).wait_recv()
    for i in range(count):
        for t in range(2):
            weights = jnp.where(real, four(spans[i, t * 8 : t * 8 + 8]), 0.0)
            span_cat[i, :, t * 128 : t * 128 + 128] = weights.astype(bf16)
    remote(
        "part_core", q_part.at[:, half_of(1 - c)], q_part.at[:, half_of(1 - c)], 0, d, over_core
    ).wait_recv()
    span_sums = mm_tn(
        span_cat[...].reshape(pairs * count, 256), q_part[...].reshape(pairs * count, 256)
    )
    span = one(span_sums[:128]).astype(bf16)
    d_sums = one(span_sums[128:])
    d_sum[pl.ds(0, pairs), :] = d_sums[:, :128]
    d_sum[pl.ds(pairs, pairs), :] = d_sums[:, 128:]
    for b in range(2):
        source = 4 * x + 2 * c + b
        pl.when(source != j)(lambda b=b, source=source: w_copy(b, source).wait_recv())
    rows_a, rows_b = mm_nt(span, w_in[0]), mm_nt(span, w_in[1])
    for i in range(count):
        tail_stage[i, pl.ds(0, 2)] = jnp.broadcast_to(rows_a[2 * i : 2 * i + 1], (2, 128))
        tail_stage[i, pl.ds(2, 2)] = jnp.broadcast_to(rows_b[2 * i : 2 * i + 1], (2, 128))
        tail_stage[i, pl.ds(4, 4)] = jnp.broadcast_to(loss_part, (4, 128))

    def tail_part(p):
        return remote("tail_part", tail_stage.at[p], tail_slots.at[d], 0, p, j)

    others(lambda p: tail_part(p).start(), d)
    tail_slots[d] = tail_stage[d]

    pass_from_y(1)
    loop(2, 4, softmax_rows)

    d_stage[...] = jnp.zeros_like(d_stage)
    for r in range(2):
        for half in range(2):
            d_stage[pl.ds(2 * r + half, count, stride=8), :] = d_sum[
                pl.ds(half * pairs + r, count, stride=2), :
            ]

    def d_rows(s):
        return pl.ds(pl.multiple_of(s * 8, 8), 8)

    def d_copy(p):
        return remote("d_out", d_stage.at[d_rows(p), :], d_in.at[d_rows(d), :], 0, p, j)

    others(lambda p: d_copy(p).start(), d)
    d_in[d_rows(d), :] = d_stage[d_rows(d), :]

    for b in range(count):
        q_term = mm(mine, four(p_cols[b]))
        for half in range(2):
            rows = pl.ds(2 * b + half, pairs, stride=chunks)
            q_terms[rows, :] = q_term[:, half * 128 : half * 128 + 128]
    core_send = remote("term_core", q_terms.at[p_rows(8 * (1 - c), 8), :], core_in, 0, d, over_core)
    core_send.start()
    kv_arrive(1)
    bulk("grad", grad_stage.at[pl.ds(0, 7)]).wait_recv()
    row = lax.broadcasted_iota(jnp.int32, (512, 1), 0)
    row_token = (row & 255) + 256 * y

    def core_copy(t, a):
        name = ("core_sum_k", "core_sum_v")[t]
        return remote(name, dkv.at[t, a, :, 1 - c], core_slots.at[t, a], a, d, over_core)

    def y_copy(t, a):
        return remote(("y_sum_k", "y_sum_v")[t], y_stage.at[t, a], y_slots.at[t, a], a, d, over_y)

    def x_copy(t, to):
        name = ("x_out_k", "x_out_v")[t]
        return remote(name, x_stage.at[t, to], x_slots.at[t, x], 0, d, beside(to))

    def dq_copy(a, e):
        return remote("dq", dq_stage.at[a, :, e], dq_slots.at[rank], 0, d, 4 * a + 2 * y + e)

    def send_y(t, a):
        core_copy(t, a).wait_recv()
        y_stage[t, a] = dkv[t, a, 1 - y, c] + core_slots[t, a, 1 - y]
        y_copy(t, a).start()

    def send_x(t, a):
        y_copy(t, a).wait_recv()
        total = dkv[t, a, y, c] + core_slots[t, a, y] + y_slots[t, a]
        if t == 1:
            total = total + last_term(a)
        x_stage[t, a] = total.astype(bf16)

        @pl.when(a != x)
        def _():
            x_copy(t, a).start()

        @pl.when(a == x)
        def _():
            x_slots[t, x] = x_stage[t, a]

    def make_grad(a):
        spot = row_token + 512 * a
        extra = jnp.where(row < 256, tail_in[0:1], tail_in[2:3])
        last = jnp.where(spot == length - 1, 1.0, 0.0)
        grad = grad_h[a].reshape(512, 128).astype(f32) + last * extra
        grad_low[a] = jnp.where(spot < length, grad, 0.0).astype(bf16)

    def turned_block(block):
        return jnp.transpose(block.reshape(512, 128).astype(f32))

    def turn_block(b):
        k_turn[b] = turned_block(kv_h[0, b]).astype(bf16)
        v_turn[b] = turned_block(kv_h[1, b]).astype(bf16)

    loop(0, 4, turn_block)

    last_lane = lax.broadcasted_iota(jnp.int32, (512, 128), 1)

    def first_grad(a):
        spot = row_token + 512 * a
        early = jnp.where(spot < length - 1, grad_h[a].reshape(512, 128).astype(f32), 0.0)
        grad_cat[a, :, :128] = early.astype(bf16)
        last = jnp.where(spot == length - 1, 1.0, 0.0)
        grad_cat[a, :, 128:] = jnp.where(last_lane == row >> 8, last, 0.0).astype(bf16)

    loop(0, 4, first_grad)
    attn[...] = jnp.zeros_like(attn)

    def value_block(o):
        b = 3 - o

        def rows(a):
            spot = spot_of(a, b)
            low_b = jnp.concatenate(
                [
                    (scores[spot, i * 128 : i * 128 + 128] * factors[a, b, i : i + 1]).astype(bf16)
                    for i in range(4)
                ],
                axis=0,
            )
            dkv[1, b] += mm(low_b, grad_cat[a, :, :128]).reshape(2, 2, 128, 128)
            attn[a] += mm(v_turn[b], low_b)

        loop(b, 4, rows)
        core_copy(1, b).start()
        pl.when(o >= 1)(lambda: send_y(1, b + 1))

    loop(0, 4, value_block)
    core_send.wait_recv()
    both = q_terms[p_rows(8 * c, 8), :] + core_in[...]
    q_mid[...] = both.reshape(4, 128, 128)

    def term_x(p):
        return remote("term_x", q_mid.at[p], q_in.at[x], 0, d, beside(p))

    others(lambda p: term_x(p).start(), x, 4)
    q_in[x] = q_mid[x]

    send_y(1, 0)

    bulk("tail_part", tail_slots.at[pl.ds(0, count - 1)]).wait_recv()
    tails = slot_sum(tail_slots)
    loss_out[...] = tails[4:5] / (pairs * count)
    tail_in[...] = tails

    last_query, last_grad = jnp.zeros((128, 128), f32), jnp.zeros((128, 128), f32)
    row_lane = lax.broadcasted_iota(jnp.int32, (1, 512), 1)
    peaks, parts_of = [0.0, 0.0], [0.0, 0.0]
    for a in range(4):
        last_query = last_query + mm_tn(grad_cat[a, :, 128:], q_h[a].reshape(512, 128))
        last_grad = last_grad + mm_tn(grad_cat[a, :, 128:], grad_h[a].reshape(512, 128))
        found = (row_lane & 255) + 256 * y + 512 * a == length - 1
        for h in range(2):
            mine_too = found & (row_lane >> 8 == h)
            for held, line_of in ((peaks, 0), (parts_of, 1)):
                value = jnp.where(mine_too, stats[a, line_of : line_of + 1], 0.0)
                held[h] = held[h] + jnp.sum(value, axis=1, keepdims=True)
    last_send[0:2] = last_query[0:2]
    for h in range(2):
        low = (last_grad[h : h + 1] + tails[2 * h : 2 * h + 1]).astype(bf16)
        last_send[2 + h : 3 + h] = low.astype(f32)
        last_send[4 + h : 5 + h] = jnp.broadcast_to(peaks[h], (1, 128))
        last_send[6 + h : 7 + h] = jnp.broadcast_to(parts_of[h], (1, 128))
    here = 2 * y + c

    def last_copy(p):
        return remote("last", last_send, last_in.at[here], 0, d, 4 * x + p)

    others(lambda p: last_copy(p).start(), here, 4)
    last_in[here] = last_send[...]

    def last_arrive():
        bulk("last", last_in.at[pl.ds(0, 3)]).wait_recv()
        for p in range(4):
            for kind in range(4):
                last_rows[kind, 2 * p : 2 * p + 2] = last_in[p, 2 * kind : 2 * kind + 2]

    def last_term(a):
        keys_a = kv_h[0, a, y, c]
        s = mm_nt(last_rows[0].astype(bf16), keys_a) * (scaling * math.log2(math.e))
        key = 512 * a + 256 * y + 128 * c + lax.broadcasted_iota(jnp.int32, (8, 128), 1)
        s = jnp.where(key < length, s, lowest)
        low = (jnp.exp2(s - last_rows[2]) * last_rows[3]).astype(bf16)
        return mm_tn(low, last_rows[1].astype(bf16))

    def all_grad(a):
        make_grad(a)
        grad_turn[a] = turned_block(grad_low[a])

    loop(0, 4, all_grad)

    def quarter(o):
        a = 3 - o
        q = q_h[a].reshape(512, 128)
        row_dot = jnp.sum(grad_turn[a] * attn[a], axis=0, keepdims=True)
        dq_acc[...] = jnp.zeros_like(dq_acc)

        def keys_of(b):
            spot = spot_of(a, b)
            values_b = kv_h[1, b].reshape(4, 128, 128)
            parts = []
            for i in range(4):
                prob_grad = mm_nt(values_b[i], grad_low[a])
                probs = scores[spot, i * 128 : i * 128 + 128] * (factors[a, b, i : i + 1] * scaling)
                parts.append((probs * (prob_grad - row_dot)).astype(bf16))
            sg = jnp.concatenate(parts, axis=0)
            dkv[0, b] += mm(sg, q).reshape(2, 2, 128, 128)
            dq_acc[...] += mm(k_turn[b], sg)

        loop(0, a + 1, keys_of)
        core_copy(0, a).start()
        dq_stage[a] = jnp.transpose(dq_acc[...]).astype(bf16).reshape(2, 2, 128, 128)
        for e in range(2):

            @pl.when(2 * a + e != rank)
            def _():
                dq_copy(a, e).start()

            @pl.when(2 * a + e == rank)
            def _():
                dq_slots[rank] = dq_stage[a, :, e]

        pl.when(o >= 1)(lambda: send_y(0, a + 1))
        pl.when(o == 0)(last_arrive)
        send_x(1, a)
        pl.when(o >= 2)(lambda: send_x(0, a + 2))

    loop(0, 4, quarter)
    send_y(0, 0)
    bulk("term_x", q_in.at[pl.ds(0, 3)]).wait_recv()
    q_last[...] = (q_in[0] + q_in[1] + q_in[2] + q_in[3]).reshape(2, 64, 128)
    term_y = remote("term_y", q_last.at[1 - y], q_end, 0, d, over_y)
    term_y.start()
    send_x(0, 1)

    bulk("dq", dq_slots.at[pl.ds(0, 7)]).wait_recv()

    def gain_fold(block):
        return jnp.sum(block.reshape(16, 8, 128), axis=0)

    def query_head(h, total):
        grad = dq_slots[h // 2, h % 2].astype(f32)
        dx, part = normed_rope_back(
            queries[:, lanes(h)].astype(f32), q_gain[...], cosine[...], sine[...], grad
        )
        q_cot[:, lanes(h)] = dx.astype(bf16)
        return total + gain_fold(part)

    q_total = lax.fori_loop(0, 16, query_head, jnp.zeros((8, 128), f32), unroll=4)
    send_x(0, 0)
    term_y.wait_recv()
    bulk("d_out", d_in.at[pl.ds(0, 8 * (count - 1)), :]).wait_recv()
    q_f32[pl.ds(0, 2 * chunks), :] = q_last[y] + q_end[...]
    for i in range(chunks):
        part = pl.ds(i * 128, 128)
        q_grad_out[:, part] = q_f32[pl.ds(i, 2, stride=chunks), :].astype(bf16)
        d_row = 8 * (i // 2) + i % 2
        d_grad_out[:, part] = d_in[pl.ds(d_row, 2, stride=2), :].astype(bf16)
    bulk("x_out_v", x_slots.at[1, pl.ds(0, 3)]).wait_recv()
    bulk("x_out_k", x_slots.at[0, pl.ds(0, 3)]).wait_recv()

    def key_head(g, total):
        v_cot[:, lanes(g)] = x_slots[1, g]
        dx, part = normed_rope_back(
            keys[:, lanes(g)].astype(f32), k_gain[...], cosine[...], sine[...],
            x_slots[0, g].astype(f32),
        )
        k_cot[:, lanes(g)] = dx.astype(bf16)
        return total + gain_fold(part)

    k_total = lax.fori_loop(0, 4, key_head, jnp.zeros((8, 128), f32), unroll=True)
    seq_slots[j, pl.ds(0, 4)] = q_total[:4] + q_total[4:]
    seq_slots[j, pl.ds(4, 4)] = k_total[:4] + k_total[4:]

    def gain_seq(p):
        return remote("gain_seq", seq_slots.at[j], seq_slots.at[j], 0, d, p)

    others(lambda p: gain_seq(p).start(), j)
    bulk("gain_seq", seq_slots.at[pl.ds(0, count - 1)]).wait_recv()
    dp_slots[d] = slot_sum(seq_slots)

    def gain_dp(p):
        return remote("gain_dp", dp_slots.at[d], dp_slots.at[d], 0, p, j)

    others(lambda p: gain_dp(p).start(), d)
    bulk("gain_dp", dp_slots.at[pl.ds(0, count - 1)]).wait_recv()
    gains = slot_sum(dp_slots)
    gains_out[0:1, :] = jnp.sum(gains[:4], axis=0, keepdims=True)
    gains_out[1:2, :] = jnp.sum(gains[4:], axis=0, keepdims=True)

    for name, ref in (
        ("q_msg", q_all.at[q_rows(0, count - 1), :]),
        ("p_msg", p_all.at[p_rows(0, count - 1), :]),
        ("tile", tiles.at[pl.ds(0, count - 1)]),
        ("part", q_part.at[pl.ds(0, count - 1), pl.ds(0, 16)]),
        ("span", spans.at[pl.ds(0, count - 1)]),
        ("tail_part", tail_slots.at[pl.ds(0, count - 1)]),
        ("d_out", d_in.at[pl.ds(0, 8 * (count - 1)), :]),
        ("term_x", q_in.at[pl.ds(0, 3)]),
        ("gain_seq", seq_slots.at[pl.ds(0, count - 1)]),
        ("gain_dp", dp_slots.at[pl.ds(0, count - 1)]),
        ("k_x", kv_stage.at[pl.ds(0, 3), 0]),
        ("v_x", kv_stage.at[pl.ds(0, 3), 1]),
        ("k_y", kv_h.at[0, :, 0, 0]),
        ("v_y", kv_h.at[1, :, 0, 0]),
        ("k_core", kv_h.at[0, :, 0, 0]),
        ("v_core", kv_h.at[1, :, 0, 0]),
        ("k_both", kv_h.at[0, :, 0, 0]),
        ("v_both", kv_h.at[1, :, 0, 0]),
        ("q", q_stage.at[pl.ds(0, 7)]),
        ("grad", grad_stage.at[pl.ds(0, 7)]),
        ("dq", dq_slots.at[pl.ds(0, 7)]),
        ("core_sum_k", core_slots.at[0]),
        ("core_sum_v", core_slots.at[1]),
        ("y_sum_k", y_stage.at[0]),
        ("y_sum_v", y_stage.at[1]),
        ("x_out_k", x_slots.at[0, pl.ds(0, 3)]),
        ("x_out_v", x_slots.at[1, pl.ds(0, 3)]),
        ("last", last_in.at[pl.ds(0, 3)]),
    ):
        bulk(name, ref).wait_send()
    core_send.wait_send()
    term_y.wait_send()
    part_core.wait_send()
    w_targets(lambda copy: copy.wait_send())


def finish(loss, gains, *refs):
    size = (len(refs) - 3) // 2
    loss_out, q_out, k_out = refs[size : size + 3]
    loss_out[...] = loss[0:1, 0:1]
    q_out[...] = gains[0:1, :]
    k_out[...] = gains[1:2, :]
    for made, out in zip(refs[:size], refs[size + 3 :]):
        out[...] = made[...]


def shards(
    question_embedding_matrix,
    passage_embedding_matrix,
    positive,
    queries,
    keys,
    values,
    later_grad,
    lengths,
    q_gain,
    k_gain,
    out_weight,
):
    angles = np.arange(2048)[:, None] * rope_base ** (-2.0 * np.arange(64) / 128)[None, :]
    table = jnp.asarray(np.concatenate([np.cos(angles), np.sin(angles)], axis=1).astype(np.float32))
    out = jax.ShapeDtypeStruct
    vm = pltpu.VMEM
    smem = pl.BlockSpec(memory_space=pltpu.SMEM)
    anywhere = pl.BlockSpec(memory_space=pl.ANY)
    results = [
        out(question_embedding_matrix.shape, bf16),
        out(passage_embedding_matrix.shape, bf16),
        out(queries.shape[1:], bf16),
        out(keys.shape[1:], bf16),
        out(values.shape[1:], bf16),
    ]
    loss, gains, *made = pl.pallas_call(
        whole,
        out_shape=[out((1, 128), f32), out((2, 128), f32)] + results,
        in_specs=[smem, smem, anywhere] + [VMEM] * 9,
        out_specs=[VMEM] * 7,
        scratch_shapes=[
            vm((128, 128), f32),
            vm((128, 128), f32),
            vm((128, 128), f32),
            vm((2 * q_stride, 128), f32),
            vm((2 * chunks, 128), f32),
            vm((2 * q_stride * count, 128), bf16),
            vm((2 * chunks * count, 128), bf16),
            vm((2 * q_stride * count, 128), f32),
            vm((2 * chunks * count, 128), f32),
            vm((count, pairs, 256), bf16),
            vm((count, pairs, 256), bf16),
            vm((count, 8, 128), f32),
            vm((count, pairs, 256), bf16),
            vm((count, 16, 128), f32),
            vm((count, pairs, 256), bf16),
            vm((pairs * chunks, 128), f32),
            vm((pairs * chunks // 2, 128), f32),
            vm((4, 128, 128), f32),
            vm((4, 128, 128), f32),
            vm((2, 64, 128), f32),
            vm((64, 128), f32),
            vm((2 * pairs, 128), f32),
            vm((8 * count, 128), f32),
            vm((8 * count, 128), f32),
            vm((count, 8, 128), f32),
            vm((count, 8, 128), f32),
            vm((8, 128), f32),
            vm((2, 128, 256), bf16),
            vm((4, 2, 128, 128), bf16),
            vm((8, 2, 128, 128), bf16),
            vm((8, 2, 128, 128), bf16),
            vm((2, 4, 2, 2, 128, 128), bf16),
            vm((4, 2, 2, 128, 128), bf16),
            vm((4, 2, 2, 128, 128), bf16),
            vm((4, 512, 128), bf16),
            vm((4, 128, 512), f32),
            vm((4, 512, 256), bf16),
            vm((4, 8, 512), f32),
            vm((8, 128), f32),
            vm((4, 8, 128), f32),
            vm((4, 8, 128), f32),
            vm((10, 512, 512), f32),
            vm((4, 4, 8, 512), f32),
            vm((4, 4, 8, 512), f32),
            vm((4, 4, 8, 512), f32),
            vm((4, 128, 512), f32),
            vm((4, 128, 512), bf16),
            vm((4, 128, 512), bf16),
            vm((128, 512), f32),
            vm((2, 4, 2, 2, 128, 128), f32),
            vm((4, 2, 2, 128, 128), bf16),
            vm((8, 2, 128, 128), bf16),
            vm((2, 4, 2, 128, 128), f32),
            vm((2, 4, 128, 128), f32),
            vm((2, 4, 128, 128), f32),
            vm((2, 4, 128, 128), bf16),
            vm((2, 4, 128, 128), bf16),
            vm((count, 8, 128), f32),
            vm((count, 8, 128), f32),
            pltpu.SemaphoreType.DMA((len(phases),)),
            pltpu.SemaphoreType.DMA((len(phases), 4)),
            pltpu.SemaphoreType.DMA((1,)),
        ],
        compiler_params=pltpu.CompilerParams(
            collective_id=0, has_side_effects=True, vmem_limit_bytes=limit
        ),
    )(
        lengths, positive, table, queries[0], keys[0], values[0], later_grad[0],
        question_embedding_matrix, passage_embedding_matrix, out_weight,
        q_gain[None, :], k_gain[None, :],
    )
    loss, q_gain_grad, k_gain_grad, query_grad, doc_grad, query_cot, key_cot, value_cot = (
        pl.pallas_call(
            finish,
            out_shape=[out((1, 1), f32), out((1, 128), f32), out((1, 128), f32)] + results,
            in_specs=[VMEM] * 7,
            out_specs=[VMEM] * 8,
        )(loss, gains, *made)
    )
    return (
        loss.reshape(()),
        query_grad,
        doc_grad,
        query_cot[None],
        key_cot[None],
        value_cot[None],
        q_gain_grad[0],
        k_gain_grad[0],
    )


def solution(mesh):
    in_specs = (
        P(("dp", "seq"), None),
        P(("dp", "seq"), None),
        P(("dp", "seq")),
        P("dp", "seq", None),
        P("dp", "seq", None),
        P("dp", "seq", None),
        P("dp", "seq", None),
        P("dp"),
        P(),
        P(),
        P("seq", "dp"),
    )
    out_specs = (
        P(),
        P(("dp", "seq"), None),
        P(("dp", "seq"), None),
        P("dp", "seq", None),
        P("dp", "seq", None),
        P("dp", "seq", None),
        P(),
        P(),
    )
    return jax.shard_map(
        shards, mesh=mesh, in_specs=in_specs, out_specs=out_specs, check_vma=False
    )
```

```python
import functools
import math

import jax
import jax.numpy as jnp
import numpy as np
from jax import lax
from jax.experimental import pallas as pl
from jax.experimental.pallas import tpu as pltpu
from jax.sharding import PartitionSpec as P

sharpness = 0.05
epsilon = 1e-06
rope_base = 1000000.0
lowest = -1e30
MESH = pl.DeviceIdType.MESH
f32 = jnp.float32
bf16 = jnp.bfloat16
VMEM = pl.BlockSpec(memory_space=pltpu.VMEM)
limit = 58 * 1024 * 1024
count = 16
pairs = 32
chunks = 32
q_stride = 40
scaling = 128 ** (-0.5)
phases = (
    "q_msg", "p_msg", "tile", "part", "part_core", "span", "tail_part", "w_out",
    "d_out", "term_core", "term_x", "term_y", "gain_seq", "gain_dp",
    "k_x", "k_y", "k_core", "k_both", "v_x", "v_y", "v_core", "v_both", "q", "grad", "dq", "core_sum_k", "core_sum_v", "y_sum_k", "y_sum_v",
    "x_out_k", "x_out_v",
)
phase_of = {name: i for i, name in enumerate(phases)}


def mm(a, b):
    return lax.dot_general(a, b, (((1,), (0,)), ((), ())), preferred_element_type=f32)


def mm_nt(a, b):
    return lax.dot_general(a, b, (((1,), (1,)), ((), ())), preferred_element_type=f32)


def mm_tn(a, b):
    return lax.dot_general(a, b, (((0,), (0,)), ((), ())), preferred_element_type=f32)


def loop(first, last, step, unroll=None):
    def body(i, carry):
        step(i)
        return carry

    lax.fori_loop(first, last, body, 0, unroll=unroll)


def swap_halves(x):
    return pltpu.roll(x, 64, 1)


def normed_rope(x, gain, cosine, sine):
    scale = lax.rsqrt(jnp.mean(x * x, axis=-1, keepdims=True) + epsilon)
    y = x * scale * gain
    return y * cosine + swap_halves(y) * sine


def normed_rope_back(x, gain, cosine, sine, grad):
    scale = lax.rsqrt(jnp.mean(x * x, axis=-1, keepdims=True) + epsilon)
    n = x * scale
    dy = grad * cosine - swap_halves(grad) * sine
    gain_part = dy * n
    dn = dy * gain
    dx = scale * (dn - n * jnp.mean(dn * n, axis=-1, keepdims=True))
    return dx, gain_part


def slot_sum(ref):
    total = ref[0]
    for i in range(1, count):
        total = total + ref[i]
    return total


def whole(
    lengths, positive_in, table, queries, keys, values, later, q_emb, p_emb, out_w, q_gain, k_gain,
    loss_out, gains_out, q_grad_out, d_grad_out, q_cot, k_cot, v_cot,
    turn, cosine, sine,
    q_f32, p_f32, q_all, p_all, q_wide, p_wide, q_cols, p_cols, tiles,
    q_part, spans, span_cat, q_terms, core_in, q_mid, q_in, q_last, q_end,
    d_sum, d_stage, d_in, tail_stage, tail_slots, tail_in, w_in,
    kv_stage, q_stage, grad_stage, kv_h, q_h, grad_h,
    grad_low, grad_turn, grad_cat, last_probs, scores, tops, sums, factors, attn, k_turn, v_turn, dq_acc, dkv, dq_stage, dq_slots,
    core_slots, y_stage, y_slots, x_stage, x_slots, seq_slots, dp_slots,
    send_sem, recv_sem, own_sem,
):
    d, j = lax.axis_index("dp"), lax.axis_index("seq")
    x, y, c = j // 4, (j // 2) % 2, j % 2
    z, low = d // 2, d % 2
    rank = 2 * x + c
    barrier = pltpu.get_barrier_semaphore()

    def remote(name, src, dst, slot, dp, seq):
        phase = phase_of[name]
        return pltpu.make_async_remote_copy(
            src_ref=src,
            dst_ref=dst,
            send_sem=send_sem.at[phase],
            recv_sem=recv_sem.at[phase, slot],
            device_id=(dp, seq),
            device_id_type=MESH,
        )

    def bulk(name, ref):
        return remote(name, ref, ref, 0, d, j)

    def others(step, me, size=count):
        for o in sorted(range(1, size), key=lambda o: abs(o - size // 2)):
            step(lax.rem(me + o, size))

    others(
        lambda p: pl.semaphore_signal(barrier, inc=1, device_id=(d, p), device_id_type=MESH), j
    )
    others(
        lambda p: pl.semaphore_signal(barrier, inc=1, device_id=(p, j), device_id_type=MESH), d
    )
    turn_copy = pltpu.make_async_copy(
        table.at[pl.ds(pl.multiple_of(j * 128, 128), 128)], turn, own_sem.at[0]
    )
    turn_copy.start()

    def lanes(h):
        return pl.ds(pl.multiple_of(h * 128, 128), 128)

    def q_rows(s, size=1):
        return pl.ds(pl.multiple_of(s * 2 * q_stride, 16), size * 2 * q_stride)

    def p_rows(s, size=1):
        return pl.ds(pl.multiple_of(s * 2 * chunks, 16), size * 2 * chunks)

    place = 8 * c + 2 * x + y
    q_f32[...] = jnp.zeros_like(q_f32)
    q_own, p_own = q_emb[...].astype(f32), p_emb[...].astype(f32)
    for i in range(chunks):
        q_f32[pl.ds(i, 2, stride=q_stride), :] = q_own[:, i * 128 : i * 128 + 128]
        p_f32[pl.ds(i, 2, stride=chunks), :] = p_own[:, i * 128 : i * 128 + 128]
    for i in range(2):
        index = positive_in[i]
        spot = i * q_stride + chunks
        q_f32[spot : spot + 1, :] = jnp.full((1, 128), index >> 1, jnp.int32).astype(f32)
        q_f32[spot + 1 : spot + 2, :] = jnp.full((1, 128), index & 1, jnp.int32).astype(f32)
    q_all[q_rows(place), :] = q_f32[...].astype(bf16)
    p_all[p_rows(d), :] = p_f32[...].astype(bf16)
    turn_copy.wait()
    first_half = lax.broadcasted_iota(jnp.int32, (128, 128), 1) < 64
    turned = swap_halves(turn[...])
    cosine[...] = jnp.where(first_half, turn[...], turned)
    sine[...] = jnp.where(first_half, -turned, turn[...])

    def stage_kv(g):
        rot = normed_rope(keys[:, lanes(g)].astype(f32), k_gain[...], cosine[...], sine[...])
        kv_stage[g, 0] = rot.astype(bf16)
        kv_stage[g, 1] = values[:, lanes(g)]

    loop(0, 4, stage_kv, unroll=True)
    pl.semaphore_wait(barrier, 2 * (count - 1))

    over_y = 4 * x + 2 * (1 - y) + c
    over_core = 4 * x + 2 * y + (1 - c)
    over_low = d + 1 - 2 * low

    def beside(p):
        return 4 * p + 2 * y + c

    def q_copy(p):
        rows = q_all.at[q_rows(place), :]
        return remote("q_msg", rows, rows, 0, d, p)

    def p_copy(p):
        rows = p_all.at[p_rows(d), :]
        return remote("p_msg", rows, rows, 0, p, j)

    others(lambda p: q_copy(p).start(), j)
    others(lambda p: p_copy(p).start(), d)

    def x_copies(t, step):
        def copy(to):
            name, src = ("k_x", "v_x")[t], kv_stage.at[to, t]
            step(remote(name, src, kv_h.at[t, x, y, c], 0, d, beside(to)))

        others(copy, x, 4)

    def kv_pass(t, way, of_y, of_core, seq):
        block = kv_h.at[t, :, of_y, of_core]
        return remote("kv"[t] + way, block, block, 0, d, seq)

    def pass_on(t):
        bulk(("k_x", "v_x")[t], kv_h.at[t, pl.ds(0, 3), y, c]).wait_recv()
        kv_pass(t, "_y", y, c, over_y).start()
        kv_pass(t, "_core", y, c, over_core).start()

    def pass_from_y(t):
        kv_pass(t, "_y", 1 - y, c, over_y).wait_recv()
        kv_pass(t, "_both", 1 - y, c, over_core).start()

    def kv_arrive(t):
        kv_pass(t, "_core", y, 1 - c, over_core).wait_recv()
        kv_pass(t, "_both", 1 - y, 1 - c, over_core).wait_recv()

    x_copies(0, lambda copy: copy.start())
    kv_h[:, x, y, c] = kv_stage[x]

    def stage_q(h):
        rot = normed_rope(queries[:, lanes(h)].astype(f32), q_gain[...], cosine[...], sine[...])
        q_stage[h // 2, h % 2] = rot.astype(bf16)

    def seat(r):
        return 4 * (r // 2) + 2 * y + r % 2

    def head_send(name, stage, held):
        others(
            lambda p: remote(
                name, stage.at[p], held.at[x, :, c], 0, d, seat(p)
            ).start(),
            rank,
            8,
        )
        held[x, :, c] = stage[rank]

    loop(0, 16, stage_q, unroll=4)

    def w_copy(slot, seq):
        return remote("w_out", out_w, w_in.at[slot], slot, d, seq)

    def w_targets(step):
        for b in range(2):
            to = 4 * x + 2 * b + y
            pl.when(to != j)(lambda to=to: step(w_copy(j % 2, to)))

    w_targets(lambda copy: copy.start())

    @pl.when(c == y)
    def _():
        w_in[j % 2] = out_w[...]

    pass_on(0)
    head_send("q", q_stage, q_h)

    def stage_grad(h):
        grad_stage[h // 2, h % 2] = later[:, lanes(h)]

    loop(0, 16, stage_grad, unroll=4)
    dkv[...] = jnp.zeros_like(dkv)

    bulk("q_msg", q_all.at[q_rows(0, count - 1), :]).wait_recv()
    bulk("p_msg", p_all.at[p_rows(0, count - 1), :]).wait_recv()
    q_wide[...] = q_all[...].astype(f32)
    p_wide[...] = p_all[...].astype(f32)
    for i in range(chunks):
        half = pl.ds((i % 2) * 128, 128)
        q_cols[i // 2, :, half] = q_wide[pl.ds(i, pairs, stride=q_stride), :].astype(bf16)
        p_cols[i // 2, :, half] = p_wide[pl.ds(i, pairs, stride=chunks), :].astype(bf16)
    positive = (
        2.0 * q_wide[pl.ds(chunks, pairs, stride=q_stride), :]
        + q_wide[pl.ds(chunks + 1, pairs, stride=q_stride), :]
    )

    def four(block):
        return jnp.concatenate([block] * (128 // pairs), axis=0)

    def one(block):
        return block[:32] + block[32:64] + block[64:96] + block[96:]

    logits = mm_nt(q_cols[0], four(p_cols[0]))
    for b in range(1, count):
        logits = logits + mm_nt(q_cols[b], four(p_cols[b]))
    logits = logits / sharpness
    quarter_of = lax.broadcasted_iota(jnp.int32, (8, 128), 1) >> 5

    def pack(block):
        packed = block[:8]
        for i in range(1, 4):
            packed = jnp.where(quarter_of == i, block[8 * i : 8 * i + 8], packed)
        return packed

    tiles[j] = pack(logits)

    def tile_copy(p):
        return remote("tile", tiles.at[j], tiles.at[j], 0, d, p)

    others(lambda p: tile_copy(p).start(), j)
    def half_of(core):
        return pl.ds(pl.multiple_of(16 * core, 16), 16)

    def part_copy(p):
        return remote(
            "part", q_cols.at[p, half_of(c)], q_part.at[d, half_of(c)], 0, p, j
        )

    others(lambda p: part_copy(p).start(), d)
    q_part[d, half_of(c)] = q_cols[d, half_of(c)]
    lane = lax.broadcasted_iota(jnp.int32, (pairs, 128), 1)
    line = lax.broadcasted_iota(jnp.int32, (pairs, 128), 0)
    real = (lane >> 5) == (line >> 3)
    base = jnp.where(real, ((lane & 31) >> 1) * pairs + (lane & 1), -(1 << 20)).astype(f32)

    pass_from_y(0)

    bulk("tile", tiles.at[pl.ds(0, count - 1)]).wait_recv()
    high = tiles[0]
    for i in range(1, count):
        high = jnp.maximum(high, tiles[i])
    high = jnp.max(jnp.where(real, four(high), lowest), axis=1, keepdims=True)
    mass = jnp.zeros((pairs, 128), f32)
    hit = jnp.zeros((pairs, 128), f32)
    for i in range(count):
        tile = four(tiles[i])
        mass = mass + jnp.where(real, jnp.exp(tile - high), 0.0)
        hit = hit + jnp.where(base + 2.0 * i == positive, tile, 0.0)
    log_total = high + jnp.log(jnp.sum(mass, axis=1, keepdims=True))
    picked = jnp.sum(hit, axis=1, keepdims=True)
    loss_part = jnp.sum(log_total - picked, axis=0, keepdims=True)

    def weights_of(tile, index):
        onehot = jnp.where(base + 2.0 * index == positive, 1.0, 0.0)
        return jnp.where(real, (jnp.exp(four(tile) - log_total) - onehot) / sharpness, 0.0)

    mine = weights_of(tiles[j], j.astype(f32)).astype(bf16)
    spans[d, pl.ds(0, 8)] = pack(weights_of(tiles[0], 0.0).astype(bf16).astype(f32))
    spans[d, pl.ds(8, 8)] = pack(mine.astype(f32))

    def span_copy(p):
        return remote("span", spans.at[d], spans.at[d], 0, p, j)

    others(lambda p: span_copy(p).start(), d)
    x_copies(1, lambda copy: copy.start())
    head_send("grad", grad_stage, grad_h)
    kv_arrive(0)
    bulk("q", q_stage.at[pl.ds(0, 7)]).wait_recv()
    length = lengths[0]
    key_line = lax.broadcasted_iota(jnp.int32, (128, 1), 0)
    ahead = lax.broadcasted_iota(jnp.int32, (128, 256), 0) - lax.broadcasted_iota(
        jnp.int32, (128, 256), 1
    )
    tops[...] = jnp.full_like(tops, lowest)
    sums[...] = jnp.zeros_like(sums)

    def spot_of(a, b):
        return (a * (a + 1)) // 2 + b

    def softmax_rows(o):
        a = 3 - o

        def strips(b, diagonal):
            keys_b = kv_h[0, b].reshape(4, 128, 128)
            for half in range(2):
                q = q_h[a, half].reshape(256, 128)
                across = slice(half * 256, half * 256 + 256)
                for i in range(4):
                    start = b * 512 + i * 128
                    bias = jnp.where(key_line < length - start, 0.0, lowest)
                    s = mm_nt(keys_b[i], q) * (scaling * math.log2(math.e)) + bias
                    if diagonal:
                        s = jnp.where(ahead <= 256 * y - i * 128, s, lowest)
                    top = jnp.max(s, axis=0, keepdims=True)
                    e = jnp.exp2(s - top)
                    scores[spot_of(a, b), i * 128 : i * 128 + 128, across] = e
                    tops[a, b, i : i + 1, across] = top
                    sums[a, b, i : i + 1, across] = jnp.sum(e, axis=0, keepdims=True)

        loop(0, a, lambda b: strips(b, False))
        strips(a, True)
        part_tops = tops[a].reshape(32, 512)
        part = jnp.exp2(part_tops - jnp.max(part_tops, axis=0, keepdims=True))
        total = jnp.sum(part * sums[a].reshape(32, 512), axis=0, keepdims=True)
        factors[a] = (part * (1.0 / total)).reshape(4, 8, 512)

    softmax_rows(0)
    bulk("part", q_part.at[pl.ds(0, count - 1), pl.ds(0, 16)]).wait_recv()
    part_core = remote(
        "part_core", q_part.at[:, half_of(c)], q_part.at[:, half_of(c)], 0, d, over_core
    )
    part_core.start()
    pass_on(1)
    softmax_rows(1)

    bulk("span", spans.at[pl.ds(0, count - 1)]).wait_recv()
    for i in range(count):
        for t in range(2):
            weights = jnp.where(real, four(spans[i, t * 8 : t * 8 + 8]), 0.0)
            span_cat[i, :, t * 128 : t * 128 + 128] = weights.astype(bf16)
    remote(
        "part_core", q_part.at[:, half_of(1 - c)], q_part.at[:, half_of(1 - c)], 0, d, over_core
    ).wait_recv()
    span_sums = mm_tn(
        span_cat[...].reshape(pairs * count, 256), q_part[...].reshape(pairs * count, 256)
    )
    span = one(span_sums[:128]).astype(bf16)
    d_sums = one(span_sums[128:])
    d_sum[pl.ds(0, pairs), :] = d_sums[:, :128]
    d_sum[pl.ds(pairs, pairs), :] = d_sums[:, 128:]
    for b in range(2):
        source = 4 * x + 2 * c + b
        pl.when(source != j)(lambda b=b, source=source: w_copy(b, source).wait_recv())
    rows_a, rows_b = mm_nt(span, w_in[0]), mm_nt(span, w_in[1])
    for i in range(count):
        tail_stage[i, pl.ds(0, 2)] = jnp.broadcast_to(rows_a[2 * i : 2 * i + 1], (2, 128))
        tail_stage[i, pl.ds(2, 2)] = jnp.broadcast_to(rows_b[2 * i : 2 * i + 1], (2, 128))
        tail_stage[i, pl.ds(4, 4)] = jnp.broadcast_to(loss_part, (4, 128))

    def tail_part(p):
        return remote("tail_part", tail_stage.at[p], tail_slots.at[d], 0, p, j)

    others(lambda p: tail_part(p).start(), d)
    tail_slots[d] = tail_stage[d]

    pass_from_y(1)
    loop(2, 4, softmax_rows)

    d_stage[...] = jnp.zeros_like(d_stage)
    for r in range(2):
        for half in range(2):
            d_stage[pl.ds(2 * r + half, count, stride=8), :] = d_sum[
                pl.ds(half * pairs + r, count, stride=2), :
            ]

    def d_rows(s):
        return pl.ds(pl.multiple_of(s * 8, 8), 8)

    def d_copy(p):
        return remote("d_out", d_stage.at[d_rows(p), :], d_in.at[d_rows(d), :], 0, p, j)

    others(lambda p: d_copy(p).start(), d)
    d_in[d_rows(d), :] = d_stage[d_rows(d), :]

    for b in range(count):
        q_term = mm(mine, four(p_cols[b]))
        for half in range(2):
            rows = pl.ds(2 * b + half, pairs, stride=chunks)
            q_terms[rows, :] = q_term[:, half * 128 : half * 128 + 128]
    core_send = remote("term_core", q_terms.at[p_rows(8 * (1 - c), 8), :], core_in, 0, d, over_core)
    core_send.start()
    kv_arrive(1)
    bulk("grad", grad_stage.at[pl.ds(0, 7)]).wait_recv()
    row = lax.broadcasted_iota(jnp.int32, (512, 1), 0)
    row_token = (row & 255) + 256 * y

    def core_copy(t, a):
        name = ("core_sum_k", "core_sum_v")[t]
        return remote(name, dkv.at[t, a, :, 1 - c], core_slots.at[t, a], a, d, over_core)

    def y_copy(t, a):
        return remote(("y_sum_k", "y_sum_v")[t], y_stage.at[t, a], y_slots.at[t, a], a, d, over_y)

    def x_copy(t, to):
        name = ("x_out_k", "x_out_v")[t]
        return remote(name, x_stage.at[t, to], x_slots.at[t, x], 0, d, beside(to))

    def dq_copy(a, e):
        return remote("dq", dq_stage.at[a, :, e], dq_slots.at[rank], 0, d, 4 * a + 2 * y + e)

    def send_y(t, a):
        core_copy(t, a).wait_recv()
        y_stage[t, a] = dkv[t, a, 1 - y, c] + core_slots[t, a, 1 - y]
        y_copy(t, a).start()

    def send_x(t, a):
        y_copy(t, a).wait_recv()
        total = dkv[t, a, y, c] + core_slots[t, a, y] + y_slots[t, a]
        x_stage[t, a] = total.astype(bf16)

        @pl.when(a != x)
        def _():
            x_copy(t, a).start()

        @pl.when(a == x)
        def _():
            x_slots[t, x] = x_stage[t, a]

    def make_grad(a):
        spot = row_token + 512 * a
        extra = jnp.where(row < 256, tail_in[0:1], tail_in[2:3])
        last = jnp.where(spot == length - 1, 1.0, 0.0)
        grad = grad_h[a].reshape(512, 128).astype(f32) + last * extra
        grad_low[a] = jnp.where(spot < length, grad, 0.0).astype(bf16)

    def turned_block(block):
        return jnp.transpose(block.reshape(512, 128).astype(f32))

    def turn_block(b):
        k_turn[b] = turned_block(kv_h[0, b]).astype(bf16)
        v_turn[b] = turned_block(kv_h[1, b]).astype(bf16)

    loop(0, 4, turn_block)

    last_lane = lax.broadcasted_iota(jnp.int32, (512, 128), 1)

    def first_grad(a):
        spot = row_token + 512 * a
        early = jnp.where(spot < length - 1, grad_h[a].reshape(512, 128).astype(f32), 0.0)
        grad_cat[a, :, :128] = early.astype(bf16)
        last = jnp.where(spot == length - 1, 1.0, 0.0)
        grad_cat[a, :, 128:] = jnp.where(last_lane == row >> 8, last, 0.0).astype(bf16)

    loop(0, 4, first_grad)
    last_probs[...] = jnp.zeros_like(last_probs)
    attn[...] = jnp.zeros_like(attn)

    def value_block(o):
        b = 3 - o

        def rows(a):
            spot = spot_of(a, b)
            low_b = jnp.concatenate(
                [
                    (scores[spot, i * 128 : i * 128 + 128] * factors[a, b, i : i + 1]).astype(bf16)
                    for i in range(4)
                ],
                axis=0,
            )
            terms = mm(low_b, grad_cat[a])
            dkv[1, b] += terms[:, :128].reshape(2, 2, 128, 128)
            last_probs[b] += terms[:, 128:]
            attn[a] += mm(v_turn[b], low_b)

        loop(b, 4, rows)

    loop(0, 4, value_block)
    core_send.wait_recv()
    both = q_terms[p_rows(8 * c, 8), :] + core_in[...]
    q_mid[...] = both.reshape(4, 128, 128)

    def term_x(p):
        return remote("term_x", q_mid.at[p], q_in.at[x], 0, d, beside(p))

    others(lambda p: term_x(p).start(), x, 4)
    q_in[x] = q_mid[x]

    bulk("tail_part", tail_slots.at[pl.ds(0, count - 1)]).wait_recv()
    tails = slot_sum(tail_slots)
    loss_out[...] = tails[4:5] / (pairs * count)
    tail_in[...] = tails

    last_grad = jnp.zeros((128, 128), f32)
    for a in range(4):
        last_grad = last_grad + mm_tn(grad_cat[a, :, 128:], grad_h[a].reshape(512, 128))
    head_line = lax.broadcasted_iota(jnp.int32, (128, 128), 0)
    both_tails = jnp.where(head_line == 0, tails[0:1], jnp.where(head_line == 1, tails[2:3], 0.0))
    last_low = (last_grad + both_tails).astype(bf16)

    def last_row(o):
        b = 3 - o
        dkv[1, b] += mm(last_probs[b].astype(bf16), last_low).reshape(2, 2, 128, 128)
        core_copy(1, b).start()

    loop(0, 4, last_row)

    def all_grad(a):
        make_grad(a)
        grad_turn[a] = turned_block(grad_low[a])

    loop(0, 4, all_grad)
    loop(0, 4, lambda o: send_y(1, 3 - o))

    def quarter(o):
        a = 3 - o
        q = q_h[a].reshape(512, 128)
        row_dot = jnp.sum(grad_turn[a] * attn[a], axis=0, keepdims=True)
        dq_acc[...] = jnp.zeros_like(dq_acc)

        def keys_of(b):
            spot = spot_of(a, b)
            values_b = kv_h[1, b].reshape(4, 128, 128)
            parts = []
            for i in range(4):
                prob_grad = mm_nt(values_b[i], grad_low[a])
                probs = scores[spot, i * 128 : i * 128 + 128] * (factors[a, b, i : i + 1] * scaling)
                parts.append((probs * (prob_grad - row_dot)).astype(bf16))
            sg = jnp.concatenate(parts, axis=0)
            dkv[0, b] += mm(sg, q).reshape(2, 2, 128, 128)
            dq_acc[...] += mm(k_turn[b], sg)

        loop(0, a + 1, keys_of)
        core_copy(0, a).start()
        dq_stage[a] = jnp.transpose(dq_acc[...]).astype(bf16).reshape(2, 2, 128, 128)
        for e in range(2):

            @pl.when(2 * a + e != rank)
            def _():
                dq_copy(a, e).start()

            @pl.when(2 * a + e == rank)
            def _():
                dq_slots[rank] = dq_stage[a, :, e]

        pl.when(o >= 1)(lambda: send_y(0, a + 1))
        send_x(1, a)
        pl.when(o >= 2)(lambda: send_x(0, a + 2))

    loop(0, 4, quarter)
    send_y(0, 0)
    bulk("term_x", q_in.at[pl.ds(0, 3)]).wait_recv()
    q_last[...] = (q_in[0] + q_in[1] + q_in[2] + q_in[3]).reshape(2, 64, 128)
    term_y = remote("term_y", q_last.at[1 - y], q_end, 0, d, over_y)
    term_y.start()
    send_x(0, 1)

    bulk("dq", dq_slots.at[pl.ds(0, 7)]).wait_recv()

    def gain_fold(block):
        return jnp.sum(block.reshape(16, 8, 128), axis=0)

    def query_head(h, total):
        grad = dq_slots[h // 2, h % 2].astype(f32)
        dx, part = normed_rope_back(
            queries[:, lanes(h)].astype(f32), q_gain[...], cosine[...], sine[...], grad
        )
        q_cot[:, lanes(h)] = dx.astype(bf16)
        return total + gain_fold(part)

    q_total = lax.fori_loop(0, 16, query_head, jnp.zeros((8, 128), f32), unroll=4)
    send_x(0, 0)
    term_y.wait_recv()
    bulk("d_out", d_in.at[pl.ds(0, 8 * (count - 1)), :]).wait_recv()
    q_f32[pl.ds(0, 2 * chunks), :] = q_last[y] + q_end[...]
    for i in range(chunks):
        part = pl.ds(i * 128, 128)
        q_grad_out[:, part] = q_f32[pl.ds(i, 2, stride=chunks), :].astype(bf16)
        d_row = 8 * (i // 2) + i % 2
        d_grad_out[:, part] = d_in[pl.ds(d_row, 2, stride=2), :].astype(bf16)
    bulk("x_out_v", x_slots.at[1, pl.ds(0, 3)]).wait_recv()
    bulk("x_out_k", x_slots.at[0, pl.ds(0, 3)]).wait_recv()

    def key_head(g, total):
        v_cot[:, lanes(g)] = x_slots[1, g]
        dx, part = normed_rope_back(
            keys[:, lanes(g)].astype(f32), k_gain[...], cosine[...], sine[...],
            x_slots[0, g].astype(f32),
        )
        k_cot[:, lanes(g)] = dx.astype(bf16)
        return total + gain_fold(part)

    k_total = lax.fori_loop(0, 4, key_head, jnp.zeros((8, 128), f32), unroll=True)
    seq_slots[j, pl.ds(0, 4)] = q_total[:4] + q_total[4:]
    seq_slots[j, pl.ds(4, 4)] = k_total[:4] + k_total[4:]

    def gain_seq(p):
        return remote("gain_seq", seq_slots.at[j], seq_slots.at[j], 0, d, p)

    others(lambda p: gain_seq(p).start(), j)
    bulk("gain_seq", seq_slots.at[pl.ds(0, count - 1)]).wait_recv()
    dp_slots[d] = slot_sum(seq_slots)

    def gain_dp(p):
        return remote("gain_dp", dp_slots.at[d], dp_slots.at[d], 0, p, j)

    others(lambda p: gain_dp(p).start(), d)
    bulk("gain_dp", dp_slots.at[pl.ds(0, count - 1)]).wait_recv()
    gains = slot_sum(dp_slots)
    gains_out[0:1, :] = jnp.sum(gains[:4], axis=0, keepdims=True)
    gains_out[1:2, :] = jnp.sum(gains[4:], axis=0, keepdims=True)

    for name, ref in (
        ("q_msg", q_all.at[q_rows(0, count - 1), :]),
        ("p_msg", p_all.at[p_rows(0, count - 1), :]),
        ("tile", tiles.at[pl.ds(0, count - 1)]),
        ("part", q_part.at[pl.ds(0, count - 1), pl.ds(0, 16)]),
        ("span", spans.at[pl.ds(0, count - 1)]),
        ("tail_part", tail_slots.at[pl.ds(0, count - 1)]),
        ("d_out", d_in.at[pl.ds(0, 8 * (count - 1)), :]),
        ("term_x", q_in.at[pl.ds(0, 3)]),
        ("gain_seq", seq_slots.at[pl.ds(0, count - 1)]),
        ("gain_dp", dp_slots.at[pl.ds(0, count - 1)]),
        ("k_x", kv_stage.at[pl.ds(0, 3), 0]),
        ("v_x", kv_stage.at[pl.ds(0, 3), 1]),
        ("k_y", kv_h.at[0, :, 0, 0]),
        ("v_y", kv_h.at[1, :, 0, 0]),
        ("k_core", kv_h.at[0, :, 0, 0]),
        ("v_core", kv_h.at[1, :, 0, 0]),
        ("k_both", kv_h.at[0, :, 0, 0]),
        ("v_both", kv_h.at[1, :, 0, 0]),
        ("q", q_stage.at[pl.ds(0, 7)]),
        ("grad", grad_stage.at[pl.ds(0, 7)]),
        ("dq", dq_slots.at[pl.ds(0, 7)]),
        ("core_sum_k", core_slots.at[0]),
        ("core_sum_v", core_slots.at[1]),
        ("y_sum_k", y_stage.at[0]),
        ("y_sum_v", y_stage.at[1]),
        ("x_out_k", x_slots.at[0, pl.ds(0, 3)]),
        ("x_out_v", x_slots.at[1, pl.ds(0, 3)]),
    ):
        bulk(name, ref).wait_send()
    core_send.wait_send()
    term_y.wait_send()
    part_core.wait_send()
    w_targets(lambda copy: copy.wait_send())


def finish(loss, gains, *refs):
    size = (len(refs) - 3) // 2
    loss_out, q_out, k_out = refs[size : size + 3]
    loss_out[...] = loss[0:1, 0:1]
    q_out[...] = gains[0:1, :]
    k_out[...] = gains[1:2, :]
    for made, out in zip(refs[:size], refs[size + 3 :]):
        out[...] = made[...]


def shards(
    question_embedding_matrix,
    passage_embedding_matrix,
    positive,
    queries,
    keys,
    values,
    later_grad,
    lengths,
    q_gain,
    k_gain,
    out_weight,
):
    angles = np.arange(2048)[:, None] * rope_base ** (-2.0 * np.arange(64) / 128)[None, :]
    table = jnp.asarray(np.concatenate([np.cos(angles), np.sin(angles)], axis=1).astype(np.float32))
    out = jax.ShapeDtypeStruct
    vm = pltpu.VMEM
    smem = pl.BlockSpec(memory_space=pltpu.SMEM)
    anywhere = pl.BlockSpec(memory_space=pl.ANY)
    results = [
        out(question_embedding_matrix.shape, bf16),
        out(passage_embedding_matrix.shape, bf16),
        out(queries.shape[1:], bf16),
        out(keys.shape[1:], bf16),
        out(values.shape[1:], bf16),
    ]
    loss, gains, *made = pl.pallas_call(
        whole,
        out_shape=[out((1, 128), f32), out((2, 128), f32)] + results,
        in_specs=[smem, smem, anywhere] + [VMEM] * 9,
        out_specs=[VMEM] * 7,
        scratch_shapes=[
            vm((128, 128), f32),
            vm((128, 128), f32),
            vm((128, 128), f32),
            vm((2 * q_stride, 128), f32),
            vm((2 * chunks, 128), f32),
            vm((2 * q_stride * count, 128), bf16),
            vm((2 * chunks * count, 128), bf16),
            vm((2 * q_stride * count, 128), f32),
            vm((2 * chunks * count, 128), f32),
            vm((count, pairs, 256), bf16),
            vm((count, pairs, 256), bf16),
            vm((count, 8, 128), f32),
            vm((count, pairs, 256), bf16),
            vm((count, 16, 128), f32),
            vm((count, pairs, 256), bf16),
            vm((pairs * chunks, 128), f32),
            vm((pairs * chunks // 2, 128), f32),
            vm((4, 128, 128), f32),
            vm((4, 128, 128), f32),
            vm((2, 64, 128), f32),
            vm((64, 128), f32),
            vm((2 * pairs, 128), f32),
            vm((8 * count, 128), f32),
            vm((8 * count, 128), f32),
            vm((count, 8, 128), f32),
            vm((count, 8, 128), f32),
            vm((8, 128), f32),
            vm((2, 128, 256), bf16),
            vm((4, 2, 128, 128), bf16),
            vm((8, 2, 128, 128), bf16),
            vm((8, 2, 128, 128), bf16),
            vm((2, 4, 2, 2, 128, 128), bf16),
            vm((4, 2, 2, 128, 128), bf16),
            vm((4, 2, 2, 128, 128), bf16),
            vm((4, 512, 128), bf16),
            vm((4, 128, 512), f32),
            vm((4, 512, 256), bf16),
            vm((4, 512, 128), f32),
            vm((10, 512, 512), f32),
            vm((4, 4, 8, 512), f32),
            vm((4, 4, 8, 512), f32),
            vm((4, 4, 8, 512), f32),
            vm((4, 128, 512), f32),
            vm((4, 128, 512), bf16),
            vm((4, 128, 512), bf16),
            vm((128, 512), f32),
            vm((2, 4, 2, 2, 128, 128), f32),
            vm((4, 2, 2, 128, 128), bf16),
            vm((8, 2, 128, 128), bf16),
            vm((2, 4, 2, 128, 128), f32),
            vm((2, 4, 128, 128), f32),
            vm((2, 4, 128, 128), f32),
            vm((2, 4, 128, 128), bf16),
            vm((2, 4, 128, 128), bf16),
            vm((count, 8, 128), f32),
            vm((count, 8, 128), f32),
            pltpu.SemaphoreType.DMA((len(phases),)),
            pltpu.SemaphoreType.DMA((len(phases), 4)),
            pltpu.SemaphoreType.DMA((1,)),
        ],
        compiler_params=pltpu.CompilerParams(
            collective_id=0, has_side_effects=True, vmem_limit_bytes=limit
        ),
    )(
        lengths, positive, table, queries[0], keys[0], values[0], later_grad[0],
        question_embedding_matrix, passage_embedding_matrix, out_weight,
        q_gain[None, :], k_gain[None, :],
    )
    loss, q_gain_grad, k_gain_grad, query_grad, doc_grad, query_cot, key_cot, value_cot = (
        pl.pallas_call(
            finish,
            out_shape=[out((1, 1), f32), out((1, 128), f32), out((1, 128), f32)] + results,
            in_specs=[VMEM] * 7,
            out_specs=[VMEM] * 8,
        )(loss, gains, *made)
    )
    return (
        loss.reshape(()),
        query_grad,
        doc_grad,
        query_cot[None],
        key_cot[None],
        value_cot[None],
        q_gain_grad[0],
        k_gain_grad[0],
    )


def solution(mesh):
    in_specs = (
        P(("dp", "seq"), None),
        P(("dp", "seq"), None),
        P(("dp", "seq")),
        P("dp", "seq", None),
        P("dp", "seq", None),
        P("dp", "seq", None),
        P("dp", "seq", None),
        P("dp"),
        P(),
        P(),
        P("seq", "dp"),
    )
    out_specs = (
        P(),
        P(("dp", "seq"), None),
        P(("dp", "seq"), None),
        P("dp", "seq", None),
        P("dp", "seq", None),
        P("dp", "seq", None),
        P(),
        P(),
    )
    return jax.shard_map(
        shards, mesh=mesh, in_specs=in_specs, out_specs=out_specs, check_vma=False
    )
```

```python
import functools
import math

import jax
import jax.numpy as jnp
import numpy as np
from jax import lax
from jax.experimental import pallas as pl
from jax.experimental.pallas import tpu as pltpu
from jax.sharding import PartitionSpec as P

sharpness = 0.05
epsilon = 1e-06
rope_base = 1000000.0
lowest = -1e30
MESH = pl.DeviceIdType.MESH
f32 = jnp.float32
bf16 = jnp.bfloat16
VMEM = pl.BlockSpec(memory_space=pltpu.VMEM)
limit = 58 * 1024 * 1024
count = 16
pairs = 32
chunks = 32
q_stride = 40
scaling = 128 ** (-0.5)
phases = (
    "q_msg", "p_msg", "tile", "part", "part_core", "span", "tail_part", "w_out",
    "d_out", "term_core", "term_x", "term_y", "gain_seq", "gain_dp",
    "k_x", "k_y", "k_core", "k_both", "v_x", "v_y", "v_core", "v_both", "q", "grad", "dq", "core_sum_k", "core_sum_v", "y_sum_k", "y_sum_v",
    "x_out_k", "x_out_v",
)
phase_of = {name: i for i, name in enumerate(phases)}


def mm(a, b):
    return lax.dot_general(a, b, (((1,), (0,)), ((), ())), preferred_element_type=f32)


def mm_nt(a, b):
    return lax.dot_general(a, b, (((1,), (1,)), ((), ())), preferred_element_type=f32)


def mm_tn(a, b):
    return lax.dot_general(a, b, (((0,), (0,)), ((), ())), preferred_element_type=f32)


def loop(first, last, step, unroll=None):
    def body(i, carry):
        step(i)
        return carry

    lax.fori_loop(first, last, body, 0, unroll=unroll)


def swap_halves(x):
    return pltpu.roll(x, 64, 1)


def normed_rope(x, gain, cosine, sine):
    scale = lax.rsqrt(jnp.mean(x * x, axis=-1, keepdims=True) + epsilon)
    y = x * scale * gain
    return y * cosine + swap_halves(y) * sine


def normed_rope_back(x, gain, cosine, sine, grad):
    scale = lax.rsqrt(jnp.mean(x * x, axis=-1, keepdims=True) + epsilon)
    n = x * scale
    dy = grad * cosine - swap_halves(grad) * sine
    gain_part = dy * n
    dn = dy * gain
    dx = scale * (dn - n * jnp.mean(dn * n, axis=-1, keepdims=True))
    return dx, gain_part


def slot_sum(ref):
    total = ref[0]
    for i in range(1, count):
        total = total + ref[i]
    return total


def whole(
    lengths, positive_in, table, queries, keys, values, later, q_emb, p_emb, out_w, q_gain, k_gain,
    loss_out, gains_out, q_grad_out, d_grad_out, q_cot, k_cot, v_cot,
    turn, cosine, sine,
    q_f32, p_f32, q_all, p_all, q_wide, p_wide, q_cols, p_cols, tiles,
    q_part, spans, span_cat, q_terms, core_in, q_mid, q_in, q_last, q_end,
    d_sum, d_stage, d_in, tail_stage, tail_slots, tail_in, w_in,
    kv_stage, q_stage, grad_stage, kv_h, q_h, grad_h,
    grad_low, grad_turn, grad_cat, last_probs, scores, tops, sums, factors, attn, k_turn, v_turn, dq_acc, dkv, dq_stage, dq_slots,
    core_slots, y_stage, y_slots, x_stage, x_slots, seq_slots, dp_slots,
    send_sem, recv_sem, own_sem,
):
    d, j = lax.axis_index("dp"), lax.axis_index("seq")
    x, y, c = j // 4, (j // 2) % 2, j % 2
    z, low = d // 2, d % 2
    rank = 2 * x + c
    barrier = pltpu.get_barrier_semaphore()

    def remote(name, src, dst, slot, dp, seq):
        phase = phase_of[name]
        return pltpu.make_async_remote_copy(
            src_ref=src,
            dst_ref=dst,
            send_sem=send_sem.at[phase],
            recv_sem=recv_sem.at[phase, slot],
            device_id=(dp, seq),
            device_id_type=MESH,
        )

    def bulk(name, ref):
        return remote(name, ref, ref, 0, d, j)

    def others(step, me, size=count):
        for o in sorted(range(1, size), key=lambda o: abs(o - size // 2)):
            step(lax.rem(me + o, size))

    others(
        lambda p: pl.semaphore_signal(barrier, inc=1, device_id=(d, p), device_id_type=MESH), j
    )
    others(
        lambda p: pl.semaphore_signal(barrier, inc=1, device_id=(p, j), device_id_type=MESH), d
    )
    turn_copy = pltpu.make_async_copy(
        table.at[pl.ds(pl.multiple_of(j * 128, 128), 128)], turn, own_sem.at[0]
    )
    turn_copy.start()

    def lanes(h):
        return pl.ds(pl.multiple_of(h * 128, 128), 128)

    def q_rows(s, size=1):
        return pl.ds(pl.multiple_of(s * 2 * q_stride, 16), size * 2 * q_stride)

    def p_rows(s, size=1):
        return pl.ds(pl.multiple_of(s * 2 * chunks, 16), size * 2 * chunks)

    place = 8 * c + 2 * x + y
    q_f32[...] = jnp.zeros_like(q_f32)
    q_own, p_own = q_emb[...].astype(f32), p_emb[...].astype(f32)
    for i in range(chunks):
        q_f32[pl.ds(i, 2, stride=q_stride), :] = q_own[:, i * 128 : i * 128 + 128]
        p_f32[pl.ds(i, 2, stride=chunks), :] = p_own[:, i * 128 : i * 128 + 128]
    for i in range(2):
        index = positive_in[i]
        spot = i * q_stride + chunks
        q_f32[spot : spot + 1, :] = jnp.full((1, 128), index >> 1, jnp.int32).astype(f32)
        q_f32[spot + 1 : spot + 2, :] = jnp.full((1, 128), index & 1, jnp.int32).astype(f32)
    q_all[q_rows(place), :] = q_f32[...].astype(bf16)
    p_all[p_rows(d), :] = p_f32[...].astype(bf16)
    turn_copy.wait()
    first_half = lax.broadcasted_iota(jnp.int32, (128, 128), 1) < 64
    turned = swap_halves(turn[...])
    cosine[...] = jnp.where(first_half, turn[...], turned)
    sine[...] = jnp.where(first_half, -turned, turn[...])

    def stage_kv(g):
        rot = normed_rope(keys[:, lanes(g)].astype(f32), k_gain[...], cosine[...], sine[...])
        kv_stage[g, 0] = rot.astype(bf16)
        kv_stage[g, 1] = values[:, lanes(g)]

    loop(0, 4, stage_kv, unroll=True)
    pl.semaphore_wait(barrier, 2 * (count - 1))

    over_y = 4 * x + 2 * (1 - y) + c
    over_core = 4 * x + 2 * y + (1 - c)
    over_low = d + 1 - 2 * low

    def beside(p):
        return 4 * p + 2 * y + c

    def q_copy(p):
        rows = q_all.at[q_rows(place), :]
        return remote("q_msg", rows, rows, 0, d, p)

    def p_copy(p):
        rows = p_all.at[p_rows(d), :]
        return remote("p_msg", rows, rows, 0, p, j)

    others(lambda p: q_copy(p).start(), j)
    others(lambda p: p_copy(p).start(), d)

    def x_copies(t, step):
        def copy(to):
            name, src = ("k_x", "v_x")[t], kv_stage.at[to, t]
            step(remote(name, src, kv_h.at[t, x, y, c], 0, d, beside(to)))

        others(copy, x, 4)

    def kv_pass(t, way, of_y, of_core, seq):
        block = kv_h.at[t, :, of_y, of_core]
        return remote("kv"[t] + way, block, block, 0, d, seq)

    def pass_on(t):
        bulk(("k_x", "v_x")[t], kv_h.at[t, pl.ds(0, 3), y, c]).wait_recv()
        kv_pass(t, "_y", y, c, over_y).start()
        kv_pass(t, "_core", y, c, over_core).start()

    def pass_from_y(t):
        kv_pass(t, "_y", 1 - y, c, over_y).wait_recv()
        kv_pass(t, "_both", 1 - y, c, over_core).start()

    def kv_arrive(t):
        kv_pass(t, "_core", y, 1 - c, over_core).wait_recv()
        kv_pass(t, "_both", 1 - y, 1 - c, over_core).wait_recv()

    x_copies(0, lambda copy: copy.start())
    kv_h[:, x, y, c] = kv_stage[x]

    def stage_q(h):
        rot = normed_rope(queries[:, lanes(h)].astype(f32), q_gain[...], cosine[...], sine[...])
        q_stage[h // 2, h % 2] = rot.astype(bf16)

    def seat(r):
        return 4 * (r // 2) + 2 * y + r % 2

    def head_send(name, stage, held):
        others(
            lambda p: remote(
                name, stage.at[p], held.at[x, :, c], 0, d, seat(p)
            ).start(),
            rank,
            8,
        )
        held[x, :, c] = stage[rank]

    loop(0, 16, stage_q, unroll=4)

    def w_copy(slot, seq):
        return remote("w_out", out_w, w_in.at[slot], slot, d, seq)

    def w_targets(step):
        for b in range(2):
            to = 4 * x + 2 * b + y
            pl.when(to != j)(lambda to=to: step(w_copy(j % 2, to)))

    w_targets(lambda copy: copy.start())

    @pl.when(c == y)
    def _():
        w_in[j % 2] = out_w[...]

    pass_on(0)
    head_send("q", q_stage, q_h)

    def stage_grad(h):
        grad_stage[h // 2, h % 2] = later[:, lanes(h)]

    loop(0, 16, stage_grad)
    dkv[...] = jnp.zeros_like(dkv)

    bulk("q_msg", q_all.at[q_rows(0, count - 1), :]).wait_recv()
    bulk("p_msg", p_all.at[p_rows(0, count - 1), :]).wait_recv()
    q_wide[...] = q_all[...].astype(f32)
    p_wide[...] = p_all[...].astype(f32)
    for i in range(chunks):
        half = pl.ds((i % 2) * 128, 128)
        q_cols[i // 2, :, half] = q_wide[pl.ds(i, pairs, stride=q_stride), :].astype(bf16)
        p_cols[i // 2, :, half] = p_wide[pl.ds(i, pairs, stride=chunks), :].astype(bf16)
    positive = (
        2.0 * q_wide[pl.ds(chunks, pairs, stride=q_stride), :]
        + q_wide[pl.ds(chunks + 1, pairs, stride=q_stride), :]
    )

    def four(block):
        return jnp.concatenate([block] * (128 // pairs), axis=0)

    def one(block):
        return block[:32] + block[32:64] + block[64:96] + block[96:]

    logits = mm_nt(q_cols[0], four(p_cols[0]))
    for b in range(1, count):
        logits = logits + mm_nt(q_cols[b], four(p_cols[b]))
    logits = logits / sharpness
    quarter_of = lax.broadcasted_iota(jnp.int32, (8, 128), 1) >> 5

    def pack(block):
        packed = block[:8]
        for i in range(1, 4):
            packed = jnp.where(quarter_of == i, block[8 * i : 8 * i + 8], packed)
        return packed

    tiles[j] = pack(logits)

    def tile_copy(p):
        return remote("tile", tiles.at[j], tiles.at[j], 0, d, p)

    others(lambda p: tile_copy(p).start(), j)
    x_copies(1, lambda copy: copy.start())

    def half_of(core):
        return pl.ds(pl.multiple_of(16 * core, 16), 16)

    def part_copy(p):
        return remote(
            "part", q_cols.at[p, half_of(c)], q_part.at[d, half_of(c)], 0, p, j
        )

    others(lambda p: part_copy(p).start(), d)
    q_part[d, half_of(c)] = q_cols[d, half_of(c)]
    head_send("grad", grad_stage, grad_h)
    lane = lax.broadcasted_iota(jnp.int32, (pairs, 128), 1)
    line = lax.broadcasted_iota(jnp.int32, (pairs, 128), 0)
    real = (lane >> 5) == (line >> 3)
    base = jnp.where(real, ((lane & 31) >> 1) * pairs + (lane & 1), -(1 << 20)).astype(f32)

    pass_from_y(0)

    bulk("tile", tiles.at[pl.ds(0, count - 1)]).wait_recv()
    high = tiles[0]
    for i in range(1, count):
        high = jnp.maximum(high, tiles[i])
    high = jnp.max(jnp.where(real, four(high), lowest), axis=1, keepdims=True)
    mass = jnp.zeros((pairs, 128), f32)
    hit = jnp.zeros((pairs, 128), f32)
    for i in range(count):
        tile = four(tiles[i])
        mass = mass + jnp.where(real, jnp.exp(tile - high), 0.0)
        hit = hit + jnp.where(base + 2.0 * i == positive, tile, 0.0)
    log_total = high + jnp.log(jnp.sum(mass, axis=1, keepdims=True))
    picked = jnp.sum(hit, axis=1, keepdims=True)
    loss_part = jnp.sum(log_total - picked, axis=0, keepdims=True)

    def weights_of(tile, index):
        onehot = jnp.where(base + 2.0 * index == positive, 1.0, 0.0)
        return jnp.where(real, (jnp.exp(four(tile) - log_total) - onehot) / sharpness, 0.0)

    mine = weights_of(tiles[j], j.astype(f32)).astype(bf16)
    spans[d, pl.ds(0, 8)] = pack(weights_of(tiles[0], 0.0).astype(bf16).astype(f32))
    spans[d, pl.ds(8, 8)] = pack(mine.astype(f32))

    def span_copy(p):
        return remote("span", spans.at[d], spans.at[d], 0, p, j)

    others(lambda p: span_copy(p).start(), d)
    pass_on(1)

    kv_arrive(0)
    bulk("q", q_stage.at[pl.ds(0, 7)]).wait_recv()
    length = lengths[0]
    key_line = lax.broadcasted_iota(jnp.int32, (128, 1), 0)
    ahead = lax.broadcasted_iota(jnp.int32, (128, 256), 0) - lax.broadcasted_iota(
        jnp.int32, (128, 256), 1
    )
    tops[...] = jnp.full_like(tops, lowest)
    sums[...] = jnp.zeros_like(sums)

    def spot_of(a, b):
        return (a * (a + 1)) // 2 + b

    def softmax_rows(o):
        a = 3 - o

        def strips(b, diagonal):
            keys_b = kv_h[0, b].reshape(4, 128, 128)
            for half in range(2):
                q = q_h[a, half].reshape(256, 128)
                across = slice(half * 256, half * 256 + 256)
                for i in range(4):
                    start = b * 512 + i * 128
                    bias = jnp.where(key_line < length - start, 0.0, lowest)
                    s = mm_nt(keys_b[i], q) * (scaling * math.log2(math.e)) + bias
                    if diagonal:
                        s = jnp.where(ahead <= 256 * y - i * 128, s, lowest)
                    top = jnp.max(s, axis=0, keepdims=True)
                    e = jnp.exp2(s - top)
                    scores[spot_of(a, b), i * 128 : i * 128 + 128, across] = e
                    tops[a, b, i : i + 1, across] = top
                    sums[a, b, i : i + 1, across] = jnp.sum(e, axis=0, keepdims=True)

        loop(0, a, lambda b: strips(b, False))
        strips(a, True)
        part_tops = tops[a].reshape(32, 512)
        part = jnp.exp2(part_tops - jnp.max(part_tops, axis=0, keepdims=True))
        total = jnp.sum(part * sums[a].reshape(32, 512), axis=0, keepdims=True)
        factors[a] = (part * (1.0 / total)).reshape(4, 8, 512)

    softmax_rows(0)
    bulk("part", q_part.at[pl.ds(0, count - 1), pl.ds(0, 16)]).wait_recv()
    part_core = remote(
        "part_core", q_part.at[:, half_of(c)], q_part.at[:, half_of(c)], 0, d, over_core
    )
    part_core.start()
    softmax_rows(1)

    bulk("span", spans.at[pl.ds(0, count - 1)]).wait_recv()
    for i in range(count):
        for t in range(2):
            weights = jnp.where(real, four(spans[i, t * 8 : t * 8 + 8]), 0.0)
            span_cat[i, :, t * 128 : t * 128 + 128] = weights.astype(bf16)
    remote(
        "part_core", q_part.at[:, half_of(1 - c)], q_part.at[:, half_of(1 - c)], 0, d, over_core
    ).wait_recv()
    span_sums = mm_tn(
        span_cat[...].reshape(pairs * count, 256), q_part[...].reshape(pairs * count, 256)
    )
    span = one(span_sums[:128]).astype(bf16)
    d_sums = one(span_sums[128:])
    d_sum[pl.ds(0, pairs), :] = d_sums[:, :128]
    d_sum[pl.ds(pairs, pairs), :] = d_sums[:, 128:]
    for b in range(2):
        source = 4 * x + 2 * c + b
        pl.when(source != j)(lambda b=b, source=source: w_copy(b, source).wait_recv())
    rows_a, rows_b = mm_nt(span, w_in[0]), mm_nt(span, w_in[1])
    for i in range(count):
        tail_stage[i, pl.ds(0, 2)] = jnp.broadcast_to(rows_a[2 * i : 2 * i + 1], (2, 128))
        tail_stage[i, pl.ds(2, 2)] = jnp.broadcast_to(rows_b[2 * i : 2 * i + 1], (2, 128))
        tail_stage[i, pl.ds(4, 4)] = jnp.broadcast_to(loss_part, (4, 128))

    def tail_part(p):
        return remote("tail_part", tail_stage.at[p], tail_slots.at[d], 0, p, j)

    others(lambda p: tail_part(p).start(), d)
    tail_slots[d] = tail_stage[d]

    pass_from_y(1)
    loop(2, 4, softmax_rows)

    d_stage[...] = jnp.zeros_like(d_stage)
    for r in range(2):
        for half in range(2):
            d_stage[pl.ds(2 * r + half, count, stride=8), :] = d_sum[
                pl.ds(half * pairs + r, count, stride=2), :
            ]

    def d_rows(s):
        return pl.ds(pl.multiple_of(s * 8, 8), 8)

    def d_copy(p):
        return remote("d_out", d_stage.at[d_rows(p), :], d_in.at[d_rows(d), :], 0, p, j)

    others(lambda p: d_copy(p).start(), d)
    d_in[d_rows(d), :] = d_stage[d_rows(d), :]

    for b in range(count):
        q_term = mm(mine, four(p_cols[b]))
        for half in range(2):
            rows = pl.ds(2 * b + half, pairs, stride=chunks)
            q_terms[rows, :] = q_term[:, half * 128 : half * 128 + 128]
    core_send = remote("term_core", q_terms.at[p_rows(8 * (1 - c), 8), :], core_in, 0, d, over_core)
    core_send.start()
    kv_arrive(1)
    bulk("grad", grad_stage.at[pl.ds(0, 7)]).wait_recv()
    row = lax.broadcasted_iota(jnp.int32, (512, 1), 0)
    row_token = (row & 255) + 256 * y

    def core_copy(t, a):
        name = ("core_sum_k", "core_sum_v")[t]
        return remote(name, dkv.at[t, a, :, 1 - c], core_slots.at[t, a], a, d, over_core)

    def y_copy(t, a):
        return remote(("y_sum_k", "y_sum_v")[t], y_stage.at[t, a], y_slots.at[t, a], a, d, over_y)

    def x_copy(t, to):
        name = ("x_out_k", "x_out_v")[t]
        return remote(name, x_stage.at[t, to], x_slots.at[t, x], 0, d, beside(to))

    def dq_copy(a, e):
        return remote("dq", dq_stage.at[a, :, e], dq_slots.at[rank], 0, d, 4 * a + 2 * y + e)

    def send_y(t, a):
        core_copy(t, a).wait_recv()
        y_stage[t, a] = dkv[t, a, 1 - y, c] + core_slots[t, a, 1 - y]
        y_copy(t, a).start()

    def send_x(t, a):
        y_copy(t, a).wait_recv()
        total = dkv[t, a, y, c] + core_slots[t, a, y] + y_slots[t, a]
        x_stage[t, a] = total.astype(bf16)

        @pl.when(a != x)
        def _():
            x_copy(t, a).start()

        @pl.when(a == x)
        def _():
            x_slots[t, x] = x_stage[t, a]

    def make_grad(a):
        spot = row_token + 512 * a
        extra = jnp.where(row < 256, tail_in[0:1], tail_in[2:3])
        last = jnp.where(spot == length - 1, 1.0, 0.0)
        grad = grad_h[a].reshape(512, 128).astype(f32) + last * extra
        grad_low[a] = jnp.where(spot < length, grad, 0.0).astype(bf16)

    def turned_block(block):
        return jnp.transpose(block.reshape(512, 128).astype(f32))

    def turn_block(b):
        k_turn[b] = turned_block(kv_h[0, b]).astype(bf16)
        v_turn[b] = turned_block(kv_h[1, b]).astype(bf16)

    loop(0, 4, turn_block)

    last_lane = lax.broadcasted_iota(jnp.int32, (512, 128), 1)

    def first_grad(a):
        spot = row_token + 512 * a
        early = jnp.where(spot < length - 1, grad_h[a].reshape(512, 128).astype(f32), 0.0)
        grad_cat[a, :, :128] = early.astype(bf16)
        last = jnp.where(spot == length - 1, 1.0, 0.0)
        grad_cat[a, :, 128:] = jnp.where(last_lane == row >> 8, last, 0.0).astype(bf16)

    loop(0, 4, first_grad)
    last_probs[...] = jnp.zeros_like(last_probs)
    attn[...] = jnp.zeros_like(attn)

    def value_block(o):
        b = 3 - o

        def rows(a):
            spot = spot_of(a, b)
            low_b = jnp.concatenate(
                [
                    (scores[spot, i * 128 : i * 128 + 128] * factors[a, b, i : i + 1]).astype(bf16)
                    for i in range(4)
                ],
                axis=0,
            )
            terms = mm(low_b, grad_cat[a])
            dkv[1, b] += terms[:, :128].reshape(2, 2, 128, 128)
            last_probs[b] += terms[:, 128:]
            attn[a] += mm(v_turn[b], low_b)

        loop(b, 4, rows)

    loop(0, 4, value_block)
    core_send.wait_recv()
    both = q_terms[p_rows(8 * c, 8), :] + core_in[...]
    q_mid[...] = both.reshape(4, 128, 128)

    def term_x(p):
        return remote("term_x", q_mid.at[p], q_in.at[x], 0, d, beside(p))

    others(lambda p: term_x(p).start(), x, 4)
    q_in[x] = q_mid[x]

    bulk("tail_part", tail_slots.at[pl.ds(0, count - 1)]).wait_recv()
    tails = slot_sum(tail_slots)
    loss_out[...] = tails[4:5] / (pairs * count)
    tail_in[...] = tails

    last_grad = jnp.zeros((128, 128), f32)
    for a in range(4):
        last_grad = last_grad + mm_tn(grad_cat[a, :, 128:], grad_h[a].reshape(512, 128))
    head_line = lax.broadcasted_iota(jnp.int32, (128, 128), 0)
    both_tails = jnp.where(head_line == 0, tails[0:1], jnp.where(head_line == 1, tails[2:3], 0.0))
    last_low = (last_grad + both_tails).astype(bf16)

    def last_row(o):
        b = 3 - o
        dkv[1, b] += mm(last_probs[b].astype(bf16), last_low).reshape(2, 2, 128, 128)
        core_copy(1, b).start()

    loop(0, 4, last_row)

    def all_grad(a):
        make_grad(a)
        grad_turn[a] = turned_block(grad_low[a])

    loop(0, 4, all_grad)
    loop(0, 4, lambda o: send_y(1, 3 - o))

    def quarter(o):
        a = 3 - o
        q = q_h[a].reshape(512, 128)
        row_dot = jnp.sum(grad_turn[a] * attn[a], axis=0, keepdims=True)
        dq_acc[...] = jnp.zeros_like(dq_acc)

        def keys_of(b):
            spot = spot_of(a, b)
            values_b = kv_h[1, b].reshape(4, 128, 128)
            parts = []
            for i in range(4):
                prob_grad = mm_nt(values_b[i], grad_low[a])
                probs = scores[spot, i * 128 : i * 128 + 128] * (factors[a, b, i : i + 1] * scaling)
                parts.append((probs * (prob_grad - row_dot)).astype(bf16))
            sg = jnp.concatenate(parts, axis=0)
            dkv[0, b] += mm(sg, q).reshape(2, 2, 128, 128)
            dq_acc[...] += mm(k_turn[b], sg)

        loop(0, a + 1, keys_of)
        core_copy(0, a).start()
        dq_stage[a] = jnp.transpose(dq_acc[...]).astype(bf16).reshape(2, 2, 128, 128)
        for e in range(2):

            @pl.when(2 * a + e != rank)
            def _():
                dq_copy(a, e).start()

            @pl.when(2 * a + e == rank)
            def _():
                dq_slots[rank] = dq_stage[a, :, e]

        pl.when(o >= 1)(lambda: send_y(0, a + 1))
        send_x(1, a)
        pl.when(o >= 2)(lambda: send_x(0, a + 2))

    loop(0, 4, quarter)
    send_y(0, 0)
    bulk("term_x", q_in.at[pl.ds(0, 3)]).wait_recv()
    q_last[...] = (q_in[0] + q_in[1] + q_in[2] + q_in[3]).reshape(2, 64, 128)
    term_y = remote("term_y", q_last.at[1 - y], q_end, 0, d, over_y)
    term_y.start()
    send_x(0, 1)

    send_x(0, 0)
    bulk("dq", dq_slots.at[pl.ds(0, 7)]).wait_recv()

    def gain_fold(block):
        return jnp.sum(block.reshape(16, 8, 128), axis=0)

    def query_head(h, total):
        grad = dq_slots[h // 2, h % 2].astype(f32)
        dx, part = normed_rope_back(
            queries[:, lanes(h)].astype(f32), q_gain[...], cosine[...], sine[...], grad
        )
        q_cot[:, lanes(h)] = dx.astype(bf16)
        return total + gain_fold(part)

    q_total = lax.fori_loop(0, 16, query_head, jnp.zeros((8, 128), f32), unroll=8)
    term_y.wait_recv()
    bulk("d_out", d_in.at[pl.ds(0, 8 * (count - 1)), :]).wait_recv()
    q_f32[pl.ds(0, 2 * chunks), :] = q_last[y] + q_end[...]
    for i in range(chunks):
        part = pl.ds(i * 128, 128)
        q_grad_out[:, part] = q_f32[pl.ds(i, 2, stride=chunks), :].astype(bf16)
        d_row = 8 * (i // 2) + i % 2
        d_grad_out[:, part] = d_in[pl.ds(d_row, 2, stride=2), :].astype(bf16)
    bulk("x_out_v", x_slots.at[1, pl.ds(0, 3)]).wait_recv()
    bulk("x_out_k", x_slots.at[0, pl.ds(0, 3)]).wait_recv()

    def key_head(g, total):
        v_cot[:, lanes(g)] = x_slots[1, g]
        dx, part = normed_rope_back(
            keys[:, lanes(g)].astype(f32), k_gain[...], cosine[...], sine[...],
            x_slots[0, g].astype(f32),
        )
        k_cot[:, lanes(g)] = dx.astype(bf16)
        return total + gain_fold(part)

    k_total = lax.fori_loop(0, 4, key_head, jnp.zeros((8, 128), f32), unroll=True)
    seq_slots[j, pl.ds(0, 4)] = q_total[:4] + q_total[4:]
    seq_slots[j, pl.ds(4, 4)] = k_total[:4] + k_total[4:]

    def gain_seq(p):
        return remote("gain_seq", seq_slots.at[j], seq_slots.at[j], 0, d, p)

    others(lambda p: gain_seq(p).start(), j)
    bulk("gain_seq", seq_slots.at[pl.ds(0, count - 1)]).wait_recv()
    dp_slots[d] = slot_sum(seq_slots)

    def gain_dp(p):
        return remote("gain_dp", dp_slots.at[d], dp_slots.at[d], 0, p, j)

    others(lambda p: gain_dp(p).start(), d)
    bulk("gain_dp", dp_slots.at[pl.ds(0, count - 1)]).wait_recv()
    gains = slot_sum(dp_slots)
    gains_out[0:1, :] = jnp.sum(gains[:4], axis=0, keepdims=True)
    gains_out[1:2, :] = jnp.sum(gains[4:], axis=0, keepdims=True)

    for name, ref in (
        ("q_msg", q_all.at[q_rows(0, count - 1), :]),
        ("p_msg", p_all.at[p_rows(0, count - 1), :]),
        ("tile", tiles.at[pl.ds(0, count - 1)]),
        ("part", q_part.at[pl.ds(0, count - 1), pl.ds(0, 16)]),
        ("span", spans.at[pl.ds(0, count - 1)]),
        ("tail_part", tail_slots.at[pl.ds(0, count - 1)]),
        ("d_out", d_in.at[pl.ds(0, 8 * (count - 1)), :]),
        ("term_x", q_in.at[pl.ds(0, 3)]),
        ("gain_seq", seq_slots.at[pl.ds(0, count - 1)]),
        ("gain_dp", dp_slots.at[pl.ds(0, count - 1)]),
        ("k_x", kv_stage.at[pl.ds(0, 3), 0]),
        ("v_x", kv_stage.at[pl.ds(0, 3), 1]),
        ("k_y", kv_h.at[0, :, 0, 0]),
        ("v_y", kv_h.at[1, :, 0, 0]),
        ("k_core", kv_h.at[0, :, 0, 0]),
        ("v_core", kv_h.at[1, :, 0, 0]),
        ("k_both", kv_h.at[0, :, 0, 0]),
        ("v_both", kv_h.at[1, :, 0, 0]),
        ("q", q_stage.at[pl.ds(0, 7)]),
        ("grad", grad_stage.at[pl.ds(0, 7)]),
        ("dq", dq_slots.at[pl.ds(0, 7)]),
        ("core_sum_k", core_slots.at[0]),
        ("core_sum_v", core_slots.at[1]),
        ("y_sum_k", y_stage.at[0]),
        ("y_sum_v", y_stage.at[1]),
        ("x_out_k", x_slots.at[0, pl.ds(0, 3)]),
        ("x_out_v", x_slots.at[1, pl.ds(0, 3)]),
    ):
        bulk(name, ref).wait_send()
    core_send.wait_send()
    term_y.wait_send()
    part_core.wait_send()
    w_targets(lambda copy: copy.wait_send())


def finish(loss, gains, *refs):
    size = (len(refs) - 3) // 2
    loss_out, q_out, k_out = refs[size : size + 3]
    loss_out[...] = loss[0:1, 0:1]
    q_out[...] = gains[0:1, :]
    k_out[...] = gains[1:2, :]
    for made, out in zip(refs[:size], refs[size + 3 :]):
        out[...] = made[...]


def shards(
    question_embedding_matrix,
    passage_embedding_matrix,
    positive,
    queries,
    keys,
    values,
    later_grad,
    lengths,
    q_gain,
    k_gain,
    out_weight,
):
    angles = np.arange(2048)[:, None] * rope_base ** (-2.0 * np.arange(64) / 128)[None, :]
    table = jnp.asarray(np.concatenate([np.cos(angles), np.sin(angles)], axis=1).astype(np.float32))
    out = jax.ShapeDtypeStruct
    vm = pltpu.VMEM
    smem = pl.BlockSpec(memory_space=pltpu.SMEM)
    anywhere = pl.BlockSpec(memory_space=pl.ANY)
    results = [
        out(question_embedding_matrix.shape, bf16),
        out(passage_embedding_matrix.shape, bf16),
        out(queries.shape[1:], bf16),
        out(keys.shape[1:], bf16),
        out(values.shape[1:], bf16),
    ]
    loss, gains, *made = pl.pallas_call(
        whole,
        out_shape=[out((1, 128), f32), out((2, 128), f32)] + results,
        in_specs=[smem, smem, anywhere] + [VMEM] * 9,
        out_specs=[VMEM] * 7,
        scratch_shapes=[
            vm((128, 128), f32),
            vm((128, 128), f32),
            vm((128, 128), f32),
            vm((2 * q_stride, 128), f32),
            vm((2 * chunks, 128), f32),
            vm((2 * q_stride * count, 128), bf16),
            vm((2 * chunks * count, 128), bf16),
            vm((2 * q_stride * count, 128), f32),
            vm((2 * chunks * count, 128), f32),
            vm((count, pairs, 256), bf16),
            vm((count, pairs, 256), bf16),
            vm((count, 8, 128), f32),
            vm((count, pairs, 256), bf16),
            vm((count, 16, 128), f32),
            vm((count, pairs, 256), bf16),
            vm((pairs * chunks, 128), f32),
            vm((pairs * chunks // 2, 128), f32),
            vm((4, 128, 128), f32),
            vm((4, 128, 128), f32),
            vm((2, 64, 128), f32),
            vm((64, 128), f32),
            vm((2 * pairs, 128), f32),
            vm((8 * count, 128), f32),
            vm((8 * count, 128), f32),
            vm((count, 8, 128), f32),
            vm((count, 8, 128), f32),
            vm((8, 128), f32),
            vm((2, 128, 256), bf16),
            vm((4, 2, 128, 128), bf16),
            vm((8, 2, 128, 128), bf16),
            vm((8, 2, 128, 128), bf16),
            vm((2, 4, 2, 2, 128, 128), bf16),
            vm((4, 2, 2, 128, 128), bf16),
            vm((4, 2, 2, 128, 128), bf16),
            vm((4, 512, 128), bf16),
            vm((4, 128, 512), f32),
            vm((4, 512, 256), bf16),
            vm((4, 512, 128), f32),
            vm((10, 512, 512), f32),
            vm((4, 4, 8, 512), f32),
            vm((4, 4, 8, 512), f32),
            vm((4, 4, 8, 512), f32),
            vm((4, 128, 512), f32),
            vm((4, 128, 512), bf16),
            vm((4, 128, 512), bf16),
            vm((128, 512), f32),
            vm((2, 4, 2, 2, 128, 128), f32),
            vm((4, 2, 2, 128, 128), bf16),
            vm((8, 2, 128, 128), bf16),
            vm((2, 4, 2, 128, 128), f32),
            vm((2, 4, 128, 128), f32),
            vm((2, 4, 128, 128), f32),
            vm((2, 4, 128, 128), bf16),
            vm((2, 4, 128, 128), bf16),
            vm((count, 8, 128), f32),
            vm((count, 8, 128), f32),
            pltpu.SemaphoreType.DMA((len(phases),)),
            pltpu.SemaphoreType.DMA((len(phases), 4)),
            pltpu.SemaphoreType.DMA((1,)),
        ],
        compiler_params=pltpu.CompilerParams(
            collective_id=0, has_side_effects=True, vmem_limit_bytes=limit
        ),
    )(
        lengths, positive, table, queries[0], keys[0], values[0], later_grad[0],
        question_embedding_matrix, passage_embedding_matrix, out_weight,
        q_gain[None, :], k_gain[None, :],
    )
    loss, q_gain_grad, k_gain_grad, query_grad, doc_grad, query_cot, key_cot, value_cot = (
        pl.pallas_call(
            finish,
            out_shape=[out((1, 1), f32), out((1, 128), f32), out((1, 128), f32)] + results,
            in_specs=[VMEM] * 7,
            out_specs=[VMEM] * 8,
        )(loss, gains, *made)
    )
    return (
        loss.reshape(()),
        query_grad,
        doc_grad,
        query_cot[None],
        key_cot[None],
        value_cot[None],
        q_gain_grad[0],
        k_gain_grad[0],
    )


def solution(mesh):
    in_specs = (
        P(("dp", "seq"), None),
        P(("dp", "seq"), None),
        P(("dp", "seq")),
        P("dp", "seq", None),
        P("dp", "seq", None),
        P("dp", "seq", None),
        P("dp", "seq", None),
        P("dp"),
        P(),
        P(),
        P("seq", "dp"),
    )
    out_specs = (
        P(),
        P(("dp", "seq"), None),
        P(("dp", "seq"), None),
        P("dp", "seq", None),
        P("dp", "seq", None),
        P("dp", "seq", None),
        P(),
        P(),
    )
    return jax.shard_map(
        shards, mesh=mesh, in_specs=in_specs, out_specs=out_specs, check_vma=False
    )
```

```python
import functools
import math

import jax
import jax.numpy as jnp
import numpy as np
from jax import lax
from jax.experimental import pallas as pl
from jax.experimental.pallas import tpu as pltpu
from jax.sharding import PartitionSpec as P

sharpness = 0.05
epsilon = 1e-06
rope_base = 1000000.0
lowest = -1e30
MESH = pl.DeviceIdType.MESH
f32 = jnp.float32
bf16 = jnp.bfloat16
VMEM = pl.BlockSpec(memory_space=pltpu.VMEM)
limit = 58 * 1024 * 1024
count = 16
pairs = 32
chunks = 32
q_stride = 40
scaling = 128 ** (-0.5)
phases = (
    "q_msg", "p_msg", "tile", "part", "part_core", "span", "tail_part", "w_out",
    "d_out", "term_core", "term_x", "term_y", "gain_seq", "gain_dp",
    "k_x", "k_y", "k_core", "k_both", "v_x", "v_y", "v_core", "v_both", "q", "grad", "dq", "core_sum_k", "core_sum_v", "y_sum_k", "y_sum_v",
    "x_out_k", "x_out_v",
)
phase_of = {name: i for i, name in enumerate(phases)}


def mm(a, b):
    return lax.dot_general(a, b, (((1,), (0,)), ((), ())), preferred_element_type=f32)


def mm_nt(a, b):
    return lax.dot_general(a, b, (((1,), (1,)), ((), ())), preferred_element_type=f32)


def mm_tn(a, b):
    return lax.dot_general(a, b, (((0,), (0,)), ((), ())), preferred_element_type=f32)


def loop(first, last, step, unroll=None):
    def body(i, carry):
        step(i)
        return carry

    lax.fori_loop(first, last, body, 0, unroll=unroll)


def swap_halves(x):
    return pltpu.roll(x, 64, 1)


def normed_rope(x, gain, cosine, sine):
    scale = lax.rsqrt(jnp.mean(x * x, axis=-1, keepdims=True) + epsilon)
    y = x * scale * gain
    return y * cosine + swap_halves(y) * sine


def normed_rope_back(x, gain, cosine, sine, grad):
    scale = lax.rsqrt(jnp.mean(x * x, axis=-1, keepdims=True) + epsilon)
    n = x * scale
    dy = grad * cosine - swap_halves(grad) * sine
    gain_part = dy * n
    dn = dy * gain
    dx = scale * (dn - n * jnp.mean(dn * n, axis=-1, keepdims=True))
    return dx, gain_part


def slot_sum(ref):
    total = ref[0]
    for i in range(1, count):
        total = total + ref[i]
    return total


def whole(
    lengths, positive_in, table, queries, keys, values, later, q_emb, p_emb, out_w, q_gain, k_gain,
    loss_out, gains_out, q_grad_out, d_grad_out, q_cot, k_cot, v_cot,
    turn, cosine, sine,
    q_f32, p_f32, q_all, p_all, q_wide, p_wide, q_cols, p_cols, tiles,
    q_part, spans, span_cat, q_terms, core_in, q_mid, q_in, q_last, q_end,
    d_sum, d_stage, d_in, tail_stage, tail_slots, tail_in, w_in,
    kv_stage, q_stage, grad_stage, kv_h, q_h, grad_h,
    grad_low, grad_turn, grad_cat, last_probs, scores, tops, sums, factors, attn, k_turn, v_turn, dq_acc, dkv, dq_stage, dq_slots,
    core_slots, y_stage, y_slots, x_stage, x_slots, seq_slots, dp_slots,
    send_sem, recv_sem, own_sem,
):
    d, j = lax.axis_index("dp"), lax.axis_index("seq")
    x, y, c = j // 4, (j // 2) % 2, j % 2
    z, low = d // 2, d % 2
    rank = 2 * x + c
    barrier = pltpu.get_barrier_semaphore()

    def remote(name, src, dst, slot, dp, seq):
        phase = phase_of[name]
        return pltpu.make_async_remote_copy(
            src_ref=src,
            dst_ref=dst,
            send_sem=send_sem.at[phase],
            recv_sem=recv_sem.at[phase, slot],
            device_id=(dp, seq),
            device_id_type=MESH,
        )

    def bulk(name, ref):
        return remote(name, ref, ref, 0, d, j)

    def others(step, me, size=count):
        for o in sorted(range(1, size), key=lambda o: abs(o - size // 2)):
            step(lax.rem(me + o, size))

    others(
        lambda p: pl.semaphore_signal(barrier, inc=1, device_id=(d, p), device_id_type=MESH), j
    )
    others(
        lambda p: pl.semaphore_signal(barrier, inc=1, device_id=(p, j), device_id_type=MESH), d
    )
    turn_copy = pltpu.make_async_copy(
        table.at[pl.ds(pl.multiple_of(j * 128, 128), 128)], turn, own_sem.at[0]
    )
    turn_copy.start()

    def lanes(h):
        return pl.ds(pl.multiple_of(h * 128, 128), 128)

    def q_rows(s, size=1):
        return pl.ds(pl.multiple_of(s * 2 * q_stride, 16), size * 2 * q_stride)

    def p_rows(s, size=1):
        return pl.ds(pl.multiple_of(s * 2 * chunks, 16), size * 2 * chunks)

    place = 8 * c + 2 * x + y
    q_f32[...] = jnp.zeros_like(q_f32)
    q_own, p_own = q_emb[...].astype(f32), p_emb[...].astype(f32)
    for i in range(chunks):
        q_f32[pl.ds(i, 2, stride=q_stride), :] = q_own[:, i * 128 : i * 128 + 128]
        p_f32[pl.ds(i, 2, stride=chunks), :] = p_own[:, i * 128 : i * 128 + 128]
    for i in range(2):
        index = positive_in[i]
        spot = i * q_stride + chunks
        q_f32[spot : spot + 1, :] = jnp.full((1, 128), index >> 1, jnp.int32).astype(f32)
        q_f32[spot + 1 : spot + 2, :] = jnp.full((1, 128), index & 1, jnp.int32).astype(f32)
    q_all[q_rows(place), :] = q_f32[...].astype(bf16)
    p_all[p_rows(d), :] = p_f32[...].astype(bf16)
    turn_copy.wait()
    first_half = lax.broadcasted_iota(jnp.int32, (128, 128), 1) < 64
    turned = swap_halves(turn[...])
    cosine[...] = jnp.where(first_half, turn[...], turned)
    sine[...] = jnp.where(first_half, -turned, turn[...])

    def stage_kv(g):
        rot = normed_rope(keys[:, lanes(g)].astype(f32), k_gain[...], cosine[...], sine[...])
        kv_stage[g, 0] = rot.astype(bf16)
        kv_stage[g, 1] = values[:, lanes(g)]

    loop(0, 4, stage_kv, unroll=True)
    pl.semaphore_wait(barrier, 2 * (count - 1))

    over_y = 4 * x + 2 * (1 - y) + c
    over_core = 4 * x + 2 * y + (1 - c)
    over_low = d + 1 - 2 * low

    def beside(p):
        return 4 * p + 2 * y + c

    def q_copy(p):
        rows = q_all.at[q_rows(place), :]
        return remote("q_msg", rows, rows, 0, d, p)

    def p_copy(p):
        rows = p_all.at[p_rows(d), :]
        return remote("p_msg", rows, rows, 0, p, j)

    others(lambda p: q_copy(p).start(), j)
    others(lambda p: p_copy(p).start(), d)

    def x_copies(t, step):
        def copy(to):
            name, src = ("k_x", "v_x")[t], kv_stage.at[to, t]
            step(remote(name, src, kv_h.at[t, x, y, c], 0, d, beside(to)))

        others(copy, x, 4)

    def kv_pass(t, way, of_y, of_core, seq):
        block = kv_h.at[t, :, of_y, of_core]
        return remote("kv"[t] + way, block, block, 0, d, seq)

    def pass_on(t):
        bulk(("k_x", "v_x")[t], kv_h.at[t, pl.ds(0, 3), y, c]).wait_recv()
        kv_pass(t, "_y", y, c, over_y).start()
        kv_pass(t, "_core", y, c, over_core).start()

    def pass_from_y(t):
        kv_pass(t, "_y", 1 - y, c, over_y).wait_recv()
        kv_pass(t, "_both", 1 - y, c, over_core).start()

    def kv_arrive(t):
        kv_pass(t, "_core", y, 1 - c, over_core).wait_recv()
        kv_pass(t, "_both", 1 - y, 1 - c, over_core).wait_recv()

    x_copies(0, lambda copy: copy.start())
    kv_h[:, x, y, c] = kv_stage[x]

    def stage_q(h):
        rot = normed_rope(queries[:, lanes(h)].astype(f32), q_gain[...], cosine[...], sine[...])
        q_stage[h // 2, h % 2] = rot.astype(bf16)

    def seat(r):
        return 4 * (r // 2) + 2 * y + r % 2

    def head_send(name, stage, held):
        others(
            lambda p: remote(
                name, stage.at[p], held.at[x, :, c], 0, d, seat(p)
            ).start(),
            rank,
            8,
        )
        held[x, :, c] = stage[rank]

    loop(0, 16, stage_q, unroll=4)

    def w_copy(slot, seq):
        return remote("w_out", out_w, w_in.at[slot], slot, d, seq)

    def w_targets(step):
        for b in range(2):
            to = 4 * x + 2 * b + y
            pl.when(to != j)(lambda to=to: step(w_copy(j % 2, to)))

    w_targets(lambda copy: copy.start())

    @pl.when(c == y)
    def _():
        w_in[j % 2] = out_w[...]

    pass_on(0)
    head_send("q", q_stage, q_h)

    def stage_grad(h):
        grad_stage[h // 2, h % 2] = later[:, lanes(h)]

    loop(0, 16, stage_grad)
    dkv[...] = jnp.zeros_like(dkv)

    bulk("q_msg", q_all.at[q_rows(0, count - 1), :]).wait_recv()
    bulk("p_msg", p_all.at[p_rows(0, count - 1), :]).wait_recv()
    q_wide[...] = q_all[...].astype(f32)
    p_wide[...] = p_all[...].astype(f32)
    for i in range(chunks):
        half = pl.ds((i % 2) * 128, 128)
        q_cols[i // 2, :, half] = q_wide[pl.ds(i, pairs, stride=q_stride), :].astype(bf16)
        p_cols[i // 2, :, half] = p_wide[pl.ds(i, pairs, stride=chunks), :].astype(bf16)
    positive = (
        2.0 * q_wide[pl.ds(chunks, pairs, stride=q_stride), :]
        + q_wide[pl.ds(chunks + 1, pairs, stride=q_stride), :]
    )

    def four(block):
        return jnp.concatenate([block] * (128 // pairs), axis=0)

    def one(block):
        return block[:32] + block[32:64] + block[64:96] + block[96:]

    logits = mm_nt(q_cols[0], four(p_cols[0]))
    for b in range(1, count):
        logits = logits + mm_nt(q_cols[b], four(p_cols[b]))
    logits = logits / sharpness
    quarter_of = lax.broadcasted_iota(jnp.int32, (8, 128), 1) >> 5

    def pack(block):
        packed = block[:8]
        for i in range(1, 4):
            packed = jnp.where(quarter_of == i, block[8 * i : 8 * i + 8], packed)
        return packed

    tiles[j] = pack(logits)

    def tile_copy(p):
        return remote("tile", tiles.at[j], tiles.at[j], 0, d, p)

    others(lambda p: tile_copy(p).start(), j)
    x_copies(1, lambda copy: copy.start())
    head_send("grad", grad_stage, grad_h)

    def half_of(core):
        return pl.ds(pl.multiple_of(16 * core, 16), 16)

    def part_copy(p):
        return remote(
            "part", q_cols.at[p, half_of(c)], q_part.at[d, half_of(c)], 0, p, j
        )

    others(lambda p: part_copy(p).start(), d)
    q_part[d, half_of(c)] = q_cols[d, half_of(c)]
    lane = lax.broadcasted_iota(jnp.int32, (pairs, 128), 1)
    line = lax.broadcasted_iota(jnp.int32, (pairs, 128), 0)
    real = (lane >> 5) == (line >> 3)
    base = jnp.where(real, ((lane & 31) >> 1) * pairs + (lane & 1), -(1 << 20)).astype(f32)

    pass_from_y(0)

    bulk("tile", tiles.at[pl.ds(0, count - 1)]).wait_recv()
    high = tiles[0]
    for i in range(1, count):
        high = jnp.maximum(high, tiles[i])
    high = jnp.max(jnp.where(real, four(high), lowest), axis=1, keepdims=True)
    mass = jnp.zeros((pairs, 128), f32)
    hit = jnp.zeros((pairs, 128), f32)
    for i in range(count):
        tile = four(tiles[i])
        mass = mass + jnp.where(real, jnp.exp(tile - high), 0.0)
        hit = hit + jnp.where(base + 2.0 * i == positive, tile, 0.0)
    log_total = high + jnp.log(jnp.sum(mass, axis=1, keepdims=True))
    picked = jnp.sum(hit, axis=1, keepdims=True)
    loss_part = jnp.sum(log_total - picked, axis=0, keepdims=True)

    def weights_of(tile, index):
        onehot = jnp.where(base + 2.0 * index == positive, 1.0, 0.0)
        return jnp.where(real, (jnp.exp(four(tile) - log_total) - onehot) / sharpness, 0.0)

    mine = weights_of(tiles[j], j.astype(f32)).astype(bf16)
    spans[d, pl.ds(0, 8)] = pack(weights_of(tiles[0], 0.0).astype(bf16).astype(f32))
    spans[d, pl.ds(8, 8)] = pack(mine.astype(f32))

    def span_copy(p):
        return remote("span", spans.at[d], spans.at[d], 0, p, j)

    others(lambda p: span_copy(p).start(), d)
    pass_on(1)

    kv_arrive(0)
    bulk("q", q_stage.at[pl.ds(0, 7)]).wait_recv()
    length = lengths[0]
    key_line = lax.broadcasted_iota(jnp.int32, (128, 1), 0)
    ahead = lax.broadcasted_iota(jnp.int32, (128, 256), 0) - lax.broadcasted_iota(
        jnp.int32, (128, 256), 1
    )
    tops[...] = jnp.full_like(tops, lowest)
    sums[...] = jnp.zeros_like(sums)

    def spot_of(a, b):
        return (a * (a + 1)) // 2 + b

    def softmax_rows(o):
        a = 3 - o

        def strips(b, diagonal):
            keys_b = kv_h[0, b].reshape(4, 128, 128)
            for half in range(2):
                q = q_h[a, half].reshape(256, 128)
                across = slice(half * 256, half * 256 + 256)
                for i in range(4):
                    start = b * 512 + i * 128
                    bias = jnp.where(key_line < length - start, 0.0, lowest)
                    s = mm_nt(keys_b[i], q) * (scaling * math.log2(math.e)) + bias
                    if diagonal:
                        s = jnp.where(ahead <= 256 * y - i * 128, s, lowest)
                    top = jnp.max(s, axis=0, keepdims=True)
                    e = jnp.exp2(s - top)
                    scores[spot_of(a, b), i * 128 : i * 128 + 128, across] = e
                    tops[a, b, i : i + 1, across] = top
                    sums[a, b, i : i + 1, across] = jnp.sum(e, axis=0, keepdims=True)

        loop(0, a, lambda b: strips(b, False))
        strips(a, True)
        part_tops = tops[a].reshape(32, 512)
        part = jnp.exp2(part_tops - jnp.max(part_tops, axis=0, keepdims=True))
        total = jnp.sum(part * sums[a].reshape(32, 512), axis=0, keepdims=True)
        factors[a] = (part * (1.0 / total)).reshape(4, 8, 512)

    softmax_rows(0)
    bulk("part", q_part.at[pl.ds(0, count - 1), pl.ds(0, 16)]).wait_recv()
    part_core = remote(
        "part_core", q_part.at[:, half_of(c)], q_part.at[:, half_of(c)], 0, d, over_core
    )
    part_core.start()
    softmax_rows(1)

    bulk("span", spans.at[pl.ds(0, count - 1)]).wait_recv()
    for i in range(count):
        for t in range(2):
            weights = jnp.where(real, four(spans[i, t * 8 : t * 8 + 8]), 0.0)
            span_cat[i, :, t * 128 : t * 128 + 128] = weights.astype(bf16)
    remote(
        "part_core", q_part.at[:, half_of(1 - c)], q_part.at[:, half_of(1 - c)], 0, d, over_core
    ).wait_recv()
    span_sums = mm_tn(
        span_cat[...].reshape(pairs * count, 256), q_part[...].reshape(pairs * count, 256)
    )
    span = one(span_sums[:128]).astype(bf16)
    d_sums = one(span_sums[128:])
    d_sum[pl.ds(0, pairs), :] = d_sums[:, :128]
    d_sum[pl.ds(pairs, pairs), :] = d_sums[:, 128:]
    for b in range(2):
        source = 4 * x + 2 * c + b
        pl.when(source != j)(lambda b=b, source=source: w_copy(b, source).wait_recv())
    rows_a, rows_b = mm_nt(span, w_in[0]), mm_nt(span, w_in[1])
    for i in range(count):
        tail_stage[i, pl.ds(0, 2)] = jnp.broadcast_to(rows_a[2 * i : 2 * i + 1], (2, 128))
        tail_stage[i, pl.ds(2, 2)] = jnp.broadcast_to(rows_b[2 * i : 2 * i + 1], (2, 128))
        tail_stage[i, pl.ds(4, 4)] = jnp.broadcast_to(loss_part, (4, 128))

    def tail_part(p):
        return remote("tail_part", tail_stage.at[p], tail_slots.at[d], 0, p, j)

    others(lambda p: tail_part(p).start(), d)
    tail_slots[d] = tail_stage[d]

    pass_from_y(1)
    loop(2, 4, softmax_rows)

    d_stage[...] = jnp.zeros_like(d_stage)
    for r in range(2):
        for half in range(2):
            d_stage[pl.ds(2 * r + half, count, stride=8), :] = d_sum[
                pl.ds(half * pairs + r, count, stride=2), :
            ]

    def d_rows(s):
        return pl.ds(pl.multiple_of(s * 8, 8), 8)

    def d_copy(p):
        return remote("d_out", d_stage.at[d_rows(p), :], d_in.at[d_rows(d), :], 0, p, j)

    others(lambda p: d_copy(p).start(), d)
    d_in[d_rows(d), :] = d_stage[d_rows(d), :]

    for b in range(count):
        q_term = mm(mine, four(p_cols[b]))
        for half in range(2):
            rows = pl.ds(2 * b + half, pairs, stride=chunks)
            q_terms[rows, :] = q_term[:, half * 128 : half * 128 + 128]
    core_send = remote("term_core", q_terms.at[p_rows(8 * (1 - c), 8), :], core_in, 0, d, over_core)
    core_send.start()
    kv_arrive(1)
    bulk("grad", grad_stage.at[pl.ds(0, 7)]).wait_recv()
    row = lax.broadcasted_iota(jnp.int32, (512, 1), 0)
    row_token = (row & 255) + 256 * y

    def core_copy(t, a):
        name = ("core_sum_k", "core_sum_v")[t]
        return remote(name, dkv.at[t, a, :, 1 - c], core_slots.at[t, a], a, d, over_core)

    def y_copy(t, a):
        return remote(("y_sum_k", "y_sum_v")[t], y_stage.at[t, a], y_slots.at[t, a], a, d, over_y)

    def x_copy(t, to):
        name = ("x_out_k", "x_out_v")[t]
        return remote(name, x_stage.at[t, to], x_slots.at[t, x], 0, d, beside(to))

    def dq_copy(a, e):
        return remote("dq", dq_stage.at[a, :, e], dq_slots.at[rank], 0, d, 4 * a + 2 * y + e)

    def send_y(t, a):
        core_copy(t, a).wait_recv()
        y_stage[t, a] = dkv[t, a, 1 - y, c] + core_slots[t, a, 1 - y]
        y_copy(t, a).start()

    def send_x(t, a):
        y_copy(t, a).wait_recv()
        total = dkv[t, a, y, c] + core_slots[t, a, y] + y_slots[t, a]
        x_stage[t, a] = total.astype(bf16)

        @pl.when(a != x)
        def _():
            x_copy(t, a).start()

        @pl.when(a == x)
        def _():
            x_slots[t, x] = x_stage[t, a]

    def make_grad(a):
        spot = row_token + 512 * a
        extra = jnp.where(row < 256, tail_in[0:1], tail_in[2:3])
        last = jnp.where(spot == length - 1, 1.0, 0.0)
        grad = grad_h[a].reshape(512, 128).astype(f32) + last * extra
        grad_low[a] = jnp.where(spot < length, grad, 0.0).astype(bf16)

    def turned_block(block):
        return jnp.transpose(block.reshape(512, 128).astype(f32))

    def turn_block(b):
        k_turn[b] = turned_block(kv_h[0, b]).astype(bf16)
        v_turn[b] = turned_block(kv_h[1, b]).astype(bf16)

    loop(0, 4, turn_block)

    last_lane = lax.broadcasted_iota(jnp.int32, (512, 128), 1)

    def first_grad(a):
        spot = row_token + 512 * a
        early = jnp.where(spot < length - 1, grad_h[a].reshape(512, 128).astype(f32), 0.0)
        grad_cat[a, :, :128] = early.astype(bf16)
        last = jnp.where(spot == length - 1, 1.0, 0.0)
        grad_cat[a, :, 128:] = jnp.where(last_lane == row >> 8, last, 0.0).astype(bf16)

    loop(0, 4, first_grad)
    last_probs[...] = jnp.zeros_like(last_probs)
    attn[...] = jnp.zeros_like(attn)

    def value_block(o):
        b = 3 - o

        def rows(a):
            spot = spot_of(a, b)
            low_b = jnp.concatenate(
                [
                    (scores[spot, i * 128 : i * 128 + 128] * factors[a, b, i : i + 1]).astype(bf16)
                    for i in range(4)
                ],
                axis=0,
            )
            terms = mm(low_b, grad_cat[a])
            dkv[1, b] += terms[:, :128].reshape(2, 2, 128, 128)
            last_probs[b] += terms[:, 128:]
            attn[a] += mm(v_turn[b], low_b)

        loop(b, 4, rows)

    loop(0, 4, value_block)
    core_send.wait_recv()
    both = q_terms[p_rows(8 * c, 8), :] + core_in[...]
    q_mid[...] = both.reshape(4, 128, 128)

    def term_x(p):
        return remote("term_x", q_mid.at[p], q_in.at[x], 0, d, beside(p))

    others(lambda p: term_x(p).start(), x, 4)
    q_in[x] = q_mid[x]

    bulk("tail_part", tail_slots.at[pl.ds(0, count - 1)]).wait_recv()
    tails = slot_sum(tail_slots)
    loss_out[...] = tails[4:5] / (pairs * count)
    tail_in[...] = tails

    last_grad = jnp.zeros((128, 128), f32)
    for a in range(4):
        last_grad = last_grad + mm_tn(grad_cat[a, :, 128:], grad_h[a].reshape(512, 128))
    head_line = lax.broadcasted_iota(jnp.int32, (128, 128), 0)
    both_tails = jnp.where(head_line == 0, tails[0:1], jnp.where(head_line == 1, tails[2:3], 0.0))
    last_low = (last_grad + both_tails).astype(bf16)

    def last_row(o):
        b = 3 - o
        dkv[1, b] += mm(last_probs[b].astype(bf16), last_low).reshape(2, 2, 128, 128)
        core_copy(1, b).start()

    loop(0, 4, last_row)

    def all_grad(a):
        make_grad(a)
        grad_turn[a] = turned_block(grad_low[a])

    loop(0, 4, all_grad)
    loop(0, 4, lambda o: send_y(1, 3 - o))

    def quarter(o):
        a = 3 - o
        q = q_h[a].reshape(512, 128)
        row_dot = jnp.sum(grad_turn[a] * attn[a], axis=0, keepdims=True)
        dq_acc[...] = jnp.zeros_like(dq_acc)

        def keys_of(b):
            spot = spot_of(a, b)
            values_b = kv_h[1, b].reshape(4, 128, 128)
            parts = []
            for i in range(4):
                prob_grad = mm_nt(values_b[i], grad_low[a])
                probs = scores[spot, i * 128 : i * 128 + 128] * (factors[a, b, i : i + 1] * scaling)
                parts.append((probs * (prob_grad - row_dot)).astype(bf16))
            sg = jnp.concatenate(parts, axis=0)
            dkv[0, b] += mm(sg, q).reshape(2, 2, 128, 128)
            dq_acc[...] += mm(k_turn[b], sg)

        loop(0, a + 1, keys_of)
        core_copy(0, a).start()
        dq_stage[a] = jnp.transpose(dq_acc[...]).astype(bf16).reshape(2, 2, 128, 128)
        for e in range(2):

            @pl.when(2 * a + e != rank)
            def _():
                dq_copy(a, e).start()

            @pl.when(2 * a + e == rank)
            def _():
                dq_slots[rank] = dq_stage[a, :, e]

        pl.when(o >= 1)(lambda: send_y(0, a + 1))
        send_x(1, a)
        pl.when(o >= 2)(lambda: send_x(0, a + 2))

    loop(0, 4, quarter)
    send_y(0, 0)
    bulk("term_x", q_in.at[pl.ds(0, 3)]).wait_recv()
    q_last[...] = (q_in[0] + q_in[1] + q_in[2] + q_in[3]).reshape(2, 64, 128)
    term_y = remote("term_y", q_last.at[1 - y], q_end, 0, d, over_y)
    term_y.start()
    send_x(0, 1)

    send_x(0, 0)
    bulk("dq", dq_slots.at[pl.ds(0, 7)]).wait_recv()

    def gain_fold(block):
        return jnp.sum(block.reshape(16, 8, 128), axis=0)

    def query_head(h, total):
        grad = dq_slots[h // 2, h % 2].astype(f32)
        dx, part = normed_rope_back(
            queries[:, lanes(h)].astype(f32), q_gain[...], cosine[...], sine[...], grad
        )
        q_cot[:, lanes(h)] = dx.astype(bf16)
        return total + gain_fold(part)

    q_total = lax.fori_loop(0, 16, query_head, jnp.zeros((8, 128), f32), unroll=8)
    term_y.wait_recv()
    bulk("d_out", d_in.at[pl.ds(0, 8 * (count - 1)), :]).wait_recv()
    q_f32[pl.ds(0, 2 * chunks), :] = q_last[y] + q_end[...]
    for i in range(chunks):
        part = pl.ds(i * 128, 128)
        q_grad_out[:, part] = q_f32[pl.ds(i, 2, stride=chunks), :].astype(bf16)
        d_row = 8 * (i // 2) + i % 2
        d_grad_out[:, part] = d_in[pl.ds(d_row, 2, stride=2), :].astype(bf16)
    bulk("x_out_v", x_slots.at[1, pl.ds(0, 3)]).wait_recv()
    bulk("x_out_k", x_slots.at[0, pl.ds(0, 3)]).wait_recv()

    def key_head(g, total):
        v_cot[:, lanes(g)] = x_slots[1, g]
        dx, part = normed_rope_back(
            keys[:, lanes(g)].astype(f32), k_gain[...], cosine[...], sine[...],
            x_slots[0, g].astype(f32),
        )
        k_cot[:, lanes(g)] = dx.astype(bf16)
        return total + gain_fold(part)

    k_total = lax.fori_loop(0, 4, key_head, jnp.zeros((8, 128), f32), unroll=True)
    seq_slots[j, pl.ds(0, 4)] = q_total[:4] + q_total[4:]
    seq_slots[j, pl.ds(4, 4)] = k_total[:4] + k_total[4:]

    def gain_seq(p):
        return remote("gain_seq", seq_slots.at[j], seq_slots.at[j], 0, d, p)

    others(lambda p: gain_seq(p).start(), j)
    bulk("gain_seq", seq_slots.at[pl.ds(0, count - 1)]).wait_recv()
    dp_slots[d] = slot_sum(seq_slots)

    def gain_dp(p):
        return remote("gain_dp", dp_slots.at[d], dp_slots.at[d], 0, p, j)

    others(lambda p: gain_dp(p).start(), d)
    bulk("gain_dp", dp_slots.at[pl.ds(0, count - 1)]).wait_recv()
    gains = slot_sum(dp_slots)
    gains_out[0:1, :] = jnp.sum(gains[:4], axis=0, keepdims=True)
    gains_out[1:2, :] = jnp.sum(gains[4:], axis=0, keepdims=True)

    for name, ref in (
        ("q_msg", q_all.at[q_rows(0, count - 1), :]),
        ("p_msg", p_all.at[p_rows(0, count - 1), :]),
        ("tile", tiles.at[pl.ds(0, count - 1)]),
        ("part", q_part.at[pl.ds(0, count - 1), pl.ds(0, 16)]),
        ("span", spans.at[pl.ds(0, count - 1)]),
        ("tail_part", tail_slots.at[pl.ds(0, count - 1)]),
        ("d_out", d_in.at[pl.ds(0, 8 * (count - 1)), :]),
        ("term_x", q_in.at[pl.ds(0, 3)]),
        ("gain_seq", seq_slots.at[pl.ds(0, count - 1)]),
        ("gain_dp", dp_slots.at[pl.ds(0, count - 1)]),
        ("k_x", kv_stage.at[pl.ds(0, 3), 0]),
        ("v_x", kv_stage.at[pl.ds(0, 3), 1]),
        ("k_y", kv_h.at[0, :, 0, 0]),
        ("v_y", kv_h.at[1, :, 0, 0]),
        ("k_core", kv_h.at[0, :, 0, 0]),
        ("v_core", kv_h.at[1, :, 0, 0]),
        ("k_both", kv_h.at[0, :, 0, 0]),
        ("v_both", kv_h.at[1, :, 0, 0]),
        ("q", q_stage.at[pl.ds(0, 7)]),
        ("grad", grad_stage.at[pl.ds(0, 7)]),
        ("dq", dq_slots.at[pl.ds(0, 7)]),
        ("core_sum_k", core_slots.at[0]),
        ("core_sum_v", core_slots.at[1]),
        ("y_sum_k", y_stage.at[0]),
        ("y_sum_v", y_stage.at[1]),
        ("x_out_k", x_slots.at[0, pl.ds(0, 3)]),
        ("x_out_v", x_slots.at[1, pl.ds(0, 3)]),
    ):
        bulk(name, ref).wait_send()
    core_send.wait_send()
    term_y.wait_send()
    part_core.wait_send()
    w_targets(lambda copy: copy.wait_send())


def finish(loss, gains, *refs):
    size = (len(refs) - 3) // 2
    loss_out, q_out, k_out = refs[size : size + 3]
    loss_out[...] = loss[0:1, 0:1]
    q_out[...] = gains[0:1, :]
    k_out[...] = gains[1:2, :]
    for made, out in zip(refs[:size], refs[size + 3 :]):
        out[...] = made[...]


def shards(
    question_embedding_matrix,
    passage_embedding_matrix,
    positive,
    queries,
    keys,
    values,
    later_grad,
    lengths,
    q_gain,
    k_gain,
    out_weight,
):
    angles = np.arange(2048)[:, None] * rope_base ** (-2.0 * np.arange(64) / 128)[None, :]
    table = jnp.asarray(np.concatenate([np.cos(angles), np.sin(angles)], axis=1).astype(np.float32))
    out = jax.ShapeDtypeStruct
    vm = pltpu.VMEM
    smem = pl.BlockSpec(memory_space=pltpu.SMEM)
    anywhere = pl.BlockSpec(memory_space=pl.ANY)
    results = [
        out(question_embedding_matrix.shape, bf16),
        out(passage_embedding_matrix.shape, bf16),
        out(queries.shape[1:], bf16),
        out(keys.shape[1:], bf16),
        out(values.shape[1:], bf16),
    ]
    loss, gains, *made = pl.pallas_call(
        whole,
        out_shape=[out((1, 128), f32), out((2, 128), f32)] + results,
        in_specs=[smem, smem, anywhere] + [VMEM] * 9,
        out_specs=[VMEM] * 7,
        scratch_shapes=[
            vm((128, 128), f32),
            vm((128, 128), f32),
            vm((128, 128), f32),
            vm((2 * q_stride, 128), f32),
            vm((2 * chunks, 128), f32),
            vm((2 * q_stride * count, 128), bf16),
            vm((2 * chunks * count, 128), bf16),
            vm((2 * q_stride * count, 128), f32),
            vm((2 * chunks * count, 128), f32),
            vm((count, pairs, 256), bf16),
            vm((count, pairs, 256), bf16),
            vm((count, 8, 128), f32),
            vm((count, pairs, 256), bf16),
            vm((count, 16, 128), f32),
            vm((count, pairs, 256), bf16),
            vm((pairs * chunks, 128), f32),
            vm((pairs * chunks // 2, 128), f32),
            vm((4, 128, 128), f32),
            vm((4, 128, 128), f32),
            vm((2, 64, 128), f32),
            vm((64, 128), f32),
            vm((2 * pairs, 128), f32),
            vm((8 * count, 128), f32),
            vm((8 * count, 128), f32),
            vm((count, 8, 128), f32),
            vm((count, 8, 128), f32),
            vm((8, 128), f32),
            vm((2, 128, 256), bf16),
            vm((4, 2, 128, 128), bf16),
            vm((8, 2, 128, 128), bf16),
            vm((8, 2, 128, 128), bf16),
            vm((2, 4, 2, 2, 128, 128), bf16),
            vm((4, 2, 2, 128, 128), bf16),
            vm((4, 2, 2, 128, 128), bf16),
            vm((4, 512, 128), bf16),
            vm((4, 128, 512), f32),
            vm((4, 512, 256), bf16),
            vm((4, 512, 128), f32),
            vm((10, 512, 512), f32),
            vm((4, 4, 8, 512), f32),
            vm((4, 4, 8, 512), f32),
            vm((4, 4, 8, 512), f32),
            vm((4, 128, 512), f32),
            vm((4, 128, 512), bf16),
            vm((4, 128, 512), bf16),
            vm((128, 512), f32),
            vm((2, 4, 2, 2, 128, 128), f32),
            vm((4, 2, 2, 128, 128), bf16),
            vm((8, 2, 128, 128), bf16),
            vm((2, 4, 2, 128, 128), f32),
            vm((2, 4, 128, 128), f32),
            vm((2, 4, 128, 128), f32),
            vm((2, 4, 128, 128), bf16),
            vm((2, 4, 128, 128), bf16),
            vm((count, 8, 128), f32),
            vm((count, 8, 128), f32),
            pltpu.SemaphoreType.DMA((len(phases),)),
            pltpu.SemaphoreType.DMA((len(phases), 4)),
            pltpu.SemaphoreType.DMA((1,)),
        ],
        compiler_params=pltpu.CompilerParams(
            collective_id=0, has_side_effects=True, vmem_limit_bytes=limit
        ),
    )(
        lengths, positive, table, queries[0], keys[0], values[0], later_grad[0],
        question_embedding_matrix, passage_embedding_matrix, out_weight,
        q_gain[None, :], k_gain[None, :],
    )
    loss, q_gain_grad, k_gain_grad, query_grad, doc_grad, query_cot, key_cot, value_cot = (
        pl.pallas_call(
            finish,
            out_shape=[out((1, 1), f32), out((1, 128), f32), out((1, 128), f32)] + results,
            in_specs=[VMEM] * 7,
            out_specs=[VMEM] * 8,
        )(loss, gains, *made)
    )
    return (
        loss.reshape(()),
        query_grad,
        doc_grad,
        query_cot[None],
        key_cot[None],
        value_cot[None],
        q_gain_grad[0],
        k_gain_grad[0],
    )


def solution(mesh):
    in_specs = (
        P(("dp", "seq"), None),
        P(("dp", "seq"), None),
        P(("dp", "seq")),
        P("dp", "seq", None),
        P("dp", "seq", None),
        P("dp", "seq", None),
        P("dp", "seq", None),
        P("dp"),
        P(),
        P(),
        P("seq", "dp"),
    )
    out_specs = (
        P(),
        P(("dp", "seq"), None),
        P(("dp", "seq"), None),
        P("dp", "seq", None),
        P("dp", "seq", None),
        P("dp", "seq", None),
        P(),
        P(),
    )
    return jax.shard_map(
        shards, mesh=mesh, in_specs=in_specs, out_specs=out_specs, check_vma=False
    )
```
